32 devices in a mesh: row: 8 (over y, x, core), col: 4 (over z).
Axes of the slice: x: 2, y: 2, z: 4, core: 2. Of those that a mesh axis runs over, the one named last changes fastest.
Arguments:
- hidden: bfloat16 [3072, 5120], P('row', 'col'), may hold values from -6 to 6
- modulation: float32 [2, 5120], replicated, may hold values from -3 to 3
- w_query: bfloat16 [5120, 5120], P('row', 'col'), may hold values from -2 to 2
- w_key: bfloat16 [5120, 5120], P('row', 'col'), may hold values from -2 to 2
- w_value: bfloat16 [5120, 5120], P('row', 'col'), may hold values from -0.078125 to 0.078125
- q_gain: float32 [5120], P('col'), may hold values from 0.4 to 4.3
- k_gain: float32 [5120], P('col'), may hold values from 0.4 to 4.3
- positions: int32 [3, 3072], P(None, 'row'), may hold values from 0 to 63
- segment_ids: int32 [3072], replicated, may hold values from 0 to 11, never falling along the last dimension, each value on 1 to 1536 neighbouring positions
- page_table: int32 [24], replicated, may hold values from 0 to 23, each once
Outputs:
- attended: bfloat16 [3072, 5120], P('row', 'col')
- page_store: bfloat16 [2, 24, 128, 5120], P(None, 'row', None, 'col')
The draws below stay inside these ranges and needn't reach their ends.
Inputs may be any that keep to these rules, and one draw needn't show every extreme that they name: `segment_ids`: segment numbers never fall along the tokens; each segment holds at most 1536 tokens, and one holds exactly 1536. `page_table`: every slot is named by exactly one block.
All inputs are finite; a program needn't handle non-finite values.
Results may differ from the reference program's by a relative error of at most 0.015.
Values may be sent and summed in bfloat16 or wider, within the bound.
No kernel may reach another device: no remote copies, remote signals or barrier semaphores. Data moves between devices by JAX's collectives and lax.ppermute only.
A program may use at most 128 MiB of HBM per device.

```python
import math
import jax
import jax.numpy as jnp
import numpy as np
from jax import lax

D = 5120
HEADS = 40
HEAD_DIM = 128
PAGE = 128
SEGS = 12
TOKENS = 3072
MOST = 1536
PAGES = 24
FEAT_BLK = 640


def column_scale(key):
    fraction = jnp.arange(D, dtype=jnp.float32) / (D - 1)
    spread = jax.random.uniform(key, (D,), jnp.float32, 0.0, math.log(4.0))
    return jnp.exp(math.log(3.0) * fraction + spread)


def draw_w_query(key, part):
    shared = jax.random.normal(jax.random.fold_in(key, 1), (D, D), jnp.float32)
    return (shared * D ** (-0.5) * column_scale(jax.random.fold_in(key, 3))).astype(jnp.bfloat16)


def draw_w_key(key, part):
    separate = jax.random.normal(jax.random.fold_in(key, 2), (D, D), jnp.float32)
    mixture = separate
    scaled = column_scale(jax.random.fold_in(key, 4))
    return (mixture * D ** (-0.5) * scaled).astype(jnp.bfloat16)


def gain_draw(key):
    jitter = jax.random.uniform(jax.random.fold_in(key, 5), (D,), jnp.float32, 0.6, 1.6)
    return jitter


def draw_q_gain(key, part):
    return gain_draw(jax.random.fold_in(key, 21))


def draw_k_gain(key, part):
    return gain_draw(jax.random.fold_in(key, 22))


def plant(result, rng, smallest, high):
    longest = result.shape.index(max(result.shape))
    spots = []
    for shift in (0, 1):
        where = [jax.random.randint(jax.random.fold_in(rng, axis), (), 0, length) for axis, length in enumerate(result.shape)]
        where[longest] = (where[longest] + shift) % result.shape[longest]
        spots.append(tuple(where))
    return result.at[spots[0]].set(smallest).at[spots[1]].set(high)


def shard_levels(key, dims, pieces, low, top_value):
    factor_of = 1.0
    for axis_at, parts in pieces:
        draws = jax.random.uniform(jax.random.fold_in(jax.random.fold_in(key, 6), axis_at), (parts,), jnp.float32, low / len(pieces), top_value / len(pieces))
        factor_of = factor_of * jnp.repeat(jnp.exp(draws), dims[axis_at] // parts).reshape((-1,) + (1,) * (len(dims) - 1 - axis_at))
    return factor_of


def length_profile(amount, total, reach, skew):
    portions = [(1 << 20) // math.isqrt(grade ** skew) + 1 for grade in range(2, amount + 1)]
    surplus, holding = total - reach - (amount - 1), [1] * (amount - 1)
    while surplus > 0:
        candidates = [i for i in range(amount - 1) if holding[i] < reach]
        whole, budget = sum([portions[i] for i in candidates]), surplus
        for i in candidates:
            more = min(reach - holding[i], max(1, budget * portions[i] // whole), surplus)
            holding[i] = holding[i] + more
            surplus = surplus - more
    return np.array([reach] + holding)


def uneven(stream_key, count, total, most, lean):
    if count == 2:
        one = jax.random.randint(stream_key, (), max(1, total - most), min(most, total - 1) + 1)
        return jnp.stack([one, total - one])
    lengths = jnp.asarray(length_profile(count, total, most, lean), jnp.int32)
    pairs = (count - 1) // 2
    giver, sink = lengths[1:1 + 2 * pairs:2], lengths[2:2 + 2 * pairs:2]
    room = jnp.minimum(giver - 1, most - sink)
    passed = jax.random.randint(jax.random.fold_in(stream_key, 1), (pairs,), 0, 1 << 20) % (room + 1)
    lengths = lengths.at[1:1 + 2 * pairs:2].set(giver - passed).at[2:2 + 2 * pairs:2].set(sink + passed)
    return lengths[jax.random.permutation(jax.random.fold_in(stream_key, 2), count)]


def scatter_about(rng, dims, scale, reach, split=(), kind=jnp.bfloat16):
    loudness = shard_levels(rng, dims, split, -0.22, 0.18) if split else 1.0
    array = jax.random.normal(rng, dims, jnp.float32) * scale * loudness
    return jnp.minimum(jnp.maximum(array, -reach), reach).astype(kind)


def setup_inputs(seed: int = 0) -> dict:
    keys = jax.random.split(jax.random.key(seed), 11)
    hidden = scatter_about(keys[0], (TOKENS, D), 1.0, 6.0, ((0, 8), (1, 4)))
    modulation = scatter_about(keys[1], (2, D), 0.5, 3.0, (), jnp.float32)
    w_query = draw_w_query(jax.random.fold_in(keys[10], 71), 0)
    w_key = draw_w_key(jax.random.fold_in(keys[10], 71), 0)
    w_value = scatter_about(keys[4], (D, D), D ** -0.5, 0.078125, ((0, 8), (1, 4)))
    q_gain = draw_q_gain(jax.random.fold_in(keys[10], 71), 0)
    k_gain = draw_k_gain(jax.random.fold_in(keys[10], 71), 0)
    positions = plant(jax.random.randint(keys[7], (3, TOKENS), 0, 64), jax.random.fold_in(keys[7], 1), 0, 63).astype(jnp.int32)
    segment_ids = jnp.searchsorted(jnp.cumsum(uneven(keys[8], SEGS, TOKENS, MOST, 2)), jnp.arange(TOKENS), side="right").astype(jnp.int32)
    page_table = jax.random.permutation(keys[9], PAGES).astype(jnp.int32)
    return dict(hidden=hidden, modulation=modulation, w_query=w_query, w_key=w_key, w_value=w_value, q_gain=q_gain, k_gain=k_gain, positions=positions, segment_ids=segment_ids, page_table=page_table)


epsilon = 1e-06

def rotary_table(positions, pair_count):
    frame_pairs = pair_count - 2 * (pair_count // 3)
    side_pairs = pair_count // 3
    column = jnp.arange(pair_count)
    frame_rate = 10000.0 ** (-column.astype(jnp.float32) / frame_pairs)
    height_rate = 10000.0 ** (-(column - frame_pairs).astype(jnp.float32) / side_pairs)
    width_rate = 10000.0 ** (-(column - frame_pairs - side_pairs).astype(jnp.float32) / side_pairs)
    coords = positions.astype(jnp.float32)
    angles = jnp.where(column < frame_pairs, coords[0][:, None] * frame_rate, jnp.where(column < frame_pairs + side_pairs, coords[1][:, None] * height_rate, coords[2][:, None] * width_rate))
    return (jnp.cos(angles), jnp.sin(angles))

def rotate(values, cosine, sine_table, head_dim):
    row_count = values.shape[0]
    head_count = values.shape[1] // head_dim
    paired = values.reshape(row_count, head_count, head_dim // 2, 2)
    former = paired[..., 0]
    latter = paired[..., 1]
    cosine = cosine[:, None, :]
    sine_table = sine_table[:, None, :]
    turned = jnp.stack([former * cosine - latter * sine_table, former * sine_table + latter * cosine], axis=-1)
    return turned.reshape(row_count, head_count * head_dim)

def modulate(activations, modulation):
    average = lax.optimization_barrier(jnp.mean(activations, axis=1, keepdims=True))
    centred = activations - average
    variance = lax.optimization_barrier(jnp.mean(centred * centred, axis=1, keepdims=True))
    normed = centred * lax.rsqrt(variance + epsilon)
    return (normed * (1.0 + modulation[1]) + modulation[0]).astype(jnp.bfloat16)

def project(modulated, weight):

    def add_block(summed, block_number):
        columns = lax.dynamic_slice_in_dim(modulated, block_number * FEAT_BLK, FEAT_BLK, 1)
        weight_rows = lax.dynamic_slice_in_dim(weight, block_number * FEAT_BLK, FEAT_BLK, 0)
        partial_value = jnp.dot(columns, weight_rows, preferred_element_type=jnp.float32).astype(jnp.bfloat16)
        partial_value = lax.optimization_barrier(partial_value)
        return (summed + partial_value.astype(jnp.float32), None)
    starting = jnp.zeros((modulated.shape[0], weight.shape[1]), jnp.float32)
    summed, _ = lax.scan(add_block, starting, jnp.arange(D // FEAT_BLK, dtype=jnp.int32))
    return summed

def reference(hidden, modulation, w_query, w_key, w_value, q_gain, k_gain, positions, segment_ids, page_table):
    modulated = modulate(hidden.astype(jnp.float32), modulation)
    query_raw = project(modulated, w_query)
    key_raw = project(modulated, w_key)
    value_raw = project(modulated, w_value)
    query_normed = query_raw * lax.rsqrt(lax.optimization_barrier(jnp.mean(query_raw * query_raw, axis=1, keepdims=True)) + epsilon) * q_gain
    key_normed = key_raw * lax.rsqrt(lax.optimization_barrier(jnp.mean(key_raw * key_raw, axis=1, keepdims=True)) + epsilon) * k_gain
    cosine, sine_table = rotary_table(positions, HEAD_DIM // 2)
    query = rotate(query_normed, cosine, sine_table, HEAD_DIM).astype(jnp.bfloat16)
    key = rotate(key_normed, cosine, sine_table, HEAD_DIM).astype(jnp.bfloat16)
    value = value_raw.astype(jnp.bfloat16)
    heads_query = query.reshape(TOKENS, HEADS, HEAD_DIM).transpose(1, 0, 2)
    heads_key = key.reshape(TOKENS, HEADS, HEAD_DIM).transpose(1, 0, 2)
    heads_value = value.reshape(TOKENS, HEADS, HEAD_DIM).transpose(1, 0, 2)
    allowed = segment_ids[:, None] == segment_ids[None, :]

    def one_head(operands):
        head_query, head_key, head_value = operands
        scores = jnp.dot(head_query, head_key.T, preferred_element_type=jnp.float32) * HEAD_DIM ** (-0.5)
        highest = lax.optimization_barrier(jnp.max(jnp.where(allowed, scores, -1e+30), axis=1, keepdims=True))
        probabilities = jnp.where(allowed, jnp.exp(scores - highest), 0.0)
        summed = lax.optimization_barrier(jnp.sum(probabilities, axis=1, keepdims=True))
        mixed = jnp.dot(probabilities.astype(jnp.bfloat16), head_value, preferred_element_type=jnp.float32)
        return mixed / summed
    outputs = lax.map(one_head, (heads_query, heads_key, heads_value))
    attended = outputs.transpose(1, 0, 2).reshape(TOKENS, D).astype(jnp.bfloat16)
    paged = jnp.stack([key, value]).reshape(2, PAGES, PAGE, D)
    page_store = jnp.zeros_like(paged).at[:, page_table].set(paged)
    return (attended, page_store)
```

```python
import functools
import jax
import jax.numpy as jnp
from jax import lax
from jax.experimental import pallas as pl
from jax.experimental.pallas import tpu as pltpu
from jax.sharding import PartitionSpec as P

HEAD_DIM = 128
PAGE = 128
KEY_TILE = 256
VMEM = 48 * 1024 * 1024
LOG2E = 1.4426950408889634

epsilon = 1e-06


def rotary_table(positions, pair_count):
    frame_pairs = pair_count - 2 * (pair_count // 3)
    side_pairs = pair_count // 3
    column = jnp.arange(pair_count)
    frame_rate = 10000.0 ** (-column.astype(jnp.float32) / frame_pairs)
    height_rate = 10000.0 ** (-(column - frame_pairs).astype(jnp.float32) / side_pairs)
    width_rate = 10000.0 ** (-(column - frame_pairs - side_pairs).astype(jnp.float32) / side_pairs)
    coords = positions.astype(jnp.float32)
    angles = jnp.where(
        column < frame_pairs,
        coords[0][:, None] * frame_rate,
        jnp.where(
            column < frame_pairs + side_pairs,
            coords[1][:, None] * height_rate,
            coords[2][:, None] * width_rate,
        ),
    )
    return (jnp.cos(angles), jnp.sin(angles))


def rotary_lanes(positions, head_dim):
    cosine, sine_table = rotary_table(positions, head_dim // 2)
    own = jnp.repeat(cosine, 2, axis=1)
    sine = jnp.repeat(sine_table, 2, axis=1)
    even = (jnp.arange(head_dim) % 2 == 0)[None, :]
    return own, jnp.where(even, -sine, 0.0), jnp.where(even, 0.0, sine)


def modulate(activations, modulation):
    average = jnp.mean(activations, axis=1, keepdims=True)
    centred = activations - average
    variance = jnp.mean(centred * centred, axis=1, keepdims=True)
    normed = centred * lax.rsqrt(variance + epsilon)
    return (normed * (1.0 + modulation[1]) + modulation[0]).astype(jnp.bfloat16)


def modulate_kernel(me_ref, rows_ref, modulation_ref, out_ref):
    rows = rows_ref[...].astype(jnp.float32)
    width = rows.shape[1]
    blocks, _, feats = out_ref.shape
    average = jnp.sum(rows, axis=1, keepdims=True) * (1.0 / width)
    centred = rows - average
    variance = jnp.sum(centred * centred, axis=1, keepdims=True) * (1.0 / width)
    scale = lax.rsqrt(variance + epsilon)
    me = me_ref[0]
    for block in range(blocks):
        cols = pl.ds(pl.multiple_of((me ^ block) * feats, feats), feats)
        part = rows_ref[:, cols].astype(jnp.float32) - average
        gain = 1.0 + modulation_ref[1:2, cols]
        out_ref[block] = (part * scale * gain + modulation_ref[0:1, cols]).astype(jnp.bfloat16)


def modulate_blocks(rows, modulation, me, blocks):
    count, width = rows.shape
    tile = 128
    feats = width // blocks
    return pl.pallas_call(
        modulate_kernel,
        grid_spec=pltpu.PrefetchScalarGridSpec(
            num_scalar_prefetch=1,
            grid=(count // tile,),
            in_specs=[
                pl.BlockSpec((tile, width), lambda i, me: (i, 0)),
                pl.BlockSpec((2, width), lambda i, me: (0, 0)),
            ],
            out_specs=pl.BlockSpec((blocks, tile, feats), lambda i, me: (0, i, 0)),
        ),
        out_shape=jax.ShapeDtypeStruct((blocks, count, feats), jnp.bfloat16),
        compiler_params=pltpu.CompilerParams(vmem_limit_bytes=VMEM),
        cost_estimate=pl.CostEstimate(
            flops=10 * count * width, bytes_accessed=4 * count * width, transcendentals=count
        ),
        name="modulate_blocks",
    )(me.reshape(1), rows, modulation)


def project_kernel(order, *refs):
    blocks = len(order[0])
    mod_refs = refs[: len(order)]
    weight_refs = refs[len(order) : len(order) + blocks]
    out_ref = refs[-1]
    for number, places in enumerate(order):
        total = None
        for first in range(0, blocks, 2):
            left = jnp.concatenate(
                [mod_refs[number][places[first]], mod_refs[number][places[first + 1]]], axis=1
            )
            right = jnp.concatenate(
                [weight_refs[first][...], weight_refs[first + 1][...]], axis=0
            )
            part = jnp.dot(left, right, preferred_element_type=jnp.float32)
            total = part if total is None else total + part
        out_ref[number] = total.astype(out_ref.dtype)


def project(mods, order, weights, dtype):
    blocks, rows, feats = mods[0].shape
    cols = weights[0].shape[1]
    groups = len(mods)
    return pl.pallas_call(
        functools.partial(project_kernel, order),
        in_specs=[pl.BlockSpec(memory_space=pltpu.VMEM)] * (groups + blocks),
        out_specs=pl.BlockSpec(memory_space=pltpu.VMEM),
        out_shape=jax.ShapeDtypeStruct((groups, rows, cols), dtype),
        compiler_params=pltpu.CompilerParams(vmem_limit_bytes=VMEM),
        cost_estimate=pl.CostEstimate(
            flops=2 * groups * rows * blocks * feats * cols,
            bytes_accessed=2 * blocks * feats * (groups * rows + cols) + 4 * groups * rows * cols,
            transcendentals=0,
        ),
        name="project",
    )(*mods, *weights)


def turn_kernel(raw_ref, scale_ref, gain_ref, own_ref, upper_ref, lower_ref, out_ref):
    dim = own_ref.shape[1]
    scale = scale_ref[...]
    own, upper, lower = own_ref[...], upper_ref[...], lower_ref[...]
    for head in range(raw_ref.shape[1] // dim):
        cols = slice(head * dim, (head + 1) * dim)
        normed = raw_ref[:, cols] * scale * gain_ref[:, cols]
        turned = (
            normed * own
            + pltpu.roll(normed, dim - 1, 1) * upper
            + pltpu.roll(normed, 1, 1) * lower
        )
        out_ref[:, cols] = turned.astype(out_ref.dtype)


def turn(raw, scale, gain, tables):
    rows, cols = raw.shape
    tile = 128
    dim = tables[0].shape[1]
    return pl.pallas_call(
        turn_kernel,
        grid=(rows // tile,),
        in_specs=[
            pl.BlockSpec((tile, cols), lambda i: (i, 0)),
            pl.BlockSpec((tile, 1), lambda i: (i, 0)),
            pl.BlockSpec((1, cols), lambda i: (0, 0)),
        ]
        + [pl.BlockSpec((tile, dim), lambda i: (i, 0))] * 3,
        out_specs=pl.BlockSpec((tile, cols), lambda i: (i, 0)),
        out_shape=jax.ShapeDtypeStruct((rows, cols), jnp.bfloat16),
        cost_estimate=pl.CostEstimate(
            flops=8 * rows * cols, bytes_accessed=6 * rows * cols, transcendentals=0
        ),
        name="turn",
    )(raw, scale[:, None], gain[None, :], *tables)


def attend_kernel(places, tile, me_ref, bounds_ref, q_ref, *refs):
    count = len(places)
    key_refs, value_refs = refs[:count], refs[count : 2 * count]
    query_seg_ref, key_seg_ref, out_ref, keys, values = refs[2 * count :]
    me = me_ref[0]
    rows = key_refs[0].shape[1]
    for piece, owners in enumerate(places):
        for at, owner in enumerate(owners):
            where = pl.ds(pl.multiple_of((me ^ owner) * rows, rows), rows)
            keys[where, :] = key_refs[piece][at]
            values[where, :] = value_refs[piece][at]
    factor = keys.shape[1] ** (-0.5) * LOG2E
    for number in range(q_ref.shape[0] // tile):
        span = slice(number * tile, (number + 1) * tile)
        query = q_ref[span, :]
        query_seg = query_seg_ref[span, :]

        def step(block, carry):
            highest, total, mixed = carry
            where = pl.ds(pl.multiple_of(block * KEY_TILE, KEY_TILE), KEY_TILE)
            scores = lax.dot_general(
                query, keys[where, :], (((1,), (1,)), ((), ())), preferred_element_type=jnp.float32
            )
            scores = jnp.where(query_seg == key_seg_ref[block], scores * factor, -1e30)
            newest = jnp.maximum(highest, jnp.max(scores, axis=1, keepdims=True))
            weights = jnp.exp2(scores - newest)
            shrink = jnp.exp2(highest - newest)
            total = total * shrink + jnp.sum(weights, axis=1, keepdims=True)
            mixed = mixed * shrink + jnp.dot(
                weights.astype(jnp.bfloat16), values[where, :], preferred_element_type=jnp.float32
            )
            return newest, total, mixed

        start = (
            jnp.full((tile, 1), -1e29, jnp.float32),
            jnp.zeros((tile, 1), jnp.float32),
            jnp.zeros((tile, keys.shape[1]), jnp.float32),
        )
        _, total, mixed = lax.fori_loop(bounds_ref[number, 0], bounds_ref[number, 1], step, start)
        out_ref[span, :] = (mixed / total).astype(out_ref.dtype)


def attend(query, key_pieces, value_pieces, places, me, query_seg, segment_ids, tile):
    rows, cols = query.shape
    tokens = segment_ids.shape[0]
    dim = HEAD_DIM
    heads = cols // dim
    tiled = query_seg.reshape(rows // tile, tile)
    first, last = tiled[:, 0], tiled[:, -1]
    low = jnp.sum(segment_ids[None, :] < first[:, None], axis=1, dtype=jnp.int32)
    high = jnp.sum(segment_ids[None, :] <= last[:, None], axis=1, dtype=jnp.int32)
    bounds = jnp.stack([low // KEY_TILE, (high + KEY_TILE - 1) // KEY_TILE], axis=1)
    piece_specs = [
        pl.BlockSpec((piece.shape[0], piece.shape[1], dim), lambda h, *_: (0, 0, h))
        for piece in key_pieces
    ]
    return pl.pallas_call(
        functools.partial(attend_kernel, places, tile),
        grid_spec=pltpu.PrefetchScalarGridSpec(
            num_scalar_prefetch=2,
            grid=(heads,),
            in_specs=[pl.BlockSpec((rows, dim), lambda h, *_: (0, h))]
            + piece_specs
            + piece_specs
            + [
                pl.BlockSpec((rows, 1), lambda h, *_: (0, 0)),
                pl.BlockSpec((tokens // KEY_TILE, 1, KEY_TILE), lambda h, *_: (0, 0, 0)),
            ],
            out_specs=pl.BlockSpec((rows, dim), lambda h, *_: (0, h)),
            scratch_shapes=[
                pltpu.VMEM((tokens, dim), jnp.bfloat16),
                pltpu.VMEM((tokens, dim), jnp.bfloat16),
            ],
        ),
        out_shape=jax.ShapeDtypeStruct((rows, cols), jnp.bfloat16),
        compiler_params=pltpu.CompilerParams(vmem_limit_bytes=VMEM),
        cost_estimate=pl.CostEstimate(
            flops=2 * rows * tokens * cols,
            bytes_accessed=4 * tokens * cols + 4 * rows * cols,
            transcendentals=rows * tokens * heads // 2,
        ),
        name="attend",
    )(
        me.reshape(1),
        bounds,
        query,
        *key_pieces,
        *value_pieces,
        query_seg[:, None],
        segment_ids.reshape(tokens // KEY_TILE, 1, KEY_TILE),
    )


def pages_kernel(places, me_ref, page_ref, *refs):
    count = len(places)
    sources, out_ref, sems = refs[: 2 * count], refs[2 * count], refs[2 * count + 1]
    per_block = sources[0].shape[1] // PAGE
    me = me_ref[0]
    wanted = out_ref.shape[1]
    for kind in range(2):
        for number in range(wanted):
            page = page_ref[number]
            block = me ^ (page // per_block)
            rows = pl.ds(pl.multiple_of((page % per_block) * PAGE, PAGE), PAGE)
            for piece, owners in enumerate(places):
                for at, owner in enumerate(owners):

                    @pl.when(block == owner)
                    def _(kind=kind, number=number, piece=piece, at=at, rows=rows):
                        pltpu.make_async_copy(
                            sources[kind * count + piece].at[at, rows, :],
                            out_ref.at[kind, number],
                            sems.at[kind, number],
                        ).start()

    for kind in range(2):
        for number in range(wanted):
            pltpu.make_async_copy(
                sources[kind * count].at[0, pl.ds(0, PAGE), :],
                out_ref.at[kind, number],
                sems.at[kind, number],
            ).wait()


def pick_pages(key_pieces, value_pieces, places, me, pages):
    cols = key_pieces[0].shape[2]
    wanted = pages.shape[0]
    smem = pl.BlockSpec(memory_space=pltpu.SMEM)
    anywhere = pl.BlockSpec(memory_space=pl.ANY)
    return pl.pallas_call(
        functools.partial(pages_kernel, places),
        in_specs=[smem, smem] + [anywhere] * (2 * len(places)),
        out_specs=anywhere,
        out_shape=jax.ShapeDtypeStruct((2, wanted, PAGE, cols), jnp.bfloat16),
        scratch_shapes=[pltpu.SemaphoreType.DMA((2, wanted))],
        cost_estimate=pl.CostEstimate(
            flops=0, bytes_accessed=8 * wanted * PAGE * cols, transcendentals=0
        ),
        name="pick_pages",
    )(me.reshape(1), pages, *key_pieces, *value_pieces)


def own_pages(page_table, start, count):
    page_total = page_table.shape[0]
    inverse = (
        jnp.zeros((page_total,), jnp.int32)
        .at[page_table]
        .set(jnp.arange(page_total, dtype=jnp.int32))
    )
    return lax.dynamic_slice_in_dim(inverse, start, count, 0)


def whole_heads(ring, hidden, modulation, weights, gains, positions, segment_ids, page_table):
    tok_rows = hidden.shape[0]
    me = lax.axis_index("row")
    full_rows = lax.all_gather(hidden, "col", axis=1, tiled=True)
    modulated = modulate(full_rows.astype(jnp.float32), modulation)
    width = full_rows.shape[1]
    raws = [
        jnp.dot(
            modulated,
            lax.all_gather(weight, "row", axis=0, tiled=True),
            preferred_element_type=jnp.float32,
        )
        for weight in weights
    ]
    squares = lax.psum(tuple(jnp.sum(raw * raw, axis=1) for raw in raws[:2]), "col")
    scales = [lax.rsqrt(square / width + epsilon) for square in squares]
    tables = rotary_lanes(positions, HEAD_DIM)
    query, key = [turn(raw, scale, gain, tables) for raw, scale, gain in zip(raws, scales, gains)]
    value = raws[2].astype(jnp.bfloat16)
    keys_all = lax.all_gather(key, "row", axis=0)
    values_all = lax.all_gather(value, "row", axis=0)
    places = (tuple(range(ring)),)
    none = jnp.zeros((), jnp.int32)
    query_seg = lax.dynamic_slice_in_dim(segment_ids, me * tok_rows, tok_rows, 0)
    attended = attend(
        query, [keys_all], [values_all], places, none, query_seg, segment_ids, tok_rows
    )
    count = tok_rows // PAGE
    pages = own_pages(page_table, me * count, count)
    return attended, pick_pages([keys_all], [values_all], places, none, pages)


def split_heads(ring, ranks, hidden, modulation, weights, gains, positions, segment_ids, page_table):
    tok_rows = hidden.shape[0]
    me = lax.axis_index("row")
    top = ring // 2
    half = me // top
    cols = weights[0].shape[1] // 2
    steps = []
    bit = top // 2
    while bit:
        steps.append(bit)
        bit //= 2

    def swap(value, bit):
        return lax.ppermute(value, "row", [(i, i ^ bit) for i in range(ring)])

    def half_of(value, which):
        return lax.dynamic_slice_in_dim(value, which * cols, cols, value.ndim - 1)

    def spread(blocks):
        for bit in steps:
            blocks.update({number | bit: swap(blocks[number], bit) for number in list(blocks)})
        return blocks

    full_rows = lax.all_gather(hidden, "col", axis=1, tiled=True)
    width = full_rows.shape[1]
    mod_own = modulate_blocks(full_rows, modulation, me, ring)
    mod_partner = swap(mod_own, top)
    order = (tuple(range(ring)), tuple(i ^ top for i in range(ring)))

    def gathered(weight):
        blocks = spread({0: half_of(weight, half), top: swap(half_of(weight, 1 - half), top)})
        return [blocks[number] for number in range(ring)]

    w_query, w_key, w_value = weights
    key_blocks, value_blocks, query_blocks = gathered(w_key), gathered(w_value), gathered(w_query)

    def scale_of(raw):
        own = jnp.sum(raw * raw, axis=2)
        partners = [(row, rank) for row in (0, top) for rank in range(ranks)][1:]
        total = own
        for row, rank in partners:
            perm = [
                (r * ranks + c, (r ^ row) * ranks + (c + rank) % ranks)
                for r in range(ring)
                for c in range(ranks)
            ]
            other = lax.ppermute(own, ("row", "col"), perm)
            total = total + (other[::-1] if row else other)
        return lax.rsqrt(total.reshape(-1) / width + epsilon)

    both_positions = jnp.concatenate([positions, swap(positions, top)], axis=1)
    tables = rotary_lanes(both_positions, HEAD_DIM)
    q_gain, k_gain = [half_of(gain, half) for gain in gains]
    mods = (mod_own, mod_partner)
    flat = (2 * tok_rows, cols)

    key_raw = project(mods, order, key_blocks, jnp.float32)
    key_scale = scale_of(key_raw)
    value = project(mods, order, value_blocks, jnp.bfloat16)
    values = spread({0: value})
    key = turn(key_raw.reshape(flat), key_scale, k_gain, tables).reshape(value.shape)
    keys = spread({0: key})
    query_raw = project(mods, order, query_blocks, jnp.float32)
    query = turn(query_raw.reshape(flat), scale_of(query_raw), q_gain, tables)

    places = tuple((number, number | top) for number in range(top))
    key_pieces = [keys[number] for number in range(top)]
    value_pieces = [values[number] for number in range(top)]
    count = tok_rows // PAGE
    pages = jnp.concatenate(
        [own_pages(page_table, owner * count, count) for owner in (me, me ^ top)]
    )
    picked = pick_pages(key_pieces, value_pieces, places, me, pages)
    picked_other = swap(picked[:, count:], top)

    query_seg = jnp.concatenate(
        [
            lax.dynamic_slice_in_dim(segment_ids, owner * tok_rows, tok_rows, 0)
            for owner in (me, me ^ top)
        ]
    )
    attended = attend(
        query, key_pieces, value_pieces, places, me, query_seg, segment_ids, tok_rows
    )
    attended_other = swap(attended[tok_rows:], top)

    def joined(mine, other):
        return jnp.where(
            half == 0,
            jnp.concatenate([mine, other], axis=-1),
            jnp.concatenate([other, mine], axis=-1),
        )

    return (joined(attended[:tok_rows], attended_other), joined(picked[:, :count], picked_other))


def solution(mesh):
    ring, ranks = mesh.shape["row"], mesh.shape["col"]

    def body(
        hidden, modulation, w_query, w_key, w_value, q_gain, k_gain, positions, segment_ids, page_table
    ):
        rest = (
            hidden,
            modulation,
            (w_query, w_key, w_value),
            (q_gain, k_gain),
            positions,
            segment_ids,
            page_table,
        )
        heads = w_query.shape[1] // HEAD_DIM
        feats = w_query.shape[0]
        if heads % 2 == 0 and ring % 2 == 0 and ring & (ring - 1) == 0 and feats % 128 == 0:
            return split_heads(ring, ranks, *rest)
        return whole_heads(ring, *rest)

    in_specs = (
        P("row", "col"),
        P(),
        P("row", "col"),
        P("row", "col"),
        P("row", "col"),
        P("col"),
        P("col"),
        P(None, "row"),
        P(),
        P(),
    )
    out_specs = (P("row", "col"), P(None, "row", None, "col"))
    return jax.shard_map(body, mesh=mesh, in_specs=in_specs, out_specs=out_specs, check_vma=False)
```

```python
import functools
import jax
import jax.numpy as jnp
from jax import lax
from jax.experimental import pallas as pl
from jax.experimental.pallas import tpu as pltpu
from jax.sharding import PartitionSpec as P

HEAD_DIM = 128
PAGE = 128
KEY_TILE = 512
VMEM = 48 * 1024 * 1024
LOG2E = 1.4426950408889634

epsilon = 1e-06


def rotary_table(positions, pair_count):
    frame_pairs = pair_count - 2 * (pair_count // 3)
    side_pairs = pair_count // 3
    column = jnp.arange(pair_count)
    frame_rate = 10000.0 ** (-column.astype(jnp.float32) / frame_pairs)
    height_rate = 10000.0 ** (-(column - frame_pairs).astype(jnp.float32) / side_pairs)
    width_rate = 10000.0 ** (-(column - frame_pairs - side_pairs).astype(jnp.float32) / side_pairs)
    coords = positions.astype(jnp.float32)
    angles = jnp.where(
        column < frame_pairs,
        coords[0][:, None] * frame_rate,
        jnp.where(
            column < frame_pairs + side_pairs,
            coords[1][:, None] * height_rate,
            coords[2][:, None] * width_rate,
        ),
    )
    return (jnp.cos(angles), jnp.sin(angles))


def rotary_lanes(positions, head_dim):
    cosine, sine_table = rotary_table(positions, head_dim // 2)
    own = jnp.repeat(cosine, 2, axis=1)
    sine = jnp.repeat(sine_table, 2, axis=1)
    even = (jnp.arange(head_dim) % 2 == 0)[None, :]
    return own, jnp.where(even, -sine, 0.0), jnp.where(even, 0.0, sine)


def modulate(activations, modulation):
    average = jnp.mean(activations, axis=1, keepdims=True)
    centred = activations - average
    variance = jnp.mean(centred * centred, axis=1, keepdims=True)
    normed = centred * lax.rsqrt(variance + epsilon)
    return (normed * (1.0 + modulation[1]) + modulation[0]).astype(jnp.bfloat16)


def project_kernel(spots, ranks, me_ref, mod_ref, *refs):
    count = len(spots)
    sources = refs[: -8]
    key_ref, query_ref, value_ref, mods, weights, total, mod_sems, weight_sems = refs[-8:]
    me = me_ref[0]
    groups, _, feats = mods.shape[1:]
    cols = weights.shape[3]
    per_rank = mod_ref.shape[2] // feats
    copies = []
    for block, spot in enumerate(spots):
        owner = me ^ block
        span = pl.ds(pl.multiple_of((owner % per_rank) * feats, feats), feats)
        mine = [
            pltpu.make_async_copy(
                mod_ref.at[group * ranks + owner // per_rank, :, span],
                mods.at[block, group],
                mod_sems.at[block, group],
            )
            for group in range(groups)
        ]
        for number, (source, at) in enumerate(spot):
            mine.append(
                pltpu.make_async_copy(
                    sources[source] if at is None else sources[source].at[at],
                    weights.at[block, number],
                    weight_sems.at[block, number],
                )
            )
        for copy in mine:
            copy.start()
        copies.append(mine)
    for first in range(0, count, 2):
        for copy in copies[first] + copies[first + 1]:
            copy.wait()
        right = jnp.concatenate(
            [
                jnp.concatenate([weights[first, m], weights[first + 1, m]], axis=0)
                for m in range(3)
            ],
            axis=1,
        )
        for group in range(groups):
            left = jnp.concatenate([mods[first, group], mods[first + 1, group]], axis=1)
            part = jnp.dot(left, right, preferred_element_type=jnp.float32)
            if first:
                part = part + total[group]
            if first < count - 2:
                total[group] = part
            else:
                key_ref[group] = part[:, :cols]
                value_ref[group] = part[:, cols : 2 * cols].astype(value_ref.dtype)
                query_ref[group] = part[:, 2 * cols :]


def project(mod_all, ranks, me, spots, sources, feats, cols):
    rows = mod_all.shape[1]
    groups = mod_all.shape[0] // ranks
    blocks = len(spots)
    raw = jax.ShapeDtypeStruct((groups, rows, cols), jnp.float32)
    anywhere = pl.BlockSpec(memory_space=pl.ANY)
    whole = pl.BlockSpec(memory_space=pltpu.VMEM)
    return pl.pallas_call(
        functools.partial(project_kernel, spots, ranks),
        in_specs=[pl.BlockSpec(memory_space=pltpu.SMEM), anywhere] + [anywhere] * len(sources),
        out_specs=[whole] * 3,
        out_shape=[raw, raw, jax.ShapeDtypeStruct(raw.shape, jnp.bfloat16)],
        scratch_shapes=[
            pltpu.VMEM((blocks, groups, rows, feats), jnp.bfloat16),
            pltpu.VMEM((blocks, 3, feats, cols), jnp.bfloat16),
            pltpu.VMEM((groups, rows, 3 * cols), jnp.float32),
            pltpu.SemaphoreType.DMA((blocks, groups)),
            pltpu.SemaphoreType.DMA((blocks, 3)),
        ],
        compiler_params=pltpu.CompilerParams(vmem_limit_bytes=VMEM),
        cost_estimate=pl.CostEstimate(
            flops=6 * groups * rows * blocks * feats * cols,
            bytes_accessed=2 * blocks * feats * (groups * rows + 3 * cols)
            + 10 * groups * rows * cols,
            transcendentals=0,
        ),
        name="project",
    )(me.reshape(1), mod_all, *sources)


def turn_kernel(raw_ref, scale_ref, gain_ref, own_ref, upper_ref, lower_ref, out_ref):
    dim = own_ref.shape[1]
    scale = scale_ref[...]
    own, upper, lower = own_ref[...], upper_ref[...], lower_ref[...]
    for head in range(raw_ref.shape[1] // dim):
        cols = slice(head * dim, (head + 1) * dim)
        normed = raw_ref[:, cols] * scale * gain_ref[:, cols]
        turned = (
            normed * own
            + pltpu.roll(normed, dim - 1, 1) * upper
            + pltpu.roll(normed, 1, 1) * lower
        )
        out_ref[:, cols] = turned.astype(out_ref.dtype)


def turn(raw, scale, gain, tables):
    rows, cols = raw.shape
    tile = rows // 2
    dim = tables[0].shape[1]
    return pl.pallas_call(
        turn_kernel,
        grid=(rows // tile,),
        in_specs=[
            pl.BlockSpec((tile, cols), lambda i: (i, 0)),
            pl.BlockSpec((tile, 1), lambda i: (i, 0)),
            pl.BlockSpec((1, cols), lambda i: (0, 0)),
        ]
        + [pl.BlockSpec((tile, dim), lambda i: (i, 0))] * 3,
        out_specs=pl.BlockSpec((tile, cols), lambda i: (i, 0)),
        out_shape=jax.ShapeDtypeStruct((rows, cols), jnp.bfloat16),
        compiler_params=pltpu.CompilerParams(vmem_limit_bytes=VMEM),
        cost_estimate=pl.CostEstimate(
            flops=8 * rows * cols, bytes_accessed=6 * rows * cols, transcendentals=0
        ),
        name="turn",
    )(raw, scale[:, None], gain[None, :], *tables)


def attend_kernel(places, tile, me_ref, bounds_ref, q_ref, *refs):
    count = len(places)
    sources = refs[: 2 * count]
    query_seg_ref, key_seg_ref, out_ref, keys, values, highest, mixed, sems = refs[2 * count :]
    me = me_ref[0]
    rows = sources[0].shape[1]
    copies = []
    for piece, owners in enumerate(places):
        for at, owner in enumerate(owners):
            where = pl.ds(pl.multiple_of(owner(me) * rows, rows), rows)
            for kind, held in enumerate((keys, values)):
                copies.append(
                    pltpu.make_async_copy(
                        sources[kind * count + piece].at[at],
                        held.at[where, :],
                        sems.at[kind, piece, at],
                    )
                )
    for copy in copies:
        copy.start()
    for copy in copies:
        copy.wait()
    dim = HEAD_DIM
    heads = q_ref.shape[1] // dim
    factor = dim ** (-0.5) * LOG2E
    ones = jnp.ones((KEY_TILE, dim), jnp.bfloat16)
    for number in range(q_ref.shape[0] // tile):
        span = slice(number * tile, (number + 1) * tile)
        highest[...] = jnp.full_like(highest, -1e29)
        mixed[...] = jnp.zeros_like(mixed)

        def step(block, carry):
            where = pl.ds(pl.multiple_of(block * KEY_TILE, KEY_TILE), KEY_TILE)
            same = query_seg_ref[span, :] == key_seg_ref[block]
            for head in range(heads):
                cols = slice(head * dim, (head + 1) * dim)
                scores = lax.dot_general(
                    q_ref[span, cols],
                    keys[where, cols],
                    (((1,), (1,)), ((), ())),
                    preferred_element_type=jnp.float32,
                )
                scores = jnp.where(same, scores * factor, -1e30)
                former = highest[head]
                newest = jnp.maximum(former, jnp.max(scores, axis=1, keepdims=True))
                highest[head] = newest
                weights = jnp.exp2(scores - newest[:, :1]).astype(jnp.bfloat16)
                right = jnp.concatenate([values[where, cols], ones], axis=1)
                part = jnp.dot(weights, right, preferred_element_type=jnp.float32)
                shrink = jnp.exp2(former - newest)
                mixed[head, :, :dim] = mixed[head, :, :dim] * shrink + part[:, :dim]
                mixed[head, :, dim:] = mixed[head, :, dim:] * shrink + part[:, dim:]
            return carry

        lax.fori_loop(bounds_ref[number, 0], bounds_ref[number, 1], step, 0)
        for head in range(heads):
            out_ref[span, head * dim : (head + 1) * dim] = (
                mixed[head, :, :dim] / mixed[head, :, dim:]
            ).astype(out_ref.dtype)


def attend(query, key_pieces, value_pieces, places, me, query_seg, segment_ids, tile):
    rows, cols = query.shape
    tokens = segment_ids.shape[0]
    dim = HEAD_DIM
    heads = cols // dim
    tiled = query_seg.reshape(rows // tile, tile)
    first, last = tiled[:, 0], tiled[:, -1]
    low = jnp.sum(segment_ids[None, :] < first[:, None], axis=1, dtype=jnp.int32)
    high = jnp.sum(segment_ids[None, :] <= last[:, None], axis=1, dtype=jnp.int32)
    bounds = jnp.stack([low // KEY_TILE, (high + KEY_TILE - 1) // KEY_TILE], axis=1)
    smem = pl.BlockSpec(memory_space=pltpu.SMEM)
    whole = pl.BlockSpec(memory_space=pltpu.VMEM)
    anywhere = pl.BlockSpec(memory_space=pl.ANY)
    return pl.pallas_call(
        functools.partial(attend_kernel, places, tile),
        in_specs=[smem, smem, whole] + [anywhere] * (2 * len(places)) + [whole, whole],
        out_specs=whole,
        scratch_shapes=[
            pltpu.VMEM((tokens, cols), jnp.bfloat16),
            pltpu.VMEM((tokens, cols), jnp.bfloat16),
            pltpu.VMEM((heads, tile, dim), jnp.float32),
            pltpu.VMEM((heads, tile, 2 * dim), jnp.float32),
            pltpu.SemaphoreType.DMA((2, len(places), len(places[0]))),
        ],
        out_shape=jax.ShapeDtypeStruct((rows, cols), jnp.bfloat16),
        compiler_params=pltpu.CompilerParams(vmem_limit_bytes=VMEM),
        cost_estimate=pl.CostEstimate(
            flops=2 * rows * tokens * cols,
            bytes_accessed=4 * tokens * cols + 4 * rows * cols,
            transcendentals=rows * tokens * heads // 2,
        ),
        name="attend",
    )(
        me.reshape(1),
        bounds,
        query,
        *key_pieces,
        *value_pieces,
        query_seg[:, None],
        segment_ids.reshape(tokens // KEY_TILE, 1, KEY_TILE),
    )


def pages_kernel(places, me_ref, page_ref, *refs):
    count = len(places)
    sources, out_ref, sems = refs[: 2 * count], refs[2 * count], refs[2 * count + 1]
    per_block = sources[0].shape[1] // PAGE
    me = me_ref[0]
    wanted = out_ref.shape[1]
    for kind in range(2):
        for number in range(wanted):
            page = page_ref[number]
            block = page // per_block
            rows = pl.ds(pl.multiple_of((page % per_block) * PAGE, PAGE), PAGE)
            for piece, owners in enumerate(places):
                for at, owner in enumerate(owners):

                    @pl.when(block == owner(me))
                    def _(kind=kind, number=number, piece=piece, at=at, rows=rows):
                        pltpu.make_async_copy(
                            sources[kind * count + piece].at[at, rows, :],
                            out_ref.at[kind, number],
                            sems.at[kind, number],
                        ).start()

    for kind in range(2):
        for number in range(wanted):
            pltpu.make_async_copy(
                sources[kind * count].at[0, pl.ds(0, PAGE), :],
                out_ref.at[kind, number],
                sems.at[kind, number],
            ).wait()


def pick_pages(key_pieces, value_pieces, places, me, pages):
    cols = key_pieces[0].shape[2]
    wanted = pages.shape[0]
    smem = pl.BlockSpec(memory_space=pltpu.SMEM)
    anywhere = pl.BlockSpec(memory_space=pl.ANY)
    return pl.pallas_call(
        functools.partial(pages_kernel, places),
        in_specs=[smem, smem] + [anywhere] * (2 * len(places)),
        out_specs=pl.BlockSpec(memory_space=pltpu.VMEM),
        out_shape=jax.ShapeDtypeStruct((2, wanted, PAGE, cols), jnp.bfloat16),
        scratch_shapes=[pltpu.SemaphoreType.DMA((2, wanted))],
        cost_estimate=pl.CostEstimate(
            flops=0, bytes_accessed=8 * wanted * PAGE * cols, transcendentals=0
        ),
        name="pick_pages",
    )(me.reshape(1), pages, *key_pieces, *value_pieces)


def own_pages(page_table, start, count):
    page_total = page_table.shape[0]
    inverse = (
        jnp.zeros((page_total,), jnp.int32)
        .at[page_table]
        .set(jnp.arange(page_total, dtype=jnp.int32))
    )
    return lax.dynamic_slice_in_dim(inverse, start, count, 0)


def whole_heads(ring, hidden, modulation, weights, gains, positions, segment_ids, page_table):
    tok_rows = hidden.shape[0]
    me = lax.axis_index("row")
    full_rows = lax.all_gather(hidden, "col", axis=1, tiled=True)
    modulated = modulate(full_rows.astype(jnp.float32), modulation)
    width = full_rows.shape[1]
    raws = [
        jnp.dot(
            modulated,
            lax.all_gather(weight, "row", axis=0, tiled=True),
            preferred_element_type=jnp.float32,
        )
        for weight in weights
    ]
    squares = lax.psum(tuple(jnp.sum(raw * raw, axis=1) for raw in raws[:2]), "col")
    scales = [lax.rsqrt(square / width + epsilon) for square in squares]
    tables = rotary_lanes(positions, HEAD_DIM)
    query, key = [turn(raw, scale, gain, tables) for raw, scale, gain in zip(raws, scales, gains)]
    value = raws[2].astype(jnp.bfloat16)
    keys_all = lax.all_gather(key, "row", axis=0)
    values_all = lax.all_gather(value, "row", axis=0)
    places = (tuple(lambda me, at=at: at for at in range(ring)),)
    none = jnp.zeros((), jnp.int32)
    query_seg = lax.dynamic_slice_in_dim(segment_ids, me * tok_rows, tok_rows, 0)
    attended = attend(
        query, [keys_all], [values_all], places, none, query_seg, segment_ids, tok_rows
    )
    count = tok_rows // PAGE
    pages = own_pages(page_table, me * count, count)
    return attended, pick_pages([keys_all], [values_all], places, none, pages)


def split_heads(ring, ranks, hidden, modulation, weights, gains, positions, segment_ids, page_table):
    tok_rows, shard = hidden.shape
    feats = weights[0].shape[0]
    width = ring * feats
    me = lax.axis_index("row")
    rank = lax.axis_index("col")
    top = ring // 2
    half = me // top
    low = me % top
    cols = weights[0].shape[1] // 2
    steps = []
    bit = top // 2
    while bit:
        steps.append(bit)
        bit //= 2

    def swap(value, bit):
        return lax.ppermute(value, "row", [(i, i ^ bit) for i in range(ring)])

    def half_of(value, which):
        return lax.dynamic_slice_in_dim(value, which * cols, cols, value.ndim - 1)

    def in_order(mine, other, axis):
        return jnp.where(
            half == 0,
            jnp.concatenate([mine, other], axis=axis),
            jnp.concatenate([other, mine], axis=axis),
        )

    def spread(blocks):
        for bit in steps:
            blocks.update(
                {
                    number | bit: jax.tree.map(lambda part: swap(part, bit), blocks[number])
                    for number in list(blocks)
                }
            )
        return blocks

    rows = hidden.astype(jnp.float32)
    local_mean = jnp.mean(rows, axis=1)
    local_square = jnp.sum(jnp.square(rows - local_mean[:, None]), axis=1)
    stats = jnp.stack([local_mean, local_square])
    all_stats = [stats] + [
        lax.ppermute(stats, "col", [(c, (c + step) % ranks) for c in range(ranks)])
        for step in range(1, ranks)
    ]
    average = sum(part[0] for part in all_stats) / ranks
    variance = (
        sum(part[1] + shard * jnp.square(part[0] - average) for part in all_stats) / width
    )
    shift = lax.dynamic_slice_in_dim(modulation, rank * shard, shard, 1)
    mod = (rows - average[:, None]) * lax.rsqrt(variance + epsilon)[:, None]
    mod = (mod * (1.0 + shift[1]) + shift[0]).astype(jnp.bfloat16)
    groups = [
        [row * ranks + c for row in (first, first + top) for c in range(ranks)]
        for first in range(top)
    ]
    mod_all = lax.all_gather(mod, ("row", "col"), axis_index_groups=groups, axis=0)

    w_query, w_key, w_value = weights
    ordered = (w_key, w_value, w_query)
    own = jnp.stack([half_of(weight, half) for weight in ordered])
    blocks = spread({0: own, top: [swap(half_of(weight, 1 - half), top) for weight in ordered]})
    sources, spots = [], []
    for number in range(ring):
        held = blocks[number]
        if isinstance(held, list):
            spots.append(tuple((len(sources) + m, None) for m in range(3)))
            sources.extend(held)
        else:
            spots.append(tuple((len(sources), m) for m in range(3)))
            sources.append(held)
    key_raw, query_raw, value = project(
        mod_all, ranks, me, tuple(spots), sources, feats, cols
    )

    squares = jnp.stack([jnp.sum(raw * raw, axis=2) for raw in (key_raw, query_raw)])
    squares = squares + swap(squares, top)
    bit = 1
    while bit < ranks:
        squares = squares + lax.ppermute(squares, "col", [(c, c ^ bit) for c in range(ranks)])
        bit *= 2
    scales = lax.rsqrt(squares / width + epsilon).reshape(2, -1)

    tables = rotary_lanes(in_order(positions, swap(positions, top), 1), HEAD_DIM)
    q_gain, k_gain = [half_of(gain, half) for gain in gains]
    flat = (2 * tok_rows, cols)
    values = spread({0: value})
    key = turn(key_raw.reshape(flat), scales[0], k_gain, tables).reshape(value.shape)
    keys = spread({0: key})
    query = turn(query_raw.reshape(flat), scales[1], q_gain, tables)

    places = tuple(
        tuple(lambda me, n=number, g=group: ((me % top) ^ n) + g * top for group in range(2))
        for number in range(top)
    )
    key_pieces = [keys[number] for number in range(top)]
    value_pieces = [values[number] for number in range(top)]
    count = tok_rows // PAGE
    pages = jnp.concatenate(
        [own_pages(page_table, owner * count, count) for owner in (me, me ^ top)]
    )
    picked = pick_pages(key_pieces, value_pieces, places, me, pages)
    picked_other = swap(picked[:, count:], top)

    query_seg = jnp.concatenate(
        [
            lax.dynamic_slice_in_dim(segment_ids, owner * tok_rows, tok_rows, 0)
            for owner in (low, low + top)
        ]
    )
    attended = attend(
        query, key_pieces, value_pieces, places, me, query_seg, segment_ids, tok_rows
    )
    mine = lax.dynamic_slice_in_dim(attended, half * tok_rows, tok_rows, 0)
    other = swap(lax.dynamic_slice_in_dim(attended, (1 - half) * tok_rows, tok_rows, 0), top)
    return (in_order(mine, other, -1), in_order(picked[:, :count], picked_other, -1))


def solution(mesh):
    ring, ranks = mesh.shape["row"], mesh.shape["col"]

    def body(
        hidden, modulation, w_query, w_key, w_value, q_gain, k_gain, positions, segment_ids, page_table
    ):
        rest = (
            hidden,
            modulation,
            (w_query, w_key, w_value),
            (q_gain, k_gain),
            positions,
            segment_ids,
            page_table,
        )
        heads = w_query.shape[1] // HEAD_DIM
        feats, shard = w_query.shape[0], hidden.shape[1]
        powers = ring & (ring - 1) == 0 and ranks & (ranks - 1) == 0
        if heads % 2 == 0 and ring % 2 == 0 and powers and feats % 128 == 0 and shard % feats == 0:
            return split_heads(ring, ranks, *rest)
        return whole_heads(ring, *rest)

    in_specs = (
        P("row", "col"),
        P(),
        P("row", "col"),
        P("row", "col"),
        P("row", "col"),
        P("col"),
        P("col"),
        P(None, "row"),
        P(),
        P(),
    )
    out_specs = (P("row", "col"), P(None, "row", None, "col"))
    return jax.shard_map(body, mesh=mesh, in_specs=in_specs, out_specs=out_specs, check_vma=False)
```

```python
import functools
import jax
import jax.numpy as jnp
from jax import lax
from jax.experimental import pallas as pl
from jax.experimental.pallas import tpu as pltpu
from jax.sharding import PartitionSpec as P

HEAD_DIM = 128
PAGE = 128
KEY_TILE = 512
VMEM = 60 * 1024 * 1024
LOG2E = 1.4426950408889634

epsilon = 1e-06


def rotary_table(positions, pair_count):
    frame_pairs = pair_count - 2 * (pair_count // 3)
    side_pairs = pair_count // 3
    column = jnp.arange(pair_count)
    frame_rate = 10000.0 ** (-column.astype(jnp.float32) / frame_pairs)
    height_rate = 10000.0 ** (-(column - frame_pairs).astype(jnp.float32) / side_pairs)
    width_rate = 10000.0 ** (-(column - frame_pairs - side_pairs).astype(jnp.float32) / side_pairs)
    coords = positions.astype(jnp.float32)
    angles = jnp.where(
        column < frame_pairs,
        coords[0][:, None] * frame_rate,
        jnp.where(
            column < frame_pairs + side_pairs,
            coords[1][:, None] * height_rate,
            coords[2][:, None] * width_rate,
        ),
    )
    return (jnp.cos(angles), jnp.sin(angles))


def rotary_lanes(positions, head_dim):
    cosine, sine_table = rotary_table(positions, head_dim // 2)
    own = jnp.repeat(cosine, 2, axis=1)
    sine = jnp.repeat(sine_table, 2, axis=1)
    even = (jnp.arange(head_dim) % 2 == 0)[None, :]
    return own, jnp.where(even, -sine, 0.0), jnp.where(even, 0.0, sine)


def modulate(activations, modulation):
    average = jnp.mean(activations, axis=1, keepdims=True)
    centred = activations - average
    variance = jnp.mean(centred * centred, axis=1, keepdims=True)
    normed = centred * lax.rsqrt(variance + epsilon)
    return (normed * (1.0 + modulation[1]) + modulation[0]).astype(jnp.bfloat16)


def project_kernel(spots, ranks, chunks, me_ref, mod_ref, *refs):
    count = len(spots)
    tail = len(refs) - 8 - chunks
    sources, outs, scratch = refs[:tail], refs[tail:-5], refs[-5:]
    key_ref, query_ref, squares_ref = outs[:3]
    value_refs = outs[3:]
    mods, weights, total, mod_sems, weight_sems = scratch
    me = me_ref[0]
    groups, _, feats = mods.shape[1:]
    cols = weights.shape[3]
    per_rank = mod_ref.shape[2] // feats
    copies = []
    for block, spot in enumerate(spots):
        owner = me ^ block
        span = pl.ds(pl.multiple_of((owner % per_rank) * feats, feats), feats)
        mine = [
            pltpu.make_async_copy(
                mod_ref.at[group * ranks + owner // per_rank, :, span],
                mods.at[block, group],
                mod_sems.at[block, group],
            )
            for group in range(groups)
        ]
        for number, (source, at) in enumerate(spot):
            mine.append(
                pltpu.make_async_copy(
                    sources[source] if at is None else sources[source].at[at],
                    weights.at[block, number],
                    weight_sems.at[block, number],
                )
            )
        for copy in mine:
            copy.start()
        copies.append(mine)
    for first in range(0, count, 2):
        for copy in copies[first] + copies[first + 1]:
            copy.wait()
        right = jnp.concatenate(
            [
                jnp.concatenate([weights[first, m], weights[first + 1, m]], axis=0)
                for m in range(3)
            ],
            axis=1,
        )
        for group in range(groups):
            left = jnp.concatenate([mods[first, group], mods[first + 1, group]], axis=1)
            part = jnp.dot(left, right, preferred_element_type=jnp.float32)
            if first:
                part = part + total[group]
            if first < count - 2:
                total[group] = part
            else:
                key_ref[group] = part[:, :cols]
                query_ref[group] = part[:, 2 * cols :]
                start = cols
                for value_ref in value_refs:
                    value_ref[group] = part[:, start : start + value_ref.shape[2]].astype(
                        value_ref.dtype
                    )
                    start += value_ref.shape[2]
                for kind, raw in enumerate((part[:, :cols], part[:, 2 * cols :])):
                    summed = jnp.sum(raw * raw, axis=1, keepdims=True)
                    summed = jnp.transpose(jnp.broadcast_to(summed, (summed.shape[0], 128)))
                    at = kind * groups + group
                    squares_ref[at : at + 1, :] = summed[:1]


def project(mod_all, ranks, me, spots, sources, feats, cols, chunk_cols):
    rows = mod_all.shape[1]
    groups = mod_all.shape[0] // ranks
    blocks = len(spots)
    raw = jax.ShapeDtypeStruct((groups, rows, cols), jnp.float32)
    anywhere = pl.BlockSpec(memory_space=pl.ANY)
    whole = pl.BlockSpec(memory_space=pltpu.VMEM)
    return pl.pallas_call(
        functools.partial(project_kernel, spots, ranks, len(chunk_cols)),
        in_specs=[pl.BlockSpec(memory_space=pltpu.SMEM), anywhere] + [anywhere] * len(sources),
        out_specs=[whole] * (3 + len(chunk_cols)),
        out_shape=[raw, raw, jax.ShapeDtypeStruct((2 * groups, rows), jnp.float32)]
        + [jax.ShapeDtypeStruct((groups, rows, part), jnp.bfloat16) for part in chunk_cols],
        scratch_shapes=[
            pltpu.VMEM((blocks, groups, rows, feats), jnp.bfloat16),
            pltpu.VMEM((blocks, 3, feats, cols), jnp.bfloat16),
            pltpu.VMEM((groups, rows, 3 * cols), jnp.float32),
            pltpu.SemaphoreType.DMA((blocks, groups)),
            pltpu.SemaphoreType.DMA((blocks, 3)),
        ],
        compiler_params=pltpu.CompilerParams(vmem_limit_bytes=VMEM),
        cost_estimate=pl.CostEstimate(
            flops=6 * groups * rows * blocks * feats * cols,
            bytes_accessed=2 * blocks * feats * (groups * rows + 3 * cols)
            + 10 * groups * rows * cols,
            transcendentals=0,
        ),
        name="project",
    )(me.reshape(1), mod_all, *sources)


def turn_kernel(width, raw_ref, mine_ref, other_ref, gain_ref, own_ref, upper_ref, lower_ref, *outs):
    dim = own_ref.shape[1]
    rows = raw_ref.shape[0]
    scale = lax.rsqrt((mine_ref[0] + other_ref[0]) * (1.0 / width) + epsilon)
    scale = jnp.transpose(jnp.broadcast_to(scale, (128, rows)))
    own, upper, lower = own_ref[...], upper_ref[...], lower_ref[...]
    start = 0
    for out_ref in outs:
        for head in range(out_ref.shape[1] // dim):
            cols = slice(start + head * dim, start + (head + 1) * dim)
            normed = raw_ref[:, cols] * scale * gain_ref[:, cols]
            turned = (
                normed * own
                + pltpu.roll(normed, dim - 1, 1) * upper
                + pltpu.roll(normed, 1, 1) * lower
            )
            out_ref[:, head * dim : (head + 1) * dim] = turned.astype(out_ref.dtype)
        start += out_ref.shape[1]


def turn(raw, mine, other, gain, tables, width, chunk_cols):
    rows, cols = raw.shape
    groups = mine.shape[0]
    tile = rows // groups
    dim = tables[0].shape[1]
    sums = [part.reshape(groups, 1, tile) for part in (mine, other)]
    return pl.pallas_call(
        functools.partial(turn_kernel, width),
        grid=(groups,),
        in_specs=[pl.BlockSpec((tile, cols), lambda i: (i, 0))]
        + [pl.BlockSpec((1, 1, tile), lambda i: (i, 0, 0))] * 2
        + [pl.BlockSpec((1, cols), lambda i: (0, 0))]
        + [pl.BlockSpec((tile, dim), lambda i: (i, 0))] * 3,
        out_specs=[pl.BlockSpec((tile, part), lambda i: (i, 0)) for part in chunk_cols],
        out_shape=[jax.ShapeDtypeStruct((rows, part), jnp.bfloat16) for part in chunk_cols],
        compiler_params=pltpu.CompilerParams(vmem_limit_bytes=VMEM),
        cost_estimate=pl.CostEstimate(
            flops=8 * rows * cols, bytes_accessed=6 * rows * cols, transcendentals=0
        ),
        name="turn",
    )(raw, *sums, gain[None, :], *tables)


def attend_kernel(places, tile, me_ref, bounds_ref, q_ref, *refs):
    count = len(places)
    sources = refs[: 2 * count]
    query_seg_ref, key_seg_ref, out_ref, keys, values, highest, mixed, sems = refs[2 * count :]
    me = me_ref[0]
    rows = sources[0].shape[1]
    copies = []
    for piece, owners in enumerate(places):
        for at, owner in enumerate(owners):
            where = pl.ds(pl.multiple_of(owner(me) * rows, rows), rows)
            for kind, held in enumerate((keys, values)):
                copies.append(
                    pltpu.make_async_copy(
                        sources[kind * count + piece].at[at],
                        held.at[where, :],
                        sems.at[kind, piece, at],
                    )
                )
    for copy in copies:
        copy.start()
    for copy in copies:
        copy.wait()
    dim = HEAD_DIM
    heads = q_ref.shape[1] // dim
    factor = dim ** (-0.5) * LOG2E
    ones = jnp.ones((KEY_TILE, dim), jnp.bfloat16)
    for number in range(q_ref.shape[0] // tile):
        span = slice(number * tile, (number + 1) * tile)
        highest[...] = jnp.full_like(highest, -1e29)
        mixed[...] = jnp.zeros_like(mixed)

        def step(block, carry):
            where = pl.ds(pl.multiple_of(block * KEY_TILE, KEY_TILE), KEY_TILE)
            same = query_seg_ref[span, :] == key_seg_ref[block]
            for head in range(heads):
                cols = slice(head * dim, (head + 1) * dim)
                scores = lax.dot_general(
                    q_ref[span, cols],
                    keys[where, cols],
                    (((1,), (1,)), ((), ())),
                    preferred_element_type=jnp.float32,
                )
                scores = jnp.where(same, scores * factor, -1e30)
                former = highest[head]
                newest = jnp.maximum(former, jnp.max(scores, axis=1, keepdims=True))
                highest[head] = newest
                weights = jnp.exp2(scores - newest[:, :1]).astype(jnp.bfloat16)
                right = jnp.concatenate([values[where, cols], ones], axis=1)
                part = jnp.dot(weights, right, preferred_element_type=jnp.float32)
                shrink = jnp.exp2(former - newest)
                mixed[head, :, :dim] = mixed[head, :, :dim] * shrink + part[:, :dim]
                mixed[head, :, dim:] = mixed[head, :, dim:] * shrink + part[:, dim:]
            return carry

        lax.fori_loop(bounds_ref[number, 0], bounds_ref[number, 1], step, 0)
        for head in range(heads):
            out_ref[span, head * dim : (head + 1) * dim] = (
                mixed[head, :, :dim] / mixed[head, :, dim:]
            ).astype(out_ref.dtype)


def key_bounds(query_seg, segment_ids, tile):
    rows = query_seg.shape[0]
    tiled = query_seg.reshape(rows // tile, tile)
    first, last = tiled[:, 0], tiled[:, -1]
    low = jnp.sum(segment_ids[None, :] < first[:, None], axis=1, dtype=jnp.int32)
    high = jnp.sum(segment_ids[None, :] <= last[:, None], axis=1, dtype=jnp.int32)
    return jnp.stack([low // KEY_TILE, (high + KEY_TILE - 1) // KEY_TILE], axis=1)


def attend(query, key_pieces, value_pieces, places, me, bounds, query_seg, key_seg, tile):
    rows, cols = query.shape
    tokens = key_seg.shape[0] * KEY_TILE
    dim = HEAD_DIM
    heads = cols // dim
    smem = pl.BlockSpec(memory_space=pltpu.SMEM)
    whole = pl.BlockSpec(memory_space=pltpu.VMEM)
    anywhere = pl.BlockSpec(memory_space=pl.ANY)
    return pl.pallas_call(
        functools.partial(attend_kernel, places, tile),
        in_specs=[smem, smem, whole] + [anywhere] * (2 * len(places)) + [whole, whole],
        out_specs=whole,
        scratch_shapes=[
            pltpu.VMEM((tokens, cols), jnp.bfloat16),
            pltpu.VMEM((tokens, cols), jnp.bfloat16),
            pltpu.VMEM((heads, tile, dim), jnp.float32),
            pltpu.VMEM((heads, tile, 2 * dim), jnp.float32),
            pltpu.SemaphoreType.DMA((2, len(places), len(places[0]))),
        ],
        out_shape=jax.ShapeDtypeStruct((rows, cols), jnp.bfloat16),
        compiler_params=pltpu.CompilerParams(vmem_limit_bytes=VMEM),
        cost_estimate=pl.CostEstimate(
            flops=2 * rows * tokens * cols,
            bytes_accessed=4 * tokens * cols + 4 * rows * cols,
            transcendentals=rows * tokens * heads // 2,
        ),
        name="attend",
    )(
        me.reshape(1),
        bounds,
        query,
        *key_pieces,
        *value_pieces,
        query_seg,
        key_seg,
    )


def pages_kernel(places, me_ref, page_ref, *refs):
    count = len(places)
    out_ref, sems = refs[-2:]
    me = me_ref[0]
    wanted = out_ref.shape[0]
    chunks = (len(refs) - 2) // count
    per_block = refs[0].shape[1] // PAGE
    waits = []
    for number in range(wanted):
        page = page_ref[number]
        rows = pl.ds(pl.multiple_of((page % per_block) * PAGE, PAGE), PAGE)
        start = 0
        for chunk in range(chunks):
            sources = refs[chunk * count : (chunk + 1) * count]
            cols = pl.ds(start, sources[0].shape[2])
            start += sources[0].shape[2]
            sem = sems.at[number, chunk]
            target = out_ref.at[number, :, cols]
            for piece, owners in enumerate(places):
                for at, owner in enumerate(owners):

                    @pl.when(page // per_block == owner(me))
                    def _(source=sources[piece].at[at, rows, :], target=target, sem=sem):
                        pltpu.make_async_copy(source, target, sem).start()

            waits.append(
                pltpu.make_async_copy(sources[0].at[0, pl.ds(0, PAGE), :], target, sem)
            )
    for copy in waits:
        copy.wait()


def pick_pages(chunks, places, me, pages):
    cols = sum(pieces[0].shape[2] for pieces in chunks)
    wanted = pages.shape[0]
    smem = pl.BlockSpec(memory_space=pltpu.SMEM)
    anywhere = pl.BlockSpec(memory_space=pl.ANY)
    return pl.pallas_call(
        functools.partial(pages_kernel, places),
        in_specs=[smem, smem] + [anywhere] * (len(chunks) * len(places)),
        out_specs=pl.BlockSpec(memory_space=pltpu.VMEM),
        out_shape=jax.ShapeDtypeStruct((wanted, PAGE, cols), jnp.bfloat16),
        scratch_shapes=[pltpu.SemaphoreType.DMA((wanted, len(chunks)))],
        compiler_params=pltpu.CompilerParams(vmem_limit_bytes=VMEM),
        cost_estimate=pl.CostEstimate(
            flops=0, bytes_accessed=4 * wanted * PAGE * cols, transcendentals=0
        ),
        name="pick_pages",
    )(me.reshape(1), pages, *[piece for pieces in chunks for piece in pieces])


def own_pages(page_table, start, count):
    page_total = page_table.shape[0]
    inverse = (
        jnp.zeros((page_total,), jnp.int32)
        .at[page_table]
        .set(jnp.arange(page_total, dtype=jnp.int32))
    )
    return lax.dynamic_slice_in_dim(inverse, start, count, 0)


def whole_heads(ring, hidden, modulation, weights, gains, positions, segment_ids, page_table):
    tok_rows = hidden.shape[0]
    me = lax.axis_index("row")
    full_rows = lax.all_gather(hidden, "col", axis=1, tiled=True)
    modulated = modulate(full_rows.astype(jnp.float32), modulation)
    width = full_rows.shape[1]
    raws = [
        jnp.dot(
            modulated,
            lax.all_gather(weight, "row", axis=0, tiled=True),
            preferred_element_type=jnp.float32,
        )
        for weight in weights
    ]
    squares = lax.psum(tuple(jnp.sum(raw * raw, axis=1) for raw in raws[:2]), "col")
    tables = rotary_lanes(positions, HEAD_DIM)
    cols = raws[0].shape[1]
    query, key = [
        turn(raw, total[None], jnp.zeros_like(total)[None], gain, tables, width, (cols,))[0]
        for raw, total, gain in zip(raws, squares, gains)
    ]
    value = raws[2].astype(jnp.bfloat16)
    keys_all = lax.all_gather(key, "row", axis=0)
    values_all = lax.all_gather(value, "row", axis=0)
    places = (tuple(lambda me, at=at: at for at in range(ring)),)
    none = jnp.zeros((), jnp.int32)
    query_seg = lax.dynamic_slice_in_dim(segment_ids, me * tok_rows, tok_rows, 0)
    attended = attend(
        query,
        [keys_all],
        [values_all],
        places,
        none,
        key_bounds(query_seg, segment_ids, tok_rows),
        query_seg[:, None],
        segment_ids.reshape(-1, 1, KEY_TILE),
        tok_rows,
    )
    count = tok_rows // PAGE
    pages = own_pages(page_table, me * count, count)
    picked = [pick_pages([[held]], places, none, pages) for held in (keys_all, values_all)]
    return attended, jnp.stack(picked)


def split_heads(ring, ranks, hidden, modulation, weights, gains, positions, segment_ids, page_table):
    tok_rows, shard = hidden.shape
    feats = weights[0].shape[0]
    width = ring * feats
    me = lax.axis_index("row")
    rank = lax.axis_index("col")
    top = ring // 2
    half = me // top
    low = me % top
    cols = weights[0].shape[1] // 2
    steps = []
    bit = top // 2
    while bit:
        steps.append(bit)
        bit //= 2

    def swap(value, bit):
        return lax.ppermute(value, "row", [(i, i ^ bit) for i in range(ring)])

    def half_of(value, which):
        return lax.dynamic_slice_in_dim(value, which * cols, cols, value.ndim - 1)

    def in_order(mine, other, axis):
        return jnp.where(
            half == 0,
            jnp.concatenate([mine, other], axis=axis),
            jnp.concatenate([other, mine], axis=axis),
        )

    def spread(blocks):
        for bit in steps:
            blocks.update(
                {
                    number | bit: jax.tree.map(lambda part: swap(part, bit), blocks[number])
                    for number in list(blocks)
                }
            )
        return blocks

    heads = cols // HEAD_DIM
    chunk_cols = (heads // 2 * HEAD_DIM, (heads - heads // 2) * HEAD_DIM)
    w_query, w_key, w_value = weights
    ordered = (w_key, w_value, w_query)
    sends = [half_of(weight, 1 - half) for weight in ordered]
    positions_other = swap(positions, top)
    positions_other, sends[0] = lax.optimization_barrier((positions_other, sends[0]))

    rows = hidden.astype(jnp.float32)
    local_mean = jnp.mean(rows, axis=1)
    local_square = jnp.sum(jnp.square(rows - local_mean[:, None]), axis=1)
    stats = jnp.stack([local_mean, local_square])
    all_stats = [stats] + [
        lax.ppermute(stats, "col", [(c, (c + step) % ranks) for c in range(ranks)])
        for step in range(1, ranks)
    ]
    all_stats, sends = lax.optimization_barrier((all_stats, sends))
    average = sum(part[0] for part in all_stats) / ranks
    variance = (
        sum(part[1] + shard * jnp.square(part[0] - average) for part in all_stats) / width
    )
    shift = lax.dynamic_slice_in_dim(modulation, rank * shard, shard, 1)
    mod = (rows - average[:, None]) * lax.rsqrt(variance + epsilon)[:, None]
    mod = (mod * (1.0 + shift[1]) + shift[0]).astype(jnp.bfloat16)
    groups = [
        [row * ranks + c for row in (first, first + top) for c in range(ranks)]
        for first in range(top)
    ]
    mod_all = lax.all_gather(mod, ("row", "col"), axis_index_groups=groups, axis=0)

    own = jnp.stack([half_of(weight, half) for weight in ordered])
    blocks = spread({0: own, top: [swap(part, top) for part in sends]})
    sources, spots = [], []
    for number in range(ring):
        held = blocks[number]
        if isinstance(held, list):
            spots.append(tuple((len(sources) + m, None) for m in range(3)))
            sources.extend(held)
        else:
            spots.append(tuple((len(sources), m) for m in range(3)))
            sources.append(held)

    tables = rotary_lanes(in_order(positions, positions_other, 1), HEAD_DIM)
    q_gain, k_gain = [half_of(gain, half) for gain in gains]
    count = tok_rows // PAGE
    pages = jnp.concatenate(
        [own_pages(page_table, owner * count, count) for owner in (me, me ^ top)]
    )
    query_seg = jnp.concatenate(
        [
            lax.dynamic_slice_in_dim(segment_ids, owner * tok_rows, tok_rows, 0)
            for owner in (low, low + top)
        ]
    )
    bounds = key_bounds(query_seg, segment_ids, tok_rows)
    prepared = (tables, q_gain, k_gain, pages, query_seg[:, None], bounds)
    mod_all, prepared = lax.optimization_barrier((mod_all, prepared))
    tables, q_gain, k_gain, pages, query_seg, bounds = prepared
    key_seg = segment_ids.reshape(-1, 1, KEY_TILE)

    key_raw, query_raw, squares, *values = project(
        mod_all, ranks, me, tuple(spots), sources, feats, cols, chunk_cols
    )
    places = tuple(
        tuple(lambda me, n=number, g=group: ((me % top) ^ n) + g * top for group in range(2))
        for number in range(top)
    )

    def pieces_of(value):
        held = spread({0: value})
        return [held[number] for number in range(top)]

    value_pieces = [pieces_of(value) for value in values]
    squares = squares + swap(squares, top)
    bit = 1
    while 2 * bit < ranks:
        squares = squares + lax.ppermute(squares, "col", [(c, c ^ bit) for c in range(ranks)])
        bit *= 2
    squares_other = lax.ppermute(squares, "col", [(c, c ^ bit) for c in range(ranks)])
    squares_other, value_pieces[0] = lax.optimization_barrier((squares_other, value_pieces[0]))
    flat = (2 * tok_rows, cols)
    shape = (2, tok_rows, -1)
    keys = turn(
        key_raw.reshape(flat), squares[:2], squares_other[:2], k_gain, tables, width, chunk_cols
    )
    key_pieces = [pieces_of(key.reshape(shape)) for key in keys]
    queries = turn(
        query_raw.reshape(flat), squares[2:], squares_other[2:], q_gain, tables, width, chunk_cols
    )

    picked = [pick_pages(pieces, places, me, pages) for pieces in (key_pieces, value_pieces)]
    picked_other = [swap(part[count:], top) for part in picked]
    own_parts, other_parts = [], []
    for chunk in range(2):
        attended = attend(
            queries[chunk],
            key_pieces[chunk],
            value_pieces[chunk],
            places,
            me,
            bounds,
            query_seg,
            key_seg,
            tok_rows,
        )
        own_parts.append(lax.dynamic_slice_in_dim(attended, half * tok_rows, tok_rows, 0))
        sent = lax.dynamic_slice_in_dim(attended, (1 - half) * tok_rows, tok_rows, 0)
        other_parts.append(swap(sent, top))
    page_store = [in_order(a[:count], b, -1) for a, b in zip(picked, picked_other)]
    return (
        in_order(jnp.concatenate(own_parts, axis=1), jnp.concatenate(other_parts, axis=1), -1),
        jnp.stack(page_store),
    )


def solution(mesh):
    ring, ranks = mesh.shape["row"], mesh.shape["col"]

    def body(
        hidden, modulation, w_query, w_key, w_value, q_gain, k_gain, positions, segment_ids, page_table
    ):
        rest = (
            hidden,
            modulation,
            (w_query, w_key, w_value),
            (q_gain, k_gain),
            positions,
            segment_ids,
            page_table,
        )
        heads = w_query.shape[1] // HEAD_DIM
        feats, shard = w_query.shape[0], hidden.shape[1]
        powers = ring & (ring - 1) == 0 and ranks & (ranks - 1) == 0
        if heads % 2 == 0 and ring % 2 == 0 and powers and feats % 128 == 0 and shard % feats == 0:
            return split_heads(ring, ranks, *rest)
        return whole_heads(ring, *rest)

    in_specs = (
        P("row", "col"),
        P(),
        P("row", "col"),
        P("row", "col"),
        P("row", "col"),
        P("col"),
        P("col"),
        P(None, "row"),
        P(),
        P(),
    )
    out_specs = (P("row", "col"), P(None, "row", None, "col"))
    return jax.shard_map(body, mesh=mesh, in_specs=in_specs, out_specs=out_specs, check_vma=False)
```

```python
import functools
import jax
import jax.numpy as jnp
from jax import lax
from jax.experimental import pallas as pl
from jax.experimental.pallas import tpu as pltpu
from jax.sharding import PartitionSpec as P

HEAD_DIM = 128
PAGE = 128
KEY_TILE = 512
VMEM = 60 * 1024 * 1024
LOG2E = 1.4426950408889634

epsilon = 1e-06


def rotary_table(positions, pair_count):
    frame_pairs = pair_count - 2 * (pair_count // 3)
    side_pairs = pair_count // 3
    column = jnp.arange(pair_count)
    frame_rate = 10000.0 ** (-column.astype(jnp.float32) / frame_pairs)
    height_rate = 10000.0 ** (-(column - frame_pairs).astype(jnp.float32) / side_pairs)
    width_rate = 10000.0 ** (-(column - frame_pairs - side_pairs).astype(jnp.float32) / side_pairs)
    coords = positions.astype(jnp.float32)
    angles = jnp.where(
        column < frame_pairs,
        coords[0][:, None] * frame_rate,
        jnp.where(
            column < frame_pairs + side_pairs,
            coords[1][:, None] * height_rate,
            coords[2][:, None] * width_rate,
        ),
    )
    return (jnp.cos(angles), jnp.sin(angles))


def rotary_lanes(positions, head_dim):
    cosine, sine_table = rotary_table(positions, head_dim // 2)
    own = jnp.repeat(cosine, 2, axis=1)
    sine = jnp.repeat(sine_table, 2, axis=1)
    even = (jnp.arange(head_dim) % 2 == 0)[None, :]
    return own, jnp.where(even, -sine, 0.0), jnp.where(even, 0.0, sine)


def modulate(activations, modulation):
    average = jnp.mean(activations, axis=1, keepdims=True)
    centred = activations - average
    variance = jnp.mean(centred * centred, axis=1, keepdims=True)
    normed = centred * lax.rsqrt(variance + epsilon)
    return (normed * (1.0 + modulation[1]) + modulation[0]).astype(jnp.bfloat16)


def cut_kernel(half_ref, *refs):
    count = (len(refs) - 1) // 2
    own_ref, send_refs = refs[count], refs[count + 1 :]
    cols = own_ref.shape[2]
    half = half_ref[0]
    for number in range(count):
        own_ref[number] = refs[number][:, pl.ds(pl.multiple_of(half * cols, cols), cols)]
        send_refs[number][...] = refs[number][
            :, pl.ds(pl.multiple_of((1 - half) * cols, cols), cols)
        ]


def cut(weights, half):
    rows, width = weights[0].shape
    cols = width // 2
    tile = 128
    count = len(weights)
    return pl.pallas_call(
        cut_kernel,
        grid_spec=pltpu.PrefetchScalarGridSpec(
            num_scalar_prefetch=1,
            grid=(rows // tile,),
            in_specs=[pl.BlockSpec((tile, width), lambda i, _: (i, 0))] * count,
            out_specs=[pl.BlockSpec((count, tile, cols), lambda i, _: (0, i, 0))]
            + [pl.BlockSpec((tile, cols), lambda i, _: (i, 0))] * count,
        ),
        out_shape=[jax.ShapeDtypeStruct((count, rows, cols), jnp.bfloat16)]
        + [jax.ShapeDtypeStruct((rows, cols), jnp.bfloat16)] * count,
        compiler_params=pltpu.CompilerParams(vmem_limit_bytes=VMEM),
        cost_estimate=pl.CostEstimate(
            flops=0, bytes_accessed=4 * count * rows * width, transcendentals=0
        ),
        name="cut",
    )(half.reshape(1), *weights)


def project_kernel(spots, ranks, chunks, me_ref, stats_ref, modulation_ref, hidden_ref, *refs):
    count = len(spots)
    tail = len(refs) - 9 - chunks
    sources, outs, scratch = refs[:tail], refs[tail:-6], refs[-6:]
    key_ref, query_ref, squares_ref = outs[:3]
    value_refs = outs[3:]
    raws, weights, ready, total, raw_sems, weight_sems = scratch
    me = me_ref[0]
    feats, cols = weights.shape[2:]
    rows = hidden_ref.shape[1]
    groups = raws.shape[1] // rows
    per_rank = hidden_ref.shape[2] // feats
    copies = []
    for block, spot in enumerate(spots):
        owner = me ^ block
        span = pl.ds(pl.multiple_of((owner % per_rank) * feats, feats), feats)
        parts = [
            pltpu.make_async_copy(
                hidden_ref.at[group * ranks + owner // per_rank, :, span],
                raws.at[block, pl.ds(group * rows, rows), :],
                raw_sems.at[block, group],
            )
            for group in range(groups)
        ]
        matrices = [
            pltpu.make_async_copy(
                sources[source] if at is None else sources[source].at[at],
                weights.at[block, number],
                weight_sems.at[block, number],
            )
            for number, (source, at) in enumerate(spot)
        ]
        for copy in parts + matrices:
            copy.start()
        copies.append((parts, matrices))

    def column(at):
        return jnp.transpose(jnp.broadcast_to(stats_ref[at : at + 1, :], (128, rows)))

    means = [column(group) for group in range(groups)]
    scales = [column(groups + group) for group in range(groups)]

    def prepare(first):
        for block in (first, first + 1):
            for copy in copies[block][0]:
                copy.wait()
            span = pl.ds(pl.multiple_of((me ^ block) * feats, feats), feats)
            shift = modulation_ref[0:1, span]
            gain = 1.0 + modulation_ref[1:2, span]
            left = (block - first) * feats
            for group in range(groups):
                lines = slice(group * rows, (group + 1) * rows)
                for start in range(0, feats, 128):
                    lanes = slice(start, start + 128)
                    part = raws[block, lines, lanes].astype(jnp.float32)
                    part = (part - means[group]) * scales[group] * gain[:, lanes] + shift[:, lanes]
                    ready[first // 2 % 2, lines, left + start : left + start + 128] = part.astype(
                        jnp.bfloat16
                    )

    prepare(0)
    for first in range(0, count, 2):
        for copy in copies[first][1] + copies[first + 1][1]:
            copy.wait()
        if first + 2 < count:
            prepare(first + 2)
        right = jnp.concatenate(
            [
                jnp.concatenate([weights[first, m], weights[first + 1, m]], axis=0)
                for m in range(3)
            ],
            axis=1,
        )
        part = jnp.dot(ready[first // 2 % 2], right, preferred_element_type=jnp.float32)
        if first:
            part = part + total[...]
        if first < count - 2:
            total[...] = part
        else:
            key_ref[...] = part[:, :cols]
            query_ref[...] = part[:, 2 * cols :]
            start = cols
            for value_ref in value_refs:
                value_ref[...] = part[:, start : start + value_ref.shape[1]].astype(
                    value_ref.dtype
                )
                start += value_ref.shape[1]
            for kind, raw in enumerate((part[:, :cols], part[:, 2 * cols :])):
                for group in range(groups):
                    mine = raw[group * rows : (group + 1) * rows]
                    summed = jnp.sum(mine * mine, axis=1, keepdims=True)
                    summed = jnp.transpose(jnp.broadcast_to(summed, (rows, 128)))
                    at = kind * groups + group
                    squares_ref[at : at + 1, :] = summed[:1]


def project(hidden_all, stats, modulation, ranks, me, spots, sources, feats, cols, chunk_cols):
    rows = hidden_all.shape[1]
    groups = hidden_all.shape[0] // ranks
    lines = groups * rows
    blocks = len(spots)
    raw = jax.ShapeDtypeStruct((lines, cols), jnp.float32)
    anywhere = pl.BlockSpec(memory_space=pl.ANY)
    whole = pl.BlockSpec(memory_space=pltpu.VMEM)
    return pl.pallas_call(
        functools.partial(project_kernel, spots, ranks, len(chunk_cols)),
        in_specs=[pl.BlockSpec(memory_space=pltpu.SMEM), whole, whole, anywhere]
        + [anywhere] * len(sources),
        out_specs=[whole] * (3 + len(chunk_cols)),
        out_shape=[raw, raw, jax.ShapeDtypeStruct((2 * groups, rows), jnp.float32)]
        + [jax.ShapeDtypeStruct((lines, part), jnp.bfloat16) for part in chunk_cols],
        scratch_shapes=[
            pltpu.VMEM((blocks, lines, feats), jnp.bfloat16),
            pltpu.VMEM((blocks, 3, feats, cols), jnp.bfloat16),
            pltpu.VMEM((2, lines, 2 * feats), jnp.bfloat16),
            pltpu.VMEM((lines, 3 * cols), jnp.float32),
            pltpu.SemaphoreType.DMA((blocks, groups)),
            pltpu.SemaphoreType.DMA((blocks, 3)),
        ],
        compiler_params=pltpu.CompilerParams(vmem_limit_bytes=VMEM),
        cost_estimate=pl.CostEstimate(
            flops=6 * lines * blocks * feats * cols,
            bytes_accessed=2 * blocks * feats * (lines + 3 * cols) + 10 * lines * cols,
            transcendentals=0,
        ),
        name="project",
    )(me.reshape(1), stats, modulation, hidden_all, *sources)


def turn_kernel(width, raw_ref, mine_ref, other_ref, gain_ref, own_ref, upper_ref, lower_ref, *outs):
    dim = own_ref.shape[1]
    rows = raw_ref.shape[0]
    scale = lax.rsqrt((mine_ref[0] + other_ref[0]) * (1.0 / width) + epsilon)
    scale = jnp.transpose(jnp.broadcast_to(scale, (128, rows)))
    own, upper, lower = own_ref[...], upper_ref[...], lower_ref[...]
    start = 0
    for out_ref in outs:
        for head in range(out_ref.shape[1] // dim):
            cols = slice(start + head * dim, start + (head + 1) * dim)
            normed = raw_ref[:, cols] * scale * gain_ref[:, cols]
            turned = (
                normed * own
                + pltpu.roll(normed, dim - 1, 1) * upper
                + pltpu.roll(normed, 1, 1) * lower
            )
            out_ref[:, head * dim : (head + 1) * dim] = turned.astype(out_ref.dtype)
        start += out_ref.shape[1]


def turn(raw, mine, other, gain, tables, width, chunk_cols):
    rows, cols = raw.shape
    groups = mine.shape[0]
    tile = rows // groups
    dim = tables[0].shape[1]
    sums = [part.reshape(groups, 1, tile) for part in (mine, other)]
    return pl.pallas_call(
        functools.partial(turn_kernel, width),
        grid=(groups,),
        in_specs=[pl.BlockSpec((tile, cols), lambda i: (i, 0))]
        + [pl.BlockSpec((1, 1, tile), lambda i: (i, 0, 0))] * 2
        + [pl.BlockSpec((1, cols), lambda i: (0, 0))]
        + [pl.BlockSpec((tile, dim), lambda i: (i, 0))] * 3,
        out_specs=[pl.BlockSpec((tile, part), lambda i: (i, 0)) for part in chunk_cols],
        out_shape=[jax.ShapeDtypeStruct((rows, part), jnp.bfloat16) for part in chunk_cols],
        compiler_params=pltpu.CompilerParams(vmem_limit_bytes=VMEM),
        cost_estimate=pl.CostEstimate(
            flops=8 * rows * cols, bytes_accessed=6 * rows * cols, transcendentals=0
        ),
        name="turn",
    )(raw, *sums, gain[None, :], *tables)


def attend_kernel(places, tile, me_ref, order_ref, bounds_ref, q_ref, *refs):
    count = len(places)
    sources, (query_seg_ref, key_seg_ref) = refs[: 2 * count], refs[2 * count : 2 * count + 2]
    out_refs = refs[2 * count + 2 : -5]
    keys, values, highest, mixed, sems = refs[-5:]
    me = me_ref[0]
    rows = sources[0].shape[1]
    copies = []
    for piece, owners in enumerate(places):
        for at, owner in enumerate(owners):
            where = pl.ds(pl.multiple_of(owner(me) * rows, rows), rows)
            for kind, held in enumerate((keys, values)):
                copies.append(
                    pltpu.make_async_copy(
                        sources[kind * count + piece].at[at],
                        held.at[where, :],
                        sems.at[kind, piece, at],
                    )
                )
    for copy in copies:
        copy.start()
    for copy in copies:
        copy.wait()
    dim = HEAD_DIM
    heads = q_ref.shape[1] // dim
    factor = dim ** (-0.5) * LOG2E
    ones = jnp.ones((KEY_TILE, dim), jnp.bfloat16)
    for place, out_ref in enumerate(out_refs):
        number = order_ref[place]
        span = pl.ds(pl.multiple_of(number * tile, tile), tile)
        highest[...] = jnp.full_like(highest, -1e29)
        mixed[...] = jnp.zeros_like(mixed)

        def step(block, carry):
            where = pl.ds(pl.multiple_of(block * KEY_TILE, KEY_TILE), KEY_TILE)
            same = query_seg_ref[span, :] == key_seg_ref[block]
            for head in range(heads):
                cols = slice(head * dim, (head + 1) * dim)
                scores = lax.dot_general(
                    q_ref[span, cols],
                    keys[where, cols],
                    (((1,), (1,)), ((), ())),
                    preferred_element_type=jnp.float32,
                )
                scores = jnp.where(same, scores * factor, -1e30)
                former = highest[head]
                newest = jnp.maximum(former, jnp.max(scores, axis=1, keepdims=True))
                highest[head] = newest
                weights = jnp.exp2(scores - newest[:, :1]).astype(jnp.bfloat16)
                right = jnp.concatenate([values[where, cols], ones], axis=1)
                part = jnp.dot(weights, right, preferred_element_type=jnp.float32)
                shrink = jnp.exp2(former - newest)
                mixed[head, :, :dim] = mixed[head, :, :dim] * shrink + part[:, :dim]
                mixed[head, :, dim:] = mixed[head, :, dim:] * shrink + part[:, dim:]
            return carry

        lax.fori_loop(bounds_ref[number, 0], bounds_ref[number, 1], step, 0)
        for head in range(heads):
            out_ref[:, head * dim : (head + 1) * dim] = (
                mixed[head, :, :dim] / mixed[head, :, dim:]
            ).astype(out_ref.dtype)


def key_bounds(query_seg, segment_ids, tile):
    rows = query_seg.shape[0]
    tiled = query_seg.reshape(rows // tile, tile)
    first, last = tiled[:, 0], tiled[:, -1]
    low = jnp.sum(segment_ids[None, :] < first[:, None], axis=1, dtype=jnp.int32)
    high = jnp.sum(segment_ids[None, :] <= last[:, None], axis=1, dtype=jnp.int32)
    return jnp.stack([low // KEY_TILE, (high + KEY_TILE - 1) // KEY_TILE], axis=1)


def attend(query, key_pieces, value_pieces, places, me, order, bounds, query_seg, key_seg, tile):
    rows, cols = query.shape
    tokens = key_seg.shape[0] * KEY_TILE
    dim = HEAD_DIM
    heads = cols // dim
    smem = pl.BlockSpec(memory_space=pltpu.SMEM)
    whole = pl.BlockSpec(memory_space=pltpu.VMEM)
    anywhere = pl.BlockSpec(memory_space=pl.ANY)
    return pl.pallas_call(
        functools.partial(attend_kernel, places, tile),
        in_specs=[smem, smem, smem, whole] + [anywhere] * (2 * len(places)) + [whole, whole],
        out_specs=[whole] * (rows // tile),
        scratch_shapes=[
            pltpu.VMEM((tokens, cols), jnp.bfloat16),
            pltpu.VMEM((tokens, cols), jnp.bfloat16),
            pltpu.VMEM((heads, tile, dim), jnp.float32),
            pltpu.VMEM((heads, tile, 2 * dim), jnp.float32),
            pltpu.SemaphoreType.DMA((2, len(places), len(places[0]))),
        ],
        out_shape=[jax.ShapeDtypeStruct((tile, cols), jnp.bfloat16)] * (rows // tile),
        compiler_params=pltpu.CompilerParams(vmem_limit_bytes=VMEM),
        cost_estimate=pl.CostEstimate(
            flops=2 * rows * tokens * cols,
            bytes_accessed=4 * tokens * cols + 4 * rows * cols,
            transcendentals=rows * tokens * heads // 2,
        ),
        name="attend",
    )(
        me.reshape(1),
        order,
        bounds,
        query,
        *key_pieces,
        *value_pieces,
        query_seg,
        key_seg,
    )


def pages_kernel(places, me_ref, page_ref, *refs):
    count = len(places)
    sems = refs[-1]
    wanted, chunks = sems.shape
    out_refs = refs[chunks * count : -1]
    me = me_ref[0]
    each = wanted // len(out_refs)
    per_block = refs[0].shape[1] // PAGE
    waits = []
    for number in range(wanted):
        page = page_ref[number]
        rows = pl.ds(pl.multiple_of((page % per_block) * PAGE, PAGE), PAGE)
        start = 0
        for chunk in range(chunks):
            sources = refs[chunk * count : (chunk + 1) * count]
            cols = pl.ds(start, sources[0].shape[2])
            start += sources[0].shape[2]
            sem = sems.at[number, chunk]
            target = out_refs[number // each].at[number % each, :, cols]
            for piece, owners in enumerate(places):
                for at, owner in enumerate(owners):

                    @pl.when(page // per_block == owner(me))
                    def _(source=sources[piece].at[at, rows, :], target=target, sem=sem):
                        pltpu.make_async_copy(source, target, sem).start()

            waits.append(
                pltpu.make_async_copy(sources[0].at[0, pl.ds(0, PAGE), :], target, sem)
            )
    for copy in waits:
        copy.wait()


def pick_pages(chunks, places, me, pages, parts):
    cols = sum(pieces[0].shape[2] for pieces in chunks)
    wanted = pages.shape[0]
    smem = pl.BlockSpec(memory_space=pltpu.SMEM)
    anywhere = pl.BlockSpec(memory_space=pl.ANY)
    return pl.pallas_call(
        functools.partial(pages_kernel, places),
        in_specs=[smem, smem] + [anywhere] * (len(chunks) * len(places)),
        out_specs=[pl.BlockSpec(memory_space=pltpu.VMEM)] * parts,
        out_shape=[jax.ShapeDtypeStruct((wanted // parts, PAGE, cols), jnp.bfloat16)] * parts,
        scratch_shapes=[pltpu.SemaphoreType.DMA((wanted, len(chunks)))],
        compiler_params=pltpu.CompilerParams(vmem_limit_bytes=VMEM),
        cost_estimate=pl.CostEstimate(
            flops=0, bytes_accessed=4 * wanted * PAGE * cols, transcendentals=0
        ),
        name="pick_pages",
    )(me.reshape(1), pages, *[piece for pieces in chunks for piece in pieces])


def own_pages(page_table, start, count):
    page_total = page_table.shape[0]
    inverse = (
        jnp.zeros((page_total,), jnp.int32)
        .at[page_table]
        .set(jnp.arange(page_total, dtype=jnp.int32))
    )
    return lax.dynamic_slice_in_dim(inverse, start, count, 0)


def whole_heads(ring, hidden, modulation, weights, gains, positions, segment_ids, page_table):
    tok_rows = hidden.shape[0]
    me = lax.axis_index("row")
    full_rows = lax.all_gather(hidden, "col", axis=1, tiled=True)
    modulated = modulate(full_rows.astype(jnp.float32), modulation)
    width = full_rows.shape[1]
    raws = [
        jnp.dot(
            modulated,
            lax.all_gather(weight, "row", axis=0, tiled=True),
            preferred_element_type=jnp.float32,
        )
        for weight in weights
    ]
    squares = lax.psum(tuple(jnp.sum(raw * raw, axis=1) for raw in raws[:2]), "col")
    tables = rotary_lanes(positions, HEAD_DIM)
    cols = raws[0].shape[1]
    query, key = [
        turn(raw, total[None], jnp.zeros_like(total)[None], gain, tables, width, (cols,))[0]
        for raw, total, gain in zip(raws, squares, gains)
    ]
    value = raws[2].astype(jnp.bfloat16)
    keys_all = lax.all_gather(key, "row", axis=0)
    values_all = lax.all_gather(value, "row", axis=0)
    places = (tuple(lambda me, at=at: at for at in range(ring)),)
    none = jnp.zeros((), jnp.int32)
    query_seg = lax.dynamic_slice_in_dim(segment_ids, me * tok_rows, tok_rows, 0)
    attended = attend(
        query,
        [keys_all],
        [values_all],
        places,
        none,
        none.reshape(1),
        key_bounds(query_seg, segment_ids, tok_rows),
        query_seg[:, None],
        segment_ids.reshape(-1, 1, KEY_TILE),
        tok_rows,
    )[0]
    count = tok_rows // PAGE
    pages = own_pages(page_table, me * count, count)
    picked = [pick_pages([[held]], places, none, pages, 1)[0] for held in (keys_all, values_all)]
    return attended, jnp.stack(picked)


def split_heads(ring, ranks, hidden, modulation, weights, gains, positions, segment_ids, page_table):
    tok_rows, shard = hidden.shape
    feats = weights[0].shape[0]
    width = ring * feats
    me = lax.axis_index("row")
    rank = lax.axis_index("col")
    top = ring // 2
    half = me // top
    low = me % top
    cols = weights[0].shape[1] // 2
    steps = []
    bit = top // 2
    while bit:
        steps.append(bit)
        bit //= 2

    def swap(value, bit):
        return lax.ppermute(value, "row", [(i, i ^ bit) for i in range(ring)])

    def half_of(value, which):
        return lax.dynamic_slice_in_dim(value, which * cols, cols, value.ndim - 1)

    def in_order(mine, other, axis):
        return jnp.where(
            half == 0,
            jnp.concatenate([mine, other], axis=axis),
            jnp.concatenate([other, mine], axis=axis),
        )

    def spread(blocks):
        for bit in steps:
            blocks.update(
                {
                    number | bit: jax.tree.map(lambda part: swap(part, bit), blocks[number])
                    for number in list(blocks)
                }
            )
        return blocks

    heads = cols // HEAD_DIM
    chunk_cols = ((heads - heads // 2) * HEAD_DIM, heads // 2 * HEAD_DIM)
    groups = [
        [row * ranks + c for row in (first, first + top) for c in range(ranks)]
        for first in range(top)
    ]
    hidden_all = lax.all_gather(hidden, ("row", "col"), axis_index_groups=groups, axis=0)

    rows = hidden.astype(jnp.float32)
    local_mean = jnp.mean(rows, axis=1)
    local_square = jnp.sum(jnp.square(rows - local_mean[:, None]), axis=1)
    stats = jnp.stack([local_mean, local_square])
    stats_other = swap(stats, top)
    positions_other = swap(positions, top)
    w_query, w_key, w_value = weights
    own, *sends = cut((w_key, w_value, w_query), half)
    stats_other, positions_other, sends = lax.optimization_barrier(
        (stats_other, positions_other, sends)
    )
    both = jnp.stack([stats, stats_other])
    all_stats = [both] + [
        lax.ppermute(both, "col", [(c, (c + step) % ranks) for c in range(ranks)])
        for step in range(1, ranks)
    ]
    average = sum(part[:, 0] for part in all_stats) / ranks
    variance = (
        sum(part[:, 1] + shard * jnp.square(part[:, 0] - average) for part in all_stats) / width
    )
    scale = lax.rsqrt(variance + epsilon)
    norm_stats = in_order(
        jnp.stack([average[0:1], scale[0:1]]), jnp.stack([average[1:2], scale[1:2]]), 1
    ).reshape(4, tok_rows)

    blocks = spread({0: own, top: [swap(part, top) for part in sends]})
    sources, spots = [], []
    for number in range(ring):
        held = blocks[number]
        if isinstance(held, list):
            spots.append(tuple((len(sources) + m, None) for m in range(3)))
            sources.extend(held)
        else:
            spots.append(tuple((len(sources), m) for m in range(3)))
            sources.append(held)

    tables = rotary_lanes(in_order(positions, positions_other, 1), HEAD_DIM)
    q_gain, k_gain = [half_of(gain, half) for gain in gains]
    count = tok_rows // PAGE
    pages = jnp.concatenate(
        [own_pages(page_table, owner * count, count) for owner in (me ^ top, me)]
    )
    query_seg = jnp.concatenate(
        [
            lax.dynamic_slice_in_dim(segment_ids, owner * tok_rows, tok_rows, 0)
            for owner in (low, low + top)
        ]
    )
    bounds = key_bounds(query_seg, segment_ids, tok_rows)
    prepared = (norm_stats, tables, q_gain, k_gain, pages, query_seg[:, None], bounds)
    hidden_all, prepared = lax.optimization_barrier((hidden_all, prepared))
    norm_stats, tables, q_gain, k_gain, pages, query_seg, bounds = prepared
    key_seg = segment_ids.reshape(-1, 1, KEY_TILE)

    key_raw, query_raw, squares, *values = project(
        hidden_all, norm_stats, modulation, ranks, me, tuple(spots), sources, feats, cols, chunk_cols
    )
    places = tuple(
        tuple(lambda me, n=number, g=group: ((me % top) ^ n) + g * top for group in range(2))
        for number in range(top)
    )

    def pieces_of(held):
        return [held[number] for number in range(top)]

    shape = (2, tok_rows, -1)
    values = [value.reshape(shape) for value in values]
    first_bit = steps[0]
    ahead = swap(values[0], first_bit)
    squares = squares + swap(squares, top)
    bit = 1
    while 2 * bit < ranks:
        squares = squares + lax.ppermute(squares, "col", [(c, c ^ bit) for c in range(ranks)])
        bit *= 2
    squares_other = lax.ppermute(squares, "col", [(c, c ^ bit) for c in range(ranks)])
    squares_other, ahead = lax.optimization_barrier((squares_other, ahead))
    held = {0: values[0], first_bit: ahead}
    for bit in steps[1:]:
        held.update({number | bit: swap(held[number], bit) for number in list(held)})
    value_pieces = [pieces_of(held), pieces_of(spread({0: values[1]}))]
    keys = turn(key_raw, squares[:2], squares_other[:2], k_gain, tables, width, chunk_cols)
    key_pieces = [pieces_of(spread({0: key.reshape(shape)})) for key in keys]
    queries = turn(query_raw, squares[2:], squares_other[2:], q_gain, tables, width, chunk_cols)

    order = jnp.stack([1 - half, half])
    picked = []
    own_parts, other_parts = [], []
    for chunk in range(2):
        query = queries[chunk]
        if chunk:
            picked = [
                pick_pages(pieces, places, me, pages, 2) for pieces in (key_pieces, value_pieces)
            ]
            query, picked = lax.optimization_barrier((query, picked))
        for_other, for_me = attend(
            query,
            key_pieces[chunk],
            value_pieces[chunk],
            places,
            me,
            order,
            bounds,
            query_seg,
            key_seg,
            tok_rows,
        )
        own_parts.append(for_me)
        other_parts.append(swap(for_other, top))
    page_store = [in_order(mine, swap(other, top), -1) for other, mine in picked]
    return (
        in_order(jnp.concatenate(own_parts, axis=1), jnp.concatenate(other_parts, axis=1), -1),
        jnp.stack(page_store),
    )


def solution(mesh):
    ring, ranks = mesh.shape["row"], mesh.shape["col"]

    def body(
        hidden, modulation, w_query, w_key, w_value, q_gain, k_gain, positions, segment_ids, page_table
    ):
        rest = (
            hidden,
            modulation,
            (w_query, w_key, w_value),
            (q_gain, k_gain),
            positions,
            segment_ids,
            page_table,
        )
        heads = w_query.shape[1] // HEAD_DIM
        feats, shard = w_query.shape[0], hidden.shape[1]
        powers = ring & (ring - 1) == 0 and ranks & (ranks - 1) == 0
        if heads % 2 == 0 and ring % 2 == 0 and powers and feats % 128 == 0 and shard % feats == 0:
            return split_heads(ring, ranks, *rest)
        return whole_heads(ring, *rest)

    in_specs = (
        P("row", "col"),
        P(),
        P("row", "col"),
        P("row", "col"),
        P("row", "col"),
        P("col"),
        P("col"),
        P(None, "row"),
        P(),
        P(),
    )
    out_specs = (P("row", "col"), P(None, "row", None, "col"))
    return jax.shard_map(body, mesh=mesh, in_specs=in_specs, out_specs=out_specs, check_vma=False)
```

```python
import functools
import jax
import jax.numpy as jnp
from jax import lax
from jax.experimental import pallas as pl
from jax.experimental.pallas import tpu as pltpu
from jax.sharding import PartitionSpec as P

HEAD_DIM = 128
PAGE = 128
KEY_TILE = 512
VMEM = 60 * 1024 * 1024
LOG2E = 1.4426950408889634

epsilon = 1e-06


def rotary_table(positions, pair_count):
    frame_pairs = pair_count - 2 * (pair_count // 3)
    side_pairs = pair_count // 3
    column = jnp.arange(pair_count)
    frame_rate = 10000.0 ** (-column.astype(jnp.float32) / frame_pairs)
    height_rate = 10000.0 ** (-(column - frame_pairs).astype(jnp.float32) / side_pairs)
    width_rate = 10000.0 ** (-(column - frame_pairs - side_pairs).astype(jnp.float32) / side_pairs)
    coords = positions.astype(jnp.float32)
    angles = jnp.where(
        column < frame_pairs,
        coords[0][:, None] * frame_rate,
        jnp.where(
            column < frame_pairs + side_pairs,
            coords[1][:, None] * height_rate,
            coords[2][:, None] * width_rate,
        ),
    )
    return (jnp.cos(angles), jnp.sin(angles))


def rotary_lanes(positions, head_dim):
    cosine, sine_table = rotary_table(positions, head_dim // 2)
    own = jnp.repeat(cosine, 2, axis=1)
    sine = jnp.repeat(sine_table, 2, axis=1)
    even = (jnp.arange(head_dim) % 2 == 0)[None, :]
    return own, jnp.where(even, -sine, 0.0), jnp.where(even, 0.0, sine)


def modulate(activations, modulation):
    average = jnp.mean(activations, axis=1, keepdims=True)
    centred = activations - average
    variance = jnp.mean(centred * centred, axis=1, keepdims=True)
    normed = centred * lax.rsqrt(variance + epsilon)
    return (normed * (1.0 + modulation[1]) + modulation[0]).astype(jnp.bfloat16)


def cut_kernel(half_ref, *refs):
    count = (len(refs) - 1) // 2
    own_ref, send_refs = refs[count], refs[count + 1 :]
    cols = own_ref.shape[2]
    half = half_ref[0]
    for number in range(count):
        own_ref[number] = refs[number][:, pl.ds(pl.multiple_of(half * cols, cols), cols)]
        send_refs[number][...] = refs[number][
            :, pl.ds(pl.multiple_of((1 - half) * cols, cols), cols)
        ]


def cut(weights, half):
    rows, width = weights[0].shape
    cols = width // 2
    tile = 128
    count = len(weights)
    return pl.pallas_call(
        cut_kernel,
        grid_spec=pltpu.PrefetchScalarGridSpec(
            num_scalar_prefetch=1,
            grid=(rows // tile,),
            in_specs=[pl.BlockSpec((tile, width), lambda i, _: (i, 0))] * count,
            out_specs=[pl.BlockSpec((count, tile, cols), lambda i, _: (0, i, 0))]
            + [pl.BlockSpec((tile, cols), lambda i, _: (i, 0))] * count,
        ),
        out_shape=[jax.ShapeDtypeStruct((count, rows, cols), jnp.bfloat16)]
        + [jax.ShapeDtypeStruct((rows, cols), jnp.bfloat16)] * count,
        compiler_params=pltpu.CompilerParams(vmem_limit_bytes=VMEM),
        cost_estimate=pl.CostEstimate(
            flops=0, bytes_accessed=4 * count * rows * width, transcendentals=0
        ),
        name="cut",
    )(half.reshape(1), *weights)


def project_kernel(spots, early, kinds, me_ref, stats_ref, modulation_ref, *refs):
    count = len(spots)
    matrices = len(kinds)
    scratch = refs[-6:]
    raws, weights, ready, total, raw_sems, weight_sems = scratch
    outs = refs[-6 - matrices - (1 if "raw" in kinds else 0) : -6]
    sources = refs[: -6 - len(outs)]
    shards = (len(sources) - 1 - max(spot[0] for row in spots for spot in row)) // 3
    own_refs, first_refs, rest_refs = [sources[i * shards : (i + 1) * shards] for i in range(3)]
    sources = sources[3 * shards :]
    me, rank, top = me_ref[0], me_ref[1], me_ref[2]
    half = me // top
    feats, cols = weights.shape[2:]
    rows = raws.shape[1] // 2
    per_rank = own_refs[0].shape[1] // feats
    copies = []
    for block, spot in enumerate(spots):
        owner = me ^ block
        span = pl.ds(pl.multiple_of((owner % per_rank) * feats, feats), feats)
        apart = (owner // per_rank) ^ rank
        mine = pl.multiple_of(half * rows, rows)
        others = pl.multiple_of((1 - half) * rows, rows)
        parts = []
        for part, (held, begin, length) in enumerate(
            (
                (own_refs, mine, rows),
                (first_refs, others, early),
                (rest_refs, others + early, rows - early),
            )
        ):
            target = raws.at[block, pl.ds(pl.multiple_of(begin, 16), length), :]
            for step, ref in enumerate(held):
                skip = early if part == 2 and step == 0 else 0

                @pl.when(apart == step)
                def _(ref=ref, skip=skip, length=length, span=span, target=target, part=part):
                    pltpu.make_async_copy(
                        ref.at[pl.ds(skip, length), span], target, raw_sems.at[block, part]
                    ).start()

            parts.append(
                pltpu.make_async_copy(
                    held[0].at[pl.ds(0, length), span], target, raw_sems.at[block, part]
                )
            )
        blocks_in = [
            pltpu.make_async_copy(
                sources[source] if at is None else sources[source].at[at],
                weights.at[block, number],
                weight_sems.at[block, number],
            )
            for number, (source, at) in enumerate(spot)
        ]
        for copy in blocks_in:
            copy.start()
        copies.append((parts, blocks_in))

    def column(at):
        return jnp.transpose(jnp.broadcast_to(stats_ref[at : at + 1, :], (128, rows)))

    means = [column(group) for group in range(2)]
    scales = [column(2 + group) for group in range(2)]

    def prepare(first):
        for block in (first, first + 1):
            for copy in copies[block][0]:
                copy.wait()
            span = pl.ds(pl.multiple_of((me ^ block) * feats, feats), feats)
            shift = modulation_ref[0:1, span]
            gain = 1.0 + modulation_ref[1:2, span]
            left = (block - first) * feats
            for group in range(2):
                lines = slice(group * rows, (group + 1) * rows)
                for start in range(0, feats, 128):
                    lanes = slice(start, start + 128)
                    part = raws[block, lines, lanes].astype(jnp.float32)
                    part = (part - means[group]) * scales[group] * gain[:, lanes] + shift[:, lanes]
                    ready[first // 2 % 2, lines, left + start : left + start + 128] = part.astype(
                        jnp.bfloat16
                    )

    prepare(0)
    for first in range(0, count, 2):
        for copy in copies[first][1] + copies[first + 1][1]:
            copy.wait()
        if first + 2 < count:
            prepare(first + 2)
        right = jnp.concatenate(
            [
                jnp.concatenate([weights[first, m], weights[first + 1, m]], axis=0)
                for m in range(matrices)
            ],
            axis=1,
        )
        part = jnp.dot(ready[first // 2 % 2], right, preferred_element_type=jnp.float32)
        if first:
            part = part + total[...]
        if first < count - 2:
            total[...] = part
            continue
        for number, kind in enumerate(kinds):
            raw = part[:, number * cols : (number + 1) * cols]
            outs[number][...] = raw.astype(outs[number].dtype)
            if kind == "raw":
                for group in range(2):
                    mine = raw[group * rows : (group + 1) * rows]
                    summed = jnp.sum(mine * mine, axis=1, keepdims=True)
                    summed = jnp.transpose(jnp.broadcast_to(summed, (rows, 128)))
                    outs[-1][group : group + 1, :] = summed[:1]


def project(place, stats, modulation, shards, early, spots, sources, kinds):
    own, first, rest = shards
    rows, shard = own[0].shape
    feats, cols = sources[0].shape[-2:]
    blocks = len(spots)
    matrices = len(kinds)
    types = [jnp.float32 if kind == "raw" else jnp.bfloat16 for kind in kinds]
    out_shape = [jax.ShapeDtypeStruct((2 * rows, cols), dtype) for dtype in types]
    if "raw" in kinds:
        out_shape.append(jax.ShapeDtypeStruct((2, rows), jnp.float32))
    anywhere = pl.BlockSpec(memory_space=pl.ANY)
    whole = pl.BlockSpec(memory_space=pltpu.VMEM)
    return pl.pallas_call(
        functools.partial(project_kernel, spots, early, kinds),
        in_specs=[pl.BlockSpec(memory_space=pltpu.SMEM), whole, whole]
        + [anywhere] * (3 * len(own) + len(sources)),
        out_specs=[whole] * len(out_shape),
        out_shape=out_shape,
        scratch_shapes=[
            pltpu.VMEM((blocks, 2 * rows, feats), jnp.bfloat16),
            pltpu.VMEM((blocks, matrices, feats, cols), jnp.bfloat16),
            pltpu.VMEM((2, 2 * rows, 2 * feats), jnp.bfloat16),
            pltpu.VMEM((2 * rows, matrices * cols), jnp.float32),
            pltpu.SemaphoreType.DMA((blocks, 3)),
            pltpu.SemaphoreType.DMA((blocks, matrices)),
        ],
        compiler_params=pltpu.CompilerParams(vmem_limit_bytes=VMEM),
        cost_estimate=pl.CostEstimate(
            flops=4 * matrices * rows * blocks * feats * cols,
            bytes_accessed=2 * blocks * feats * (2 * rows + matrices * cols)
            + 8 * matrices * rows * cols,
            transcendentals=0,
        ),
        name="project",
    )(place, stats, modulation, *own, *first, *rest, *sources)


def turn_kernel(width, raw_ref, mine_ref, other_ref, gain_ref, own_ref, upper_ref, lower_ref, *outs):
    dim = own_ref.shape[1]
    rows = raw_ref.shape[0]
    scale = lax.rsqrt((mine_ref[0] + other_ref[0]) * (1.0 / width) + epsilon)
    scale = jnp.transpose(jnp.broadcast_to(scale, (128, rows)))
    own, upper, lower = own_ref[...], upper_ref[...], lower_ref[...]
    start = 0
    for out_ref in outs:
        for head in range(out_ref.shape[1] // dim):
            cols = slice(start + head * dim, start + (head + 1) * dim)
            normed = raw_ref[:, cols] * scale * gain_ref[:, cols]
            turned = (
                normed * own
                + pltpu.roll(normed, dim - 1, 1) * upper
                + pltpu.roll(normed, 1, 1) * lower
            )
            out_ref[:, head * dim : (head + 1) * dim] = turned.astype(out_ref.dtype)
        start += out_ref.shape[1]


def turn(raw, mine, other, gain, tables, width, chunk_cols):
    rows, cols = raw.shape
    groups = mine.shape[0]
    tile = rows // groups
    dim = tables[0].shape[1]
    sums = [part.reshape(groups, 1, tile) for part in (mine, other)]
    return pl.pallas_call(
        functools.partial(turn_kernel, width),
        grid=(groups,),
        in_specs=[pl.BlockSpec((tile, cols), lambda i: (i, 0))]
        + [pl.BlockSpec((1, 1, tile), lambda i: (i, 0, 0))] * 2
        + [pl.BlockSpec((1, cols), lambda i: (0, 0))]
        + [pl.BlockSpec((tile, dim), lambda i: (i, 0))] * 3,
        out_specs=[pl.BlockSpec((tile, part), lambda i: (i, 0)) for part in chunk_cols],
        out_shape=[jax.ShapeDtypeStruct((rows, part), jnp.bfloat16) for part in chunk_cols],
        compiler_params=pltpu.CompilerParams(vmem_limit_bytes=VMEM),
        cost_estimate=pl.CostEstimate(
            flops=8 * rows * cols, bytes_accessed=6 * rows * cols, transcendentals=0
        ),
        name="turn",
    )(raw, *sums, gain[None, :], *tables)


def attend_kernel(places, tile, me_ref, order_ref, bounds_ref, q_ref, *refs):
    count = len(places)
    sources, (query_seg_ref, key_seg_ref) = refs[: 2 * count], refs[2 * count : 2 * count + 2]
    out_refs = refs[2 * count + 2 : -5]
    keys, values, highest, mixed, sems = refs[-5:]
    me = me_ref[0]
    rows = sources[0].shape[1]
    copies = []
    for piece, owners in enumerate(places):
        for at, owner in enumerate(owners):
            where = pl.ds(pl.multiple_of(owner(me) * rows, rows), rows)
            for kind, held in enumerate((keys, values)):
                copies.append(
                    pltpu.make_async_copy(
                        sources[kind * count + piece].at[at],
                        held.at[where, :],
                        sems.at[kind, piece, at],
                    )
                )
    for copy in copies:
        copy.start()
    for copy in copies:
        copy.wait()
    dim = HEAD_DIM
    heads = q_ref.shape[1] // dim
    factor = dim ** (-0.5) * LOG2E
    ones = jnp.ones((KEY_TILE, dim), jnp.bfloat16)
    for place, out_ref in enumerate(out_refs):
        number = order_ref[place]
        span = pl.ds(pl.multiple_of(number * tile, tile), tile)
        highest[...] = jnp.full_like(highest, -1e29)
        mixed[...] = jnp.zeros_like(mixed)

        def step(block, carry):
            where = pl.ds(pl.multiple_of(block * KEY_TILE, KEY_TILE), KEY_TILE)
            same = query_seg_ref[span, :] == key_seg_ref[block]
            for head in range(heads):
                cols = slice(head * dim, (head + 1) * dim)
                scores = lax.dot_general(
                    q_ref[span, cols],
                    keys[where, cols],
                    (((1,), (1,)), ((), ())),
                    preferred_element_type=jnp.float32,
                )
                scores = jnp.where(same, scores * factor, -1e30)
                former = highest[head]
                newest = jnp.maximum(former, jnp.max(scores, axis=1, keepdims=True))
                highest[head] = newest
                weights = jnp.exp2(scores - newest[:, :1]).astype(jnp.bfloat16)
                right = jnp.concatenate([values[where, cols], ones], axis=1)
                part = jnp.dot(weights, right, preferred_element_type=jnp.float32)
                shrink = jnp.exp2(former - newest)
                mixed[head, :, :dim] = mixed[head, :, :dim] * shrink + part[:, :dim]
                mixed[head, :, dim:] = mixed[head, :, dim:] * shrink + part[:, dim:]
            return carry

        lax.fori_loop(bounds_ref[number, 0], bounds_ref[number, 1], step, 0)
        for head in range(heads):
            out_ref[:, head * dim : (head + 1) * dim] = (
                mixed[head, :, :dim] / mixed[head, :, dim:]
            ).astype(out_ref.dtype)


def key_bounds(query_seg, segment_ids, tile):
    rows = query_seg.shape[0]
    tiled = query_seg.reshape(rows // tile, tile)
    first, last = tiled[:, 0], tiled[:, -1]
    low = jnp.sum(segment_ids[None, :] < first[:, None], axis=1, dtype=jnp.int32)
    high = jnp.sum(segment_ids[None, :] <= last[:, None], axis=1, dtype=jnp.int32)
    return jnp.stack([low // KEY_TILE, (high + KEY_TILE - 1) // KEY_TILE], axis=1)


def attend(query, key_pieces, value_pieces, places, me, order, bounds, query_seg, key_seg, tile):
    rows, cols = query.shape
    tokens = key_seg.shape[0] * KEY_TILE
    outs = order.shape[0]
    dim = HEAD_DIM
    heads = cols // dim
    smem = pl.BlockSpec(memory_space=pltpu.SMEM)
    whole = pl.BlockSpec(memory_space=pltpu.VMEM)
    anywhere = pl.BlockSpec(memory_space=pl.ANY)
    return pl.pallas_call(
        functools.partial(attend_kernel, places, tile),
        in_specs=[smem, smem, smem, whole] + [anywhere] * (2 * len(places)) + [whole, whole],
        out_specs=[whole] * outs,
        scratch_shapes=[
            pltpu.VMEM((tokens, cols), jnp.bfloat16),
            pltpu.VMEM((tokens, cols), jnp.bfloat16),
            pltpu.VMEM((heads, tile, dim), jnp.float32),
            pltpu.VMEM((heads, tile, 2 * dim), jnp.float32),
            pltpu.SemaphoreType.DMA((2, len(places), len(places[0]))),
        ],
        out_shape=[jax.ShapeDtypeStruct((tile, cols), jnp.bfloat16)] * outs,
        compiler_params=pltpu.CompilerParams(vmem_limit_bytes=VMEM),
        cost_estimate=pl.CostEstimate(
            flops=2 * rows * tokens * cols,
            bytes_accessed=4 * tokens * cols + 4 * rows * cols,
            transcendentals=rows * tokens * heads // 2,
        ),
        name="attend",
    )(
        me.reshape(1),
        order,
        bounds,
        query,
        *key_pieces,
        *value_pieces,
        query_seg,
        key_seg,
    )


def pages_kernel(places, me_ref, page_ref, *refs):
    count = len(places)
    sems = refs[-1]
    wanted, chunks = sems.shape
    out_refs = refs[chunks * count : -1]
    me = me_ref[0]
    each = wanted // len(out_refs)
    per_block = refs[0].shape[1] // PAGE
    waits = []
    for number in range(wanted):
        page = page_ref[number]
        rows = pl.ds(pl.multiple_of((page % per_block) * PAGE, PAGE), PAGE)
        start = 0
        for chunk in range(chunks):
            sources = refs[chunk * count : (chunk + 1) * count]
            cols = pl.ds(start, sources[0].shape[2])
            start += sources[0].shape[2]
            sem = sems.at[number, chunk]
            target = out_refs[number // each].at[number % each, :, cols]
            for piece, owners in enumerate(places):
                for at, owner in enumerate(owners):

                    @pl.when(page // per_block == owner(me))
                    def _(source=sources[piece].at[at, rows, :], target=target, sem=sem):
                        pltpu.make_async_copy(source, target, sem).start()

            waits.append(
                pltpu.make_async_copy(sources[0].at[0, pl.ds(0, PAGE), :], target, sem)
            )
    for copy in waits:
        copy.wait()


def pick_pages(chunks, places, me, pages, parts):
    cols = sum(pieces[0].shape[2] for pieces in chunks)
    wanted = pages.shape[0]
    smem = pl.BlockSpec(memory_space=pltpu.SMEM)
    anywhere = pl.BlockSpec(memory_space=pl.ANY)
    return pl.pallas_call(
        functools.partial(pages_kernel, places),
        in_specs=[smem, smem] + [anywhere] * (len(chunks) * len(places)),
        out_specs=[pl.BlockSpec(memory_space=pltpu.VMEM)] * parts,
        out_shape=[jax.ShapeDtypeStruct((wanted // parts, PAGE, cols), jnp.bfloat16)] * parts,
        scratch_shapes=[pltpu.SemaphoreType.DMA((wanted, len(chunks)))],
        compiler_params=pltpu.CompilerParams(vmem_limit_bytes=VMEM),
        cost_estimate=pl.CostEstimate(
            flops=0, bytes_accessed=4 * wanted * PAGE * cols, transcendentals=0
        ),
        name="pick_pages",
    )(me.reshape(1), pages, *[piece for pieces in chunks for piece in pieces])


def own_pages(page_table, start, count):
    page_total = page_table.shape[0]
    inverse = (
        jnp.zeros((page_total,), jnp.int32)
        .at[page_table]
        .set(jnp.arange(page_total, dtype=jnp.int32))
    )
    return lax.dynamic_slice_in_dim(inverse, start, count, 0)


def whole_heads(ring, hidden, modulation, weights, gains, positions, segment_ids, page_table):
    tok_rows = hidden.shape[0]
    me = lax.axis_index("row")
    full_rows = lax.all_gather(hidden, "col", axis=1, tiled=True)
    modulated = modulate(full_rows.astype(jnp.float32), modulation)
    width = full_rows.shape[1]
    raws = [
        jnp.dot(
            modulated,
            lax.all_gather(weight, "row", axis=0, tiled=True),
            preferred_element_type=jnp.float32,
        )
        for weight in weights
    ]
    squares = lax.psum(tuple(jnp.sum(raw * raw, axis=1) for raw in raws[:2]), "col")
    tables = rotary_lanes(positions, HEAD_DIM)
    cols = raws[0].shape[1]
    query, key = [
        turn(raw, total[None], jnp.zeros_like(total)[None], gain, tables, width, (cols,))[0]
        for raw, total, gain in zip(raws, squares, gains)
    ]
    value = raws[2].astype(jnp.bfloat16)
    keys_all = lax.all_gather(key, "row", axis=0)
    values_all = lax.all_gather(value, "row", axis=0)
    places = (tuple(lambda me, at=at: at for at in range(ring)),)
    none = jnp.zeros((), jnp.int32)
    query_seg = lax.dynamic_slice_in_dim(segment_ids, me * tok_rows, tok_rows, 0)
    attended = attend(
        query,
        [keys_all],
        [values_all],
        places,
        none,
        none.reshape(1),
        key_bounds(query_seg, segment_ids, tok_rows),
        query_seg[:, None],
        segment_ids.reshape(-1, 1, KEY_TILE),
        tok_rows,
    )[0]
    count = tok_rows // PAGE
    pages = own_pages(page_table, me * count, count)
    picked = [pick_pages([[held]], places, none, pages, 1)[0] for held in (keys_all, values_all)]
    return attended, jnp.stack(picked)


def split_heads(ring, ranks, hidden, modulation, weights, gains, positions, segment_ids, page_table):
    tok_rows, shard = hidden.shape
    feats = weights[0].shape[0]
    width = ring * feats
    me = lax.axis_index("row")
    rank = lax.axis_index("col")
    top = ring // 2
    half = me // top
    low = me % top
    cols = weights[0].shape[1] // 2
    steps = []
    bit = top // 2
    while bit:
        steps.append(bit)
        bit //= 2

    def swap(value, bit):
        return lax.ppermute(value, "row", [(i, i ^ bit) for i in range(ring)])

    def half_of(value, which):
        return lax.dynamic_slice_in_dim(value, which * cols, cols, value.ndim - 1)

    def in_order(mine, other, axis):
        return jnp.where(
            half == 0,
            jnp.concatenate([mine, other], axis=axis),
            jnp.concatenate([other, mine], axis=axis),
        )

    def spread(blocks):
        for bit in steps:
            blocks.update(
                {
                    number | bit: jax.tree.map(lambda part: swap(part, bit), blocks[number])
                    for number in list(blocks)
                }
            )
        return blocks


    def across(value, step):
        return lax.ppermute(value, "col", [(c, c ^ step) for c in range(ranks)])

    w_query, w_key, w_value = weights
    own, *sends = cut((w_key, w_value, w_query), half)

    rows = hidden.astype(jnp.float32)
    local_mean = jnp.mean(rows, axis=1)
    local_square = jnp.sum(jnp.square(rows - local_mean[:, None]), axis=1)
    stats = jnp.stack([local_mean, local_square])
    all_stats = [stats] + [across(stats, step) for step in range(1, ranks)]
    shard_rows, all_stats = lax.optimization_barrier((hidden, all_stats))
    average = sum(part[0] for part in all_stats) / ranks
    variance = (
        sum(part[1] + shard * jnp.square(part[0] - average) for part in all_stats) / width
    )
    small = jnp.concatenate(
        [jnp.stack([average, lax.rsqrt(variance + epsilon)]), positions.astype(jnp.float32)]
    )
    small_other = swap(small, top)

    early = tok_rows // 4
    other_rows = swap(hidden, top)
    own_shards = [hidden] + [across(shard_rows, step) for step in range(1, ranks)]
    first_shards = [other_rows] + [across(other_rows[:early], step) for step in range(1, ranks)]
    rest_shards = [other_rows] + [swap(part[early:], top) for part in own_shards[1:]]

    received = [swap(part, top) for part in sends]
    small_other, received = lax.optimization_barrier((small_other, received))
    small = in_order(small[:, None], small_other[:, None], 1)
    norm_stats = small[:2].reshape(4, tok_rows)
    blocks = spread({0: own, top: received})

    tables = rotary_lanes(small[2:].reshape(3, -1), HEAD_DIM)
    q_gain, k_gain = [half_of(gain, half) for gain in gains]
    count = tok_rows // PAGE
    pages = jnp.concatenate(
        [own_pages(page_table, owner * count, count) for owner in (me ^ top, me)]
    )
    query_seg = jnp.concatenate(
        [
            lax.dynamic_slice_in_dim(segment_ids, owner * tok_rows, tok_rows, 0)
            for owner in (low, low + top)
        ]
    )
    bounds = key_bounds(query_seg, segment_ids, tok_rows)
    prepared = (norm_stats, tables, q_gain, k_gain, pages, query_seg[:, None], bounds)
    rest_shards, prepared = lax.optimization_barrier((rest_shards, prepared))
    norm_stats, tables, q_gain, k_gain, pages, query_seg, bounds = prepared
    key_seg = segment_ids.reshape(-1, 1, KEY_TILE)
    place = jnp.stack([me, rank, jnp.full((), top, jnp.int32)]).astype(jnp.int32)

    def products(first, last, kinds):
        sources, spots = [], []
        for number in range(ring):
            held = blocks[number]
            if isinstance(held, list):
                spots.append(tuple((len(sources) + m, None) for m in range(last - first)))
                sources.extend(held[first:last])
            else:
                spots.append(tuple((len(sources), m) for m in range(first, last)))
                sources.append(held)
        shards = (own_shards, first_shards, rest_shards)
        return project(
            place, norm_stats, modulation, shards, early, tuple(spots), sources, kinds
        )

    def summed(squares):
        squares = squares + swap(squares, top)
        bit = 1
        while 2 * bit < ranks:
            squares = squares + across(squares, bit)
            bit *= 2
        return squares, across(squares, bit)

    key_raw, value, squares = products(0, 2, ("raw", "value"))
    places = tuple(
        tuple(lambda me, n=number, g=group: ((me % top) ^ n) + g * top for group in range(2))
        for number in range(top)
    )
    shape = (2, tok_rows, -1)

    def finish(own_piece, ahead):
        held = {0: own_piece, steps[0]: ahead}
        for bit in steps[1:]:
            held.update({number | bit: swap(held[number], bit) for number in list(held)})
        return [held[number] for number in range(top)]

    value = value.reshape(shape)
    value_ahead = swap(value, steps[0])
    (key,) = turn(key_raw, *summed(squares), k_gain, tables, width, (cols,))
    key = key.reshape(shape)
    key_ahead = swap(key, steps[0])
    query_raw, squares = products(2, 3, ("raw",))
    (query,) = turn(query_raw, *summed(squares), q_gain, tables, width, (cols,))
    value_pieces = finish(value, value_ahead)
    values_picked = pick_pages([value_pieces], places, me, pages, 2)
    key_ahead, query, values_picked = lax.optimization_barrier((key_ahead, query, values_picked))
    key_pieces = finish(key, key_ahead)
    keys_picked = pick_pages([key_pieces], places, me, pages, 2)

    def attended(query, number):
        return attend(
            query,
            key_pieces,
            value_pieces,
            places,
            me,
            number.reshape(1),
            bounds,
            query_seg,
            key_seg,
            tok_rows,
        )[0]

    query, keys_picked = lax.optimization_barrier((query, keys_picked))
    for_other = attended(query, 1 - half)
    pages_other = [swap(picked[0], top) for picked in (keys_picked, values_picked)]
    query, pages_other, for_other = lax.optimization_barrier((query, pages_other, for_other))
    from_other = swap(for_other, top)
    for_me = attended(query, half)
    page_store = [
        in_order(picked[1], other, -1)
        for picked, other in zip((keys_picked, values_picked), pages_other)
    ]
    return in_order(for_me, from_other, -1), jnp.stack(page_store)


def solution(mesh):
    ring, ranks = mesh.shape["row"], mesh.shape["col"]

    def body(
        hidden, modulation, w_query, w_key, w_value, q_gain, k_gain, positions, segment_ids, page_table
    ):
        rest = (
            hidden,
            modulation,
            (w_query, w_key, w_value),
            (q_gain, k_gain),
            positions,
            segment_ids,
            page_table,
        )
        heads = w_query.shape[1] // HEAD_DIM
        feats, shard = w_query.shape[0], hidden.shape[1]
        powers = ring & (ring - 1) == 0 and ranks & (ranks - 1) == 0
        if heads % 2 == 0 and ring % 2 == 0 and powers and feats % 128 == 0 and shard % feats == 0:
            return split_heads(ring, ranks, *rest)
        return whole_heads(ring, *rest)

    in_specs = (
        P("row", "col"),
        P(),
        P("row", "col"),
        P("row", "col"),
        P("row", "col"),
        P("col"),
        P("col"),
        P(None, "row"),
        P(),
        P(),
    )
    out_specs = (P("row", "col"), P(None, "row", None, "col"))
    return jax.shard_map(body, mesh=mesh, in_specs=in_specs, out_specs=out_specs, check_vma=False)
```

```python
import functools
import jax
import jax.numpy as jnp
from jax import lax
from jax.experimental import pallas as pl
from jax.experimental.pallas import tpu as pltpu
from jax.sharding import PartitionSpec as P

HEAD_DIM = 128
PAGE = 128
KEY_TILE = 512
VMEM = 60 * 1024 * 1024
LOG2E = 1.4426950408889634

epsilon = 1e-06


def rotary_table(positions, pair_count):
    frame_pairs = pair_count - 2 * (pair_count // 3)
    side_pairs = pair_count // 3
    column = jnp.arange(pair_count)
    frame_rate = 10000.0 ** (-column.astype(jnp.float32) / frame_pairs)
    height_rate = 10000.0 ** (-(column - frame_pairs).astype(jnp.float32) / side_pairs)
    width_rate = 10000.0 ** (-(column - frame_pairs - side_pairs).astype(jnp.float32) / side_pairs)
    coords = positions.astype(jnp.float32)
    angles = jnp.where(
        column < frame_pairs,
        coords[0][:, None] * frame_rate,
        jnp.where(
            column < frame_pairs + side_pairs,
            coords[1][:, None] * height_rate,
            coords[2][:, None] * width_rate,
        ),
    )
    return (jnp.cos(angles), jnp.sin(angles))


def rotary_lanes(positions, head_dim):
    cosine, sine_table = rotary_table(positions, head_dim // 2)
    own = jnp.repeat(cosine, 2, axis=1)
    sine = jnp.repeat(sine_table, 2, axis=1)
    even = (jnp.arange(head_dim) % 2 == 0)[None, :]
    return own, jnp.where(even, -sine, 0.0), jnp.where(even, 0.0, sine)


def modulate(activations, modulation):
    average = jnp.mean(activations, axis=1, keepdims=True)
    centred = activations - average
    variance = jnp.mean(centred * centred, axis=1, keepdims=True)
    normed = centred * lax.rsqrt(variance + epsilon)
    return (normed * (1.0 + modulation[1]) + modulation[0]).astype(jnp.bfloat16)


def cut_kernel(half_ref, *refs):
    weights, outs = refs[:3], refs[3:]
    cols = outs[0].shape[2]
    half = half_ref[0]
    for number, weight in enumerate(weights):
        out, at = (0, number) if number < 2 else (2, 0)
        outs[out][at] = weight[:, pl.ds(pl.multiple_of(half * cols, cols), cols)]
        outs[out + 1][at] = weight[:, pl.ds(pl.multiple_of((1 - half) * cols, cols), cols)]


def cut(weights, half):
    rows, width = weights[0].shape
    cols = width // 2
    tile = 128
    sizes = (2, 2, 1, 1)
    return pl.pallas_call(
        cut_kernel,
        grid_spec=pltpu.PrefetchScalarGridSpec(
            num_scalar_prefetch=1,
            grid=(rows // tile,),
            in_specs=[pl.BlockSpec((tile, width), lambda i, _: (i, 0))] * 3,
            out_specs=[pl.BlockSpec((size, tile, cols), lambda i, _: (0, i, 0)) for size in sizes],
        ),
        out_shape=[jax.ShapeDtypeStruct((size, rows, cols), jnp.bfloat16) for size in sizes],
        compiler_params=pltpu.CompilerParams(vmem_limit_bytes=VMEM),
        cost_estimate=pl.CostEstimate(
            flops=0, bytes_accessed=12 * rows * width, transcendentals=0
        ),
        name="cut",
    )(half.reshape(1), *weights)


def project_kernel(parts, count, place_ref, stats_ref, modulation_ref, *refs):
    total_parts = sum(len(part[1]) for part in parts)
    shards, pairs = refs[:total_parts], refs[total_parts : total_parts + count]
    singles = refs[total_parts + count : total_parts + 2 * count]
    key_ref, query_ref, value_ref, squares_ref = refs[total_parts + 2 * count : -6]
    raws, weights, ready, total, raw_sems, weight_sems = refs[-6:]
    me, rank = place_ref[0], place_ref[1]
    feats, cols = weights.shape[2:]
    rows = raws.shape[1]
    per_rank = shards[0].shape[-1] // feats
    copies = []
    for block in range(count):
        owner = me ^ block
        span = pl.ds(pl.multiple_of((owner % per_rank) * feats, feats), feats)
        holder = owner // per_rank
        mine = []
        begin, first = 0, 0
        for number, (length, places, by_rank) in enumerate(parts):
            target = raws.at[block, pl.ds(begin, length), :]
            sem = raw_sems.at[block, number]
            if by_rank:
                copy = pltpu.make_async_copy(
                    shards[first].at[holder, pl.ds(places[0][1], length), span], target, sem
                )
                copy.start()
            else:
                for step, (at, skip) in enumerate(places):
                    ref = shards[first + step]
                    if at is not None:
                        ref = ref.at[at]
                    source = ref.at[pl.ds(skip, length), span]

                    @pl.when((holder ^ rank) == step)
                    def _(source=source, target=target, sem=sem):
                        pltpu.make_async_copy(source, target, sem).start()

                copy = pltpu.make_async_copy(source, target, sem)
            mine.append(copy)
            begin += length
            first += len(places)
        matrices = [
            pltpu.make_async_copy(source, weights.at[block, number], weight_sems.at[block, number])
            for number, source in enumerate(
                (pairs[block].at[0], pairs[block].at[1], singles[block].at[0])
            )
        ]
        for copy in matrices:
            copy.start()
        copies.append((mine, matrices))

    def column(at):
        return jnp.transpose(jnp.broadcast_to(stats_ref[at : at + 1, :], (128, rows)))

    mean, scale = column(0), column(1)

    def prepare(first):
        for block in (first, first + 1):
            for copy in copies[block][0]:
                copy.wait()
            span = pl.ds(pl.multiple_of((me ^ block) * feats, feats), feats)
            shift = modulation_ref[0:1, span]
            gain = 1.0 + modulation_ref[1:2, span]
            left = (block - first) * feats
            for start in range(0, feats, 128):
                lanes = slice(start, start + 128)
                part = raws[block, :, lanes].astype(jnp.float32)
                part = (part - mean) * scale * gain[:, lanes] + shift[:, lanes]
                ready[first // 2 % 2, :, left + start : left + start + 128] = part.astype(
                    jnp.bfloat16
                )

    prepare(0)
    for first in range(0, count, 2):
        for copy in copies[first][1] + copies[first + 1][1]:
            copy.wait()
        if first + 2 < count:
            prepare(first + 2)
        right = jnp.concatenate(
            [
                jnp.concatenate([weights[first, m], weights[first + 1, m]], axis=0)
                for m in range(3)
            ],
            axis=1,
        )
        part = jnp.dot(ready[first // 2 % 2], right, preferred_element_type=jnp.float32)
        if first:
            part = part + total[...]
        if first < count - 2:
            total[...] = part
            continue
        key, value, query = [part[:, m * cols : (m + 1) * cols] for m in range(3)]
        key_ref[...] = key
        query_ref[...] = query
        value_ref[...] = value.astype(value_ref.dtype)
        for number, raw in enumerate((key, query)):
            summed = jnp.sum(raw * raw, axis=1, keepdims=True)
            summed = jnp.transpose(jnp.broadcast_to(summed, (rows, 128)))
            squares_ref[number : number + 1, :] = summed[:1]


def project(place, stats, modulation, parts, shards, pairs, singles):
    rows = sum(part[0] for part in parts)
    _, feats, cols = singles[0].shape
    count = len(singles)
    raw = jax.ShapeDtypeStruct((rows, cols), jnp.float32)
    anywhere = pl.BlockSpec(memory_space=pl.ANY)
    whole = pl.BlockSpec(memory_space=pltpu.VMEM)
    return pl.pallas_call(
        functools.partial(project_kernel, parts, count),
        in_specs=[pl.BlockSpec(memory_space=pltpu.SMEM), whole, whole]
        + [anywhere] * (len(shards) + 2 * count),
        out_specs=[whole] * 4,
        out_shape=[
            raw,
            raw,
            jax.ShapeDtypeStruct(raw.shape, jnp.bfloat16),
            jax.ShapeDtypeStruct((2, rows), jnp.float32),
        ],
        scratch_shapes=[
            pltpu.VMEM((count, rows, feats), jnp.bfloat16),
            pltpu.VMEM((count, 3, feats, cols), jnp.bfloat16),
            pltpu.VMEM((2, rows, 2 * feats), jnp.bfloat16),
            pltpu.VMEM((rows, 3 * cols), jnp.float32),
            pltpu.SemaphoreType.DMA((count, len(parts))),
            pltpu.SemaphoreType.DMA((count, 3)),
        ],
        compiler_params=pltpu.CompilerParams(vmem_limit_bytes=VMEM),
        cost_estimate=pl.CostEstimate(
            flops=6 * rows * count * feats * cols,
            bytes_accessed=2 * count * feats * (rows + 3 * cols) + 10 * rows * cols,
            transcendentals=0,
        ),
        name="project",
    )(place, stats, modulation, *shards, *pairs, *singles)


def turn_kernel(width, mine_ref, other_ref, gain_ref, own_ref, upper_ref, lower_ref, *refs):
    out_ref = refs[-1]
    dim = own_ref.shape[1]
    for number, raw_ref in enumerate(refs[:-1]):
        rows = raw_ref.shape[0]
        at = slice(number, number + 1)
        scale = lax.rsqrt((mine_ref[at, :] + other_ref[at, :]) * (1.0 / width) + epsilon)
        scale = jnp.transpose(jnp.broadcast_to(scale, (128, rows)))
        lines = slice(number * rows, (number + 1) * rows)
        own, upper, lower = own_ref[lines, :], upper_ref[lines, :], lower_ref[lines, :]
        for head in range(raw_ref.shape[1] // dim):
            cols = slice(head * dim, (head + 1) * dim)
            normed = raw_ref[:, cols] * scale * gain_ref[:, cols]
            turned = (
                normed * own
                + pltpu.roll(normed, dim - 1, 1) * upper
                + pltpu.roll(normed, 1, 1) * lower
            )
            out_ref[number, :, cols] = turned.astype(out_ref.dtype)


def turn(raws, mine, other, gain, tables, width):
    rows, cols = raws[0].shape
    count = len(raws)
    whole = pl.BlockSpec(memory_space=pltpu.VMEM)
    return pl.pallas_call(
        functools.partial(turn_kernel, width),
        in_specs=[whole] * (6 + count),
        out_specs=whole,
        out_shape=jax.ShapeDtypeStruct((count, rows, cols), jnp.bfloat16),
        compiler_params=pltpu.CompilerParams(vmem_limit_bytes=VMEM),
        cost_estimate=pl.CostEstimate(
            flops=8 * count * rows * cols, bytes_accessed=6 * count * rows * cols, transcendentals=0
        ),
        name="turn",
    )(mine, other, gain[None, :], *tables, *raws)


def attend_kernel(places, me_ref, bounds_ref, q_ref, *refs):
    count = len(places[0]) + len(places[1])
    sources, (query_seg_ref, key_seg_ref) = refs[:count], refs[count : count + 2]
    out_ref, keys, values, highest, mixed, sems = refs[count + 2 :]
    me = me_ref[0]
    rows = sources[0].shape[1]
    copies = []
    for kind, held in enumerate((keys, values)):
        for piece, owners in enumerate(places[kind]):
            source = sources[kind * len(places[0]) + piece]
            for at, owner in enumerate(owners):
                where = pl.ds(pl.multiple_of(owner(me) * rows, rows), rows)
                copies.append(
                    pltpu.make_async_copy(
                        source.at[at], held.at[where, :], sems.at[kind, piece, at]
                    )
                )
    for copy in copies:
        copy.start()
    dim = HEAD_DIM
    heads = q_ref.shape[1] // dim
    factor = dim ** (-0.5) * LOG2E
    ones = jnp.ones((KEY_TILE, dim), jnp.bfloat16)
    highest[...] = jnp.full_like(highest, -1e29)
    mixed[...] = jnp.zeros_like(mixed)
    for copy in copies:
        copy.wait()

    def step(block, carry):
        where = pl.ds(pl.multiple_of(block * KEY_TILE, KEY_TILE), KEY_TILE)
        same = query_seg_ref[...] == key_seg_ref[block]
        for head in range(heads):
            cols = slice(head * dim, (head + 1) * dim)
            scores = lax.dot_general(
                q_ref[:, cols],
                keys[where, cols],
                (((1,), (1,)), ((), ())),
                preferred_element_type=jnp.float32,
            )
            scores = jnp.where(same, scores * factor, -1e30)
            former = highest[head]
            newest = jnp.maximum(former, jnp.max(scores, axis=1, keepdims=True))
            highest[head] = newest
            weights = jnp.exp2(scores - newest[:, :1]).astype(jnp.bfloat16)
            right = jnp.concatenate([values[where, cols], ones], axis=1)
            part = jnp.dot(weights, right, preferred_element_type=jnp.float32)
            shrink = jnp.exp2(former - newest)
            mixed[head, :, :dim] = mixed[head, :, :dim] * shrink + part[:, :dim]
            mixed[head, :, dim:] = mixed[head, :, dim:] * shrink + part[:, dim:]
        return carry

    lax.fori_loop(bounds_ref[0], bounds_ref[1], step, 0)
    for head in range(heads):
        out_ref[:, head * dim : (head + 1) * dim] = (
            mixed[head, :, :dim] / mixed[head, :, dim:]
        ).astype(out_ref.dtype)


def key_bounds(query_seg, segment_ids):
    low = jnp.sum(segment_ids < query_seg[0], dtype=jnp.int32)
    high = jnp.sum(segment_ids <= query_seg[-1], dtype=jnp.int32)
    return jnp.stack([low // KEY_TILE, (high + KEY_TILE - 1) // KEY_TILE])


def attend(query, key_pieces, value_pieces, places, me, bounds, query_seg, key_seg):
    rows, cols = query.shape
    tokens = key_seg.shape[0] * KEY_TILE
    dim = HEAD_DIM
    heads = cols // dim
    smem = pl.BlockSpec(memory_space=pltpu.SMEM)
    whole = pl.BlockSpec(memory_space=pltpu.VMEM)
    anywhere = pl.BlockSpec(memory_space=pl.ANY)
    return pl.pallas_call(
        functools.partial(attend_kernel, places),
        in_specs=[smem, smem, whole]
        + [anywhere] * (len(places[0]) + len(places[1]))
        + [whole, whole],
        out_specs=whole,
        scratch_shapes=[
            pltpu.VMEM((tokens, cols), jnp.bfloat16),
            pltpu.VMEM((tokens, cols), jnp.bfloat16),
            pltpu.VMEM((heads, rows, dim), jnp.float32),
            pltpu.VMEM((heads, rows, 2 * dim), jnp.float32),
            pltpu.SemaphoreType.DMA(
                (2, max(map(len, places)), max(len(o) for part in places for o in part))
            ),
        ],
        out_shape=jax.ShapeDtypeStruct((rows, cols), jnp.bfloat16),
        compiler_params=pltpu.CompilerParams(vmem_limit_bytes=VMEM),
        cost_estimate=pl.CostEstimate(
            flops=2 * rows * tokens * cols,
            bytes_accessed=4 * tokens * cols + 4 * rows * cols,
            transcendentals=rows * tokens * heads // 2,
        ),
        name="attend",
    )(me.reshape(1), bounds, query, *key_pieces, *value_pieces, query_seg, key_seg)


def pages_kernel(places, me_ref, page_ref, *refs):
    count = len(places)
    sems = refs[-1]
    wanted, chunks = sems.shape
    out_refs = refs[chunks * count : -1]
    me = me_ref[0]
    each = wanted // len(out_refs)
    per_block = refs[0].shape[1] // PAGE
    waits = []
    for number in range(wanted):
        page = page_ref[number]
        rows = pl.ds(pl.multiple_of((page % per_block) * PAGE, PAGE), PAGE)
        start = 0
        for chunk in range(chunks):
            sources = refs[chunk * count : (chunk + 1) * count]
            cols = pl.ds(start, sources[0].shape[2])
            start += sources[0].shape[2]
            sem = sems.at[number, chunk]
            target = out_refs[number // each].at[number % each, :, cols]
            for piece, owners in enumerate(places):
                for at, owner in enumerate(owners):

                    @pl.when(page // per_block == owner(me))
                    def _(source=sources[piece].at[at, rows, :], target=target, sem=sem):
                        pltpu.make_async_copy(source, target, sem).start()

            waits.append(
                pltpu.make_async_copy(sources[0].at[0, pl.ds(0, PAGE), :], target, sem)
            )
    for copy in waits:
        copy.wait()


def pick_pages(chunks, places, me, pages, parts):
    cols = sum(pieces[0].shape[2] for pieces in chunks)
    wanted = pages.shape[0]
    smem = pl.BlockSpec(memory_space=pltpu.SMEM)
    anywhere = pl.BlockSpec(memory_space=pl.ANY)
    return pl.pallas_call(
        functools.partial(pages_kernel, places),
        in_specs=[smem, smem] + [anywhere] * (len(chunks) * len(places)),
        out_specs=[pl.BlockSpec(memory_space=pltpu.VMEM)] * parts,
        out_shape=[jax.ShapeDtypeStruct((wanted // parts, PAGE, cols), jnp.bfloat16)] * parts,
        scratch_shapes=[pltpu.SemaphoreType.DMA((wanted, len(chunks)))],
        compiler_params=pltpu.CompilerParams(vmem_limit_bytes=VMEM),
        cost_estimate=pl.CostEstimate(
            flops=0, bytes_accessed=4 * wanted * PAGE * cols, transcendentals=0
        ),
        name="pick_pages",
    )(me.reshape(1), pages, *[piece for pieces in chunks for piece in pieces])


def own_pages(page_table, start, count):
    page_total = page_table.shape[0]
    inverse = (
        jnp.zeros((page_total,), jnp.int32)
        .at[page_table]
        .set(jnp.arange(page_total, dtype=jnp.int32))
    )
    return lax.dynamic_slice_in_dim(inverse, start, count, 0)


def whole_heads(ring, hidden, modulation, weights, gains, positions, segment_ids, page_table):
    tok_rows = hidden.shape[0]
    me = lax.axis_index("row")
    full_rows = lax.all_gather(hidden, "col", axis=1, tiled=True)
    modulated = modulate(full_rows.astype(jnp.float32), modulation)
    width = full_rows.shape[1]
    raws = [
        jnp.dot(
            modulated,
            lax.all_gather(weight, "row", axis=0, tiled=True),
            preferred_element_type=jnp.float32,
        )
        for weight in weights
    ]
    squares = lax.psum(tuple(jnp.sum(raw * raw, axis=1) for raw in raws[:2]), "col")
    tables = rotary_lanes(positions, HEAD_DIM)
    query, key = [
        turn([raw], total[None], jnp.zeros_like(total)[None], gain, tables, width)[0]
        for raw, total, gain in zip(raws, squares, gains)
    ]
    value = raws[2].astype(jnp.bfloat16)
    keys_all = lax.all_gather(key, "row", axis=0)
    values_all = lax.all_gather(value, "row", axis=0)
    places = (tuple(lambda me, at=at: at for at in range(ring)),)
    none = jnp.zeros((), jnp.int32)
    query_seg = lax.dynamic_slice_in_dim(segment_ids, me * tok_rows, tok_rows, 0)
    attended = attend(
        query,
        [keys_all],
        [values_all],
        (places, places),
        none,
        key_bounds(query_seg, segment_ids),
        query_seg[:, None],
        segment_ids.reshape(-1, 1, KEY_TILE),
    )
    count = tok_rows // PAGE
    pages = own_pages(page_table, me * count, count)
    picked = [pick_pages([[held]], places, none, pages, 1)[0] for held in (keys_all, values_all)]
    return attended, jnp.stack(picked)


def split_heads(ring, ranks, hidden, modulation, weights, gains, positions, segment_ids, page_table):
    tok_rows, shard = hidden.shape
    width = ranks * shard
    me = lax.axis_index("row")
    rank = lax.axis_index("col")
    top = ring // 2
    half = me // top
    cols = weights[0].shape[1] // 2
    hops = []
    bit = top // 2
    while bit:
        hops.append(bit)
        bit //= 2

    def swap(value, bit):
        return lax.ppermute(value, "row", [(i, i ^ bit) for i in range(ring)])

    def across(value, step):
        return lax.ppermute(value, "col", [(c, c ^ step) for c in range(ranks)])

    def spread(blocks, bits):
        for bit in bits:
            blocks.update({number | bit: swap(blocks[number], bit) for number in list(blocks)})
        return blocks

    def in_order(mine, other, axis):
        return jnp.where(
            half == 0,
            jnp.concatenate([mine, other], axis=axis),
            jnp.concatenate([other, mine], axis=axis),
        )

    hidden_all = lax.all_gather(hidden, "col", axis=0)
    w_query, w_key, w_value = weights
    own_pair, send_pair, own_single, send_single = cut((w_key, w_value, w_query), half)
    pairs = {0: own_pair, top: swap(send_pair, top)}
    pairs[hops[0]] = swap(pairs[0], hops[0])
    pairs[hops[0] | top] = swap(pairs[top], hops[0])

    rows = hidden.astype(jnp.float32)
    local_mean = jnp.mean(rows, axis=1)
    local_square = jnp.sum(jnp.square(rows - local_mean[:, None]), axis=1)
    stats = jnp.stack([local_mean, local_square])
    all_stats = [stats] + [across(stats, step) for step in range(1, ranks)]
    average = sum(part[0] for part in all_stats) / ranks
    variance = (
        sum(part[1] + shard * jnp.square(part[0] - average) for part in all_stats) / width
    )
    small = jnp.concatenate(
        [jnp.stack([average, lax.rsqrt(variance + epsilon)]), positions.astype(jnp.float32)]
    )
    small_other = swap(small, top)
    other_rows = swap(hidden, top)
    received_single = swap(send_single, top)
    pairs[hops[0] | top], small_other, other_rows, received_single = lax.optimization_barrier(
        (pairs[hops[0] | top], small_other, other_rows, received_single)
    )
    pairs = spread(pairs, hops[1:])

    received_single, hidden_all = lax.optimization_barrier((received_single, hidden_all))
    early = tok_rows * 5 // 12 // 16 * 16
    early_shards = [across(other_rows[:early], step) for step in range(1, ranks)]
    rest = jnp.stack(
        [
            lax.dynamic_slice(hidden_all, (rank ^ step, early, 0), (1, tok_rows - early, shard))[0]
            for step in range(1, ranks)
        ]
    )
    rest = swap(rest, top)
    singles = spread({0: own_single, top: received_single}, hops)

    tables = rotary_lanes(jnp.concatenate([small[2:], small_other[2:]], axis=1), HEAD_DIM)
    q_gain, k_gain = [
        lax.dynamic_slice_in_dim(gain, half * cols, cols, 0) for gain in gains
    ]
    count = tok_rows // PAGE
    pages = jnp.concatenate(
        [own_pages(page_table, owner * count, count) for owner in (me ^ top, me)]
    )
    query_segs = [
        lax.dynamic_slice_in_dim(segment_ids, owner * tok_rows, tok_rows, 0)
        for owner in (me, me ^ top)
    ]
    bounds = [key_bounds(seg, segment_ids) for seg in query_segs]
    query_segs = [seg[:, None] for seg in query_segs]
    prepared = (tables, q_gain, k_gain, pages, query_segs, bounds)
    prepared, hidden_all = lax.optimization_barrier((prepared, hidden_all))
    tables, q_gain, k_gain, pages, query_segs, bounds = prepared
    key_seg = segment_ids.reshape(-1, 1, KEY_TILE)
    place = jnp.stack([me, rank]).astype(jnp.int32)
    held = ([pairs[i] for i in range(ring)], [singles[i] for i in range(ring)])

    own_parts = ((tok_rows, ((None, 0),), True),)
    own = project(place, small[:2], modulation, own_parts, [hidden_all], *held)
    steps = range(ranks - 1)
    other_parts = (
        (early, ((None, 0),) * ranks, False),
        (tok_rows - early, ((None, early),) + tuple((step, 0) for step in steps), False),
    )
    shards = [other_rows] + early_shards + [other_rows] + [rest] * (ranks - 1)
    other = project(place, small_other[:2], modulation, other_parts, shards, *held)

    values = {0: own[2][None], top: other[2][None]}
    ahead = {number: swap(value, hops[0]) for number, value in values.items()}
    squares = jnp.stack([own[3], other[3]])
    squares = squares + swap(squares, top)[::-1]
    bit = 1
    while 2 * bit < ranks:
        squares = squares + across(squares, bit)
        bit *= 2
    squares_other = across(squares, bit)
    key = turn(
        [own[0], other[0]], squares[:, 0], squares_other[:, 0], k_gain, tables, width
    )
    query = turn(
        [own[1], other[1]], squares[:, 1], squares_other[:, 1], q_gain, tables, width
    )
    ahead, key = lax.optimization_barrier((ahead, key))
    keys = {0: key, hops[0]: swap(key, hops[0])}
    values.update({number | hops[0]: value for number, value in ahead.items()})
    values = spread(values, hops[1:])
    value_places = tuple((lambda me, n=number: me ^ n,) for number in range(ring))
    value_pieces = [values[number] for number in range(ring)]
    values_picked = pick_pages([value_pieces], value_places, me, pages, 2)
    keys[hops[0]], query, values_picked = lax.optimization_barrier(
        (keys[hops[0]], query, values_picked)
    )
    keys = spread(keys, hops[1:])
    key_places = tuple(
        (lambda me, n=number: me ^ n, lambda me, n=number: me ^ n ^ top) for number in range(top)
    )
    key_pieces = [keys[number] for number in range(top)]
    keys_picked = pick_pages([key_pieces], key_places, me, pages, 2)
    query, keys_picked = lax.optimization_barrier((query, keys_picked))

    def attended(query, number):
        return attend(
            query[number],
            key_pieces,
            value_pieces,
            (key_places, value_places),
            me,
            bounds[number],
            query_segs[number],
            key_seg,
        )

    for_other = attended(query, 1)
    pages_other = [swap(picked[0], top) for picked in (keys_picked, values_picked)]
    query, pages_other, for_other = lax.optimization_barrier((query, pages_other, for_other))
    from_other = swap(for_other, top)
    for_me = attended(query, 0)
    page_store = [
        in_order(picked[1], received, -1)
        for picked, received in zip((keys_picked, values_picked), pages_other)
    ]
    return in_order(for_me, from_other, -1), jnp.stack(page_store)


def solution(mesh):
    ring, ranks = mesh.shape["row"], mesh.shape["col"]

    def body(
        hidden, modulation, w_query, w_key, w_value, q_gain, k_gain, positions, segment_ids, page_table
    ):
        rest = (
            hidden,
            modulation,
            (w_query, w_key, w_value),
            (q_gain, k_gain),
            positions,
            segment_ids,
            page_table,
        )
        heads = w_query.shape[1] // HEAD_DIM
        feats, shard = w_query.shape[0], hidden.shape[1]
        powers = ring & (ring - 1) == 0 and ranks & (ranks - 1) == 0
        if heads % 2 == 0 and ring % 2 == 0 and powers and feats % 128 == 0 and shard % feats == 0:
            return split_heads(ring, ranks, *rest)
        return whole_heads(ring, *rest)

    in_specs = (
        P("row", "col"),
        P(),
        P("row", "col"),
        P("row", "col"),
        P("row", "col"),
        P("col"),
        P("col"),
        P(None, "row"),
        P(),
        P(),
    )
    out_specs = (P("row", "col"), P(None, "row", None, "col"))
    return jax.shard_map(body, mesh=mesh, in_specs=in_specs, out_specs=out_specs, check_vma=False)
```

```python
import functools
import jax
import jax.numpy as jnp
from jax import lax
from jax.experimental import pallas as pl
from jax.experimental.pallas import tpu as pltpu
from jax.sharding import PartitionSpec as P

HEAD_DIM = 128
PAGE = 128
KEY_TILE = 512
VMEM = 60 * 1024 * 1024
LOG2E = 1.4426950408889634

epsilon = 1e-06


def rotary_table(positions, pair_count):
    frame_pairs = pair_count - 2 * (pair_count // 3)
    side_pairs = pair_count // 3
    column = jnp.arange(pair_count)
    frame_rate = 10000.0 ** (-column.astype(jnp.float32) / frame_pairs)
    height_rate = 10000.0 ** (-(column - frame_pairs).astype(jnp.float32) / side_pairs)
    width_rate = 10000.0 ** (-(column - frame_pairs - side_pairs).astype(jnp.float32) / side_pairs)
    coords = positions.astype(jnp.float32)
    angles = jnp.where(
        column < frame_pairs,
        coords[0][:, None] * frame_rate,
        jnp.where(
            column < frame_pairs + side_pairs,
            coords[1][:, None] * height_rate,
            coords[2][:, None] * width_rate,
        ),
    )
    return (jnp.cos(angles), jnp.sin(angles))


def rotary_lanes(positions, head_dim):
    cosine, sine_table = rotary_table(positions, head_dim // 2)
    own = jnp.repeat(cosine, 2, axis=1)
    sine = jnp.repeat(sine_table, 2, axis=1)
    even = (jnp.arange(head_dim) % 2 == 0)[None, :]
    return own, jnp.where(even, -sine, 0.0), jnp.where(even, 0.0, sine)


def modulate(activations, modulation):
    average = jnp.mean(activations, axis=1, keepdims=True)
    centred = activations - average
    variance = jnp.mean(centred * centred, axis=1, keepdims=True)
    normed = centred * lax.rsqrt(variance + epsilon)
    return (normed * (1.0 + modulation[1]) + modulation[0]).astype(jnp.bfloat16)


def cut_kernel(half_ref, *refs):
    weights, outs = refs[:3], refs[3:]
    cols = outs[0].shape[2]
    half = half_ref[0]
    for number, weight in enumerate(weights):
        out, at = (0, number) if number < 2 else (2, 0)
        outs[out][at] = weight[:, pl.ds(pl.multiple_of(half * cols, cols), cols)]
        outs[out + 1][at] = weight[:, pl.ds(pl.multiple_of((1 - half) * cols, cols), cols)]


def cut(weights, half):
    rows, width = weights[0].shape
    cols = width // 2
    tile = 128
    sizes = (2, 2, 1, 1)
    return pl.pallas_call(
        cut_kernel,
        grid_spec=pltpu.PrefetchScalarGridSpec(
            num_scalar_prefetch=1,
            grid=(rows // tile,),
            in_specs=[pl.BlockSpec((tile, width), lambda i, _: (i, 0))] * 3,
            out_specs=[pl.BlockSpec((size, tile, cols), lambda i, _: (0, i, 0)) for size in sizes],
        ),
        out_shape=[jax.ShapeDtypeStruct((size, rows, cols), jnp.bfloat16) for size in sizes],
        compiler_params=pltpu.CompilerParams(vmem_limit_bytes=VMEM),
        cost_estimate=pl.CostEstimate(
            flops=0, bytes_accessed=12 * rows * width, transcendentals=0
        ),
        name="cut",
    )(half.reshape(1), *weights)


def project_kernel(parts, count, place_ref, stats_ref, modulation_ref, *refs):
    total_parts = sum(len(part[1]) for part in parts)
    shards, pairs = refs[:total_parts], refs[total_parts : total_parts + count]
    singles = refs[total_parts + count : total_parts + 2 * count]
    key_ref, query_ref, value_ref, squares_ref = refs[total_parts + 2 * count : -6]
    raws, weights, ready, total, raw_sems, weight_sems = refs[-6:]
    me, rank = place_ref[0], place_ref[1]
    feats, cols = weights.shape[2:]
    rows = raws.shape[1]
    per_rank = shards[0].shape[-1] // feats
    copies = []
    for block in range(count):
        owner = me ^ block
        span = pl.ds(pl.multiple_of((owner % per_rank) * feats, feats), feats)
        holder = owner // per_rank
        mine = []
        begin, first = 0, 0
        for number, (length, places, by_rank) in enumerate(parts):
            target = raws.at[block, pl.ds(begin, length), :]
            sem = raw_sems.at[block, number]
            if by_rank:
                copy = pltpu.make_async_copy(
                    shards[first].at[holder, pl.ds(places[0][1], length), span], target, sem
                )
                copy.start()
            else:
                for step, (at, skip) in enumerate(places):
                    ref = shards[first + step]
                    if at is not None:
                        ref = ref.at[at]
                    source = ref.at[pl.ds(skip, length), span]

                    @pl.when((holder ^ rank) == step)
                    def _(source=source, target=target, sem=sem):
                        pltpu.make_async_copy(source, target, sem).start()

                copy = pltpu.make_async_copy(source, target, sem)
            mine.append(copy)
            begin += length
            first += len(places)
        matrices = [
            pltpu.make_async_copy(source, weights.at[block, number], weight_sems.at[block, number])
            for number, source in enumerate(
                (pairs[block].at[0], pairs[block].at[1], singles[block].at[0])
            )
        ]
        for copy in matrices:
            copy.start()
        copies.append((mine, matrices))

    def column(at):
        return jnp.transpose(jnp.broadcast_to(stats_ref[at : at + 1, :], (128, rows)))

    mean, scale = column(0), column(1)

    def prepare(first):
        for block in (first, first + 1):
            for copy in copies[block][0]:
                copy.wait()
            span = pl.ds(pl.multiple_of((me ^ block) * feats, feats), feats)
            shift = modulation_ref[0:1, span]
            gain = 1.0 + modulation_ref[1:2, span]
            left = (block - first) * feats
            for start in range(0, feats, 128):
                lanes = slice(start, start + 128)
                part = raws[block, :, lanes].astype(jnp.float32)
                part = (part - mean) * scale * gain[:, lanes] + shift[:, lanes]
                ready[first // 2 % 2, :, left + start : left + start + 128] = part.astype(
                    jnp.bfloat16
                )

    prepare(0)
    for first in range(0, count, 2):
        for copy in copies[first][1] + copies[first + 1][1]:
            copy.wait()
        if first + 2 < count:
            prepare(first + 2)
        right = jnp.concatenate(
            [
                jnp.concatenate([weights[first, m], weights[first + 1, m]], axis=0)
                for m in range(3)
            ],
            axis=1,
        )
        part = jnp.dot(ready[first // 2 % 2], right, preferred_element_type=jnp.float32)
        if first:
            part = part + total[...]
        if first < count - 2:
            total[...] = part
            continue
        key, value, query = [part[:, m * cols : (m + 1) * cols] for m in range(3)]
        key_ref[...] = key
        query_ref[...] = query
        value_ref[...] = value.astype(value_ref.dtype)
        for number, raw in enumerate((key, query)):
            summed = jnp.sum(raw * raw, axis=1, keepdims=True)
            summed = jnp.transpose(jnp.broadcast_to(summed, (rows, 128)))
            squares_ref[number : number + 1, :] = summed[:1]


def project(place, stats, modulation, parts, shards, pairs, singles):
    rows = sum(part[0] for part in parts)
    _, feats, cols = singles[0].shape
    count = len(singles)
    raw = jax.ShapeDtypeStruct((rows, cols), jnp.float32)
    anywhere = pl.BlockSpec(memory_space=pl.ANY)
    whole = pl.BlockSpec(memory_space=pltpu.VMEM)
    return pl.pallas_call(
        functools.partial(project_kernel, parts, count),
        in_specs=[pl.BlockSpec(memory_space=pltpu.SMEM), whole, whole]
        + [anywhere] * (len(shards) + 2 * count),
        out_specs=[whole] * 4,
        out_shape=[
            raw,
            raw,
            jax.ShapeDtypeStruct(raw.shape, jnp.bfloat16),
            jax.ShapeDtypeStruct((2, rows), jnp.float32),
        ],
        scratch_shapes=[
            pltpu.VMEM((count, rows, feats), jnp.bfloat16),
            pltpu.VMEM((count, 3, feats, cols), jnp.bfloat16),
            pltpu.VMEM((2, rows, 2 * feats), jnp.bfloat16),
            pltpu.VMEM((rows, 3 * cols), jnp.float32),
            pltpu.SemaphoreType.DMA((count, len(parts))),
            pltpu.SemaphoreType.DMA((count, 3)),
        ],
        compiler_params=pltpu.CompilerParams(vmem_limit_bytes=VMEM),
        cost_estimate=pl.CostEstimate(
            flops=6 * rows * count * feats * cols,
            bytes_accessed=2 * count * feats * (rows + 3 * cols) + 10 * rows * cols,
            transcendentals=0,
        ),
        name="project",
    )(place, stats, modulation, *shards, *pairs, *singles)


def turn_kernel(
    width, count, mine_ref, other_ref, gain_ref, own_ref, upper_ref, lower_ref, *refs
):
    outs = refs[count:]
    outs = outs if len(outs) == count else [outs[0].at[number] for number in range(count)]
    dim = own_ref.shape[1]
    for number, raw_ref in enumerate(refs[:count]):
        rows = raw_ref.shape[0]
        at = slice(number, number + 1)
        scale = lax.rsqrt((mine_ref[at, :] + other_ref[at, :]) * (1.0 / width) + epsilon)
        scale = jnp.transpose(jnp.broadcast_to(scale, (128, rows)))
        lines = slice(number * rows, (number + 1) * rows)
        own, upper, lower = own_ref[lines, :], upper_ref[lines, :], lower_ref[lines, :]
        for head in range(raw_ref.shape[1] // dim):
            cols = slice(head * dim, (head + 1) * dim)
            normed = raw_ref[:, cols] * scale * gain_ref[:, cols]
            turned = (
                normed * own
                + pltpu.roll(normed, dim - 1, 1) * upper
                + pltpu.roll(normed, 1, 1) * lower
            )
            outs[number][:, cols] = turned.astype(jnp.bfloat16)


def turn(raws, mine, other, gain, tables, width, joined):
    rows, cols = raws[0].shape
    count = len(raws)
    whole = pl.BlockSpec(memory_space=pltpu.VMEM)
    return pl.pallas_call(
        functools.partial(turn_kernel, width, count),
        in_specs=[whole] * (6 + count),
        out_specs=[whole] * (1 if joined else count),
        out_shape=[jax.ShapeDtypeStruct((count, rows, cols), jnp.bfloat16)]
        if joined
        else [jax.ShapeDtypeStruct((rows, cols), jnp.bfloat16)] * count,
        compiler_params=pltpu.CompilerParams(vmem_limit_bytes=VMEM),
        cost_estimate=pl.CostEstimate(
            flops=8 * count * rows * cols, bytes_accessed=6 * count * rows * cols, transcendentals=0
        ),
        name="turn",
    )(mine, other, gain[None, :], *tables, *raws)


def attend_kernel(places, me_ref, bounds_ref, q_ref, *refs):
    count = len(places[0]) + len(places[1])
    sources, (query_seg_ref, key_seg_ref) = refs[:count], refs[count : count + 2]
    out_ref, keys, values, highest, mixed, sems = refs[count + 2 :]
    me = me_ref[0]
    rows = sources[0].shape[1]
    copies = []
    for kind, held in enumerate((keys, values)):
        for piece, owners in enumerate(places[kind]):
            source = sources[kind * len(places[0]) + piece]
            for at, owner in enumerate(owners):
                where = pl.ds(pl.multiple_of(owner(me) * rows, rows), rows)
                copies.append(
                    pltpu.make_async_copy(
                        source.at[at], held.at[where, :], sems.at[kind, piece, at]
                    )
                )
    for copy in copies:
        copy.start()
    dim = HEAD_DIM
    heads = q_ref.shape[1] // dim
    factor = dim ** (-0.5) * LOG2E
    ones = jnp.ones((KEY_TILE, dim), jnp.bfloat16)
    highest[...] = jnp.full_like(highest, -1e29)
    mixed[...] = jnp.zeros_like(mixed)
    for copy in copies:
        copy.wait()

    query_seg = jnp.transpose(jnp.broadcast_to(query_seg_ref[...], (128, rows)))[:, :1]

    def step(block, carry):
        where = pl.ds(pl.multiple_of(block * KEY_TILE, KEY_TILE), KEY_TILE)
        same = query_seg == key_seg_ref[block]
        for head in range(heads):
            cols = slice(head * dim, (head + 1) * dim)
            scores = lax.dot_general(
                q_ref[:, cols],
                keys[where, cols],
                (((1,), (1,)), ((), ())),
                preferred_element_type=jnp.float32,
            )
            scores = jnp.where(same, scores * factor, -1e30)
            former = highest[head]
            newest = jnp.maximum(former, jnp.max(scores, axis=1, keepdims=True))
            highest[head] = newest
            weights = jnp.exp2(scores - newest[:, :1]).astype(jnp.bfloat16)
            right = jnp.concatenate([values[where, cols], ones], axis=1)
            part = jnp.dot(weights, right, preferred_element_type=jnp.float32)
            shrink = jnp.exp2(former - newest)
            mixed[head, :, :dim] = mixed[head, :, :dim] * shrink + part[:, :dim]
            mixed[head, :, dim:] = mixed[head, :, dim:] * shrink + part[:, dim:]
        return carry

    lax.fori_loop(bounds_ref[0], bounds_ref[1], step, 0)
    for head in range(heads):
        out_ref[:, head * dim : (head + 1) * dim] = (
            mixed[head, :, :dim] / mixed[head, :, dim:]
        ).astype(out_ref.dtype)


def key_bounds(query_seg, segment_ids):
    low = jnp.sum(segment_ids < query_seg[0], dtype=jnp.int32)
    high = jnp.sum(segment_ids <= query_seg[-1], dtype=jnp.int32)
    return jnp.stack([low // KEY_TILE, (high + KEY_TILE - 1) // KEY_TILE])


def attend(query, key_pieces, value_pieces, places, me, bounds, query_seg, key_seg):
    rows, cols = query.shape
    tokens = key_seg.shape[0] * KEY_TILE
    dim = HEAD_DIM
    heads = cols // dim
    smem = pl.BlockSpec(memory_space=pltpu.SMEM)
    whole = pl.BlockSpec(memory_space=pltpu.VMEM)
    anywhere = pl.BlockSpec(memory_space=pl.ANY)
    return pl.pallas_call(
        functools.partial(attend_kernel, places),
        in_specs=[smem, smem, whole]
        + [anywhere] * (len(places[0]) + len(places[1]))
        + [whole, whole],
        out_specs=whole,
        scratch_shapes=[
            pltpu.VMEM((tokens, cols), jnp.bfloat16),
            pltpu.VMEM((tokens, cols), jnp.bfloat16),
            pltpu.VMEM((heads, rows, dim), jnp.float32),
            pltpu.VMEM((heads, rows, 2 * dim), jnp.float32),
            pltpu.SemaphoreType.DMA(
                (2, max(map(len, places)), max(len(o) for part in places for o in part))
            ),
        ],
        out_shape=jax.ShapeDtypeStruct((rows, cols), jnp.bfloat16),
        compiler_params=pltpu.CompilerParams(vmem_limit_bytes=VMEM),
        cost_estimate=pl.CostEstimate(
            flops=2 * rows * tokens * cols,
            bytes_accessed=4 * tokens * cols + 4 * rows * cols,
            transcendentals=rows * tokens * heads // 2,
        ),
        name="attend",
    )(me.reshape(1), bounds, query, *key_pieces, *value_pieces, query_seg, key_seg)


def pages_kernel(places, me_ref, page_ref, *refs):
    count = len(places)
    sems = refs[-1]
    wanted, chunks = sems.shape
    out_refs = refs[chunks * count : -1]
    me = me_ref[0]
    each = wanted // len(out_refs)
    per_block = refs[0].shape[1] // PAGE
    waits = []
    for number in range(wanted):
        page = page_ref[number]
        rows = pl.ds(pl.multiple_of((page % per_block) * PAGE, PAGE), PAGE)
        start = 0
        for chunk in range(chunks):
            sources = refs[chunk * count : (chunk + 1) * count]
            cols = pl.ds(start, sources[0].shape[2])
            start += sources[0].shape[2]
            sem = sems.at[number, chunk]
            target = out_refs[number // each].at[number % each, :, cols]
            for piece, owners in enumerate(places):
                for at, owner in enumerate(owners):

                    @pl.when(page // per_block == owner(me))
                    def _(source=sources[piece].at[at, rows, :], target=target, sem=sem):
                        pltpu.make_async_copy(source, target, sem).start()

            waits.append(
                pltpu.make_async_copy(sources[0].at[0, pl.ds(0, PAGE), :], target, sem)
            )
    for copy in waits:
        copy.wait()


def pick_pages(chunks, places, me, pages, parts):
    cols = sum(pieces[0].shape[2] for pieces in chunks)
    wanted = pages.shape[0]
    smem = pl.BlockSpec(memory_space=pltpu.SMEM)
    anywhere = pl.BlockSpec(memory_space=pl.ANY)
    return pl.pallas_call(
        functools.partial(pages_kernel, places),
        in_specs=[smem, smem] + [anywhere] * (len(chunks) * len(places)),
        out_specs=[pl.BlockSpec(memory_space=pltpu.VMEM)] * parts,
        out_shape=[jax.ShapeDtypeStruct((wanted // parts, PAGE, cols), jnp.bfloat16)] * parts,
        scratch_shapes=[pltpu.SemaphoreType.DMA((wanted, len(chunks)))],
        compiler_params=pltpu.CompilerParams(vmem_limit_bytes=VMEM),
        cost_estimate=pl.CostEstimate(
            flops=0, bytes_accessed=4 * wanted * PAGE * cols, transcendentals=0
        ),
        name="pick_pages",
    )(me.reshape(1), pages, *[piece for pieces in chunks for piece in pieces])


def own_pages(page_table, start, count):
    page_total = page_table.shape[0]
    inverse = (
        jnp.zeros((page_total,), jnp.int32)
        .at[page_table]
        .set(jnp.arange(page_total, dtype=jnp.int32))
    )
    return lax.dynamic_slice_in_dim(inverse, start, count, 0)


def whole_heads(ring, hidden, modulation, weights, gains, positions, segment_ids, page_table):
    tok_rows = hidden.shape[0]
    me = lax.axis_index("row")
    full_rows = lax.all_gather(hidden, "col", axis=1, tiled=True)
    modulated = modulate(full_rows.astype(jnp.float32), modulation)
    width = full_rows.shape[1]
    raws = [
        jnp.dot(
            modulated,
            lax.all_gather(weight, "row", axis=0, tiled=True),
            preferred_element_type=jnp.float32,
        )
        for weight in weights
    ]
    squares = lax.psum(tuple(jnp.sum(raw * raw, axis=1) for raw in raws[:2]), "col")
    tables = rotary_lanes(positions, HEAD_DIM)
    query, key = [
        turn([raw], total[None], jnp.zeros_like(total)[None], gain, tables, width, False)[0]
        for raw, total, gain in zip(raws, squares, gains)
    ]
    value = raws[2].astype(jnp.bfloat16)
    keys_all = lax.all_gather(key, "row", axis=0)
    values_all = lax.all_gather(value, "row", axis=0)
    places = (tuple(lambda me, at=at: at for at in range(ring)),)
    none = jnp.zeros((), jnp.int32)
    query_seg = lax.dynamic_slice_in_dim(segment_ids, me * tok_rows, tok_rows, 0)
    attended = attend(
        query,
        [keys_all],
        [values_all],
        (places, places),
        none,
        key_bounds(query_seg, segment_ids),
        query_seg.astype(jnp.float32)[None, :],
        segment_ids.astype(jnp.float32).reshape(-1, 1, KEY_TILE),
    )
    count = tok_rows // PAGE
    pages = own_pages(page_table, me * count, count)
    picked = [pick_pages([[held]], places, none, pages, 1)[0] for held in (keys_all, values_all)]
    return attended, jnp.stack(picked)


def split_heads(ring, ranks, hidden, modulation, weights, gains, positions, segment_ids, page_table):
    tok_rows, shard = hidden.shape
    width = ranks * shard
    me = lax.axis_index("row")
    rank = lax.axis_index("col")
    top = ring // 2
    half = me // top
    cols = weights[0].shape[1] // 2
    hops = []
    bit = top // 2
    while bit:
        hops.append(bit)
        bit //= 2

    def swap(value, bit):
        return lax.ppermute(value, "row", [(i, i ^ bit) for i in range(ring)])

    def across(value, step):
        return lax.ppermute(value, "col", [(c, c ^ step) for c in range(ranks)])

    def spread(blocks, bits):
        for bit in bits:
            blocks.update({number | bit: swap(blocks[number], bit) for number in list(blocks)})
        return blocks

    def in_order(mine, other, axis):
        return jnp.where(
            half == 0,
            jnp.concatenate([mine, other], axis=axis),
            jnp.concatenate([other, mine], axis=axis),
        )

    hidden_all = lax.all_gather(hidden, "col", axis=0)
    w_query, w_key, w_value = weights
    own_pair, send_pair, own_single, send_single = cut((w_key, w_value, w_query), half)
    pairs = {0: own_pair, top: swap(send_pair, top)}
    pairs[hops[0]] = swap(pairs[0], hops[0])
    pairs[hops[0] | top] = swap(pairs[top], hops[0])

    rows = hidden.astype(jnp.float32)
    local_mean = jnp.mean(rows, axis=1)
    local_square = jnp.sum(jnp.square(rows - local_mean[:, None]), axis=1)
    stats = jnp.stack([local_mean, local_square])
    all_stats = [stats] + [across(stats, step) for step in range(1, ranks)]
    average = sum(part[0] for part in all_stats) / ranks
    variance = (
        sum(part[1] + shard * jnp.square(part[0] - average) for part in all_stats) / width
    )
    small = jnp.concatenate(
        [jnp.stack([average, lax.rsqrt(variance + epsilon)]), positions.astype(jnp.float32)]
    )
    small_other = swap(small, top)
    other_rows = swap(hidden, top)
    singles = {0: own_single, top: swap(send_single, top)}
    singles[hops[0]] = swap(own_single, hops[0])
    pairs[hops[0] | top], small_other, other_rows, singles = lax.optimization_barrier(
        (pairs[hops[0] | top], small_other, other_rows, singles)
    )
    pairs = spread(pairs, hops[1:])

    singles, hidden_all = lax.optimization_barrier((singles, hidden_all))
    singles[hops[0] | top] = swap(singles[top], hops[0])
    early = tok_rows * 5 // 12 // 16 * 16
    early_shards = [across(other_rows[:early], step) for step in range(1, ranks)]
    rest = [
        swap(
            lax.dynamic_slice(hidden_all, (rank ^ step, early, 0), (1, tok_rows - early, shard))[0],
            top,
        )
        for step in range(1, ranks)
    ]
    singles, rest[:-1], early_shards[:-1] = lax.optimization_barrier(
        (singles, rest[:-1], early_shards[:-1])
    )
    singles = spread(singles, hops[1:])

    tables = rotary_lanes(jnp.concatenate([small[2:], small_other[2:]], axis=1), HEAD_DIM)
    q_gain, k_gain = [
        lax.dynamic_slice_in_dim(gain, half * cols, cols, 0) for gain in gains
    ]
    count = tok_rows // PAGE
    pages = jnp.concatenate(
        [own_pages(page_table, owner * count, count) for owner in (me ^ top, me)]
    )
    query_segs = [
        lax.dynamic_slice_in_dim(segment_ids, owner * tok_rows, tok_rows, 0)
        for owner in (me, me ^ top)
    ]
    bounds = [key_bounds(seg, segment_ids) for seg in query_segs]
    query_segs = [seg.astype(jnp.float32)[None, :] for seg in query_segs]
    key_seg = segment_ids.astype(jnp.float32).reshape(-1, 1, KEY_TILE)
    prepared = (tables, q_gain, k_gain, pages, query_segs, key_seg, bounds)
    prepared, hidden_all = lax.optimization_barrier((prepared, hidden_all))
    tables, q_gain, k_gain, pages, query_segs, key_seg, bounds = prepared
    place = jnp.stack([me, rank]).astype(jnp.int32)
    held = ([pairs[i] for i in range(ring)], [singles[i] for i in range(ring)])

    own_parts = ((tok_rows, ((None, 0),), True),)
    own = project(place, small[:2], modulation, own_parts, [hidden_all], *held)
    other_parts = (
        (early, ((None, 0),) * ranks, False),
        (tok_rows - early, ((None, early),) + ((None, 0),) * (ranks - 1), False),
    )
    shards = [other_rows] + early_shards + [other_rows] + rest
    other = project(place, small_other[:2], modulation, other_parts, shards, *held)

    values = {0: own[2][None], top: other[2][None]}
    ahead = {number: swap(value, hops[0]) for number, value in values.items()}
    squares = jnp.stack([own[3], other[3]])
    squares, ahead[0] = lax.optimization_barrier((squares, ahead[0]))
    squares = squares + swap(squares, top)[::-1]
    bit = 1
    while 2 * bit < ranks:
        squares = squares + across(squares, bit)
        bit *= 2
    squares_other = across(squares, bit)
    squares_other, ahead[top] = lax.optimization_barrier((squares_other, ahead[top]))
    (key,) = turn(
        [own[0], other[0]], squares[:, 0], squares_other[:, 0], k_gain, tables, width, True
    )
    query = turn(
        [own[1], other[1]], squares[:, 1], squares_other[:, 1], q_gain, tables, width, False
    )
    keys = {0: key, hops[0]: swap(key, hops[0])}
    ahead, _ = lax.optimization_barrier((ahead, key))
    values.update({number | hops[0]: value for number, value in ahead.items()})
    values = spread(values, hops[1:])
    value_places = tuple((lambda me, n=number: me ^ n,) for number in range(ring))
    value_pieces = [values[number] for number in range(ring)]
    values_picked = pick_pages([value_pieces], value_places, me, pages, 2)
    keys[hops[0]], query, values_picked = lax.optimization_barrier(
        (keys[hops[0]], query, values_picked)
    )
    keys = spread(keys, hops[1:])
    key_places = tuple(
        (lambda me, n=number: me ^ n, lambda me, n=number: me ^ n ^ top) for number in range(top)
    )
    key_pieces = [keys[number] for number in range(top)]
    keys_picked = pick_pages([key_pieces], key_places, me, pages, 2)
    query, keys_picked = lax.optimization_barrier((query, keys_picked))

    def attended(query, number):
        return attend(
            query[number],
            key_pieces,
            value_pieces,
            (key_places, value_places),
            me,
            bounds[number],
            query_segs[number],
            key_seg,
        )

    for_other = attended(query, 1)
    pages_other = [swap(picked[0], top) for picked in (keys_picked, values_picked)]
    query, pages_other, for_other = lax.optimization_barrier((query, pages_other, for_other))
    from_other = swap(for_other, top)
    for_me = attended(query, 0)
    page_store = [
        in_order(picked[1], received, -1)
        for picked, received in zip((keys_picked, values_picked), pages_other)
    ]
    return in_order(for_me, from_other, -1), jnp.stack(page_store)


def solution(mesh):
    ring, ranks = mesh.shape["row"], mesh.shape["col"]

    def body(
        hidden, modulation, w_query, w_key, w_value, q_gain, k_gain, positions, segment_ids, page_table
    ):
        rest = (
            hidden,
            modulation,
            (w_query, w_key, w_value),
            (q_gain, k_gain),
            positions,
            segment_ids,
            page_table,
        )
        heads = w_query.shape[1] // HEAD_DIM
        feats, shard = w_query.shape[0], hidden.shape[1]
        powers = ring & (ring - 1) == 0 and ranks & (ranks - 1) == 0
        if heads % 2 == 0 and ring % 2 == 0 and powers and feats % 128 == 0 and shard % feats == 0:
            return split_heads(ring, ranks, *rest)
        return whole_heads(ring, *rest)

    in_specs = (
        P("row", "col"),
        P(),
        P("row", "col"),
        P("row", "col"),
        P("row", "col"),
        P("col"),
        P("col"),
        P(None, "row"),
        P(),
        P(),
    )
    out_specs = (P("row", "col"), P(None, "row", None, "col"))
    return jax.shard_map(body, mesh=mesh, in_specs=in_specs, out_specs=out_specs, check_vma=False)
```

```python
import functools
import jax
import jax.numpy as jnp
from jax import lax
from jax.experimental import pallas as pl
from jax.experimental.pallas import tpu as pltpu
from jax.sharding import PartitionSpec as P

HEAD_DIM = 128
PAGE = 128
KEY_TILE = 512
VMEM = 60 * 1024 * 1024
LOG2E = 1.4426950408889634

epsilon = 1e-06


def rotary_table(positions, pair_count):
    frame_pairs = pair_count - 2 * (pair_count // 3)
    side_pairs = pair_count // 3
    column = jnp.arange(pair_count)
    frame_rate = 10000.0 ** (-column.astype(jnp.float32) / frame_pairs)
    height_rate = 10000.0 ** (-(column - frame_pairs).astype(jnp.float32) / side_pairs)
    width_rate = 10000.0 ** (-(column - frame_pairs - side_pairs).astype(jnp.float32) / side_pairs)
    coords = positions.astype(jnp.float32)
    angles = jnp.where(
        column < frame_pairs,
        coords[0][:, None] * frame_rate,
        jnp.where(
            column < frame_pairs + side_pairs,
            coords[1][:, None] * height_rate,
            coords[2][:, None] * width_rate,
        ),
    )
    return (jnp.cos(angles), jnp.sin(angles))


def rotary_lanes(positions, head_dim):
    cosine, sine_table = rotary_table(positions, head_dim // 2)
    own = jnp.repeat(cosine, 2, axis=1)
    sine = jnp.repeat(sine_table, 2, axis=1)
    even = (jnp.arange(head_dim) % 2 == 0)[None, :]
    return own, jnp.where(even, -sine, 0.0), jnp.where(even, 0.0, sine)


def modulate(activations, modulation):
    average = jnp.mean(activations, axis=1, keepdims=True)
    centred = activations - average
    variance = jnp.mean(centred * centred, axis=1, keepdims=True)
    normed = centred * lax.rsqrt(variance + epsilon)
    return (normed * (1.0 + modulation[1]) + modulation[0]).astype(jnp.bfloat16)


def cut_kernel(half_ref, *refs):
    weights, outs = refs[:3], refs[3:]
    cols = outs[0].shape[2]
    half = half_ref[0]
    for number, weight in enumerate(weights):
        send, at = (1, number) if number < 2 else (2, 0)
        outs[0][number] = weight[:, pl.ds(pl.multiple_of(half * cols, cols), cols)]
        outs[send][at] = weight[:, pl.ds(pl.multiple_of((1 - half) * cols, cols), cols)]


def cut(weights, half):
    rows, width = weights[0].shape
    cols = width // 2
    tile = 128
    sizes = (3, 2, 1)
    return pl.pallas_call(
        cut_kernel,
        grid_spec=pltpu.PrefetchScalarGridSpec(
            num_scalar_prefetch=1,
            grid=(rows // tile,),
            in_specs=[pl.BlockSpec((tile, width), lambda i, _: (i, 0))] * 3,
            out_specs=[pl.BlockSpec((size, tile, cols), lambda i, _: (0, i, 0)) for size in sizes],
        ),
        out_shape=[jax.ShapeDtypeStruct((size, rows, cols), jnp.bfloat16) for size in sizes],
        compiler_params=pltpu.CompilerParams(vmem_limit_bytes=VMEM),
        cost_estimate=pl.CostEstimate(
            flops=0, bytes_accessed=12 * rows * width, transcendentals=0
        ),
        name="cut",
    )(half.reshape(1), *weights)


def project_kernel(parts, spots, place_ref, stats_ref, modulation_ref, *refs):
    count = len(spots)
    total_parts = sum(len(part[1]) for part in parts)
    shards, sources = refs[:total_parts], refs[total_parts:-10]
    key_ref, query_ref, value_ref, squares_ref = refs[-10:-6]
    raws, weights, ready, total, raw_sems, weight_sems = refs[-6:]
    me, rank = place_ref[0], place_ref[1]
    feats, cols = weights.shape[2:]
    rows = raws.shape[1]
    per_rank = shards[0].shape[-1] // feats
    copies = []
    for block in range(count):
        owner = me ^ block
        span = pl.ds(pl.multiple_of((owner % per_rank) * feats, feats), feats)
        holder = owner // per_rank
        mine = []
        begin, first = 0, 0
        for number, (length, places, by_rank) in enumerate(parts):
            target = raws.at[block, pl.ds(begin, length), :]
            sem = raw_sems.at[block, number]
            if by_rank:
                copy = pltpu.make_async_copy(
                    shards[first].at[holder, pl.ds(places[0][1], length), span], target, sem
                )
                copy.start()
            else:
                for step, (at, skip) in enumerate(places):
                    ref = shards[first + step]
                    if at is not None:
                        ref = ref.at[at]
                    source = ref.at[pl.ds(skip, length), span]

                    @pl.when((holder ^ rank) == step)
                    def _(source=source, target=target, sem=sem):
                        pltpu.make_async_copy(source, target, sem).start()

                copy = pltpu.make_async_copy(source, target, sem)
            mine.append(copy)
            begin += length
            first += len(places)
        matrices = [
            pltpu.make_async_copy(
                sources[source].at[at], weights.at[block, number], weight_sems.at[block, number]
            )
            for number, (source, at) in enumerate(spots[block])
        ]
        for copy in matrices:
            copy.start()
        copies.append((mine, matrices))

    def column(at):
        return jnp.transpose(jnp.broadcast_to(stats_ref[at : at + 1, :], (128, rows)))

    mean, scale = column(0), column(1)

    def prepare(first):
        for block in (first, first + 1):
            for copy in copies[block][0]:
                copy.wait()
            span = pl.ds(pl.multiple_of((me ^ block) * feats, feats), feats)
            shift = modulation_ref[0:1, span]
            gain = 1.0 + modulation_ref[1:2, span]
            left = (block - first) * feats
            for start in range(0, feats, 128):
                lanes = slice(start, start + 128)
                part = raws[block, :, lanes].astype(jnp.float32)
                part = (part - mean) * scale * gain[:, lanes] + shift[:, lanes]
                ready[first // 2 % 2, :, left + start : left + start + 128] = part.astype(
                    jnp.bfloat16
                )

    prepare(0)
    for first in range(0, count, 2):
        for copy in copies[first][1] + copies[first + 1][1]:
            copy.wait()
        if first + 2 < count:
            prepare(first + 2)
        right = jnp.concatenate(
            [
                jnp.concatenate([weights[first, m], weights[first + 1, m]], axis=0)
                for m in range(3)
            ],
            axis=1,
        )
        part = jnp.dot(ready[first // 2 % 2], right, preferred_element_type=jnp.float32)
        if first:
            part = part + total[...]
        if first < count - 2:
            total[...] = part
            continue
        key, value, query = [part[:, m * cols : (m + 1) * cols] for m in range(3)]
        key_ref[...] = key
        query_ref[...] = query
        value_ref[...] = value.astype(value_ref.dtype)
        for number, raw in enumerate((key, query)):
            summed = jnp.sum(raw * raw, axis=1, keepdims=True)
            summed = jnp.transpose(jnp.broadcast_to(summed, (rows, 128)))
            squares_ref[number : number + 1, :] = summed[:1]


def project(place, stats, modulation, parts, shards, spots, sources):
    rows = sum(part[0] for part in parts)
    _, feats, cols = sources[0].shape
    count = len(spots)
    raw = jax.ShapeDtypeStruct((rows, cols), jnp.float32)
    anywhere = pl.BlockSpec(memory_space=pl.ANY)
    whole = pl.BlockSpec(memory_space=pltpu.VMEM)
    return pl.pallas_call(
        functools.partial(project_kernel, parts, spots),
        in_specs=[pl.BlockSpec(memory_space=pltpu.SMEM), whole, whole]
        + [anywhere] * (len(shards) + len(sources)),
        out_specs=[whole] * 4,
        out_shape=[
            raw,
            raw,
            jax.ShapeDtypeStruct(raw.shape, jnp.bfloat16),
            jax.ShapeDtypeStruct((2, rows), jnp.float32),
        ],
        scratch_shapes=[
            pltpu.VMEM((count, rows, feats), jnp.bfloat16),
            pltpu.VMEM((count, 3, feats, cols), jnp.bfloat16),
            pltpu.VMEM((2, rows, 2 * feats), jnp.bfloat16),
            pltpu.VMEM((rows, 3 * cols), jnp.float32),
            pltpu.SemaphoreType.DMA((count, len(parts))),
            pltpu.SemaphoreType.DMA((count, 3)),
        ],
        compiler_params=pltpu.CompilerParams(vmem_limit_bytes=VMEM),
        cost_estimate=pl.CostEstimate(
            flops=6 * rows * count * feats * cols,
            bytes_accessed=2 * count * feats * (rows + 3 * cols) + 10 * rows * cols,
            transcendentals=0,
        ),
        name="project",
    )(place, stats, modulation, *shards, *sources)


def turn_kernel(
    width, count, mine_ref, other_ref, gain_ref, own_ref, upper_ref, lower_ref, *refs
):
    outs = refs[count:]
    outs = outs if len(outs) == count else [outs[0].at[number] for number in range(count)]
    dim = own_ref.shape[1]
    for number, raw_ref in enumerate(refs[:count]):
        rows = raw_ref.shape[0]
        at = slice(number, number + 1)
        scale = lax.rsqrt((mine_ref[at, :] + other_ref[at, :]) * (1.0 / width) + epsilon)
        scale = jnp.transpose(jnp.broadcast_to(scale, (128, rows)))
        lines = slice(number * rows, (number + 1) * rows)
        own, upper, lower = own_ref[lines, :], upper_ref[lines, :], lower_ref[lines, :]
        for head in range(raw_ref.shape[1] // dim):
            cols = slice(head * dim, (head + 1) * dim)
            normed = raw_ref[:, cols] * scale * gain_ref[:, cols]
            turned = (
                normed * own
                + pltpu.roll(normed, dim - 1, 1) * upper
                + pltpu.roll(normed, 1, 1) * lower
            )
            outs[number][:, cols] = turned.astype(jnp.bfloat16)


def turn(raws, mine, other, gain, tables, width, joined):
    rows, cols = raws[0].shape
    count = len(raws)
    whole = pl.BlockSpec(memory_space=pltpu.VMEM)
    return pl.pallas_call(
        functools.partial(turn_kernel, width, count),
        in_specs=[whole] * (6 + count),
        out_specs=[whole] * (1 if joined else count),
        out_shape=[jax.ShapeDtypeStruct((count, rows, cols), jnp.bfloat16)]
        if joined
        else [jax.ShapeDtypeStruct((rows, cols), jnp.bfloat16)] * count,
        compiler_params=pltpu.CompilerParams(vmem_limit_bytes=VMEM),
        cost_estimate=pl.CostEstimate(
            flops=8 * count * rows * cols, bytes_accessed=6 * count * rows * cols, transcendentals=0
        ),
        name="turn",
    )(mine, other, gain[None, :], *tables, *raws)


def attend_kernel(places, me_ref, bounds_ref, q_ref, *refs):
    count = len(places[0]) + len(places[1])
    sources, (query_seg_ref, key_seg_ref) = refs[:count], refs[count : count + 2]
    out_ref, keys, values, highest, mixed, sems = refs[count + 2 :]
    me = me_ref[0]
    rows = sources[0].shape[1]
    copies = []
    for kind, held in enumerate((keys, values)):
        for piece, owners in enumerate(places[kind]):
            source = sources[kind * len(places[0]) + piece]
            for at, owner in enumerate(owners):
                where = pl.ds(pl.multiple_of(owner(me) * rows, rows), rows)
                copies.append(
                    pltpu.make_async_copy(
                        source.at[at], held.at[where, :], sems.at[kind, piece, at]
                    )
                )
    for copy in copies:
        copy.start()
    dim = HEAD_DIM
    heads = q_ref.shape[1] // dim
    factor = dim ** (-0.5) * LOG2E
    ones = jnp.ones((KEY_TILE, dim), jnp.bfloat16)
    highest[...] = jnp.full_like(highest, -1e29)
    mixed[...] = jnp.zeros_like(mixed)
    for copy in copies:
        copy.wait()

    query_seg = jnp.transpose(jnp.broadcast_to(query_seg_ref[...], (128, rows)))[:, :1]

    def step(block, carry):
        where = pl.ds(pl.multiple_of(block * KEY_TILE, KEY_TILE), KEY_TILE)
        same = query_seg == key_seg_ref[block]
        for head in range(heads):
            cols = slice(head * dim, (head + 1) * dim)
            scores = lax.dot_general(
                q_ref[:, cols],
                keys[where, cols],
                (((1,), (1,)), ((), ())),
                preferred_element_type=jnp.float32,
            )
            scores = jnp.where(same, scores * factor, -1e30)
            former = highest[head]
            newest = jnp.maximum(former, jnp.max(scores, axis=1, keepdims=True))
            highest[head] = newest
            weights = jnp.exp2(scores - newest[:, :1]).astype(jnp.bfloat16)
            right = jnp.concatenate([values[where, cols], ones], axis=1)
            part = jnp.dot(weights, right, preferred_element_type=jnp.float32)
            shrink = jnp.exp2(former - newest)
            mixed[head, :, :dim] = mixed[head, :, :dim] * shrink + part[:, :dim]
            mixed[head, :, dim:] = mixed[head, :, dim:] * shrink + part[:, dim:]
        return carry

    lax.fori_loop(bounds_ref[0], bounds_ref[1], step, 0)
    for head in range(heads):
        out_ref[:, head * dim : (head + 1) * dim] = (
            mixed[head, :, :dim] / mixed[head, :, dim:]
        ).astype(out_ref.dtype)


def key_bounds(query_seg, segment_ids):
    low = jnp.sum(segment_ids < query_seg[0], dtype=jnp.int32)
    high = jnp.sum(segment_ids <= query_seg[-1], dtype=jnp.int32)
    return jnp.stack([low // KEY_TILE, (high + KEY_TILE - 1) // KEY_TILE])


def attend(query, key_pieces, value_pieces, places, me, bounds, query_seg, key_seg):
    rows, cols = query.shape
    tokens = key_seg.shape[0] * KEY_TILE
    dim = HEAD_DIM
    heads = cols // dim
    smem = pl.BlockSpec(memory_space=pltpu.SMEM)
    whole = pl.BlockSpec(memory_space=pltpu.VMEM)
    anywhere = pl.BlockSpec(memory_space=pl.ANY)
    return pl.pallas_call(
        functools.partial(attend_kernel, places),
        in_specs=[smem, smem, whole]
        + [anywhere] * (len(places[0]) + len(places[1]))
        + [whole, whole],
        out_specs=whole,
        scratch_shapes=[
            pltpu.VMEM((tokens, cols), jnp.bfloat16),
            pltpu.VMEM((tokens, cols), jnp.bfloat16),
            pltpu.VMEM((heads, rows, dim), jnp.float32),
            pltpu.VMEM((heads, rows, 2 * dim), jnp.float32),
            pltpu.SemaphoreType.DMA(
                (2, max(map(len, places)), max(len(o) for part in places for o in part))
            ),
        ],
        out_shape=jax.ShapeDtypeStruct((rows, cols), jnp.bfloat16),
        compiler_params=pltpu.CompilerParams(vmem_limit_bytes=VMEM),
        cost_estimate=pl.CostEstimate(
            flops=2 * rows * tokens * cols,
            bytes_accessed=4 * tokens * cols + 4 * rows * cols,
            transcendentals=rows * tokens * heads // 2,
        ),
        name="attend",
    )(me.reshape(1), bounds, query, *key_pieces, *value_pieces, query_seg, key_seg)


def pages_kernel(places, me_ref, page_ref, *refs):
    count = len(places)
    sems = refs[-1]
    wanted, chunks = sems.shape
    out_refs = refs[chunks * count : -1]
    me = me_ref[0]
    each = wanted // len(out_refs)
    per_block = refs[0].shape[1] // PAGE
    waits = []
    for number in range(wanted):
        page = page_ref[number]
        rows = pl.ds(pl.multiple_of((page % per_block) * PAGE, PAGE), PAGE)
        start = 0
        for chunk in range(chunks):
            sources = refs[chunk * count : (chunk + 1) * count]
            cols = pl.ds(start, sources[0].shape[2])
            start += sources[0].shape[2]
            sem = sems.at[number, chunk]
            target = out_refs[number // each].at[number % each, :, cols]
            for piece, owners in enumerate(places):
                for at, owner in enumerate(owners):

                    @pl.when(page // per_block == owner(me))
                    def _(source=sources[piece].at[at, rows, :], target=target, sem=sem):
                        pltpu.make_async_copy(source, target, sem).start()

            waits.append(
                pltpu.make_async_copy(sources[0].at[0, pl.ds(0, PAGE), :], target, sem)
            )
    for copy in waits:
        copy.wait()


def pick_pages(chunks, places, me, pages, parts):
    cols = sum(pieces[0].shape[2] for pieces in chunks)
    wanted = pages.shape[0]
    smem = pl.BlockSpec(memory_space=pltpu.SMEM)
    anywhere = pl.BlockSpec(memory_space=pl.ANY)
    return pl.pallas_call(
        functools.partial(pages_kernel, places),
        in_specs=[smem, smem] + [anywhere] * (len(chunks) * len(places)),
        out_specs=[pl.BlockSpec(memory_space=pltpu.VMEM)] * parts,
        out_shape=[jax.ShapeDtypeStruct((wanted // parts, PAGE, cols), jnp.bfloat16)] * parts,
        scratch_shapes=[pltpu.SemaphoreType.DMA((wanted, len(chunks)))],
        compiler_params=pltpu.CompilerParams(vmem_limit_bytes=VMEM),
        cost_estimate=pl.CostEstimate(
            flops=0, bytes_accessed=4 * wanted * PAGE * cols, transcendentals=0
        ),
        name="pick_pages",
    )(me.reshape(1), pages, *[piece for pieces in chunks for piece in pieces])


def own_pages(page_table, start, count):
    page_total = page_table.shape[0]
    inverse = (
        jnp.zeros((page_total,), jnp.int32)
        .at[page_table]
        .set(jnp.arange(page_total, dtype=jnp.int32))
    )
    return lax.dynamic_slice_in_dim(inverse, start, count, 0)


def whole_heads(ring, hidden, modulation, weights, gains, positions, segment_ids, page_table):
    tok_rows = hidden.shape[0]
    me = lax.axis_index("row")
    full_rows = lax.all_gather(hidden, "col", axis=1, tiled=True)
    modulated = modulate(full_rows.astype(jnp.float32), modulation)
    width = full_rows.shape[1]
    raws = [
        jnp.dot(
            modulated,
            lax.all_gather(weight, "row", axis=0, tiled=True),
            preferred_element_type=jnp.float32,
        )
        for weight in weights
    ]
    squares = lax.psum(tuple(jnp.sum(raw * raw, axis=1) for raw in raws[:2]), "col")
    tables = rotary_lanes(positions, HEAD_DIM)
    query, key = [
        turn([raw], total[None], jnp.zeros_like(total)[None], gain, tables, width, False)[0]
        for raw, total, gain in zip(raws, squares, gains)
    ]
    value = raws[2].astype(jnp.bfloat16)
    keys_all = lax.all_gather(key, "row", axis=0)
    values_all = lax.all_gather(value, "row", axis=0)
    places = (tuple(lambda me, at=at: at for at in range(ring)),)
    none = jnp.zeros((), jnp.int32)
    query_seg = lax.dynamic_slice_in_dim(segment_ids, me * tok_rows, tok_rows, 0)
    attended = attend(
        query,
        [keys_all],
        [values_all],
        (places, places),
        none,
        key_bounds(query_seg, segment_ids),
        query_seg.astype(jnp.float32)[None, :],
        segment_ids.astype(jnp.float32).reshape(-1, 1, KEY_TILE),
    )
    count = tok_rows // PAGE
    pages = own_pages(page_table, me * count, count)
    picked = [pick_pages([[held]], places, none, pages, 1)[0] for held in (keys_all, values_all)]
    return attended, jnp.stack(picked)


def split_heads(ring, ranks, hidden, modulation, weights, gains, positions, segment_ids, page_table):
    tok_rows, shard = hidden.shape
    width = ranks * shard
    me = lax.axis_index("row")
    rank = lax.axis_index("col")
    top = ring // 2
    half = me // top
    cols = weights[0].shape[1] // 2
    hops = []
    bit = top // 2
    while bit:
        hops.append(bit)
        bit //= 2

    def swap(value, bit):
        return lax.ppermute(value, "row", [(i, i ^ bit) for i in range(ring)])

    def across(value, step):
        return lax.ppermute(value, "col", [(c, c ^ step) for c in range(ranks)])

    def spread(blocks, bits):
        for bit in bits:
            blocks.update({number | bit: swap(blocks[number], bit) for number in list(blocks)})
        return blocks

    def in_order(mine, other, axis):
        return jnp.where(
            half == 0,
            jnp.concatenate([mine, other], axis=axis),
            jnp.concatenate([other, mine], axis=axis),
        )

    hidden_all = lax.all_gather(hidden, "col", axis=0)
    w_query, w_key, w_value = weights
    own, send_pair, send_single = cut((w_key, w_value, w_query), half)
    first, rest_hops = hops[0], hops[1:]
    pair, single = swap(send_pair, top), swap(send_single, top)
    next_own = swap(own, first)
    own_blocks = spread({0: own}, rest_hops)

    rows = hidden.astype(jnp.float32)
    local_mean = jnp.mean(rows, axis=1)
    local_square = jnp.sum(jnp.square(rows - local_mean[:, None]), axis=1)
    stats = jnp.stack([local_mean, local_square])
    all_stats = [stats] + [across(stats, step) for step in range(1, ranks)]
    average = sum(part[0] for part in all_stats) / ranks
    variance = (
        sum(part[1] + shard * jnp.square(part[0] - average) for part in all_stats) / width
    )
    small = jnp.concatenate(
        [jnp.stack([average, lax.rsqrt(variance + epsilon)]), positions.astype(jnp.float32)]
    )
    small_other = swap(small, top)
    pair, single, next_own, own_blocks, small_other, hidden_late = lax.optimization_barrier(
        (pair, single, next_own, own_blocks, small_other, hidden)
    )

    next_pair = swap(pair, first)
    other_rows = swap(hidden_late, top)
    pair_blocks = spread({0: pair}, rest_hops)
    single_blocks = spread({0: single}, rest_hops)
    next_own_blocks = spread({0: next_own}, rest_hops)
    tables = rotary_lanes(jnp.concatenate([small[2:], small_other[2:]], axis=1), HEAD_DIM)
    q_gain, k_gain = [
        lax.dynamic_slice_in_dim(gain, half * cols, cols, 0) for gain in gains
    ]
    count = tok_rows // PAGE
    pages = jnp.concatenate(
        [own_pages(page_table, owner * count, count) for owner in (me ^ top, me)]
    )
    query_segs = [
        lax.dynamic_slice_in_dim(segment_ids, owner * tok_rows, tok_rows, 0)
        for owner in (me, me ^ top)
    ]
    bounds = [key_bounds(seg, segment_ids) for seg in query_segs]
    query_segs = [seg.astype(jnp.float32)[None, :] for seg in query_segs]
    key_seg = segment_ids.astype(jnp.float32).reshape(-1, 1, KEY_TILE)
    prepared = (tables, q_gain, k_gain, pages, query_segs, key_seg, bounds)
    moved = (next_pair, other_rows, pair_blocks, single_blocks, next_own_blocks)
    moved, prepared, hidden_all = lax.optimization_barrier((moved, prepared, hidden_all))
    next_pair, other_rows, pair_blocks, single_blocks, next_own_blocks = moved
    tables, q_gain, k_gain, pages, query_segs, key_seg, bounds = prepared

    next_single = swap(single_blocks[0], first)
    early = tok_rows * 5 // 12 // 16 * 16
    sent = [
        lax.dynamic_slice(hidden_all, (rank ^ step, early, 0), (1, tok_rows - early, shard))[0]
        for step in range(1, ranks)
    ]
    rest = [swap(part, top) for part in sent[:-1]]
    early_shards = [across(other_rows[:early], step) for step in range(1, ranks - 1)]
    next_single, next_pair, rest, early_shards = lax.optimization_barrier(
        (next_single, next_pair, rest, early_shards)
    )

    rest.append(swap(sent[-1], top))
    early_shards.append(across(other_rows[:early], ranks - 1))
    next_pair_blocks = spread({0: next_pair}, rest_hops)
    next_single_blocks = spread({0: next_single}, rest_hops)
    sources, spots = [], [None] * ring
    for number in own_blocks:
        for offset, whole in ((0, own_blocks), (first, next_own_blocks)):
            spots[number | offset] = tuple((len(sources), m) for m in range(3))
            sources.append(whole[number])
        for offset, pairs, singles in (
            (top, pair_blocks, single_blocks),
            (top | first, next_pair_blocks, next_single_blocks),
        ):
            at = len(sources)
            spots[number | offset] = ((at, 0), (at, 1), (at + 1, 0))
            sources.extend([pairs[number], singles[number]])
    place = jnp.stack([me, rank]).astype(jnp.int32)
    held = (tuple(spots), sources)

    own_parts = ((tok_rows, ((None, 0),), True),)
    mine = project(place, small[:2], modulation, own_parts, [hidden_all], *held)
    other_parts = (
        (early, ((None, 0),) * ranks, False),
        (tok_rows - early, ((None, early),) + ((None, 0),) * (ranks - 1), False),
    )
    shards = [other_rows] + early_shards + [other_rows] + rest
    other = project(place, small_other[:2], modulation, other_parts, shards, *held)

    values = {0: mine[2][None], top: other[2][None]}
    ahead = {number: swap(value, hops[0]) for number, value in values.items()}
    squares = jnp.stack([mine[3], other[3]])
    squares, ahead[0] = lax.optimization_barrier((squares, ahead[0]))
    squares = squares + swap(squares, top)[::-1]
    bit = 1
    while 2 * bit < ranks:
        squares = squares + across(squares, bit)
        bit *= 2
    squares_other = across(squares, bit)
    squares_other, ahead[top] = lax.optimization_barrier((squares_other, ahead[top]))
    (key,) = turn(
        [mine[0], other[0]], squares[:, 0], squares_other[:, 0], k_gain, tables, width, True
    )
    query = turn(
        [mine[1], other[1]], squares[:, 1], squares_other[:, 1], q_gain, tables, width, False
    )
    keys = {0: key, hops[0]: swap(key, hops[0])}
    ahead, _ = lax.optimization_barrier((ahead, key))
    values.update({number | hops[0]: value for number, value in ahead.items()})
    values = spread(values, hops[1:])
    value_places = tuple((lambda me, n=number: me ^ n,) for number in range(ring))
    value_pieces = [values[number] for number in range(ring)]
    values_picked = pick_pages([value_pieces], value_places, me, pages, 2)
    keys[hops[0]], query, values_picked = lax.optimization_barrier(
        (keys[hops[0]], query, values_picked)
    )
    keys = spread(keys, hops[1:])
    key_places = tuple(
        (lambda me, n=number: me ^ n, lambda me, n=number: me ^ n ^ top) for number in range(top)
    )
    key_pieces = [keys[number] for number in range(top)]
    keys_picked = pick_pages([key_pieces], key_places, me, pages, 2)
    query, keys_picked = lax.optimization_barrier((query, keys_picked))

    def attended(query, number):
        return attend(
            query[number],
            key_pieces,
            value_pieces,
            (key_places, value_places),
            me,
            bounds[number],
            query_segs[number],
            key_seg,
        )

    for_other = attended(query, 1)
    pages_other = [swap(picked[0], top) for picked in (keys_picked, values_picked)]
    query, pages_other, for_other = lax.optimization_barrier((query, pages_other, for_other))
    from_other = swap(for_other, top)
    for_me = attended(query, 0)
    page_store = [
        in_order(picked[1], received, -1)
        for picked, received in zip((keys_picked, values_picked), pages_other)
    ]
    return in_order(for_me, from_other, -1), jnp.stack(page_store)


def solution(mesh):
    ring, ranks = mesh.shape["row"], mesh.shape["col"]

    def body(
        hidden, modulation, w_query, w_key, w_value, q_gain, k_gain, positions, segment_ids, page_table
    ):
        rest = (
            hidden,
            modulation,
            (w_query, w_key, w_value),
            (q_gain, k_gain),
            positions,
            segment_ids,
            page_table,
        )
        heads = w_query.shape[1] // HEAD_DIM
        feats, shard = w_query.shape[0], hidden.shape[1]
        powers = ring & (ring - 1) == 0 and ranks & (ranks - 1) == 0
        if heads % 2 == 0 and ring % 2 == 0 and powers and feats % 128 == 0 and shard % feats == 0:
            return split_heads(ring, ranks, *rest)
        return whole_heads(ring, *rest)

    in_specs = (
        P("row", "col"),
        P(),
        P("row", "col"),
        P("row", "col"),
        P("row", "col"),
        P("col"),
        P("col"),
        P(None, "row"),
        P(),
        P(),
    )
    out_specs = (P("row", "col"), P(None, "row", None, "col"))
    return jax.shard_map(body, mesh=mesh, in_specs=in_specs, out_specs=out_specs, check_vma=False)
```

```python
import functools
import jax
import jax.numpy as jnp
from jax import lax
from jax.experimental import pallas as pl
from jax.experimental.pallas import tpu as pltpu
from jax.sharding import PartitionSpec as P

HEAD_DIM = 128
PAGE = 128
KEY_TILE = 512
VMEM = 60 * 1024 * 1024
LOG2E = 1.4426950408889634

epsilon = 1e-06


def rotary_table(positions, pair_count):
    frame_pairs = pair_count - 2 * (pair_count // 3)
    side_pairs = pair_count // 3
    column = jnp.arange(pair_count)
    frame_rate = 10000.0 ** (-column.astype(jnp.float32) / frame_pairs)
    height_rate = 10000.0 ** (-(column - frame_pairs).astype(jnp.float32) / side_pairs)
    width_rate = 10000.0 ** (-(column - frame_pairs - side_pairs).astype(jnp.float32) / side_pairs)
    coords = positions.astype(jnp.float32)
    angles = jnp.where(
        column < frame_pairs,
        coords[0][:, None] * frame_rate,
        jnp.where(
            column < frame_pairs + side_pairs,
            coords[1][:, None] * height_rate,
            coords[2][:, None] * width_rate,
        ),
    )
    return (jnp.cos(angles), jnp.sin(angles))


def rotary_lanes(positions, head_dim):
    cosine, sine_table = rotary_table(positions, head_dim // 2)
    own = jnp.repeat(cosine, 2, axis=1)
    sine = jnp.repeat(sine_table, 2, axis=1)
    even = (jnp.arange(head_dim) % 2 == 0)[None, :]
    return own, jnp.where(even, -sine, 0.0), jnp.where(even, 0.0, sine)


def modulate(activations, modulation):
    average = jnp.mean(activations, axis=1, keepdims=True)
    centred = activations - average
    variance = jnp.mean(centred * centred, axis=1, keepdims=True)
    normed = centred * lax.rsqrt(variance + epsilon)
    return (normed * (1.0 + modulation[1]) + modulation[0]).astype(jnp.bfloat16)


def cut_kernel(half_ref, *refs):
    weights, outs = refs[:3], refs[3:]
    cols = outs[0].shape[2]
    half = half_ref[0]
    for number, weight in enumerate(weights):
        send, at = (1, number) if number < 2 else (2, 0)
        outs[0][number] = weight[:, pl.ds(pl.multiple_of(half * cols, cols), cols)]
        outs[send][at] = weight[:, pl.ds(pl.multiple_of((1 - half) * cols, cols), cols)]


def cut(weights, half):
    rows, width = weights[0].shape
    cols = width // 2
    tile = 128
    sizes = (3, 2, 1)
    return pl.pallas_call(
        cut_kernel,
        grid_spec=pltpu.PrefetchScalarGridSpec(
            num_scalar_prefetch=1,
            grid=(rows // tile,),
            in_specs=[pl.BlockSpec((tile, width), lambda i, _: (i, 0))] * 3,
            out_specs=[pl.BlockSpec((size, tile, cols), lambda i, _: (0, i, 0)) for size in sizes],
        ),
        out_shape=[jax.ShapeDtypeStruct((size, rows, cols), jnp.bfloat16) for size in sizes],
        compiler_params=pltpu.CompilerParams(vmem_limit_bytes=VMEM),
        cost_estimate=pl.CostEstimate(
            flops=0, bytes_accessed=12 * rows * width, transcendentals=0
        ),
        name="cut",
    )(half.reshape(1), *weights)


def project_kernel(runs, spots, final, place_ref, stats_ref, modulation_ref, *refs):
    shard_count = sum(len(part[1]) for parts, _ in runs for part in parts)
    outs = 5 if final else 1
    shards, sources = refs[:shard_count], refs[shard_count : -5 - outs]
    outs, (raws, weights, ready, raw_sems, weight_sems) = refs[-5 - outs : -5], refs[-5:]
    if final:
        sources, partial_ref, totals = sources[:-1], sources[-1], outs[-1]
    else:
        totals = outs[0]
    me, rank = place_ref[0], place_ref[1]
    feats, cols = weights.shape[2:]
    rows = raws.shape[2]
    per_rank = shards[0].shape[-1] // feats
    used = [block for block, spot in enumerate(spots) if spot is not None]
    pairs = [(used[at], used[at + 1]) for at in range(0, len(used), 2)]
    copies = {}
    for block in used:
        owner = me ^ block
        span = pl.ds(pl.multiple_of((owner % per_rank) * feats, feats), feats)
        holder = owner // per_rank
        first = 0
        for run, (parts, blocks) in enumerate(runs):
            begin = 0
            copies[run, block] = []
            for number, (length, places, by_rank) in enumerate(parts):
                held = shards[first : first + len(places)]
                first += len(places)
                if block not in blocks:
                    continue
                target = raws.at[run, block, pl.ds(begin, length), :]
                begin += length
                sem = raw_sems.at[run, block, number]
                if by_rank:
                    copy = pltpu.make_async_copy(
                        held[0].at[holder, pl.ds(places[0], length), span], target, sem
                    )
                    copy.start()
                else:
                    for step, (ref, skip) in enumerate(zip(held, places)):
                        source = ref.at[pl.ds(skip, length), span]

                        @pl.when((holder ^ rank) == step)
                        def _(source=source, target=target, sem=sem):
                            pltpu.make_async_copy(source, target, sem).start()

                    copy = pltpu.make_async_copy(source, target, sem)
                copies[run, block].append(copy)
        copies[block] = [
            pltpu.make_async_copy(
                sources[source].at[at], weights.at[block, number], weight_sems.at[block, number]
            )
            for number, (source, at) in enumerate(spots[block])
        ]
        for copy in copies[block]:
            copy.start()

    def column(at):
        return jnp.transpose(jnp.broadcast_to(stats_ref[at : at + 1, :], (128, rows)))

    stats = [(column(2 * run), column(2 * run + 1)) for run in range(len(runs))]

    def prepare(number):
        for run, (_, blocks) in enumerate(runs):
            for at, block in enumerate(pairs[number]):
                if block not in blocks:
                    continue
                for copy in copies[run, block]:
                    copy.wait()
                span = pl.ds(pl.multiple_of((me ^ block) * feats, feats), feats)
                shift = modulation_ref[0:1, span]
                gain = 1.0 + modulation_ref[1:2, span]
                mean, scale = stats[run]
                for start in range(0, feats, 128):
                    lanes = slice(start, start + 128)
                    part = raws[run, block, :, lanes].astype(jnp.float32)
                    part = (part - mean) * scale * gain[:, lanes] + shift[:, lanes]
                    left = at * feats + start
                    ready[number % 2, run * rows : (run + 1) * rows, left : left + 128] = (
                        part.astype(jnp.bfloat16)
                    )

    prepare(0)
    for number, pair in enumerate(pairs):
        for block in pair:
            for copy in copies[block]:
                copy.wait()
        if number + 1 < len(pairs):
            prepare(number + 1)
        right = jnp.concatenate(
            [jnp.concatenate([weights[block, m] for block in pair], axis=0) for m in range(3)],
            axis=1,
        )
        active = sum(pair[0] in blocks for _, blocks in runs)
        part = jnp.dot(
            ready[number % 2, : active * rows], right, preferred_element_type=jnp.float32
        )
        sums = [part[run * rows : (run + 1) * rows] for run in range(active)]
        if number:
            sums[0] = sums[0] + totals[...]
        if number + 1 < len(pairs) or not final:
            totals[...] = sums[0]
    if not final:
        return
    sums[1] = sums[1] + partial_ref[...]
    key_ref, query_ref, value_refs, squares_ref = outs[0], outs[1], outs[2], outs[3]
    for run, total in enumerate(sums):
        at = len(sums) - 1 - run
        key, value, query = [total[:, m * cols : (m + 1) * cols] for m in range(3)]
        key_ref[at] = key
        query_ref[at] = query
        value_refs[at] = value.astype(value_refs.dtype)
        for kind, raw in enumerate((key, query)):
            summed = jnp.sum(raw * raw, axis=1, keepdims=True)
            summed = jnp.transpose(jnp.broadcast_to(summed, (rows, 128)))
            line = 2 * kind + at
            squares_ref[line : line + 1, :] = summed[:1]


def project(place, stats, modulation, runs, shards, spots, sources, partial):
    rows = sum(part[0] for part in runs[0][0])
    _, feats, cols = sources[0].shape
    count = len(spots)
    used = sum(spot is not None for spot in spots)
    final = partial is not None
    shape = (2, rows, cols)
    anywhere = pl.BlockSpec(memory_space=pl.ANY)
    whole = pl.BlockSpec(memory_space=pltpu.VMEM)
    product = jax.ShapeDtypeStruct((rows, 3 * cols), jnp.float32)
    out_shape = [product]
    if final:
        out_shape = [
            jax.ShapeDtypeStruct(shape, jnp.float32),
            jax.ShapeDtypeStruct(shape, jnp.float32),
            jax.ShapeDtypeStruct(shape, jnp.bfloat16),
            jax.ShapeDtypeStruct((4, rows), jnp.float32),
        ]
    scratch = [
        pltpu.VMEM((len(runs), count, rows, feats), jnp.bfloat16),
        pltpu.VMEM((count, 3, feats, cols), jnp.bfloat16),
        pltpu.VMEM((2, len(runs) * rows, 2 * feats), jnp.bfloat16),
        pltpu.SemaphoreType.DMA((len(runs), count, max(len(parts) for parts, _ in runs))),
        pltpu.SemaphoreType.DMA((count, 3)),
    ]
    if final:
        scratch = [pltpu.VMEM(product.shape, jnp.float32)] + scratch
    products = sum(len(blocks) for _, blocks in runs)
    return pl.pallas_call(
        functools.partial(project_kernel, runs, spots, final),
        in_specs=[pl.BlockSpec(memory_space=pltpu.SMEM), whole, whole]
        + [anywhere] * (len(shards) + len(sources))
        + [whole] * final,
        out_specs=[whole] * len(out_shape),
        out_shape=out_shape,
        scratch_shapes=scratch,
        compiler_params=pltpu.CompilerParams(vmem_limit_bytes=VMEM),
        cost_estimate=pl.CostEstimate(
            flops=6 * rows * products * feats * cols,
            bytes_accessed=2 * feats * (products * rows + 3 * used * cols) + 12 * rows * cols,
            transcendentals=0,
        ),
        name="project",
    )(place, stats, modulation, *shards, *sources, *([partial] if final else []))


def turn_kernel(
    width, mine_ref, other_ref, gain_ref, own_ref, upper_ref, lower_ref, raws_ref, *outs
):
    dim = own_ref.shape[1]
    count, rows = raws_ref.shape[:2]
    outs = outs if len(outs) == count else [outs[0].at[number] for number in range(count)]
    for number in range(count):
        raw_ref = raws_ref.at[number]
        at = slice(number, number + 1)
        scale = lax.rsqrt((mine_ref[at, :] + other_ref[at, :]) * (1.0 / width) + epsilon)
        scale = jnp.transpose(jnp.broadcast_to(scale, (128, rows)))
        lines = slice(number * rows, (number + 1) * rows)
        own, upper, lower = own_ref[lines, :], upper_ref[lines, :], lower_ref[lines, :]
        for head in range(raw_ref.shape[1] // dim):
            cols = slice(head * dim, (head + 1) * dim)
            normed = raw_ref[:, cols] * scale * gain_ref[:, cols]
            turned = (
                normed * own
                + pltpu.roll(normed, dim - 1, 1) * upper
                + pltpu.roll(normed, 1, 1) * lower
            )
            outs[number][:, cols] = turned.astype(jnp.bfloat16)


def turn(raws, mine, other, gain, tables, width, joined):
    count, rows, cols = raws.shape
    whole = pl.BlockSpec(memory_space=pltpu.VMEM)
    return pl.pallas_call(
        functools.partial(turn_kernel, width),
        in_specs=[whole] * 7,
        out_specs=[whole] * (1 if joined else count),
        out_shape=[jax.ShapeDtypeStruct((count, rows, cols), jnp.bfloat16)]
        if joined
        else [jax.ShapeDtypeStruct((rows, cols), jnp.bfloat16)] * count,
        compiler_params=pltpu.CompilerParams(vmem_limit_bytes=VMEM),
        cost_estimate=pl.CostEstimate(
            flops=8 * count * rows * cols, bytes_accessed=6 * count * rows * cols, transcendentals=0
        ),
        name="turn",
    )(mine, other, gain[None, :], *tables, raws)


def attend_kernel(places, me_ref, bounds_ref, q_ref, *refs):
    count = len(places[0]) + len(places[1])
    sources, (query_seg_ref, key_seg_ref) = refs[:count], refs[count : count + 2]
    out_ref, keys, values, highest, mixed, sems = refs[count + 2 :]
    me = me_ref[0]
    rows = sources[0].shape[1]
    copies = []
    for kind, held in enumerate((keys, values)):
        for piece, owners in enumerate(places[kind]):
            source = sources[kind * len(places[0]) + piece]
            for at, owner in enumerate(owners):
                where = pl.ds(pl.multiple_of(owner(me) * rows, rows), rows)
                copies.append(
                    pltpu.make_async_copy(
                        source.at[at], held.at[where, :], sems.at[kind, piece, at]
                    )
                )
    for copy in copies:
        copy.start()
    dim = HEAD_DIM
    heads = q_ref.shape[1] // dim
    factor = dim ** (-0.5) * LOG2E
    ones = jnp.ones((KEY_TILE, dim), jnp.bfloat16)
    highest[...] = jnp.full_like(highest, -1e29)
    mixed[...] = jnp.zeros_like(mixed)
    for copy in copies:
        copy.wait()

    query_seg = jnp.transpose(jnp.broadcast_to(query_seg_ref[...], (128, rows)))[:, :1]

    def step(block, carry):
        where = pl.ds(pl.multiple_of(block * KEY_TILE, KEY_TILE), KEY_TILE)
        same = query_seg == key_seg_ref[block]
        for head in range(heads):
            cols = slice(head * dim, (head + 1) * dim)
            scores = lax.dot_general(
                q_ref[:, cols],
                keys[where, cols],
                (((1,), (1,)), ((), ())),
                preferred_element_type=jnp.float32,
            )
            scores = jnp.where(same, scores * factor, -1e30)
            former = highest[head]
            newest = jnp.maximum(former, jnp.max(scores, axis=1, keepdims=True))
            highest[head] = newest
            weights = jnp.exp2(scores - newest[:, :1]).astype(jnp.bfloat16)
            right = jnp.concatenate([values[where, cols], ones], axis=1)
            part = jnp.dot(weights, right, preferred_element_type=jnp.float32)
            shrink = jnp.exp2(former - newest)
            mixed[head, :, :dim] = mixed[head, :, :dim] * shrink + part[:, :dim]
            mixed[head, :, dim:] = mixed[head, :, dim:] * shrink + part[:, dim:]
        return carry

    lax.fori_loop(bounds_ref[0], bounds_ref[1], step, 0)
    for head in range(heads):
        out_ref[:, head * dim : (head + 1) * dim] = (
            mixed[head, :, :dim] / mixed[head, :, dim:]
        ).astype(out_ref.dtype)


def key_bounds(query_seg, segment_ids):
    low = jnp.sum(segment_ids < query_seg[0], dtype=jnp.int32)
    high = jnp.sum(segment_ids <= query_seg[-1], dtype=jnp.int32)
    return jnp.stack([low // KEY_TILE, (high + KEY_TILE - 1) // KEY_TILE])


def attend(query, key_pieces, value_pieces, places, me, bounds, query_seg, key_seg):
    rows, cols = query.shape
    tokens = key_seg.shape[0] * KEY_TILE
    dim = HEAD_DIM
    heads = cols // dim
    smem = pl.BlockSpec(memory_space=pltpu.SMEM)
    whole = pl.BlockSpec(memory_space=pltpu.VMEM)
    anywhere = pl.BlockSpec(memory_space=pl.ANY)
    return pl.pallas_call(
        functools.partial(attend_kernel, places),
        in_specs=[smem, smem, whole]
        + [anywhere] * (len(places[0]) + len(places[1]))
        + [whole, whole],
        out_specs=whole,
        scratch_shapes=[
            pltpu.VMEM((tokens, cols), jnp.bfloat16),
            pltpu.VMEM((tokens, cols), jnp.bfloat16),
            pltpu.VMEM((heads, rows, dim), jnp.float32),
            pltpu.VMEM((heads, rows, 2 * dim), jnp.float32),
            pltpu.SemaphoreType.DMA(
                (2, max(map(len, places)), max(len(o) for part in places for o in part))
            ),
        ],
        out_shape=jax.ShapeDtypeStruct((rows, cols), jnp.bfloat16),
        compiler_params=pltpu.CompilerParams(vmem_limit_bytes=VMEM),
        cost_estimate=pl.CostEstimate(
            flops=2 * rows * tokens * cols,
            bytes_accessed=4 * tokens * cols + 4 * rows * cols,
            transcendentals=rows * tokens * heads // 2,
        ),
        name="attend",
    )(me.reshape(1), bounds, query, *key_pieces, *value_pieces, query_seg, key_seg)


def pages_kernel(places, me_ref, page_ref, *refs):
    count = len(places)
    sems = refs[-1]
    wanted, chunks = sems.shape
    out_refs = refs[chunks * count : -1]
    me = me_ref[0]
    each = wanted // len(out_refs)
    per_block = refs[0].shape[1] // PAGE
    waits = []
    for number in range(wanted):
        page = page_ref[number]
        rows = pl.ds(pl.multiple_of((page % per_block) * PAGE, PAGE), PAGE)
        start = 0
        for chunk in range(chunks):
            sources = refs[chunk * count : (chunk + 1) * count]
            cols = pl.ds(start, sources[0].shape[2])
            start += sources[0].shape[2]
            sem = sems.at[number, chunk]
            target = out_refs[number // each].at[number % each, :, cols]
            for piece, owners in enumerate(places):
                for at, owner in enumerate(owners):

                    @pl.when(page // per_block == owner(me))
                    def _(source=sources[piece].at[at, rows, :], target=target, sem=sem):
                        pltpu.make_async_copy(source, target, sem).start()

            waits.append(
                pltpu.make_async_copy(sources[0].at[0, pl.ds(0, PAGE), :], target, sem)
            )
    for copy in waits:
        copy.wait()


def pick_pages(chunks, places, me, pages, parts):
    cols = sum(pieces[0].shape[2] for pieces in chunks)
    wanted = pages.shape[0]
    smem = pl.BlockSpec(memory_space=pltpu.SMEM)
    anywhere = pl.BlockSpec(memory_space=pl.ANY)
    return pl.pallas_call(
        functools.partial(pages_kernel, places),
        in_specs=[smem, smem] + [anywhere] * (len(chunks) * len(places)),
        out_specs=[pl.BlockSpec(memory_space=pltpu.VMEM)] * parts,
        out_shape=[jax.ShapeDtypeStruct((wanted // parts, PAGE, cols), jnp.bfloat16)] * parts,
        scratch_shapes=[pltpu.SemaphoreType.DMA((wanted, len(chunks)))],
        compiler_params=pltpu.CompilerParams(vmem_limit_bytes=VMEM),
        cost_estimate=pl.CostEstimate(
            flops=0, bytes_accessed=4 * wanted * PAGE * cols, transcendentals=0
        ),
        name="pick_pages",
    )(me.reshape(1), pages, *[piece for pieces in chunks for piece in pieces])


def own_pages(page_table, start, count):
    page_total = page_table.shape[0]
    inverse = (
        jnp.zeros((page_total,), jnp.int32)
        .at[page_table]
        .set(jnp.arange(page_total, dtype=jnp.int32))
    )
    return lax.dynamic_slice_in_dim(inverse, start, count, 0)


def whole_heads(ring, hidden, modulation, weights, gains, positions, segment_ids, page_table):
    tok_rows = hidden.shape[0]
    me = lax.axis_index("row")
    full_rows = lax.all_gather(hidden, "col", axis=1, tiled=True)
    modulated = modulate(full_rows.astype(jnp.float32), modulation)
    width = full_rows.shape[1]
    raws = [
        jnp.dot(
            modulated,
            lax.all_gather(weight, "row", axis=0, tiled=True),
            preferred_element_type=jnp.float32,
        )
        for weight in weights
    ]
    squares = lax.psum(tuple(jnp.sum(raw * raw, axis=1) for raw in raws[:2]), "col")
    tables = rotary_lanes(positions, HEAD_DIM)
    query, key = [
        turn(raw[None], total[None], jnp.zeros_like(total)[None], gain, tables, width, False)[0]
        for raw, total, gain in zip(raws, squares, gains)
    ]
    value = raws[2].astype(jnp.bfloat16)
    keys_all = lax.all_gather(key, "row", axis=0)
    values_all = lax.all_gather(value, "row", axis=0)
    places = (tuple(lambda me, at=at: at for at in range(ring)),)
    none = jnp.zeros((), jnp.int32)
    query_seg = lax.dynamic_slice_in_dim(segment_ids, me * tok_rows, tok_rows, 0)
    attended = attend(
        query,
        [keys_all],
        [values_all],
        (places, places),
        none,
        key_bounds(query_seg, segment_ids),
        query_seg.astype(jnp.float32)[None, :],
        segment_ids.astype(jnp.float32).reshape(-1, 1, KEY_TILE),
    )
    count = tok_rows // PAGE
    pages = own_pages(page_table, me * count, count)
    picked = [pick_pages([[held]], places, none, pages, 1)[0] for held in (keys_all, values_all)]
    return attended, jnp.stack(picked)


def split_heads(ring, ranks, hidden, modulation, weights, gains, positions, segment_ids, page_table):
    tok_rows, shard = hidden.shape
    width = ranks * shard
    me = lax.axis_index("row")
    rank = lax.axis_index("col")
    top = ring // 2
    half = me // top
    cols = weights[0].shape[1] // 2
    hops = []
    bit = top // 2
    while bit:
        hops.append(bit)
        bit //= 2

    def swap(value, bit):
        return lax.ppermute(value, "row", [(i, i ^ bit) for i in range(ring)])

    def across(value, step):
        return lax.ppermute(value, "col", [(c, c ^ step) for c in range(ranks)])

    def spread(blocks, bits):
        for bit in bits:
            blocks.update({number | bit: swap(blocks[number], bit) for number in list(blocks)})
        return blocks

    def in_order(mine, other, axis):
        return jnp.where(
            half == 0,
            jnp.concatenate([mine, other], axis=axis),
            jnp.concatenate([other, mine], axis=axis),
        )

    hidden_all = lax.all_gather(hidden, "col", axis=0)
    w_query, w_key, w_value = weights
    own, send_pair, send_single = cut((w_key, w_value, w_query), half)
    first, rest_hops = hops[0], hops[1:]
    pair, single = swap(send_pair, top), swap(send_single, top)
    next_own = swap(own, first)
    own_blocks = spread({0: own}, rest_hops)

    rows = hidden.astype(jnp.float32)
    local_mean = jnp.mean(rows, axis=1)
    local_square = jnp.sum(jnp.square(rows - local_mean[:, None]), axis=1)
    stats = jnp.stack([local_mean, local_square])
    all_stats = [stats] + [across(stats, step) for step in range(1, ranks)]
    average = sum(part[0] for part in all_stats) / ranks
    variance = (
        sum(part[1] + shard * jnp.square(part[0] - average) for part in all_stats) / width
    )
    small = jnp.concatenate(
        [jnp.stack([average, lax.rsqrt(variance + epsilon)]), positions.astype(jnp.float32)]
    )
    pair, single, next_own, own_blocks, small, hidden_late = lax.optimization_barrier(
        (pair, single, next_own, own_blocks, small, hidden)
    )

    next_single = swap(single, first)
    small_other = swap(small, top)
    other_rows = swap(hidden_late, top)
    pair_blocks = spread({0: pair}, rest_hops)
    single_blocks = spread({0: single}, rest_hops)
    next_own_blocks = spread({0: next_own}, rest_hops)
    tables = rotary_lanes(jnp.concatenate([small[2:], small_other[2:]], axis=1), HEAD_DIM)
    q_gain, k_gain = [
        lax.dynamic_slice_in_dim(gain, half * cols, cols, 0) for gain in gains
    ]
    count = tok_rows // PAGE
    pages = jnp.concatenate(
        [own_pages(page_table, owner * count, count) for owner in (me ^ top, me)]
    )
    query_segs = [
        lax.dynamic_slice_in_dim(segment_ids, owner * tok_rows, tok_rows, 0)
        for owner in (me, me ^ top)
    ]
    bounds = [key_bounds(seg, segment_ids) for seg in query_segs]
    query_segs = [seg.astype(jnp.float32)[None, :] for seg in query_segs]
    key_seg = segment_ids.astype(jnp.float32).reshape(-1, 1, KEY_TILE)
    prepared = (tables, q_gain, k_gain, pages, query_segs, key_seg, bounds)
    moved = (next_single, other_rows, pair_blocks, single_blocks, next_own_blocks)
    moved, prepared, hidden_all = lax.optimization_barrier((moved, prepared, hidden_all))
    next_single, other_rows, pair_blocks, single_blocks, next_own_blocks = moved
    tables, q_gain, k_gain, pages, query_segs, key_seg, bounds = prepared

    next_pair = swap(pair_blocks[0], first)
    early = tok_rows * 5 // 12 // 16 * 16
    early_shards = [across(other_rows[:early], step) for step in range(1, ranks)]
    rest = swap(
        jnp.concatenate(
            [
                lax.dynamic_slice(
                    hidden_all, (rank ^ step, early, 0), (1, tok_rows - early, shard)
                )
                for step in range(1, ranks)
            ]
        ).reshape(-1, shard),
        top,
    )
    sources, spots = [], [None] * ring
    for number in own_blocks:
        for offset, whole in ((0, own_blocks), (first, next_own_blocks)):
            spots[number | offset] = tuple((len(sources), m) for m in range(3))
            sources.append(whole[number])
        at = len(sources)
        spots[number | top] = ((at, 0), (at, 1), (at + 1, 0))
        sources.extend([pair_blocks[number], single_blocks[number]])
    place = jnp.stack([me, rank]).astype(jnp.int32)
    here = tuple(number for number in range(ring) if spots[number] is not None)
    late = tuple(number for number in range(ring) if spots[number] is None)
    own_parts = ((tok_rows, (0,), True),)
    (partial,) = project(
        place,
        small[:2],
        modulation,
        ((own_parts, here),),
        [hidden_all],
        tuple(spots),
        list(sources),
        None,
    )
    next_pair, next_single, rest, early_shards, partial = lax.optimization_barrier(
        (next_pair, next_single, rest, early_shards, partial)
    )

    next_pair_blocks = spread({0: next_pair}, rest_hops)
    next_single_blocks = spread({0: next_single}, rest_hops)
    for number in own_blocks:
        at = len(sources)
        spots[number | top | first] = ((at, 0), (at, 1), (at + 1, 0))
        sources.extend([next_pair_blocks[number], next_single_blocks[number]])
    other_parts = (
        (early, (0,) * ranks, False),
        (
            tok_rows - early,
            (early,) + tuple(step * (tok_rows - early) for step in range(ranks - 1)),
            False,
        ),
    )
    key_raw, query_raw, value, squares = project(
        place,
        jnp.concatenate([small_other[:2], small[:2]]),
        modulation,
        ((other_parts, tuple(range(ring))), (own_parts, late)),
        [other_rows] + early_shards + [other_rows] + [rest] * (ranks - 1) + [hidden_all],
        tuple(spots),
        sources,
        partial,
    )

    values = {0: value[:1], top: value[1:]}
    ahead = {number: swap(part, first) for number, part in values.items()}
    squares = squares.reshape(2, 2, tok_rows)
    squares = squares + swap(squares, top)[:, ::-1]
    bit = 1
    while 2 * bit < ranks:
        squares = squares + across(squares, bit)
        bit *= 2
    squares_other = across(squares, bit)
    squares_other, ahead[0] = lax.optimization_barrier((squares_other, ahead[0]))
    (key,) = turn(key_raw, squares[0], squares_other[0], k_gain, tables, width, True)
    query = turn(query_raw, squares[1], squares_other[1], q_gain, tables, width, False)
    keys = {0: key, first: swap(key, first)}
    ahead, _ = lax.optimization_barrier((ahead, key))
    values.update({number | hops[0]: value for number, value in ahead.items()})
    values = spread(values, hops[1:])
    value_places = tuple((lambda me, n=number: me ^ n,) for number in range(ring))
    value_pieces = [values[number] for number in range(ring)]
    values_picked = pick_pages([value_pieces], value_places, me, pages, 2)
    keys[hops[0]], query, values_picked = lax.optimization_barrier(
        (keys[hops[0]], query, values_picked)
    )
    keys = spread(keys, hops[1:])
    key_places = tuple(
        (lambda me, n=number: me ^ n, lambda me, n=number: me ^ n ^ top) for number in range(top)
    )
    key_pieces = [keys[number] for number in range(top)]
    keys_picked = pick_pages([key_pieces], key_places, me, pages, 2)
    query, keys_picked = lax.optimization_barrier((query, keys_picked))

    def attended(query, number):
        return attend(
            query[number],
            key_pieces,
            value_pieces,
            (key_places, value_places),
            me,
            bounds[number],
            query_segs[number],
            key_seg,
        )

    for_other = attended(query, 1)
    pages_other = [swap(picked[0], top) for picked in (keys_picked, values_picked)]
    query, pages_other, for_other = lax.optimization_barrier((query, pages_other, for_other))
    from_other = swap(for_other, top)
    for_me = attended(query, 0)
    page_store = [
        in_order(picked[1], received, -1)
        for picked, received in zip((keys_picked, values_picked), pages_other)
    ]
    return in_order(for_me, from_other, -1), jnp.stack(page_store)


def solution(mesh):
    ring, ranks = mesh.shape["row"], mesh.shape["col"]

    def body(
        hidden, modulation, w_query, w_key, w_value, q_gain, k_gain, positions, segment_ids, page_table
    ):
        rest = (
            hidden,
            modulation,
            (w_query, w_key, w_value),
            (q_gain, k_gain),
            positions,
            segment_ids,
            page_table,
        )
        heads = w_query.shape[1] // HEAD_DIM
        feats, shard = w_query.shape[0], hidden.shape[1]
        powers = ring & (ring - 1) == 0 and ranks & (ranks - 1) == 0
        if heads % 2 == 0 and ring >= 8 and powers and feats % 128 == 0 and shard % feats == 0:
            return split_heads(ring, ranks, *rest)
        return whole_heads(ring, *rest)

    in_specs = (
        P("row", "col"),
        P(),
        P("row", "col"),
        P("row", "col"),
        P("row", "col"),
        P("col"),
        P("col"),
        P(None, "row"),
        P(),
        P(),
    )
    out_specs = (P("row", "col"), P(None, "row", None, "col"))
    return jax.shard_map(body, mesh=mesh, in_specs=in_specs, out_specs=out_specs, check_vma=False)
```

```python
import functools
import jax
import jax.numpy as jnp
from jax import lax
from jax.experimental import pallas as pl
from jax.experimental.pallas import tpu as pltpu
from jax.sharding import PartitionSpec as P

HEAD_DIM = 128
PAGE = 128
KEY_TILE = 512
VMEM = 60 * 1024 * 1024
LOG2E = 1.4426950408889634

epsilon = 1e-06


def rotary_table(positions, pair_count):
    frame_pairs = pair_count - 2 * (pair_count // 3)
    side_pairs = pair_count // 3
    column = jnp.arange(pair_count)
    frame_rate = 10000.0 ** (-column.astype(jnp.float32) / frame_pairs)
    height_rate = 10000.0 ** (-(column - frame_pairs).astype(jnp.float32) / side_pairs)
    width_rate = 10000.0 ** (-(column - frame_pairs - side_pairs).astype(jnp.float32) / side_pairs)
    coords = positions.astype(jnp.float32)
    angles = jnp.where(
        column < frame_pairs,
        coords[0][:, None] * frame_rate,
        jnp.where(
            column < frame_pairs + side_pairs,
            coords[1][:, None] * height_rate,
            coords[2][:, None] * width_rate,
        ),
    )
    return (jnp.cos(angles), jnp.sin(angles))


def rotary_lanes(positions, head_dim):
    cosine, sine_table = rotary_table(positions, head_dim // 2)
    own = jnp.repeat(cosine, 2, axis=1)
    sine = jnp.repeat(sine_table, 2, axis=1)
    even = (jnp.arange(head_dim) % 2 == 0)[None, :]
    return own, jnp.where(even, -sine, 0.0), jnp.where(even, 0.0, sine)


def modulate(activations, modulation):
    average = jnp.mean(activations, axis=1, keepdims=True)
    centred = activations - average
    variance = jnp.mean(centred * centred, axis=1, keepdims=True)
    normed = centred * lax.rsqrt(variance + epsilon)
    return (normed * (1.0 + modulation[1]) + modulation[0]).astype(jnp.bfloat16)


def cut_kernel(half_ref, *refs):
    weights, outs, sems = refs[:3], refs[3:6], refs[6]
    cols = outs[0].shape[2]
    half = half_ref[0]
    copies = []
    for number, weight in enumerate(weights):
        send, at = (1, number) if number < 2 else (2, 0)
        for which, target in ((half, outs[0].at[number]), (1 - half, outs[send].at[at])):
            span = pl.ds(pl.multiple_of(which * cols, cols), cols)
            copies.append(
                pltpu.make_async_copy(
                    weight.at[:, span], target, sems.at[number, len(copies) % 2]
                )
            )
            copies[-1].start()
    for copy in copies:
        copy.wait()


def cut(weights, half):
    rows, width = weights[0].shape
    cols = width // 2
    whole = pl.BlockSpec(memory_space=pltpu.VMEM)
    return pl.pallas_call(
        cut_kernel,
        in_specs=[pl.BlockSpec(memory_space=pltpu.SMEM)] + [pl.BlockSpec(memory_space=pl.ANY)] * 3,
        out_specs=[whole] * 3,
        out_shape=[jax.ShapeDtypeStruct((size, rows, cols), jnp.bfloat16) for size in (3, 2, 1)],
        scratch_shapes=[pltpu.SemaphoreType.DMA((3, 2))],
        compiler_params=pltpu.CompilerParams(vmem_limit_bytes=VMEM),
        cost_estimate=pl.CostEstimate(
            flops=0, bytes_accessed=12 * rows * width, transcendentals=0
        ),
        name="cut",
    )(half.reshape(1), *weights)


def turned(values, gain, tables, at):
    dim = tables[0].shape[1]
    cols = slice(at * dim, (at + 1) * dim)
    own, upper, lower = tables
    part = values[:, cols] * gain[:, cols]
    return part * own + pltpu.roll(part, dim - 1, 1) * upper + pltpu.roll(part, 1, 1) * lower


def project_kernel(parts, blocks, spots, first, final, place_ref, stats_ref, modulation_ref, *refs):
    shard_count = sum(len(part[1]) for part in parts)
    out_count = 3 if final else 1
    shards, rest = refs[:shard_count], refs[shard_count:]
    total, raws, weights, ready, raw_sems, weight_sems = rest[-6:]
    outs, sources = rest[-6 - out_count : -6], rest[: -6 - out_count]
    if final:
        sources, (gain_ref, own_ref, upper_ref, lower_ref) = sources[:-4], sources[-4:]
    if not first:
        sources, partial_ref = sources[:-1], sources[-1]
    me, rank = place_ref[0], place_ref[1]
    feats, cols = weights.shape[2:]
    rows = raws.shape[1]
    per_rank = shards[0].shape[-1] // feats
    copies = {}
    for slot, block in enumerate(blocks):
        owner = me ^ block
        span = pl.ds(pl.multiple_of((owner % per_rank) * feats, feats), feats)
        holder = owner // per_rank
        mine, begin, at = [], 0, 0
        for number, (length, places, by_rank) in enumerate(parts):
            held = shards[at : at + len(places)]
            at += len(places)
            target = raws.at[slot, pl.ds(begin, length), :]
            begin += length
            sem = raw_sems.at[slot, number]
            if by_rank:
                copy = pltpu.make_async_copy(
                    held[0].at[holder, pl.ds(places[0], length), span], target, sem
                )
                copy.start()
            else:
                for step, (ref, skip) in enumerate(zip(held, places)):
                    source = ref.at[pl.ds(skip, length), span]

                    @pl.when((holder ^ rank) == step)
                    def _(source=source, target=target, sem=sem):
                        pltpu.make_async_copy(source, target, sem).start()

                copy = pltpu.make_async_copy(source, target, sem)
            mine.append(copy)
        matrices = [
            pltpu.make_async_copy(
                sources[source].at[place], weights.at[slot, number], weight_sems.at[slot, number]
            )
            for number, (source, place) in enumerate(spots[block])
        ]
        for copy in matrices:
            copy.start()
        copies[slot] = (mine, matrices)

    def column(at):
        return jnp.transpose(jnp.broadcast_to(stats_ref[at : at + 1, :], (128, rows)))

    mean, scale = column(0), column(1)

    def prepare(first_slot):
        for slot in (first_slot, first_slot + 1):
            for copy in copies[slot][0]:
                copy.wait()
            span = pl.ds(pl.multiple_of((me ^ blocks[slot]) * feats, feats), feats)
            shift = modulation_ref[0:1, span]
            gain = 1.0 + modulation_ref[1:2, span]
            left = (slot - first_slot) * feats
            for start in range(0, feats, 128):
                lanes = slice(start, start + 128)
                part = raws[slot, :, lanes].astype(jnp.float32)
                part = (part - mean) * scale * gain[:, lanes] + shift[:, lanes]
                ready[first_slot // 2 % 2, :, left + start : left + start + 128] = part.astype(
                    jnp.bfloat16
                )

    prepare(0)
    for slot in range(0, len(blocks), 2):
        for copy in copies[slot][1] + copies[slot + 1][1]:
            copy.wait()
        if slot + 2 < len(blocks):
            prepare(slot + 2)
        right = jnp.concatenate(
            [
                jnp.concatenate([weights[slot, m], weights[slot + 1, m]], axis=0)
                for m in range(3)
            ],
            axis=1,
        )
        part = jnp.dot(ready[slot // 2 % 2], right, preferred_element_type=jnp.float32)
        if slot:
            part = part + total[...]
        elif not first:
            part = part + partial_ref[...]
        if slot + 2 < len(blocks):
            total[...] = part
    if not final:
        outs[0][...] = part
        return
    key_value_ref, query_ref, squares_ref = outs
    key, value, query = [part[:, m * cols : (m + 1) * cols] for m in range(3)]
    query_ref[...] = query
    key_value_ref[1] = value.astype(jnp.bfloat16)
    tables = (own_ref[...], upper_ref[...], lower_ref[...])
    for head in range(cols // HEAD_DIM):
        lanes = slice(head * HEAD_DIM, (head + 1) * HEAD_DIM)
        key_value_ref[0, :, lanes] = turned(key, gain_ref, tables, head).astype(jnp.bfloat16)
    for kind, raw in enumerate((key, query)):
        summed = jnp.sum(raw * raw, axis=1, keepdims=True)
        summed = jnp.transpose(jnp.broadcast_to(summed, (rows, 128)))
        squares_ref[kind : kind + 1, :] = summed[:1]


def project(place, stats, modulation, parts, blocks, shards, spots, sources, partial, finish):
    rows = sum(part[0] for part in parts)
    _, feats, cols = sources[0].shape
    count = len(blocks)
    anywhere = pl.BlockSpec(memory_space=pl.ANY)
    whole = pl.BlockSpec(memory_space=pltpu.VMEM)
    out_shape = [jax.ShapeDtypeStruct((rows, 3 * cols), jnp.float32)]
    extra = [] if partial is None else [partial]
    if finish is not None:
        extra.extend(finish)
        out_shape = [
            jax.ShapeDtypeStruct((2, rows, cols), jnp.bfloat16),
            jax.ShapeDtypeStruct((rows, cols), jnp.float32),
            jax.ShapeDtypeStruct((2, rows), jnp.float32),
        ]
    return pl.pallas_call(
        functools.partial(
            project_kernel, parts, blocks, spots, partial is None, finish is not None
        ),
        in_specs=[pl.BlockSpec(memory_space=pltpu.SMEM), whole, whole]
        + [anywhere] * (len(shards) + len(sources))
        + [whole] * len(extra),
        out_specs=[whole] * len(out_shape),
        out_shape=out_shape,
        scratch_shapes=[
            pltpu.VMEM((rows, 3 * cols), jnp.float32),
            pltpu.VMEM((count, rows, feats), jnp.bfloat16),
            pltpu.VMEM((count, 3, feats, cols), jnp.bfloat16),
            pltpu.VMEM((2, rows, 2 * feats), jnp.bfloat16),
            pltpu.SemaphoreType.DMA((count, len(parts))),
            pltpu.SemaphoreType.DMA((count, 3)),
        ],
        compiler_params=pltpu.CompilerParams(vmem_limit_bytes=VMEM),
        cost_estimate=pl.CostEstimate(
            flops=6 * rows * count * feats * cols,
            bytes_accessed=2 * count * feats * (rows + 3 * cols) + 12 * rows * cols,
            transcendentals=0,
        ),
        name="project",
    )(place, stats, modulation, *shards, *sources, *extra)


def turn_kernel(count, width, squares_ref, gain_ref, own_ref, upper_ref, lower_ref, *refs):
    for number in range(count):
        raw_ref, out_ref = refs[number], refs[count + number]
        rows, cols = raw_ref.shape
        scale = lax.rsqrt(squares_ref[number : number + 1, :] * (1.0 / width) + epsilon)
        raw = raw_ref[...] * jnp.transpose(jnp.broadcast_to(scale, (128, rows)))[:, :1]
        lines = slice(number * rows, (number + 1) * rows)
        tables = (own_ref[lines, :], upper_ref[lines, :], lower_ref[lines, :])
        for head in range(cols // HEAD_DIM):
            out_ref[:, head * HEAD_DIM : (head + 1) * HEAD_DIM] = turned(
                raw, gain_ref, tables, head
            ).astype(jnp.bfloat16)


def turn(raws, squares, gain, tables, width):
    count = len(raws)
    rows, cols = raws[0].shape
    whole = pl.BlockSpec(memory_space=pltpu.VMEM)
    return pl.pallas_call(
        functools.partial(turn_kernel, count, width),
        in_specs=[whole] * (5 + count),
        out_specs=[whole] * count,
        out_shape=[jax.ShapeDtypeStruct((rows, cols), jnp.bfloat16)] * count,
        compiler_params=pltpu.CompilerParams(vmem_limit_bytes=VMEM),
        cost_estimate=pl.CostEstimate(
            flops=8 * count * rows * cols, bytes_accessed=6 * count * rows * cols, transcendentals=0
        ),
        name="turn",
    )(squares, gain, *tables, *raws)


def attend_kernel(count, me_ref, bounds_ref, q_ref, *refs):
    pieces, (query_seg_ref, key_seg_ref, factor_ref) = refs[:count], refs[count : count + 3]
    out_ref, keys, values, highest, mixed, sems = refs[count + 3 :]
    me = me_ref[0]
    rows = pieces[0].shape[1]
    copies = []
    for number, piece in enumerate(pieces):
        where = pl.ds(pl.multiple_of((me ^ number) * rows, rows), rows)
        for kind, held in enumerate((keys, values)):
            copies.append(
                pltpu.make_async_copy(piece.at[kind], held.at[where, :], sems.at[kind, number])
            )
    for copy in copies:
        copy.start()
    dim = HEAD_DIM
    heads = q_ref.shape[1] // dim
    ones = jnp.ones((KEY_TILE, dim), jnp.bfloat16)
    highest[...] = jnp.full_like(highest, -1e29)
    mixed[...] = jnp.zeros_like(mixed)
    for copy in copies:
        copy.wait()

    query_seg = jnp.transpose(jnp.broadcast_to(query_seg_ref[...], (128, rows)))[:, :1]

    def step(block, carry):
        where = pl.ds(pl.multiple_of(block * KEY_TILE, KEY_TILE), KEY_TILE)
        same = query_seg == key_seg_ref[block]
        factor = factor_ref[block]
        for head in range(heads):
            cols = slice(head * dim, (head + 1) * dim)
            scores = lax.dot_general(
                q_ref[:, cols],
                keys[where, cols],
                (((1,), (1,)), ((), ())),
                preferred_element_type=jnp.float32,
            )
            scores = jnp.where(same, scores * factor, -1e30)
            former = highest[head]
            newest = jnp.maximum(former, jnp.max(scores, axis=1, keepdims=True))
            highest[head] = newest
            weights = jnp.exp2(scores - newest[:, :1]).astype(jnp.bfloat16)
            right = jnp.concatenate([values[where, cols], ones], axis=1)
            part = jnp.dot(weights, right, preferred_element_type=jnp.float32)
            shrink = jnp.exp2(former - newest)
            mixed[head, :, :dim] = mixed[head, :, :dim] * shrink + part[:, :dim]
            mixed[head, :, dim:] = mixed[head, :, dim:] * shrink + part[:, dim:]
        return carry

    lax.fori_loop(bounds_ref[0], bounds_ref[1], step, 0)
    for head in range(heads):
        out_ref[:, head * dim : (head + 1) * dim] = (
            mixed[head, :, :dim] / mixed[head, :, dim:]
        ).astype(out_ref.dtype)


def key_bounds(query_seg, segment_ids):
    low = jnp.sum(segment_ids < query_seg[0], dtype=jnp.int32)
    high = jnp.sum(segment_ids <= query_seg[-1], dtype=jnp.int32)
    return jnp.stack([low // KEY_TILE, (high + KEY_TILE - 1) // KEY_TILE])


def attend(query, pieces, me, bounds, query_seg, key_seg, factor):
    rows, cols = query.shape
    count = len(pieces)
    tokens = key_seg.shape[0] * KEY_TILE
    dim = HEAD_DIM
    heads = cols // dim
    smem = pl.BlockSpec(memory_space=pltpu.SMEM)
    whole = pl.BlockSpec(memory_space=pltpu.VMEM)
    return pl.pallas_call(
        functools.partial(attend_kernel, count),
        in_specs=[smem, smem, whole] + [pl.BlockSpec(memory_space=pl.ANY)] * count + [whole] * 3,
        out_specs=whole,
        scratch_shapes=[
            pltpu.VMEM((tokens, cols), jnp.bfloat16),
            pltpu.VMEM((tokens, cols), jnp.bfloat16),
            pltpu.VMEM((heads, rows, dim), jnp.float32),
            pltpu.VMEM((heads, rows, 2 * dim), jnp.float32),
            pltpu.SemaphoreType.DMA((2, count)),
        ],
        out_shape=jax.ShapeDtypeStruct((rows, cols), jnp.bfloat16),
        compiler_params=pltpu.CompilerParams(vmem_limit_bytes=VMEM),
        cost_estimate=pl.CostEstimate(
            flops=2 * rows * tokens * cols,
            bytes_accessed=4 * tokens * cols + 4 * rows * cols,
            transcendentals=rows * tokens * heads // 2,
        ),
        name="attend",
    )(me.reshape(1), bounds, query, *pieces, query_seg, key_seg, factor)


def pages_kernel(count, me_ref, page_ref, scale_ref, *refs):
    pieces, (out_ref, held, sems) = refs[:count], refs[count:]
    me = me_ref[0]
    wanted = held.shape[1]
    per_block = pieces[0].shape[1] // PAGE
    waits = []
    for number in range(wanted):
        page = page_ref[number]
        rows = pl.ds(pl.multiple_of((page % per_block) * PAGE, PAGE), PAGE)
        for kind in range(2):
            target, sem = held.at[kind, number], sems.at[kind, number]
            for at, piece in enumerate(pieces):

                @pl.when((page // per_block) == (me ^ at))
                def _(source=piece.at[kind, rows, :], target=target, sem=sem):
                    pltpu.make_async_copy(source, target, sem).start()

            waits.append(
                pltpu.make_async_copy(pieces[0].at[kind, pl.ds(0, PAGE), :], target, sem)
            )
    for number in range(wanted):
        waits[2 * number].wait()
        scale = jnp.broadcast_to(scale_ref[page_ref[number]], (128, PAGE))
        key = held[0, number].astype(jnp.float32) * jnp.transpose(scale)[:, :1]
        part, at = number * 2 // wanted, number % (wanted // 2)
        out_ref[part, 0, at] = key.astype(jnp.bfloat16)
        waits[2 * number + 1].wait()
        out_ref[part, 1, at] = held[1, number]


def pick_pages(pieces, me, pages, scale):
    _, rows, cols = pieces[0].shape
    wanted = pages.shape[0]
    count = len(pieces)
    smem = pl.BlockSpec(memory_space=pltpu.SMEM)
    whole = pl.BlockSpec(memory_space=pltpu.VMEM)
    return pl.pallas_call(
        functools.partial(pages_kernel, count),
        in_specs=[smem, smem, whole] + [pl.BlockSpec(memory_space=pl.ANY)] * count,
        out_specs=whole,
        out_shape=jax.ShapeDtypeStruct((2, 2, wanted // 2, PAGE, cols), jnp.bfloat16),
        scratch_shapes=[
            pltpu.VMEM((2, wanted, PAGE, cols), jnp.bfloat16),
            pltpu.SemaphoreType.DMA((2, wanted)),
        ],
        compiler_params=pltpu.CompilerParams(vmem_limit_bytes=VMEM),
        cost_estimate=pl.CostEstimate(
            flops=0, bytes_accessed=8 * wanted * PAGE * cols, transcendentals=0
        ),
        name="pick_pages",
    )(me.reshape(1), pages, scale, *pieces)


def own_pages(page_table, start, count):
    page_total = page_table.shape[0]
    inverse = (
        jnp.zeros((page_total,), jnp.int32)
        .at[page_table]
        .set(jnp.arange(page_total, dtype=jnp.int32))
    )
    return lax.dynamic_slice_in_dim(inverse, start, count, 0)


def whole_heads(ring, hidden, modulation, weights, gains, positions, segment_ids, page_table):
    tok_rows = hidden.shape[0]
    me = lax.axis_index("row")
    full_rows = lax.all_gather(hidden, "col", axis=1, tiled=True)
    modulated = modulate(full_rows.astype(jnp.float32), modulation)
    width = full_rows.shape[1]
    raws = [
        jnp.dot(
            modulated,
            lax.all_gather(weight, "row", axis=0, tiled=True),
            preferred_element_type=jnp.float32,
        )
        for weight in weights
    ]
    squares = lax.psum(tuple(jnp.sum(raw * raw, axis=1) for raw in raws[:2]), "col")
    tables = rotary_lanes(positions, HEAD_DIM)
    query, key = [
        turn([raw], total[None], gain[None], tables, width)[0]
        for raw, total, gain in zip(raws, squares, gains)
    ]
    held = lax.all_gather(jnp.stack([key, raws[2].astype(jnp.bfloat16)]), "row", axis=0)
    pieces = [held[number] for number in range(ring)]
    none = jnp.zeros((), jnp.int32)
    query_seg = lax.dynamic_slice_in_dim(segment_ids, me * tok_rows, tok_rows, 0)
    key_seg = segment_ids.astype(jnp.float32).reshape(-1, 1, KEY_TILE)
    attended = attend(
        query,
        pieces,
        none,
        key_bounds(query_seg, segment_ids),
        query_seg.astype(jnp.float32)[None, :],
        key_seg,
        jnp.full_like(key_seg, HEAD_DIM ** (-0.5) * LOG2E),
    )
    count = tok_rows // PAGE
    pages = own_pages(page_table, me * count, count)
    ones = jnp.ones((segment_ids.shape[0] // PAGE, 1, PAGE), jnp.float32)
    picked = pick_pages(pieces, none, jnp.concatenate([pages, pages]), ones)
    return attended, picked[0]


def split_heads(ring, ranks, hidden, modulation, weights, gains, positions, segment_ids, page_table):
    tok_rows, shard = hidden.shape
    width = ranks * shard
    me = lax.axis_index("row")
    rank = lax.axis_index("col")
    top = ring // 2
    half = me // top
    cols = weights[0].shape[1] // 2
    hops = []
    bit = top // 2
    while bit:
        hops.append(bit)
        bit //= 2

    def swap(value, bit):
        return lax.ppermute(value, "row", [(i, i ^ bit) for i in range(ring)])

    def across(value, step):
        return lax.ppermute(value, "col", [(c, c ^ step) for c in range(ranks)])

    def spread(blocks, bits):
        for bit in bits:
            blocks.update({number | bit: swap(blocks[number], bit) for number in list(blocks)})
        return blocks

    def in_order(mine, other, axis):
        return jnp.where(
            half == 0,
            jnp.concatenate([mine, other], axis=axis),
            jnp.concatenate([other, mine], axis=axis),
        )

    hidden_all = lax.all_gather(hidden, "col", axis=0)
    positions_other = swap(positions, top)
    weights, positions_other = lax.optimization_barrier((weights, positions_other))
    w_query, w_key, w_value = weights
    own, send_pair, send_single = cut((w_key, w_value, w_query), half)
    first, rest_hops = hops[0], hops[1:]
    pair, single = swap(send_pair, top), swap(send_single, top)
    next_own = swap(own, first)
    own_blocks = spread({0: own}, rest_hops)

    rows = hidden.astype(jnp.float32)
    local_mean = jnp.mean(rows, axis=1)
    local_square = jnp.sum(jnp.square(rows - local_mean[:, None]), axis=1)
    stats = jnp.stack([local_mean, local_square])
    all_stats = [stats] + [across(stats, step) for step in range(1, ranks)]
    average = sum(part[0] for part in all_stats) / ranks
    variance = (
        sum(part[1] + shard * jnp.square(part[0] - average) for part in all_stats) / width
    )
    small = jnp.stack([average, lax.rsqrt(variance + epsilon)])
    small_other = swap(small, top)
    tables = [
        rotary_lanes(part, HEAD_DIM) for part in (positions, positions_other)
    ]
    q_gain, k_gain = [
        lax.dynamic_slice_in_dim(gain, half * cols, cols, 0)[None, :] for gain in gains
    ]
    count = tok_rows // PAGE
    pages = jnp.concatenate(
        [own_pages(page_table, owner * count, count) for owner in (me ^ top, me)]
    )
    query_segs = [
        lax.dynamic_slice_in_dim(segment_ids, owner * tok_rows, tok_rows, 0)
        for owner in (me, me ^ top)
    ]
    bounds = [key_bounds(seg, segment_ids) for seg in query_segs]
    query_segs = [seg.astype(jnp.float32)[None, :] for seg in query_segs]
    key_seg = segment_ids.astype(jnp.float32).reshape(-1, 1, KEY_TILE)
    place = jnp.stack([me, rank]).astype(jnp.int32)
    prepared = (tables, q_gain, k_gain, pages, query_segs, key_seg, bounds, place, small, small_other)
    moved = (pair, single, next_own, own_blocks)
    moved, prepared, hidden_late = lax.optimization_barrier((moved, prepared, hidden))
    pair, single, next_own, own_blocks = moved
    tables, q_gain, k_gain, pages, query_segs, key_seg, bounds, place, small, small_other = prepared

    next_single = swap(single, first)
    other_rows = swap(hidden_late, top)
    pair_blocks = spread({0: pair}, rest_hops)
    single_blocks = spread({0: single}, rest_hops)
    next_own_blocks = spread({0: next_own}, rest_hops)
    moved = (next_single, other_rows, pair_blocks, single_blocks, next_own_blocks)
    moved, hidden_all = lax.optimization_barrier((moved, hidden_all))
    next_single, other_rows, pair_blocks, single_blocks, next_own_blocks = moved

    next_pair = swap(pair_blocks[0], first)
    early = tok_rows * 5 // 12 // 16 * 16
    early_shards = [across(other_rows[:early], step) for step in range(1, ranks)]
    rest = swap(
        jnp.concatenate(
            [
                lax.dynamic_slice(
                    hidden_all, (rank ^ step, early, 0), (1, tok_rows - early, shard)
                )
                for step in range(1, ranks)
            ]
        ).reshape(-1, shard),
        top,
    )
    sources, spots = [], [None] * ring
    for number in own_blocks:
        for offset, whole in ((0, own_blocks), (first, next_own_blocks)):
            spots[number | offset] = tuple((len(sources), m) for m in range(3))
            sources.append(whole[number])
        at = len(sources)
        spots[number | top] = ((at, 0), (at, 1), (at + 1, 0))
        sources.extend([pair_blocks[number], single_blocks[number]])
    here = tuple(number for number in range(ring) if spots[number] is not None)
    late = tuple(number for number in range(ring) if spots[number] is None)
    own_parts = ((tok_rows, (0,), True),)
    (partial,) = project(
        place,
        small,
        modulation,
        own_parts,
        here,
        [hidden_all],
        tuple(spots),
        list(sources),
        None,
        None,
    )
    next_pair, next_single, rest, early_shards, partial = lax.optimization_barrier(
        (next_pair, next_single, rest, early_shards, partial)
    )

    next_pair_blocks = spread({0: next_pair}, rest_hops)
    next_single_blocks = spread({0: next_single}, rest_hops)
    for number in own_blocks:
        at = len(sources)
        spots[number | top | first] = ((at, 0), (at, 1), (at + 1, 0))
        sources.extend([next_pair_blocks[number], next_single_blocks[number]])
    other_parts = (
        (early, (0,) * ranks, False),
        (
            tok_rows - early,
            (early,) + tuple(step * (tok_rows - early) for step in range(ranks - 1)),
            False,
        ),
    )
    late_sources = [part for number in own_blocks for part in (next_pair_blocks[number], next_single_blocks[number])]
    late_spots = list(spots)
    for at, number in enumerate(own_blocks):
        late_spots[number | top | first] = ((2 * at, 0), (2 * at, 1), (2 * at + 1, 0))
    own_held, own_query, own_squares = project(
        place,
        small,
        modulation,
        own_parts,
        late,
        [hidden_all],
        tuple(late_spots),
        late_sources,
        partial,
        (k_gain, *tables[0]),
    )
    own_ahead = swap(own_held, first)
    other_held, other_query, other_squares = project(
        place,
        small_other,
        modulation,
        other_parts,
        tuple(range(ring)),
        [other_rows] + early_shards + [other_rows] + [rest] * (ranks - 1),
        tuple(spots),
        sources,
        None,
        (k_gain, *tables[1]),
    )
    other_ahead = swap(other_held, first)

    squares = jnp.stack([own_squares, other_squares])
    squares = squares + swap(squares, top)[::-1]
    bit = 1
    while bit < ranks:
        squares = squares + across(squares, bit)
        bit *= 2
    squares, own_ahead = lax.optimization_barrier((squares, own_ahead))
    query = turn(
        [own_query, other_query],
        squares[:, 1],
        q_gain,
        [jnp.concatenate(pair) for pair in zip(*tables)],
        width,
    )
    key_squares = spread({0: squares[:, 0]}, hops)
    held = spread({0: own_held, first: own_ahead}, rest_hops)
    held, query, other_ahead = lax.optimization_barrier((held, query, other_ahead))
    other = spread({0: other_held, first: other_ahead}, rest_hops)
    held.update({number | top: part for number, part in other.items()})
    pieces = [held[number] for number in range(ring)]
    blocks = jnp.stack([key_squares[n % top][n // top] for n in range(ring)])
    scale = lax.rsqrt(blocks / width + epsilon)
    scale = jnp.concatenate(
        [lax.dynamic_slice_in_dim(scale, me ^ owner, 1, 0) for owner in range(ring)]
    )
    factor = (scale * (HEAD_DIM ** (-0.5) * LOG2E)).reshape(-1, 1, KEY_TILE)
    picked = pick_pages(pieces, me, pages, scale.reshape(-1, 1, PAGE))
    query, picked = lax.optimization_barrier((query, picked))
    pages_other = swap(picked[0], top)

    def attended(number):
        return attend(
            query[number], pieces, me, bounds[number], query_segs[number], key_seg, factor
        )

    for_other = attended(1)
    query, for_other = lax.optimization_barrier((query, for_other))
    from_other = swap(for_other, top)
    for_me = attended(0)
    return in_order(for_me, from_other, -1), in_order(picked[1], pages_other, -1)


def solution(mesh):
    ring, ranks = mesh.shape["row"], mesh.shape["col"]

    def body(
        hidden, modulation, w_query, w_key, w_value, q_gain, k_gain, positions, segment_ids, page_table
    ):
        rest = (
            hidden,
            modulation,
            (w_query, w_key, w_value),
            (q_gain, k_gain),
            positions,
            segment_ids,
            page_table,
        )
        heads = w_query.shape[1] // HEAD_DIM
        feats, shard = w_query.shape[0], hidden.shape[1]
        powers = ring & (ring - 1) == 0 and ranks & (ranks - 1) == 0
        if heads % 2 == 0 and ring >= 8 and powers and feats % 128 == 0 and shard % feats == 0:
            return split_heads(ring, ranks, *rest)
        return whole_heads(ring, *rest)

    in_specs = (
        P("row", "col"),
        P(),
        P("row", "col"),
        P("row", "col"),
        P("row", "col"),
        P("col"),
        P("col"),
        P(None, "row"),
        P(),
        P(),
    )
    out_specs = (P("row", "col"), P(None, "row", None, "col"))
    return jax.shard_map(body, mesh=mesh, in_specs=in_specs, out_specs=out_specs, check_vma=False)
```

```python
import functools
import jax
import jax.numpy as jnp
from jax import lax
from jax.experimental import pallas as pl
from jax.experimental.pallas import tpu as pltpu
from jax.sharding import PartitionSpec as P

HEAD_DIM = 128
PAGE = 128
KEY_TILE = 512
VMEM = 60 * 1024 * 1024
LOG2E = 1.4426950408889634

epsilon = 1e-06


def rotary_lanes(positions, head_dim):
    pair_count = head_dim // 2
    frame_pairs = pair_count - 2 * (pair_count // 3)
    side_pairs = pair_count // 3
    column = jnp.arange(head_dim) // 2
    frame_rate = 10000.0 ** (-column.astype(jnp.float32) / frame_pairs)
    height_rate = 10000.0 ** (-(column - frame_pairs).astype(jnp.float32) / side_pairs)
    width_rate = 10000.0 ** (-(column - frame_pairs - side_pairs).astype(jnp.float32) / side_pairs)
    coords = positions.astype(jnp.float32)
    angles = jnp.where(
        column < frame_pairs,
        coords[0][:, None] * frame_rate,
        jnp.where(
            column < frame_pairs + side_pairs,
            coords[1][:, None] * height_rate,
            coords[2][:, None] * width_rate,
        ),
    )
    sine = jnp.sin(angles)
    even = (jnp.arange(head_dim) % 2 == 0)[None, :]
    return jnp.cos(angles), jnp.where(even, -sine, 0.0), jnp.where(even, 0.0, sine)


def modulate(activations, modulation):
    average = jnp.mean(activations, axis=1, keepdims=True)
    centred = activations - average
    variance = jnp.mean(centred * centred, axis=1, keepdims=True)
    normed = centred * lax.rsqrt(variance + epsilon)
    return (normed * (1.0 + modulation[1]) + modulation[0]).astype(jnp.bfloat16)


def cut_kernel(half_ref, *refs):
    weights, outs, sems = refs[:3], refs[3:6], refs[6]
    cols = outs[0].shape[2]
    half = half_ref[0]
    copies = []
    for number, weight in enumerate(weights):
        send, at = (1, number) if number < 2 else (2, 0)
        for which, target in ((half, outs[0].at[number]), (1 - half, outs[send].at[at])):
            span = pl.ds(pl.multiple_of(which * cols, cols), cols)
            copies.append(
                pltpu.make_async_copy(
                    weight.at[:, span], target, sems.at[number, len(copies) % 2]
                )
            )
            copies[-1].start()
    for copy in copies:
        copy.wait()


def cut(weights, half):
    rows, width = weights[0].shape
    cols = width // 2
    whole = pl.BlockSpec(memory_space=pltpu.VMEM)
    return pl.pallas_call(
        cut_kernel,
        in_specs=[pl.BlockSpec(memory_space=pltpu.SMEM)] + [pl.BlockSpec(memory_space=pl.ANY)] * 3,
        out_specs=[whole] * 3,
        out_shape=[jax.ShapeDtypeStruct((size, rows, cols), jnp.bfloat16) for size in (3, 2, 1)],
        scratch_shapes=[pltpu.SemaphoreType.DMA((3, 2))],
        compiler_params=pltpu.CompilerParams(vmem_limit_bytes=VMEM),
        cost_estimate=pl.CostEstimate(
            flops=0, bytes_accessed=12 * rows * width, transcendentals=0
        ),
        name="cut",
    )(half.reshape(1), *weights)


def turned(values, gain, tables, at):
    dim = tables[0].shape[1]
    cols = slice(at * dim, (at + 1) * dim)
    own, upper, lower = tables
    part = values[:, cols] * gain[:, cols]
    return part * own + pltpu.roll(part, dim - 1, 1) * upper + pltpu.roll(part, 1, 1) * lower


def project_kernel(
    parts, blocks, spots, first, final, in_count, place_ref, stats_ref, modulation_ref, *refs
):
    shard_count = sum(len(part[1]) for part in parts)
    out_count = len(refs) - 6 - in_count
    shards, rest = refs[:shard_count], refs[shard_count:]
    total, raws, weights, ready, raw_sems, weight_sems = rest[-6:]
    outs, sources = rest[-6 - out_count : -6], rest[: -6 - out_count]
    if final:
        sources, (gain_ref, own_ref, upper_ref, lower_ref) = sources[:-4], sources[-4:]
    if not first:
        sources, partial_ref = sources[:-1], sources[-1]
    me, rank = place_ref[0], place_ref[1]
    feats, cols = weights.shape[2:]
    rows = raws.shape[1]
    per_rank = shards[0].shape[-1] // feats
    copies = {}
    for slot, block in enumerate(blocks):
        owner = me ^ block
        span = pl.ds(pl.multiple_of((owner % per_rank) * feats, feats), feats)
        holder = owner // per_rank
        mine, begin, at = [], 0, 0
        for number, (length, places, by_rank) in enumerate(parts):
            held = shards[at : at + len(places)]
            at += len(places)
            target = raws.at[slot, pl.ds(begin, length), :]
            begin += length
            sem = raw_sems.at[slot, number]
            if by_rank:
                copy = pltpu.make_async_copy(
                    held[0].at[holder, pl.ds(places[0], length), span], target, sem
                )
                copy.start()
            else:
                for step, (ref, skip) in enumerate(zip(held, places)):
                    source = ref.at[pl.ds(skip, length), span]

                    @pl.when((holder ^ rank) == step)
                    def _(source=source, target=target, sem=sem):
                        pltpu.make_async_copy(source, target, sem).start()

                copy = pltpu.make_async_copy(source, target, sem)
            mine.append(copy)
        matrices = [
            pltpu.make_async_copy(
                sources[source].at[place], weights.at[slot, number], weight_sems.at[slot, number]
            )
            for number, (source, place) in enumerate(spots[block])
        ]
        for copy in matrices:
            copy.start()
        copies[slot] = (mine, matrices)

    def column(at):
        return jnp.transpose(jnp.broadcast_to(stats_ref[at : at + 1, :], (128, rows)))

    mean, scale = column(0), column(1)

    def prepare(first_slot):
        for slot in (first_slot, first_slot + 1):
            for copy in copies[slot][0]:
                copy.wait()
            span = pl.ds(pl.multiple_of((me ^ blocks[slot]) * feats, feats), feats)
            shift = modulation_ref[0:1, span]
            gain = 1.0 + modulation_ref[1:2, span]
            left = (slot - first_slot) * feats
            for start in range(0, feats, 128):
                lanes = slice(start, start + 128)
                part = raws[slot, :, lanes].astype(jnp.float32)
                part = (part - mean) * scale * gain[:, lanes] + shift[:, lanes]
                ready[first_slot // 2 % 2, :, left + start : left + start + 128] = part.astype(
                    jnp.bfloat16
                )

    prepare(0)
    for slot in range(0, len(blocks), 2):
        for copy in copies[slot][1] + copies[slot + 1][1]:
            copy.wait()
        if slot + 2 < len(blocks):
            prepare(slot + 2)
        right = jnp.concatenate(
            [
                jnp.concatenate([weights[slot, m], weights[slot + 1, m]], axis=0)
                for m in range(3)
            ],
            axis=1,
        )
        part = jnp.dot(ready[slot // 2 % 2], right, preferred_element_type=jnp.float32)
        if slot:
            part = part + total[...]
        elif not first:
            part = part + partial_ref[...]
        if slot + 2 < len(blocks):
            total[...] = part
    if not final:
        outs[0][...] = part
        return
    query_ref, squares_ref = outs[:2]
    key_ref, value_ref = outs[2:] if len(outs) == 4 else (outs[2], outs[2])
    key, value, query = [part[:, m * cols : (m + 1) * cols] for m in range(3)]
    query_ref[...] = query
    value_ref[value_ref.shape[0] - 1] = value.astype(jnp.bfloat16)
    tables = (own_ref[...], upper_ref[...], lower_ref[...])
    for head in range(cols // HEAD_DIM):
        lanes = slice(head * HEAD_DIM, (head + 1) * HEAD_DIM)
        key_ref[0, :, lanes] = turned(key, gain_ref, tables, head).astype(jnp.bfloat16)
    for kind, raw in enumerate((key, query)):
        summed = jnp.sum(raw * raw, axis=1, keepdims=True)
        summed = jnp.transpose(jnp.broadcast_to(summed, (rows, 128)))
        squares_ref[kind : kind + 1, :] = summed[:1]


def project(
    place, stats, modulation, parts, blocks, shards, spots, sources, partial, finish, joint=True
):
    rows = sum(part[0] for part in parts)
    _, feats, cols = sources[0].shape
    count = len(blocks)
    anywhere = pl.BlockSpec(memory_space=pl.ANY)
    whole = pl.BlockSpec(memory_space=pltpu.VMEM)
    out_shape = [jax.ShapeDtypeStruct((rows, 3 * cols), jnp.float32)]
    extra = [] if partial is None else [partial]
    if finish is not None:
        extra.extend(finish)
        held = [2] if joint else [1, 1]
        out_shape = [
            jax.ShapeDtypeStruct((rows, cols), jnp.float32),
            jax.ShapeDtypeStruct((2, rows), jnp.float32),
        ] + [jax.ShapeDtypeStruct((size, rows, cols), jnp.bfloat16) for size in held]
    return pl.pallas_call(
        functools.partial(
            project_kernel,
            parts,
            blocks,
            spots,
            partial is None,
            finish is not None,
            len(shards) + len(sources) + len(extra),
        ),
        in_specs=[pl.BlockSpec(memory_space=pltpu.SMEM), whole, whole]
        + [anywhere] * (len(shards) + len(sources))
        + [whole] * len(extra),
        out_specs=[whole] * len(out_shape),
        out_shape=out_shape,
        scratch_shapes=[
            pltpu.VMEM((rows, 3 * cols), jnp.float32),
            pltpu.VMEM((count, rows, feats), jnp.bfloat16),
            pltpu.VMEM((count, 3, feats, cols), jnp.bfloat16),
            pltpu.VMEM((2, rows, 2 * feats), jnp.bfloat16),
            pltpu.SemaphoreType.DMA((count, len(parts))),
            pltpu.SemaphoreType.DMA((count, 3)),
        ],
        compiler_params=pltpu.CompilerParams(vmem_limit_bytes=VMEM),
        cost_estimate=pl.CostEstimate(
            flops=6 * rows * count * feats * cols,
            bytes_accessed=2 * count * feats * (rows + 3 * cols) + 12 * rows * cols,
            transcendentals=0,
        ),
        name="project",
    )(place, stats, modulation, *shards, *sources, *extra)


def turn_kernel(count, width, squares_ref, gain_ref, *refs):
    for number in range(count):
        raw_ref, out_ref = refs[number], refs[4 * count + number]
        tables = [ref[...] for ref in refs[count + 3 * number : count + 3 * number + 3]]
        rows, cols = raw_ref.shape
        scale = lax.rsqrt(squares_ref[number : number + 1, :] * (1.0 / width) + epsilon)
        raw = raw_ref[...] * jnp.transpose(jnp.broadcast_to(scale, (128, rows)))[:, :1]
        for head in range(cols // HEAD_DIM):
            out_ref[:, head * HEAD_DIM : (head + 1) * HEAD_DIM] = turned(
                raw, gain_ref, tables, head
            ).astype(jnp.bfloat16)


def turn(raws, squares, gain, tables, width):
    count = len(raws)
    rows, cols = raws[0].shape
    whole = pl.BlockSpec(memory_space=pltpu.VMEM)
    return pl.pallas_call(
        functools.partial(turn_kernel, count, width),
        in_specs=[whole] * (2 + 4 * count),
        out_specs=[whole] * count,
        out_shape=[jax.ShapeDtypeStruct((rows, cols), jnp.bfloat16)] * count,
        compiler_params=pltpu.CompilerParams(vmem_limit_bytes=VMEM),
        cost_estimate=pl.CostEstimate(flops=0, bytes_accessed=0, transcendentals=0),
        name="turn",
    )(squares, gain, *raws, *[part for table in tables for part in table])


def attend_kernel(places, me_ref, bounds_ref, q_ref, *refs):
    count = len(places)
    pieces, (query_seg_ref, key_seg_ref, factor_ref) = refs[:count], refs[count : count + 3]
    out_ref, keys, values, highest, mixed, sems = refs[count + 3 :]
    me = me_ref[0]
    rows = pieces[0].shape[1]
    copies = []
    for number, (piece, (kind, at)) in enumerate(zip(pieces, places)):
        owner = number % (count // 2)
        where = pl.ds(pl.multiple_of((me ^ owner) * rows, rows), rows)
        held = (keys, values)[kind]
        copies.append(
            pltpu.make_async_copy(piece.at[at], held.at[where, :], sems.at[kind, owner])
        )
    for copy in copies:
        copy.start()
    dim = HEAD_DIM
    heads = q_ref.shape[1] // dim
    ones = jnp.ones((KEY_TILE, dim), jnp.bfloat16)
    highest[...] = jnp.full_like(highest, -1e29)
    mixed[...] = jnp.zeros_like(mixed)
    for copy in copies:
        copy.wait()

    query_seg = jnp.transpose(jnp.broadcast_to(query_seg_ref[...], (128, rows)))[:, :1]

    def step(block, carry):
        where = pl.ds(pl.multiple_of(block * KEY_TILE, KEY_TILE), KEY_TILE)
        same = query_seg == key_seg_ref[block]
        factor = factor_ref[block]
        for head in range(heads):
            cols = slice(head * dim, (head + 1) * dim)
            scores = lax.dot_general(
                q_ref[:, cols],
                keys[where, cols],
                (((1,), (1,)), ((), ())),
                preferred_element_type=jnp.float32,
            )
            scores = jnp.where(same, scores * factor, -1e30)
            former = highest[head]
            newest = jnp.maximum(former, jnp.max(scores, axis=1, keepdims=True))
            highest[head] = newest
            weights = jnp.exp2(scores - newest[:, :1]).astype(jnp.bfloat16)
            right = jnp.concatenate([values[where, cols], ones], axis=1)
            part = jnp.dot(weights, right, preferred_element_type=jnp.float32)
            shrink = jnp.exp2(former - newest)
            mixed[head, :, :dim] = mixed[head, :, :dim] * shrink + part[:, :dim]
            mixed[head, :, dim:] = mixed[head, :, dim:] * shrink + part[:, dim:]
        return carry

    lax.fori_loop(bounds_ref[0], bounds_ref[1], step, 0)
    for head in range(heads):
        out_ref[:, head * dim : (head + 1) * dim] = (
            mixed[head, :, :dim] / mixed[head, :, dim:]
        ).astype(out_ref.dtype)


def key_bounds(query_seg, segment_ids):
    low = jnp.sum(segment_ids < query_seg[0], dtype=jnp.int32)
    high = jnp.sum(segment_ids <= query_seg[-1], dtype=jnp.int32)
    return jnp.stack([low // KEY_TILE, (high + KEY_TILE - 1) // KEY_TILE])


def attend(query, keys, values, me, bounds, query_seg, key_seg, factor):
    rows, cols = query.shape
    pieces = [array for array, _ in keys + values]
    places = tuple((0, at) for _, at in keys) + tuple((1, at) for _, at in values)
    count = len(pieces)
    tokens = key_seg.shape[0] * KEY_TILE
    dim = HEAD_DIM
    heads = cols // dim
    smem = pl.BlockSpec(memory_space=pltpu.SMEM)
    whole = pl.BlockSpec(memory_space=pltpu.VMEM)
    return pl.pallas_call(
        functools.partial(attend_kernel, places),
        in_specs=[smem, smem, whole] + [pl.BlockSpec(memory_space=pl.ANY)] * count + [whole] * 3,
        out_specs=whole,
        scratch_shapes=[
            pltpu.VMEM((tokens, cols), jnp.bfloat16),
            pltpu.VMEM((tokens, cols), jnp.bfloat16),
            pltpu.VMEM((heads, rows, dim), jnp.float32),
            pltpu.VMEM((heads, rows, 2 * dim), jnp.float32),
            pltpu.SemaphoreType.DMA((2, count // 2)),
        ],
        out_shape=jax.ShapeDtypeStruct((rows, cols), jnp.bfloat16),
        compiler_params=pltpu.CompilerParams(vmem_limit_bytes=VMEM),
        cost_estimate=pl.CostEstimate(
            flops=2 * rows * tokens * cols,
            bytes_accessed=4 * tokens * cols + 4 * rows * cols,
            transcendentals=rows * tokens * heads // 2,
        ),
        name="attend",
    )(me.reshape(1), bounds, query, *pieces, query_seg, key_seg, factor)


def pages_kernel(places, me_ref, page_ref, *refs):
    count = len(places)
    pieces, rest = refs[:count], refs[count:]
    scale_ref, (out_refs, held, sems) = (rest[0] if len(rest) == 5 else None), (
        rest[-4:-2],
        rest[-2],
        rest[-1],
    )
    me = me_ref[0]
    wanted = held.shape[0]
    per_block = pieces[0].shape[1] // PAGE
    waits = []
    for number in range(wanted):
        page = page_ref[number]
        rows = pl.ds(pl.multiple_of((page % per_block) * PAGE, PAGE), PAGE)
        target, sem = held.at[number], sems.at[number]
        for owner, (piece, at) in enumerate(zip(pieces, places)):

            @pl.when((page // per_block) == (me ^ owner))
            def _(source=piece.at[at, rows, :], target=target, sem=sem):
                pltpu.make_async_copy(source, target, sem).start()

        waits.append(pltpu.make_async_copy(pieces[0].at[0, pl.ds(0, PAGE), :], target, sem))
    for number in range(wanted):
        waits[number].wait()
        page = held[number]
        if scale_ref is not None:
            scale = jnp.broadcast_to(scale_ref[page_ref[number]], (128, PAGE))
            page = page.astype(jnp.float32) * jnp.transpose(scale)[:, :1]
        each = wanted // 2
        out_refs[number // each][number % each] = page.astype(jnp.bfloat16)


def pick_pages(pieces, me, pages, scale):
    _, rows, cols = pieces[0][0].shape
    wanted = pages.shape[0]
    smem = pl.BlockSpec(memory_space=pltpu.SMEM)
    whole = pl.BlockSpec(memory_space=pltpu.VMEM)
    extra = [] if scale is None else [scale]
    return pl.pallas_call(
        functools.partial(pages_kernel, tuple(at for _, at in pieces)),
        in_specs=[smem, smem]
        + [pl.BlockSpec(memory_space=pl.ANY)] * len(pieces)
        + [whole] * len(extra),
        out_specs=[whole] * 2,
        out_shape=[jax.ShapeDtypeStruct((wanted // 2, PAGE, cols), jnp.bfloat16)] * 2,
        scratch_shapes=[
            pltpu.VMEM((wanted, PAGE, cols), jnp.bfloat16),
            pltpu.SemaphoreType.DMA((wanted,)),
        ],
        compiler_params=pltpu.CompilerParams(vmem_limit_bytes=VMEM),
        cost_estimate=pl.CostEstimate(flops=0, bytes_accessed=0, transcendentals=0),
        name="pick_pages",
    )(me.reshape(1), pages, *[array for array, _ in pieces], *extra)


def own_pages(page_table, start, count):
    page_total = page_table.shape[0]
    inverse = (
        jnp.zeros((page_total,), jnp.int32)
        .at[page_table]
        .set(jnp.arange(page_total, dtype=jnp.int32))
    )
    return lax.dynamic_slice_in_dim(inverse, start, count, 0)


def whole_heads(ring, hidden, modulation, weights, gains, positions, segment_ids, page_table):
    tok_rows = hidden.shape[0]
    me = lax.axis_index("row")
    full_rows = lax.all_gather(hidden, "col", axis=1, tiled=True)
    modulated = modulate(full_rows.astype(jnp.float32), modulation)
    width = full_rows.shape[1]
    raws = [
        jnp.dot(
            modulated,
            lax.all_gather(weight, "row", axis=0, tiled=True),
            preferred_element_type=jnp.float32,
        )
        for weight in weights
    ]
    squares = lax.psum(tuple(jnp.sum(raw * raw, axis=1) for raw in raws[:2]), "col")
    tables = rotary_lanes(positions, HEAD_DIM)
    query, key = [
        turn([raw], total[None], gain[None], [tables], width)[0]
        for raw, total, gain in zip(raws, squares, gains)
    ]
    held = lax.all_gather(jnp.stack([key, raws[2].astype(jnp.bfloat16)]), "row", axis=0)
    keys, values = [[(held[number], kind) for number in range(ring)] for kind in range(2)]
    none = jnp.zeros((), jnp.int32)
    query_seg = lax.dynamic_slice_in_dim(segment_ids, me * tok_rows, tok_rows, 0)
    key_seg = segment_ids.astype(jnp.float32).reshape(-1, 1, KEY_TILE)
    attended = attend(
        query,
        keys,
        values,
        none,
        key_bounds(query_seg, segment_ids),
        query_seg.astype(jnp.float32)[None, :],
        key_seg,
        jnp.full_like(key_seg, HEAD_DIM ** (-0.5) * LOG2E),
    )
    count = tok_rows // PAGE
    pages = own_pages(page_table, me * count, count)
    pages = jnp.concatenate([pages, pages])
    picked = [pick_pages(pieces, none, pages, None)[0] for pieces in (keys, values)]
    return attended, jnp.stack(picked)


def split_heads(ring, ranks, hidden, modulation, weights, gains, positions, segment_ids, page_table):
    tok_rows, shard = hidden.shape
    width = ranks * shard
    me = lax.axis_index("row")
    rank = lax.axis_index("col")
    top = ring // 2
    half = me // top
    cols = weights[0].shape[1] // 2
    hops = []
    bit = top // 2
    while bit:
        hops.append(bit)
        bit //= 2

    def swap(value, bit):
        return lax.ppermute(value, "row", [(i, i ^ bit) for i in range(ring)])

    def across(value, step):
        return lax.ppermute(value, "col", [(c, c ^ step) for c in range(ranks)])

    def spread(blocks, bits):
        for bit in bits:
            blocks.update({number | bit: swap(blocks[number], bit) for number in list(blocks)})
        return blocks

    def in_order(mine, other, axis):
        return jnp.where(
            half == 0,
            jnp.concatenate([mine, other], axis=axis),
            jnp.concatenate([other, mine], axis=axis),
        )

    hidden_all = lax.all_gather(hidden, "col", axis=0)
    w_query, w_key, w_value = weights
    own, send_pair, send_single = cut((w_key, w_value, w_query), half)
    first, rest_hops = hops[0], hops[1:]
    pair, single = swap(send_pair, top), swap(send_single, top)
    next_own = swap(own, first)
    own_blocks = spread({0: own}, rest_hops)

    rows = hidden.astype(jnp.float32)
    local_mean = jnp.mean(rows, axis=1)
    local_square = jnp.sum(jnp.square(rows - local_mean[:, None]), axis=1)
    stats = jnp.stack([local_mean, local_square])
    all_stats = [stats] + [across(stats, step) for step in range(1, ranks)]
    average = sum(part[0] for part in all_stats) / ranks
    variance = (
        sum(part[1] + shard * jnp.square(part[0] - average) for part in all_stats) / width
    )
    small = jnp.concatenate(
        [jnp.stack([average, lax.rsqrt(variance + epsilon)]), positions.astype(jnp.float32)]
    )
    small_other = swap(small, top)
    moved = (pair, single, next_own, own_blocks, small, small_other)
    moved, hidden_late = lax.optimization_barrier((moved, hidden))
    pair, single, next_own, own_blocks, small, small_other = moved

    next_single = swap(single, first)
    other_rows = swap(hidden_late, top)
    pair_blocks = spread({0: pair}, rest_hops)
    single_blocks = spread({0: single}, rest_hops)
    next_own_blocks = spread({0: next_own}, rest_hops)
    moved = (next_single, other_rows, pair_blocks, single_blocks, next_own_blocks)
    plain = (small, small_other, segment_ids, page_table, gains)
    moved, hidden_all, plain = lax.optimization_barrier((moved, hidden_all, plain))
    next_single, other_rows, pair_blocks, single_blocks, next_own_blocks = moved
    small, small_other, segment_ids, page_table, gains = plain

    next_pair = swap(pair_blocks[0], first)
    early = tok_rows * 5 // 12 // 16 * 16
    early_shards = [across(other_rows[:early], step) for step in range(1, ranks)]
    rest = swap(
        jnp.concatenate(
            [
                lax.dynamic_slice(
                    hidden_all, (rank ^ step, early, 0), (1, tok_rows - early, shard)
                )
                for step in range(1, ranks)
            ]
        ).reshape(-1, shard),
        top,
    )
    sources, spots = [], [None] * ring
    for number in own_blocks:
        for offset, whole in ((0, own_blocks), (first, next_own_blocks)):
            spots[number | offset] = tuple((len(sources), m) for m in range(3))
            sources.append(whole[number])
        at = len(sources)
        spots[number | top] = ((at, 0), (at, 1), (at + 1, 0))
        sources.extend([pair_blocks[number], single_blocks[number]])
    here = tuple(number for number in range(ring) if spots[number] is not None)
    late = tuple(number for number in range(ring) if spots[number] is None)
    own_parts = ((tok_rows, (0,), True),)
    place = jnp.stack([me, rank]).astype(jnp.int32)
    (partial,) = project(
        place,
        small[:2],
        modulation,
        own_parts,
        here,
        [hidden_all],
        tuple(spots),
        list(sources),
        None,
        None,
    )
    tables = [rotary_lanes(part[2:], HEAD_DIM) for part in (small, small_other)]
    q_gain, k_gain = [
        lax.dynamic_slice_in_dim(gain, half * cols, cols, 0)[None, :] for gain in gains
    ]
    count = tok_rows // PAGE
    pages = jnp.concatenate(
        [own_pages(page_table, owner * count, count) for owner in (me ^ top, me)]
    )
    query_segs = [
        lax.dynamic_slice_in_dim(segment_ids, owner * tok_rows, tok_rows, 0)
        for owner in (me, me ^ top)
    ]
    bounds = [key_bounds(seg, segment_ids) for seg in query_segs]
    query_segs = [seg.astype(jnp.float32)[None, :] for seg in query_segs]
    key_seg = segment_ids.astype(jnp.float32).reshape(-1, 1, KEY_TILE)
    prepared = (tables, q_gain, k_gain, pages, query_segs, key_seg, bounds)
    moved = (next_pair, next_single, rest, early_shards)
    moved, prepared, partial = lax.optimization_barrier((moved, prepared, partial))
    next_pair, next_single, rest, early_shards = moved
    tables, q_gain, k_gain, pages, query_segs, key_seg, bounds = prepared

    next_pair_blocks = spread({0: next_pair}, rest_hops)
    next_single_blocks = spread({0: next_single}, rest_hops)
    for number in own_blocks:
        at = len(sources)
        spots[number | top | first] = ((at, 0), (at, 1), (at + 1, 0))
        sources.extend([next_pair_blocks[number], next_single_blocks[number]])
    other_parts = (
        (early, (0,) * ranks, False),
        (
            tok_rows - early,
            (early,) + tuple(step * (tok_rows - early) for step in range(ranks - 1)),
            False,
        ),
    )
    late_sources = [part for number in own_blocks for part in (next_pair_blocks[number], next_single_blocks[number])]
    late_spots = list(spots)
    for at, number in enumerate(own_blocks):
        late_spots[number | top | first] = ((2 * at, 0), (2 * at, 1), (2 * at + 1, 0))
    own_query, own_squares, own_held = project(
        place,
        small[:2],
        modulation,
        own_parts,
        late,
        [hidden_all],
        tuple(late_spots),
        late_sources,
        partial,
        (k_gain, *tables[0]),
    )
    own_ahead = swap(own_held, first)
    other_query, other_squares, other_key, other_value = project(
        place,
        small_other[:2],
        modulation,
        other_parts,
        tuple(range(ring)),
        [other_rows] + early_shards + [other_rows] + [rest] * (ranks - 1),
        tuple(spots),
        sources,
        None,
        (k_gain, *tables[1]),
        joint=False,
    )
    value_ahead = swap(other_value, first)

    squares = jnp.stack([own_squares, other_squares])
    squares = squares + swap(squares, top)[::-1]
    bit = 1
    while 2 * bit < ranks:
        squares = squares + across(squares, bit)
        bit *= 2
    squares, own_ahead, value_ahead = lax.optimization_barrier((squares, own_ahead, value_ahead))
    squares = squares + across(squares, bit)
    key_ahead = swap(other_key, first)
    query = turn([own_query, other_query], squares[:, 1], q_gain, tables, width)
    key_squares = spread({0: squares[:, 0]}, hops)
    held = spread({0: own_held, first: own_ahead}, rest_hops)
    other_values = spread({0: other_value, first: value_ahead}, rest_hops)
    values = [(held[n], 1) for n in range(top)] + [(other_values[n], 0) for n in range(top)]
    values_picked = pick_pages(values, me, pages, None)
    query, values_picked, key_ahead, held = lax.optimization_barrier(
        (query, values_picked, key_ahead, held)
    )
    values_other = swap(values_picked[0], top)
    other_keys = spread({0: other_key, first: key_ahead}, rest_hops)
    keys = [(held[n], 0) for n in range(top)] + [(other_keys[n], 0) for n in range(top)]
    blocks = jnp.stack([key_squares[n % top][n // top] for n in range(ring)])
    scale = lax.rsqrt(blocks / width + epsilon)
    scale = jnp.concatenate(
        [lax.dynamic_slice_in_dim(scale, me ^ owner, 1, 0) for owner in range(ring)]
    )
    factor = (scale * (HEAD_DIM ** (-0.5) * LOG2E)).reshape(-1, 1, KEY_TILE)
    keys_picked = pick_pages(keys, me, pages, scale.reshape(-1, 1, PAGE))
    query, keys_picked = lax.optimization_barrier((query, keys_picked))
    keys_other = swap(keys_picked[0], top)

    def attended(number):
        return attend(
            query[number], keys, values, me, bounds[number], query_segs[number], key_seg, factor
        )

    for_other = attended(1)
    query, for_other = lax.optimization_barrier((query, for_other))
    from_other = swap(for_other, top)
    for_me = attended(0)
    page_store = [
        in_order(keys_picked[1], keys_other, -1),
        in_order(values_picked[1], values_other, -1),
    ]
    return in_order(for_me, from_other, -1), jnp.stack(page_store)


def solution(mesh):
    ring, ranks = mesh.shape["row"], mesh.shape["col"]

    def body(
        hidden, modulation, w_query, w_key, w_value, q_gain, k_gain, positions, segment_ids, page_table
    ):
        rest = (
            hidden,
            modulation,
            (w_query, w_key, w_value),
            (q_gain, k_gain),
            positions,
            segment_ids,
            page_table,
        )
        heads = w_query.shape[1] // HEAD_DIM
        feats, shard = w_query.shape[0], hidden.shape[1]
        powers = ring & (ring - 1) == 0 and ranks & (ranks - 1) == 0
        if heads % 2 == 0 and ring >= 8 and powers and feats % 128 == 0 and shard % feats == 0:
            return split_heads(ring, ranks, *rest)
        return whole_heads(ring, *rest)

    in_specs = (
        P("row", "col"),
        P(),
        P("row", "col"),
        P("row", "col"),
        P("row", "col"),
        P("col"),
        P("col"),
        P(None, "row"),
        P(),
        P(),
    )
    out_specs = (P("row", "col"), P(None, "row", None, "col"))
    return jax.shard_map(body, mesh=mesh, in_specs=in_specs, out_specs=out_specs, check_vma=False)
```

```python
import functools
import jax
import jax.numpy as jnp
from jax import lax
from jax.experimental import pallas as pl
from jax.experimental.pallas import tpu as pltpu
from jax.sharding import PartitionSpec as P

HEAD_DIM = 128
PAGE = 128
KEY_TILE = 512
VMEM = 60 * 1024 * 1024
LOG2E = 1.4426950408889634

epsilon = 1e-06


def rotary_lanes(positions, head_dim):
    pair_count = head_dim // 2
    frame_pairs = pair_count - 2 * (pair_count // 3)
    side_pairs = pair_count // 3
    column = jnp.arange(head_dim) // 2
    frame_rate = 10000.0 ** (-column.astype(jnp.float32) / frame_pairs)
    height_rate = 10000.0 ** (-(column - frame_pairs).astype(jnp.float32) / side_pairs)
    width_rate = 10000.0 ** (-(column - frame_pairs - side_pairs).astype(jnp.float32) / side_pairs)
    coords = positions.astype(jnp.float32)
    angles = jnp.where(
        column < frame_pairs,
        coords[0][:, None] * frame_rate,
        jnp.where(
            column < frame_pairs + side_pairs,
            coords[1][:, None] * height_rate,
            coords[2][:, None] * width_rate,
        ),
    )
    sine = jnp.sin(angles)
    even = (jnp.arange(head_dim) % 2 == 0)[None, :]
    return jnp.cos(angles), jnp.where(even, -sine, 0.0), jnp.where(even, 0.0, sine)


def modulate(activations, modulation):
    average = jnp.mean(activations, axis=1, keepdims=True)
    centred = activations - average
    variance = jnp.mean(centred * centred, axis=1, keepdims=True)
    normed = centred * lax.rsqrt(variance + epsilon)
    return (normed * (1.0 + modulation[1]) + modulation[0]).astype(jnp.bfloat16)


def cut_kernel(half_ref, *refs):
    weights, outs, sems = refs[:3], refs[3:6], refs[6]
    cols = outs[0].shape[2]
    half = half_ref[0]
    copies = []
    for number, weight in enumerate(weights):
        send, at = (1, number) if number < 2 else (2, 0)
        for which, target in ((half, outs[0].at[number]), (1 - half, outs[send].at[at])):
            span = pl.ds(pl.multiple_of(which * cols, cols), cols)
            copies.append(
                pltpu.make_async_copy(
                    weight.at[:, span], target, sems.at[number, len(copies) % 2]
                )
            )
            copies[-1].start()
    for copy in copies:
        copy.wait()


def cut(weights, half):
    rows, width = weights[0].shape
    cols = width // 2
    whole = pl.BlockSpec(memory_space=pltpu.VMEM)
    return pl.pallas_call(
        cut_kernel,
        in_specs=[pl.BlockSpec(memory_space=pltpu.SMEM)] + [pl.BlockSpec(memory_space=pl.ANY)] * 3,
        out_specs=[whole] * 3,
        out_shape=[jax.ShapeDtypeStruct((size, rows, cols), jnp.bfloat16) for size in (3, 2, 1)],
        scratch_shapes=[pltpu.SemaphoreType.DMA((3, 2))],
        compiler_params=pltpu.CompilerParams(vmem_limit_bytes=VMEM),
        cost_estimate=pl.CostEstimate(
            flops=0, bytes_accessed=12 * rows * width, transcendentals=0
        ),
        name="cut",
    )(half.reshape(1), *weights)


def turned(values, gain, tables, at):
    dim = tables[0].shape[1]
    cols = slice(at * dim, (at + 1) * dim)
    own, upper, lower = tables
    part = values[:, cols] * gain[:, cols]
    return part * own + pltpu.roll(part, dim - 1, 1) * upper + pltpu.roll(part, 1, 1) * lower


def project_kernel(
    parts, blocks, spots, first, final, in_count, place_ref, stats_ref, modulation_ref, *refs
):
    shard_count = sum(len(part[1]) for part in parts)
    out_count = len(refs) - 6 - in_count
    shards, rest = refs[:shard_count], refs[shard_count:]
    total, raws, weights, ready, raw_sems, weight_sems = rest[-6:]
    outs, sources = rest[-6 - out_count : -6], rest[: -6 - out_count]
    if final:
        sources, (gain_ref, own_ref, upper_ref, lower_ref) = sources[:-4], sources[-4:]
    if not first:
        sources, partial_ref = sources[:-1], sources[-1]
    me, rank = place_ref[0], place_ref[1]
    feats, cols = weights.shape[2:]
    rows = raws.shape[1]
    per_rank = shards[0].shape[-1] // feats
    copies = {}
    for slot, block in enumerate(blocks):
        owner = me ^ block
        span = pl.ds(pl.multiple_of((owner % per_rank) * feats, feats), feats)
        holder = owner // per_rank
        mine, begin, at = [], 0, 0
        for number, (length, places, by_rank) in enumerate(parts):
            held = shards[at : at + len(places)]
            at += len(places)
            target = raws.at[slot, pl.ds(begin, length), :]
            begin += length
            sem = raw_sems.at[slot, number]
            if by_rank:
                copy = pltpu.make_async_copy(
                    held[0].at[holder, pl.ds(places[0], length), span], target, sem
                )
                copy.start()
            else:
                for step, (ref, skip) in enumerate(zip(held, places)):
                    source = ref.at[pl.ds(skip, length), span]

                    @pl.when((holder ^ rank) == step)
                    def _(source=source, target=target, sem=sem):
                        pltpu.make_async_copy(source, target, sem).start()

                copy = pltpu.make_async_copy(source, target, sem)
            mine.append(copy)
        matrices = [
            pltpu.make_async_copy(
                sources[source].at[place], weights.at[slot, number], weight_sems.at[slot, number]
            )
            for number, (source, place) in enumerate(spots[block])
        ]
        for copy in matrices:
            copy.start()
        copies[slot] = (mine, matrices)

    def column(at):
        return jnp.transpose(jnp.broadcast_to(stats_ref[at : at + 1, :], (128, rows)))

    mean, scale = column(0), column(1)

    def prepare(first_slot):
        for slot in (first_slot, first_slot + 1):
            for copy in copies[slot][0]:
                copy.wait()
            span = pl.ds(pl.multiple_of((me ^ blocks[slot]) * feats, feats), feats)
            shift = modulation_ref[0:1, span]
            gain = 1.0 + modulation_ref[1:2, span]
            left = (slot - first_slot) * feats
            for start in range(0, feats, 128):
                lanes = slice(start, start + 128)
                part = raws[slot, :, lanes].astype(jnp.float32)
                part = (part - mean) * scale * gain[:, lanes] + shift[:, lanes]
                ready[first_slot // 2 % 2, :, left + start : left + start + 128] = part.astype(
                    jnp.bfloat16
                )

    prepare(0)
    for slot in range(0, len(blocks), 2):
        for copy in copies[slot][1] + copies[slot + 1][1]:
            copy.wait()
        if slot + 2 < len(blocks):
            prepare(slot + 2)
        right = jnp.concatenate(
            [
                jnp.concatenate([weights[slot, m], weights[slot + 1, m]], axis=0)
                for m in range(3)
            ],
            axis=1,
        )
        part = jnp.dot(ready[slot // 2 % 2], right, preferred_element_type=jnp.float32)
        if slot:
            part = part + total[...]
        elif not first:
            part = part + partial_ref[...]
        if slot + 2 < len(blocks):
            total[...] = part
    if not final:
        outs[0][...] = part
        return
    query_ref, squares_ref = outs[:2]
    key_ref, value_ref = outs[2:] if len(outs) == 4 else (outs[2], outs[2])
    key, value, query = [part[:, m * cols : (m + 1) * cols] for m in range(3)]
    query_ref[...] = query
    value_ref[value_ref.shape[0] - 1] = value.astype(jnp.bfloat16)
    tables = (own_ref[...], upper_ref[...], lower_ref[...])
    for head in range(cols // HEAD_DIM):
        lanes = slice(head * HEAD_DIM, (head + 1) * HEAD_DIM)
        key_ref[0, :, lanes] = turned(key, gain_ref, tables, head).astype(jnp.bfloat16)
    for kind, raw in enumerate((key, query)):
        summed = jnp.sum(raw * raw, axis=1, keepdims=True)
        summed = jnp.transpose(jnp.broadcast_to(summed, (rows, 128)))
        squares_ref[kind : kind + 1, :] = summed[:1]


def project(
    place, stats, modulation, parts, blocks, shards, spots, sources, partial, finish, joint=True
):
    rows = sum(part[0] for part in parts)
    _, feats, cols = sources[0].shape
    count = len(blocks)
    anywhere = pl.BlockSpec(memory_space=pl.ANY)
    whole = pl.BlockSpec(memory_space=pltpu.VMEM)
    out_shape = [jax.ShapeDtypeStruct((rows, 3 * cols), jnp.float32)]
    extra = [] if partial is None else [partial]
    if finish is not None:
        extra.extend(finish)
        held = [2] if joint else [1, 1]
        out_shape = [
            jax.ShapeDtypeStruct((rows, cols), jnp.float32),
            jax.ShapeDtypeStruct((2, rows), jnp.float32),
        ] + [jax.ShapeDtypeStruct((size, rows, cols), jnp.bfloat16) for size in held]
    return pl.pallas_call(
        functools.partial(
            project_kernel,
            parts,
            blocks,
            spots,
            partial is None,
            finish is not None,
            len(shards) + len(sources) + len(extra),
        ),
        in_specs=[pl.BlockSpec(memory_space=pltpu.SMEM), whole, whole]
        + [anywhere] * (len(shards) + len(sources))
        + [whole] * len(extra),
        out_specs=[whole] * len(out_shape),
        out_shape=out_shape,
        scratch_shapes=[
            pltpu.VMEM((rows, 3 * cols), jnp.float32),
            pltpu.VMEM((count, rows, feats), jnp.bfloat16),
            pltpu.VMEM((count, 3, feats, cols), jnp.bfloat16),
            pltpu.VMEM((2, rows, 2 * feats), jnp.bfloat16),
            pltpu.SemaphoreType.DMA((count, len(parts))),
            pltpu.SemaphoreType.DMA((count, 3)),
        ],
        compiler_params=pltpu.CompilerParams(vmem_limit_bytes=VMEM),
        cost_estimate=pl.CostEstimate(
            flops=6 * rows * count * feats * cols,
            bytes_accessed=2 * count * feats * (rows + 3 * cols) + 12 * rows * cols,
            transcendentals=0,
        ),
        name="project",
    )(place, stats, modulation, *shards, *sources, *extra)


def turn_kernel(count, width, squares_ref, gain_ref, *refs):
    for number in range(count):
        raw_ref, out_ref = refs[number], refs[4 * count + number]
        tables = [ref[...] for ref in refs[count + 3 * number : count + 3 * number + 3]]
        rows, cols = raw_ref.shape
        scale = lax.rsqrt(squares_ref[number : number + 1, :] * (1.0 / width) + epsilon)
        raw = raw_ref[...] * jnp.transpose(jnp.broadcast_to(scale, (128, rows)))[:, :1]
        for head in range(cols // HEAD_DIM):
            out_ref[:, head * HEAD_DIM : (head + 1) * HEAD_DIM] = turned(
                raw, gain_ref, tables, head
            ).astype(jnp.bfloat16)


def turn(raws, squares, gain, tables, width):
    count = len(raws)
    rows, cols = raws[0].shape
    whole = pl.BlockSpec(memory_space=pltpu.VMEM)
    return pl.pallas_call(
        functools.partial(turn_kernel, count, width),
        in_specs=[whole] * (2 + 4 * count),
        out_specs=[whole] * count,
        out_shape=[jax.ShapeDtypeStruct((rows, cols), jnp.bfloat16)] * count,
        compiler_params=pltpu.CompilerParams(vmem_limit_bytes=VMEM),
        cost_estimate=pl.CostEstimate(flops=0, bytes_accessed=0, transcendentals=0),
        name="turn",
    )(squares, gain, *raws, *[part for table in tables for part in table])


def attend_kernel(places, me_ref, bounds_ref, q_ref, *refs):
    count = len(places)
    pieces, (query_seg_ref, key_seg_ref, factor_ref) = refs[:count], refs[count : count + 3]
    out_ref, keys, values, highest, mixed, sems = refs[count + 3 :]
    me = me_ref[0]
    rows = pieces[0].shape[1]
    copies = []
    for number, (piece, (kind, at)) in enumerate(zip(pieces, places)):
        owner = number % (count // 2)
        where = pl.ds(pl.multiple_of((me ^ owner) * rows, rows), rows)
        held = (keys, values)[kind]
        copies.append(
            pltpu.make_async_copy(piece.at[at], held.at[where, :], sems.at[kind, owner])
        )
    for copy in copies:
        copy.start()
    dim = HEAD_DIM
    heads = q_ref.shape[1] // dim
    ones = jnp.ones((KEY_TILE, dim), jnp.bfloat16)
    highest[...] = jnp.full_like(highest, -1e29)
    mixed[...] = jnp.zeros_like(mixed)
    for copy in copies:
        copy.wait()

    query_seg = jnp.transpose(jnp.broadcast_to(query_seg_ref[...], (128, rows)))[:, :1]

    def step(block, carry):
        where = pl.ds(pl.multiple_of(block * KEY_TILE, KEY_TILE), KEY_TILE)
        same = query_seg == key_seg_ref[block]
        factor = factor_ref[block]
        for head in range(heads):
            cols = slice(head * dim, (head + 1) * dim)
            scores = lax.dot_general(
                q_ref[:, cols],
                keys[where, cols],
                (((1,), (1,)), ((), ())),
                preferred_element_type=jnp.float32,
            )
            scores = jnp.where(same, scores * factor, -1e30)
            former = highest[head]
            newest = jnp.maximum(former, jnp.max(scores, axis=1, keepdims=True))
            highest[head] = newest
            weights = jnp.exp2(scores - newest[:, :1]).astype(jnp.bfloat16)
            right = jnp.concatenate([values[where, cols], ones], axis=1)
            part = jnp.dot(weights, right, preferred_element_type=jnp.float32)
            shrink = jnp.exp2(former - newest)
            mixed[head, :, :dim] = mixed[head, :, :dim] * shrink + part[:, :dim]
            mixed[head, :, dim:] = mixed[head, :, dim:] * shrink + part[:, dim:]
        return carry

    lax.fori_loop(bounds_ref[0], bounds_ref[1], step, 0)
    for head in range(heads):
        out_ref[:, head * dim : (head + 1) * dim] = (
            mixed[head, :, :dim] / mixed[head, :, dim:]
        ).astype(out_ref.dtype)


def key_bounds(query_seg, segment_ids):
    low = jnp.sum(segment_ids < query_seg[0], dtype=jnp.int32)
    high = jnp.sum(segment_ids <= query_seg[-1], dtype=jnp.int32)
    return jnp.stack([low // KEY_TILE, (high + KEY_TILE - 1) // KEY_TILE])


def attend(query, keys, values, me, bounds, query_seg, key_seg, factor):
    rows, cols = query.shape
    pieces = [array for array, _ in keys + values]
    places = tuple((0, at) for _, at in keys) + tuple((1, at) for _, at in values)
    count = len(pieces)
    tokens = key_seg.shape[0] * KEY_TILE
    dim = HEAD_DIM
    heads = cols // dim
    smem = pl.BlockSpec(memory_space=pltpu.SMEM)
    whole = pl.BlockSpec(memory_space=pltpu.VMEM)
    return pl.pallas_call(
        functools.partial(attend_kernel, places),
        in_specs=[smem, smem, whole] + [pl.BlockSpec(memory_space=pl.ANY)] * count + [whole] * 3,
        out_specs=whole,
        scratch_shapes=[
            pltpu.VMEM((tokens, cols), jnp.bfloat16),
            pltpu.VMEM((tokens, cols), jnp.bfloat16),
            pltpu.VMEM((heads, rows, dim), jnp.float32),
            pltpu.VMEM((heads, rows, 2 * dim), jnp.float32),
            pltpu.SemaphoreType.DMA((2, count // 2)),
        ],
        out_shape=jax.ShapeDtypeStruct((rows, cols), jnp.bfloat16),
        compiler_params=pltpu.CompilerParams(vmem_limit_bytes=VMEM),
        cost_estimate=pl.CostEstimate(
            flops=2 * rows * tokens * cols,
            bytes_accessed=4 * tokens * cols + 4 * rows * cols,
            transcendentals=rows * tokens * heads // 2,
        ),
        name="attend",
    )(me.reshape(1), bounds, query, *pieces, query_seg, key_seg, factor)


def pages_kernel(places, me_ref, page_ref, *refs):
    count = len(places)
    pieces, rest = refs[:count], refs[count:]
    scale_ref, (out_refs, held, sems) = (rest[0] if len(rest) == 5 else None), (
        rest[-4:-2],
        rest[-2],
        rest[-1],
    )
    me = me_ref[0]
    wanted = held.shape[0]
    per_block = pieces[0].shape[1] // PAGE
    waits = []
    for number in range(wanted):
        page = page_ref[number]
        rows = pl.ds(pl.multiple_of((page % per_block) * PAGE, PAGE), PAGE)
        target, sem = held.at[number], sems.at[number]
        for owner, (piece, at) in enumerate(zip(pieces, places)):

            @pl.when((page // per_block) == (me ^ owner))
            def _(source=piece.at[at, rows, :], target=target, sem=sem):
                pltpu.make_async_copy(source, target, sem).start()

        waits.append(pltpu.make_async_copy(pieces[0].at[0, pl.ds(0, PAGE), :], target, sem))
    for number in range(wanted):
        waits[number].wait()
        page = held[number]
        if scale_ref is not None:
            scale = jnp.broadcast_to(scale_ref[page_ref[number]], (128, PAGE))
            page = page.astype(jnp.float32) * jnp.transpose(scale)[:, :1]
        each = wanted // 2
        out_refs[number // each][number % each] = page.astype(jnp.bfloat16)


def pick_pages(pieces, me, pages, scale):
    _, rows, cols = pieces[0][0].shape
    wanted = pages.shape[0]
    smem = pl.BlockSpec(memory_space=pltpu.SMEM)
    whole = pl.BlockSpec(memory_space=pltpu.VMEM)
    extra = [] if scale is None else [scale]
    return pl.pallas_call(
        functools.partial(pages_kernel, tuple(at for _, at in pieces)),
        in_specs=[smem, smem]
        + [pl.BlockSpec(memory_space=pl.ANY)] * len(pieces)
        + [whole] * len(extra),
        out_specs=[whole] * 2,
        out_shape=[jax.ShapeDtypeStruct((wanted // 2, PAGE, cols), jnp.bfloat16)] * 2,
        scratch_shapes=[
            pltpu.VMEM((wanted, PAGE, cols), jnp.bfloat16),
            pltpu.SemaphoreType.DMA((wanted,)),
        ],
        compiler_params=pltpu.CompilerParams(vmem_limit_bytes=VMEM),
        cost_estimate=pl.CostEstimate(flops=0, bytes_accessed=0, transcendentals=0),
        name="pick_pages",
    )(me.reshape(1), pages, *[array for array, _ in pieces], *extra)


def own_pages(page_table, start, count):
    page_total = page_table.shape[0]
    inverse = (
        jnp.zeros((page_total,), jnp.int32)
        .at[page_table]
        .set(jnp.arange(page_total, dtype=jnp.int32))
    )
    return lax.dynamic_slice_in_dim(inverse, start, count, 0)


def whole_heads(ring, hidden, modulation, weights, gains, positions, segment_ids, page_table):
    tok_rows = hidden.shape[0]
    me = lax.axis_index("row")
    full_rows = lax.all_gather(hidden, "col", axis=1, tiled=True)
    modulated = modulate(full_rows.astype(jnp.float32), modulation)
    width = full_rows.shape[1]
    raws = [
        jnp.dot(
            modulated,
            lax.all_gather(weight, "row", axis=0, tiled=True),
            preferred_element_type=jnp.float32,
        )
        for weight in weights
    ]
    squares = lax.psum(tuple(jnp.sum(raw * raw, axis=1) for raw in raws[:2]), "col")
    tables = rotary_lanes(positions, HEAD_DIM)
    query, key = [
        turn([raw], total[None], gain[None], [tables], width)[0]
        for raw, total, gain in zip(raws, squares, gains)
    ]
    held = lax.all_gather(jnp.stack([key, raws[2].astype(jnp.bfloat16)]), "row", axis=0)
    keys, values = [[(held[number], kind) for number in range(ring)] for kind in range(2)]
    none = jnp.zeros((), jnp.int32)
    query_seg = lax.dynamic_slice_in_dim(segment_ids, me * tok_rows, tok_rows, 0)
    key_seg = segment_ids.astype(jnp.float32).reshape(-1, 1, KEY_TILE)
    attended = attend(
        query,
        keys,
        values,
        none,
        key_bounds(query_seg, segment_ids),
        query_seg.astype(jnp.float32)[None, :],
        key_seg,
        jnp.full_like(key_seg, HEAD_DIM ** (-0.5) * LOG2E),
    )
    count = tok_rows // PAGE
    pages = own_pages(page_table, me * count, count)
    pages = jnp.concatenate([pages, pages])
    picked = [pick_pages(pieces, none, pages, None)[0] for pieces in (keys, values)]
    return attended, jnp.stack(picked)


def split_heads(ring, ranks, hidden, modulation, weights, gains, positions, segment_ids, page_table):
    tok_rows, shard = hidden.shape
    width = ranks * shard
    me = lax.axis_index("row")
    rank = lax.axis_index("col")
    top = ring // 2
    half = me // top
    cols = weights[0].shape[1] // 2
    hops = []
    bit = top // 2
    while bit:
        hops.append(bit)
        bit //= 2

    def swap(value, bit):
        return lax.ppermute(value, "row", [(i, i ^ bit) for i in range(ring)])

    def across(value, step):
        return lax.ppermute(value, "col", [(c, c ^ step) for c in range(ranks)])

    def spread(blocks, bits):
        for bit in bits:
            blocks.update({number | bit: swap(blocks[number], bit) for number in list(blocks)})
        return blocks

    def in_order(mine, other, axis):
        return jnp.where(
            half == 0,
            jnp.concatenate([mine, other], axis=axis),
            jnp.concatenate([other, mine], axis=axis),
        )

    hidden_all = lax.all_gather(hidden, "col", axis=0)
    w_query, w_key, w_value = weights
    own, send_pair, send_single = cut((w_key, w_value, w_query), half)
    first, rest_hops = hops[0], hops[1:]
    pair, single = swap(send_pair, top), swap(send_single, top)
    next_own = swap(own, first)
    own_blocks = spread({0: own}, rest_hops)

    rows = hidden.astype(jnp.float32)
    local_mean = jnp.mean(rows, axis=1)
    local_square = jnp.sum(jnp.square(rows - local_mean[:, None]), axis=1)
    stats = jnp.stack([local_mean, local_square])
    all_stats = [stats] + [across(stats, step) for step in range(1, ranks)]
    average = sum(part[0] for part in all_stats) / ranks
    variance = (
        sum(part[1] + shard * jnp.square(part[0] - average) for part in all_stats) / width
    )
    small = jnp.concatenate(
        [jnp.stack([average, lax.rsqrt(variance + epsilon)]), positions.astype(jnp.float32)]
    )
    small_other = swap(small, top)
    moved = (pair, single, next_own, own_blocks, small, small_other)
    moved, hidden_late = lax.optimization_barrier((moved, hidden))
    pair, single, next_own, own_blocks, small, small_other = moved

    next_single = swap(single, first)
    other_rows = swap(hidden_late, top)
    pair_blocks = spread({0: pair}, rest_hops)
    single_blocks = spread({0: single}, rest_hops)
    next_own_blocks = spread({0: next_own}, rest_hops)
    early = tok_rows * 5 // 12 // 16 * 16
    sent = jnp.concatenate(
        [
            lax.dynamic_slice(hidden_all, (rank ^ step, early, 0), (1, tok_rows - early, shard))
            for step in range(1, ranks)
        ]
    ).reshape(-1, shard)
    moved = (next_single, other_rows, pair_blocks, single_blocks, next_own_blocks, sent)
    plain = (small, small_other, segment_ids, page_table, gains)
    moved, hidden_all, plain = lax.optimization_barrier((moved, hidden_all, plain))
    next_single, other_rows, pair_blocks, single_blocks, next_own_blocks, sent = moved
    small, small_other, segment_ids, page_table, gains = plain

    rest = swap(sent, top)
    next_pair = swap(pair_blocks[0], first)
    early_shards = [across(other_rows[:early], step) for step in range(1, ranks)]
    sources, spots = [], [None] * ring
    for number in own_blocks:
        for offset, whole in ((0, own_blocks), (first, next_own_blocks)):
            spots[number | offset] = tuple((len(sources), m) for m in range(3))
            sources.append(whole[number])
        at = len(sources)
        spots[number | top] = ((at, 0), (at, 1), (at + 1, 0))
        sources.extend([pair_blocks[number], single_blocks[number]])
    here = tuple(number for number in range(ring) if spots[number] is not None)
    late = tuple(number for number in range(ring) if spots[number] is None)
    own_parts = ((tok_rows, (0,), True),)
    place = jnp.stack([me, rank]).astype(jnp.int32)
    (partial,) = project(
        place,
        small[:2],
        modulation,
        own_parts,
        here,
        [hidden_all],
        tuple(spots),
        list(sources),
        None,
        None,
    )
    tables = [rotary_lanes(part[2:], HEAD_DIM) for part in (small, small_other)]
    q_gain, k_gain = [
        lax.dynamic_slice_in_dim(gain, half * cols, cols, 0)[None, :] for gain in gains
    ]
    count = tok_rows // PAGE
    pages = jnp.concatenate(
        [own_pages(page_table, owner * count, count) for owner in (me ^ top, me)]
    )
    query_segs = [
        lax.dynamic_slice_in_dim(segment_ids, owner * tok_rows, tok_rows, 0)
        for owner in (me, me ^ top)
    ]
    bounds = [key_bounds(seg, segment_ids) for seg in query_segs]
    query_segs = [seg.astype(jnp.float32)[None, :] for seg in query_segs]
    key_seg = segment_ids.astype(jnp.float32).reshape(-1, 1, KEY_TILE)
    prepared = (tables, q_gain, k_gain, pages, query_segs, key_seg, bounds)
    moved = (next_pair, next_single, rest, early_shards)
    moved, prepared, partial = lax.optimization_barrier((moved, prepared, partial))
    next_pair, next_single, rest, early_shards = moved
    tables, q_gain, k_gain, pages, query_segs, key_seg, bounds = prepared

    next_pair_blocks = spread({0: next_pair}, rest_hops)
    next_single_blocks = spread({0: next_single}, rest_hops)
    for number in own_blocks:
        at = len(sources)
        spots[number | top | first] = ((at, 0), (at, 1), (at + 1, 0))
        sources.extend([next_pair_blocks[number], next_single_blocks[number]])
    other_parts = (
        (early, (0,) * ranks, False),
        (
            tok_rows - early,
            (early,) + tuple(step * (tok_rows - early) for step in range(ranks - 1)),
            False,
        ),
    )
    late_sources = [part for number in own_blocks for part in (next_pair_blocks[number], next_single_blocks[number])]
    late_spots = list(spots)
    for at, number in enumerate(own_blocks):
        late_spots[number | top | first] = ((2 * at, 0), (2 * at, 1), (2 * at + 1, 0))
    own_query, own_squares, own_held = project(
        place,
        small[:2],
        modulation,
        own_parts,
        late,
        [hidden_all],
        tuple(late_spots),
        late_sources,
        partial,
        (k_gain, *tables[0]),
    )
    own_ahead = swap(own_held, first)
    other_query, other_squares, other_key, other_value = project(
        place,
        small_other[:2],
        modulation,
        other_parts,
        tuple(range(ring)),
        [other_rows] + early_shards + [other_rows] + [rest] * (ranks - 1),
        tuple(spots),
        sources,
        None,
        (k_gain, *tables[1]),
        joint=False,
    )
    value_ahead = swap(other_value, first)

    squares = jnp.stack([own_squares, other_squares])
    squares = squares + swap(squares, top)[::-1]
    bit = 1
    while bit < ranks:
        squares = squares + across(squares, bit)
        bit *= 2
    query = turn([own_query, other_query], squares[:, 1], q_gain, tables, width)
    squares, query, own_ahead, value_ahead = lax.optimization_barrier(
        (squares, query, own_ahead, value_ahead)
    )
    key_ahead = swap(other_key, first)
    key_squares = spread({0: squares[:, 0]}, hops)
    key_squares, key_ahead, own_ahead, value_ahead = lax.optimization_barrier(
        (key_squares, key_ahead, own_ahead, value_ahead)
    )
    held = spread({0: own_held, first: own_ahead}, rest_hops)
    other_values = spread({0: other_value, first: value_ahead}, rest_hops)
    values = [(held[n], 1) for n in range(top)] + [(other_values[n], 0) for n in range(top)]
    values_picked = pick_pages(values, me, pages, None)
    values_other = swap(values_picked[0], top)
    other_keys = spread({0: other_key, first: key_ahead}, rest_hops)
    keys = [(held[n], 0) for n in range(top)] + [(other_keys[n], 0) for n in range(top)]
    blocks = jnp.stack([key_squares[n % top][n // top] for n in range(ring)])
    scale = lax.rsqrt(blocks / width + epsilon)
    scale = jnp.concatenate(
        [lax.dynamic_slice_in_dim(scale, me ^ owner, 1, 0) for owner in range(ring)]
    )
    factor = (scale * (HEAD_DIM ** (-0.5) * LOG2E)).reshape(-1, 1, KEY_TILE)
    keys_picked = pick_pages(keys, me, pages, scale.reshape(-1, 1, PAGE))
    query, keys_picked = lax.optimization_barrier((query, keys_picked))
    keys_other = swap(keys_picked[0], top)

    def attended(number):
        return attend(
            query[number], keys, values, me, bounds[number], query_segs[number], key_seg, factor
        )

    for_other = attended(1)
    query, for_other = lax.optimization_barrier((query, for_other))
    from_other = swap(for_other, top)
    for_me = attended(0)
    page_store = [
        in_order(keys_picked[1], keys_other, -1),
        in_order(values_picked[1], values_other, -1),
    ]
    return in_order(for_me, from_other, -1), jnp.stack(page_store)


def solution(mesh):
    ring, ranks = mesh.shape["row"], mesh.shape["col"]

    def body(
        hidden, modulation, w_query, w_key, w_value, q_gain, k_gain, positions, segment_ids, page_table
    ):
        rest = (
            hidden,
            modulation,
            (w_query, w_key, w_value),
            (q_gain, k_gain),
            positions,
            segment_ids,
            page_table,
        )
        heads = w_query.shape[1] // HEAD_DIM
        feats, shard = w_query.shape[0], hidden.shape[1]
        powers = ring & (ring - 1) == 0 and ranks & (ranks - 1) == 0
        if heads % 2 == 0 and ring >= 8 and powers and feats % 128 == 0 and shard % feats == 0:
            return split_heads(ring, ranks, *rest)
        return whole_heads(ring, *rest)

    in_specs = (
        P("row", "col"),
        P(),
        P("row", "col"),
        P("row", "col"),
        P("row", "col"),
        P("col"),
        P("col"),
        P(None, "row"),
        P(),
        P(),
    )
    out_specs = (P("row", "col"), P(None, "row", None, "col"))
    return jax.shard_map(body, mesh=mesh, in_specs=in_specs, out_specs=out_specs, check_vma=False)
```

```python
import functools
import jax
import jax.numpy as jnp
from jax import lax
from jax.experimental import pallas as pl
from jax.experimental.pallas import tpu as pltpu
from jax.sharding import PartitionSpec as P

HEAD_DIM = 128
PAGE = 128
KEY_TILE = 512
VMEM = 60 * 1024 * 1024
LOG2E = 1.4426950408889634

epsilon = 1e-06


def rotary_lanes(positions, head_dim):
    pair_count = head_dim // 2
    frame_pairs = pair_count - 2 * (pair_count // 3)
    side_pairs = pair_count // 3
    column = jnp.arange(head_dim) // 2
    frame_rate = 10000.0 ** (-column.astype(jnp.float32) / frame_pairs)
    height_rate = 10000.0 ** (-(column - frame_pairs).astype(jnp.float32) / side_pairs)
    width_rate = 10000.0 ** (-(column - frame_pairs - side_pairs).astype(jnp.float32) / side_pairs)
    coords = positions.astype(jnp.float32)
    angles = jnp.where(
        column < frame_pairs,
        coords[0][:, None] * frame_rate,
        jnp.where(
            column < frame_pairs + side_pairs,
            coords[1][:, None] * height_rate,
            coords[2][:, None] * width_rate,
        ),
    )
    sine = jnp.sin(angles)
    even = (jnp.arange(head_dim) % 2 == 0)[None, :]
    return jnp.cos(angles), jnp.where(even, -sine, 0.0), jnp.where(even, 0.0, sine)


def modulate(activations, modulation):
    average = jnp.mean(activations, axis=1, keepdims=True)
    centred = activations - average
    variance = jnp.mean(centred * centred, axis=1, keepdims=True)
    normed = centred * lax.rsqrt(variance + epsilon)
    return (normed * (1.0 + modulation[1]) + modulation[0]).astype(jnp.bfloat16)


def cut_kernel(half_ref, *refs):
    weights, outs, sems = refs[:3], refs[3:6], refs[6]
    cols = outs[0].shape[2]
    half = half_ref[0]
    copies = []
    for number, weight in enumerate(weights):
        send, at = (1, number) if number < 2 else (2, 0)
        for which, target in ((half, outs[0].at[number]), (1 - half, outs[send].at[at])):
            span = pl.ds(pl.multiple_of(which * cols, cols), cols)
            copies.append(
                pltpu.make_async_copy(
                    weight.at[:, span], target, sems.at[number, len(copies) % 2]
                )
            )
            copies[-1].start()
    for copy in copies:
        copy.wait()


def cut(weights, half):
    rows, width = weights[0].shape
    cols = width // 2
    whole = pl.BlockSpec(memory_space=pltpu.VMEM)
    return pl.pallas_call(
        cut_kernel,
        in_specs=[pl.BlockSpec(memory_space=pltpu.SMEM)] + [pl.BlockSpec(memory_space=pl.ANY)] * 3,
        out_specs=[whole] * 3,
        out_shape=[jax.ShapeDtypeStruct((size, rows, cols), jnp.bfloat16) for size in (3, 2, 1)],
        scratch_shapes=[pltpu.SemaphoreType.DMA((3, 2))],
        compiler_params=pltpu.CompilerParams(vmem_limit_bytes=VMEM),
        cost_estimate=pl.CostEstimate(
            flops=0, bytes_accessed=12 * rows * width, transcendentals=0
        ),
        name="cut",
    )(half.reshape(1), *weights)


def turned(values, gain, tables, at):
    dim = tables[0].shape[1]
    cols = slice(at * dim, (at + 1) * dim)
    own, upper, lower = tables
    part = values[:, cols] * gain[:, cols]
    return part * own + pltpu.roll(part, dim - 1, 1) * upper + pltpu.roll(part, 1, 1) * lower


def project_kernel(
    parts, blocks, spots, first, final, in_count, place_ref, stats_ref, modulation_ref, *refs
):
    shard_count = sum(len(part[1]) for part in parts)
    out_count = len(refs) - 6 - in_count
    shards, rest = refs[:shard_count], refs[shard_count:]
    total, raws, weights, ready, raw_sems, weight_sems = rest[-6:]
    outs, sources = rest[-6 - out_count : -6], rest[: -6 - out_count]
    if final:
        sources, (gain_ref, own_ref, upper_ref, lower_ref) = sources[:-4], sources[-4:]
    if not first:
        sources, partial_ref = sources[:-1], sources[-1]
    me, rank = place_ref[0], place_ref[1]
    feats, cols = weights.shape[2:]
    rows = raws.shape[1]
    per_rank = shards[0].shape[-1] // feats
    copies = {}
    for slot, block in enumerate(blocks):
        owner = me ^ block
        span = pl.ds(pl.multiple_of((owner % per_rank) * feats, feats), feats)
        holder = owner // per_rank
        mine, begin, at = [], 0, 0
        for number, (length, places, by_rank) in enumerate(parts):
            held = shards[at : at + len(places)]
            at += len(places)
            target = raws.at[slot, pl.ds(begin, length), :]
            begin += length
            sem = raw_sems.at[slot, number]
            if by_rank:
                copy = pltpu.make_async_copy(
                    held[0].at[holder, pl.ds(places[0], length), span], target, sem
                )
                copy.start()
            else:
                for step, (ref, skip) in enumerate(zip(held, places)):
                    source = ref.at[pl.ds(skip, length), span]

                    @pl.when((holder ^ rank) == step)
                    def _(source=source, target=target, sem=sem):
                        pltpu.make_async_copy(source, target, sem).start()

                copy = pltpu.make_async_copy(source, target, sem)
            mine.append(copy)
        matrices = [
            pltpu.make_async_copy(
                sources[source].at[place], weights.at[slot, number], weight_sems.at[slot, number]
            )
            for number, (source, place) in enumerate(spots[block])
        ]
        for copy in matrices:
            copy.start()
        copies[slot] = (mine, matrices)

    def column(at):
        return jnp.transpose(jnp.broadcast_to(stats_ref[at : at + 1, :], (128, rows)))

    mean, scale = column(0), column(1)

    def prepare(first_slot):
        for slot in (first_slot, first_slot + 1):
            for copy in copies[slot][0]:
                copy.wait()
            span = pl.ds(pl.multiple_of((me ^ blocks[slot]) * feats, feats), feats)
            shift = modulation_ref[0:1, span]
            gain = 1.0 + modulation_ref[1:2, span]
            left = (slot - first_slot) * feats
            for start in range(0, feats, 128):
                lanes = slice(start, start + 128)
                part = raws[slot, :, lanes].astype(jnp.float32)
                part = (part - mean) * scale * gain[:, lanes] + shift[:, lanes]
                ready[first_slot // 2 % 2, :, left + start : left + start + 128] = part.astype(
                    jnp.bfloat16
                )

    prepare(0)
    for slot in range(0, len(blocks), 2):
        for copy in copies[slot][1] + copies[slot + 1][1]:
            copy.wait()
        if slot + 2 < len(blocks):
            prepare(slot + 2)
        right = jnp.concatenate(
            [
                jnp.concatenate([weights[slot, m], weights[slot + 1, m]], axis=0)
                for m in range(3)
            ],
            axis=1,
        )
        part = jnp.dot(ready[slot // 2 % 2], right, preferred_element_type=jnp.float32)
        if slot:
            part = part + total[...]
        elif not first:
            part = part + partial_ref[...]
        if slot + 2 < len(blocks):
            total[...] = part
    if not final:
        outs[0][...] = part
        return
    query_ref, squares_ref = outs[:2]
    key_ref, value_ref = outs[2:] if len(outs) == 4 else (outs[2], outs[2])
    key, value, query = [part[:, m * cols : (m + 1) * cols] for m in range(3)]
    query_ref[...] = query
    value_ref[value_ref.shape[0] - 1] = value.astype(jnp.bfloat16)
    tables = (own_ref[...], upper_ref[...], lower_ref[...])
    for head in range(cols // HEAD_DIM):
        lanes = slice(head * HEAD_DIM, (head + 1) * HEAD_DIM)
        key_ref[0, :, lanes] = turned(key, gain_ref, tables, head).astype(jnp.bfloat16)
    for kind, raw in enumerate((key, query)):
        summed = jnp.sum(raw * raw, axis=1, keepdims=True)
        summed = jnp.transpose(jnp.broadcast_to(summed, (rows, 128)))
        squares_ref[kind : kind + 1, :] = summed[:1]


def project(
    place, stats, modulation, parts, blocks, shards, spots, sources, partial, finish, joint=True
):
    rows = sum(part[0] for part in parts)
    _, feats, cols = sources[0].shape
    count = len(blocks)
    anywhere = pl.BlockSpec(memory_space=pl.ANY)
    whole = pl.BlockSpec(memory_space=pltpu.VMEM)
    out_shape = [jax.ShapeDtypeStruct((rows, 3 * cols), jnp.float32)]
    extra = [] if partial is None else [partial]
    if finish is not None:
        extra.extend(finish)
        held = [2] if joint else [1, 1]
        out_shape = [
            jax.ShapeDtypeStruct((rows, cols), jnp.float32),
            jax.ShapeDtypeStruct((2, rows), jnp.float32),
        ] + [jax.ShapeDtypeStruct((size, rows, cols), jnp.bfloat16) for size in held]
    return pl.pallas_call(
        functools.partial(
            project_kernel,
            parts,
            blocks,
            spots,
            partial is None,
            finish is not None,
            len(shards) + len(sources) + len(extra),
        ),
        in_specs=[pl.BlockSpec(memory_space=pltpu.SMEM), whole, whole]
        + [anywhere] * (len(shards) + len(sources))
        + [whole] * len(extra),
        out_specs=[whole] * len(out_shape),
        out_shape=out_shape,
        scratch_shapes=[
            pltpu.VMEM((rows, 3 * cols), jnp.float32),
            pltpu.VMEM((count, rows, feats), jnp.bfloat16),
            pltpu.VMEM((count, 3, feats, cols), jnp.bfloat16),
            pltpu.VMEM((2, rows, 2 * feats), jnp.bfloat16),
            pltpu.SemaphoreType.DMA((count, len(parts))),
            pltpu.SemaphoreType.DMA((count, 3)),
        ],
        compiler_params=pltpu.CompilerParams(vmem_limit_bytes=VMEM),
        cost_estimate=pl.CostEstimate(
            flops=6 * rows * count * feats * cols,
            bytes_accessed=2 * count * feats * (rows + 3 * cols) + 12 * rows * cols,
            transcendentals=0,
        ),
        name="project",
    )(place, stats, modulation, *shards, *sources, *extra)


def turn_kernel(count, width, squares_ref, gain_ref, *refs):
    for number in range(count):
        raw_ref, out_ref = refs[number], refs[4 * count + number]
        tables = [ref[...] for ref in refs[count + 3 * number : count + 3 * number + 3]]
        rows, cols = raw_ref.shape
        scale = lax.rsqrt(squares_ref[number : number + 1, :] * (1.0 / width) + epsilon)
        raw = raw_ref[...] * jnp.transpose(jnp.broadcast_to(scale, (128, rows)))[:, :1]
        for head in range(cols // HEAD_DIM):
            out_ref[:, head * HEAD_DIM : (head + 1) * HEAD_DIM] = turned(
                raw, gain_ref, tables, head
            ).astype(jnp.bfloat16)


def turn(raws, squares, gain, tables, width):
    count = len(raws)
    rows, cols = raws[0].shape
    whole = pl.BlockSpec(memory_space=pltpu.VMEM)
    return pl.pallas_call(
        functools.partial(turn_kernel, count, width),
        in_specs=[whole] * (2 + 4 * count),
        out_specs=[whole] * count,
        out_shape=[jax.ShapeDtypeStruct((rows, cols), jnp.bfloat16)] * count,
        compiler_params=pltpu.CompilerParams(vmem_limit_bytes=VMEM),
        cost_estimate=pl.CostEstimate(flops=0, bytes_accessed=0, transcendentals=0),
        name="turn",
    )(squares, gain, *raws, *[part for table in tables for part in table])


def attend_kernel(places, me_ref, bounds_ref, q_ref, *refs):
    count = len(places)
    pieces, (query_seg_ref, key_seg_ref, factor_ref) = refs[:count], refs[count : count + 3]
    out_ref, keys, values, highest, mixed, sems = refs[count + 3 :]
    me = me_ref[0]
    rows = pieces[0].shape[1]
    copies = []
    for number, (piece, (kind, at)) in enumerate(zip(pieces, places)):
        owner = number % (count // 2)
        where = pl.ds(pl.multiple_of((me ^ owner) * rows, rows), rows)
        held = (keys, values)[kind]
        copies.append(
            pltpu.make_async_copy(piece.at[at], held.at[where, :], sems.at[kind, owner])
        )
    for copy in copies:
        copy.start()
    dim = HEAD_DIM
    heads = q_ref.shape[1] // dim
    ones = jnp.ones((KEY_TILE, dim), jnp.bfloat16)
    highest[...] = jnp.full_like(highest, -1e29)
    mixed[...] = jnp.zeros_like(mixed)
    for copy in copies:
        copy.wait()

    query_seg = jnp.transpose(jnp.broadcast_to(query_seg_ref[...], (128, rows)))[:, :1]

    def step(block, carry):
        where = pl.ds(pl.multiple_of(block * KEY_TILE, KEY_TILE), KEY_TILE)
        same = query_seg == key_seg_ref[block]
        factor = factor_ref[block]
        for head in range(heads):
            cols = slice(head * dim, (head + 1) * dim)
            scores = lax.dot_general(
                q_ref[:, cols],
                keys[where, cols],
                (((1,), (1,)), ((), ())),
                preferred_element_type=jnp.float32,
            )
            scores = jnp.where(same, scores * factor, -1e30)
            former = highest[head]
            newest = jnp.maximum(former, jnp.max(scores, axis=1, keepdims=True))
            highest[head] = newest
            weights = jnp.exp2(scores - newest[:, :1]).astype(jnp.bfloat16)
            right = jnp.concatenate([values[where, cols], ones], axis=1)
            part = jnp.dot(weights, right, preferred_element_type=jnp.float32)
            shrink = jnp.exp2(former - newest)
            mixed[head, :, :dim] = mixed[head, :, :dim] * shrink + part[:, :dim]
            mixed[head, :, dim:] = mixed[head, :, dim:] * shrink + part[:, dim:]
        return carry

    lax.fori_loop(bounds_ref[0], bounds_ref[1], step, 0)
    for head in range(heads):
        out_ref[:, head * dim : (head + 1) * dim] = (
            mixed[head, :, :dim] / mixed[head, :, dim:]
        ).astype(out_ref.dtype)


def key_bounds(query_seg, segment_ids):
    low = jnp.sum(segment_ids < query_seg[0], dtype=jnp.int32)
    high = jnp.sum(segment_ids <= query_seg[-1], dtype=jnp.int32)
    return jnp.stack([low // KEY_TILE, (high + KEY_TILE - 1) // KEY_TILE])


def attend(query, keys, values, me, bounds, query_seg, key_seg, factor):
    rows, cols = query.shape
    pieces = [array for array, _ in keys + values]
    places = tuple((0, at) for _, at in keys) + tuple((1, at) for _, at in values)
    count = len(pieces)
    tokens = key_seg.shape[0] * KEY_TILE
    dim = HEAD_DIM
    heads = cols // dim
    smem = pl.BlockSpec(memory_space=pltpu.SMEM)
    whole = pl.BlockSpec(memory_space=pltpu.VMEM)
    return pl.pallas_call(
        functools.partial(attend_kernel, places),
        in_specs=[smem, smem, whole] + [pl.BlockSpec(memory_space=pl.ANY)] * count + [whole] * 3,
        out_specs=whole,
        scratch_shapes=[
            pltpu.VMEM((tokens, cols), jnp.bfloat16),
            pltpu.VMEM((tokens, cols), jnp.bfloat16),
            pltpu.VMEM((heads, rows, dim), jnp.float32),
            pltpu.VMEM((heads, rows, 2 * dim), jnp.float32),
            pltpu.SemaphoreType.DMA((2, count // 2)),
        ],
        out_shape=jax.ShapeDtypeStruct((rows, cols), jnp.bfloat16),
        compiler_params=pltpu.CompilerParams(vmem_limit_bytes=VMEM),
        cost_estimate=pl.CostEstimate(
            flops=2 * rows * tokens * cols,
            bytes_accessed=4 * tokens * cols + 4 * rows * cols,
            transcendentals=rows * tokens * heads // 2,
        ),
        name="attend",
    )(me.reshape(1), bounds, query, *pieces, query_seg, key_seg, factor)


def pages_kernel(places, me_ref, page_ref, *refs):
    count = len(places)
    pieces, rest = refs[:count], refs[count:]
    scale_ref, (out_refs, held, sems) = (rest[0] if len(rest) == 5 else None), (
        rest[-4:-2],
        rest[-2],
        rest[-1],
    )
    me = me_ref[0]
    wanted = held.shape[0]
    per_block = pieces[0].shape[1] // PAGE
    waits = []
    for number in range(wanted):
        page = page_ref[number]
        rows = pl.ds(pl.multiple_of((page % per_block) * PAGE, PAGE), PAGE)
        target, sem = held.at[number], sems.at[number]
        for owner, (piece, at) in enumerate(zip(pieces, places)):

            @pl.when((page // per_block) == (me ^ owner))
            def _(source=piece.at[at, rows, :], target=target, sem=sem):
                pltpu.make_async_copy(source, target, sem).start()

        waits.append(pltpu.make_async_copy(pieces[0].at[0, pl.ds(0, PAGE), :], target, sem))
    for number in range(wanted):
        waits[number].wait()
        page = held[number]
        if scale_ref is not None:
            scale = jnp.broadcast_to(scale_ref[page_ref[number]], (128, PAGE))
            page = page.astype(jnp.float32) * jnp.transpose(scale)[:, :1]
        each = wanted // 2
        out_refs[number // each][number % each] = page.astype(jnp.bfloat16)


def pick_pages(pieces, me, pages, scale):
    _, rows, cols = pieces[0][0].shape
    wanted = pages.shape[0]
    smem = pl.BlockSpec(memory_space=pltpu.SMEM)
    whole = pl.BlockSpec(memory_space=pltpu.VMEM)
    extra = [] if scale is None else [scale]
    return pl.pallas_call(
        functools.partial(pages_kernel, tuple(at for _, at in pieces)),
        in_specs=[smem, smem]
        + [pl.BlockSpec(memory_space=pl.ANY)] * len(pieces)
        + [whole] * len(extra),
        out_specs=[whole] * 2,
        out_shape=[jax.ShapeDtypeStruct((wanted // 2, PAGE, cols), jnp.bfloat16)] * 2,
        scratch_shapes=[
            pltpu.VMEM((wanted, PAGE, cols), jnp.bfloat16),
            pltpu.SemaphoreType.DMA((wanted,)),
        ],
        compiler_params=pltpu.CompilerParams(vmem_limit_bytes=VMEM),
        cost_estimate=pl.CostEstimate(flops=0, bytes_accessed=0, transcendentals=0),
        name="pick_pages",
    )(me.reshape(1), pages, *[array for array, _ in pieces], *extra)


def own_pages(page_table, start, count):
    page_total = page_table.shape[0]
    inverse = (
        jnp.zeros((page_total,), jnp.int32)
        .at[page_table]
        .set(jnp.arange(page_total, dtype=jnp.int32))
    )
    return lax.dynamic_slice_in_dim(inverse, start, count, 0)


def whole_heads(ring, hidden, modulation, weights, gains, positions, segment_ids, page_table):
    tok_rows = hidden.shape[0]
    me = lax.axis_index("row")
    full_rows = lax.all_gather(hidden, "col", axis=1, tiled=True)
    modulated = modulate(full_rows.astype(jnp.float32), modulation)
    width = full_rows.shape[1]
    raws = [
        jnp.dot(
            modulated,
            lax.all_gather(weight, "row", axis=0, tiled=True),
            preferred_element_type=jnp.float32,
        )
        for weight in weights
    ]
    squares = lax.psum(tuple(jnp.sum(raw * raw, axis=1) for raw in raws[:2]), "col")
    tables = rotary_lanes(positions, HEAD_DIM)
    query, key = [
        turn([raw], total[None], gain[None], [tables], width)[0]
        for raw, total, gain in zip(raws, squares, gains)
    ]
    held = lax.all_gather(jnp.stack([key, raws[2].astype(jnp.bfloat16)]), "row", axis=0)
    keys, values = [[(held[number], kind) for number in range(ring)] for kind in range(2)]
    none = jnp.zeros((), jnp.int32)
    query_seg = lax.dynamic_slice_in_dim(segment_ids, me * tok_rows, tok_rows, 0)
    key_seg = segment_ids.astype(jnp.float32).reshape(-1, 1, KEY_TILE)
    attended = attend(
        query,
        keys,
        values,
        none,
        key_bounds(query_seg, segment_ids),
        query_seg.astype(jnp.float32)[None, :],
        key_seg,
        jnp.full_like(key_seg, HEAD_DIM ** (-0.5) * LOG2E),
    )
    count = tok_rows // PAGE
    pages = own_pages(page_table, me * count, count)
    pages = jnp.concatenate([pages, pages])
    picked = [pick_pages(pieces, none, pages, None)[0] for pieces in (keys, values)]
    return attended, jnp.stack(picked)


def split_heads(ring, ranks, hidden, modulation, weights, gains, positions, segment_ids, page_table):
    tok_rows, shard = hidden.shape
    width = ranks * shard
    me = lax.axis_index("row")
    rank = lax.axis_index("col")
    top = ring // 2
    half = me // top
    cols = weights[0].shape[1] // 2
    hops = []
    bit = top // 2
    while bit:
        hops.append(bit)
        bit //= 2

    def swap(value, bit):
        return lax.ppermute(value, "row", [(i, i ^ bit) for i in range(ring)])

    def across(value, step):
        return lax.ppermute(value, "col", [(c, c ^ step) for c in range(ranks)])

    def spread(blocks, bits):
        for bit in bits:
            blocks.update({number | bit: swap(blocks[number], bit) for number in list(blocks)})
        return blocks

    def in_order(mine, other, axis):
        return jnp.where(
            half == 0,
            jnp.concatenate([mine, other], axis=axis),
            jnp.concatenate([other, mine], axis=axis),
        )

    hidden_all = lax.all_gather(hidden, "col", axis=0)
    w_query, w_key, w_value = weights
    own, send_pair, send_single = cut((w_key, w_value, w_query), half)
    first, rest_hops = hops[0], hops[1:]
    pair, single = swap(send_pair, top), swap(send_single, top)
    next_own = swap(own, first)
    own_blocks = spread({0: own}, rest_hops)

    rows = hidden.astype(jnp.float32)
    local_mean = jnp.mean(rows, axis=1)
    local_square = jnp.sum(jnp.square(rows - local_mean[:, None]), axis=1)
    stats = jnp.stack([local_mean, local_square])
    all_stats = [stats] + [across(stats, step) for step in range(1, ranks)]
    average = sum(part[0] for part in all_stats) / ranks
    variance = (
        sum(part[1] + shard * jnp.square(part[0] - average) for part in all_stats) / width
    )
    small = jnp.concatenate(
        [jnp.stack([average, lax.rsqrt(variance + epsilon)]), positions.astype(jnp.float32)]
    )
    small_other = swap(small, top)
    moved = (pair, single, next_own, own_blocks, small, small_other)
    moved, hidden_late = lax.optimization_barrier((moved, hidden))
    pair, single, next_own, own_blocks, small, small_other = moved

    next_single = swap(single, first)
    other_rows = swap(hidden_late, top)
    pair_blocks = spread({0: pair}, rest_hops)
    single_blocks = spread({0: single}, rest_hops)
    next_own_blocks = spread({0: next_own}, rest_hops)
    early = tok_rows * 11 // 24 // 16 * 16
    sent = jnp.concatenate(
        [
            lax.dynamic_slice(hidden_all, (rank ^ step, early, 0), (1, tok_rows - early, shard))
            for step in range(1, ranks)
        ]
    ).reshape(-1, shard)
    moved = (next_single, other_rows, pair_blocks, single_blocks, next_own_blocks, sent)
    plain = (small, small_other, segment_ids, page_table, gains)
    moved, hidden_all, plain = lax.optimization_barrier((moved, hidden_all, plain))
    next_single, other_rows, pair_blocks, single_blocks, next_own_blocks, sent = moved
    small, small_other, segment_ids, page_table, gains = plain

    rest = swap(sent, top)
    next_pair = swap(pair_blocks[0], first)
    early_shards = [across(other_rows[:early], step) for step in range(1, ranks)]
    sources, spots = [], [None] * ring
    for number in own_blocks:
        for offset, whole in ((0, own_blocks), (first, next_own_blocks)):
            spots[number | offset] = tuple((len(sources), m) for m in range(3))
            sources.append(whole[number])
        at = len(sources)
        spots[number | top] = ((at, 0), (at, 1), (at + 1, 0))
        sources.extend([pair_blocks[number], single_blocks[number]])
    here = tuple(number for number in range(ring) if spots[number] is not None)
    late = tuple(number for number in range(ring) if spots[number] is None)
    own_parts = ((tok_rows, (0,), True),)
    place = jnp.stack([me, rank]).astype(jnp.int32)
    (partial,) = project(
        place,
        small[:2],
        modulation,
        own_parts,
        here,
        [hidden_all],
        tuple(spots),
        list(sources),
        None,
        None,
    )
    tables = [rotary_lanes(part[2:], HEAD_DIM) for part in (small, small_other)]
    q_gain, k_gain = [
        lax.dynamic_slice_in_dim(gain, half * cols, cols, 0)[None, :] for gain in gains
    ]
    count = tok_rows // PAGE
    pages = jnp.concatenate(
        [own_pages(page_table, owner * count, count) for owner in (me ^ top, me)]
    )
    query_segs = [
        lax.dynamic_slice_in_dim(segment_ids, owner * tok_rows, tok_rows, 0)
        for owner in (me, me ^ top)
    ]
    bounds = [key_bounds(seg, segment_ids) for seg in query_segs]
    query_segs = [seg.astype(jnp.float32)[None, :] for seg in query_segs]
    key_seg = segment_ids.astype(jnp.float32).reshape(-1, 1, KEY_TILE)
    prepared = (tables, q_gain, k_gain, pages, query_segs, key_seg, bounds)
    moved = (next_pair, next_single, rest, early_shards)
    moved, prepared, partial = lax.optimization_barrier((moved, prepared, partial))
    next_pair, next_single, rest, early_shards = moved
    tables, q_gain, k_gain, pages, query_segs, key_seg, bounds = prepared

    next_pair_blocks = spread({0: next_pair}, rest_hops)
    next_single_blocks = spread({0: next_single}, rest_hops)
    for number in own_blocks:
        at = len(sources)
        spots[number | top | first] = ((at, 0), (at, 1), (at + 1, 0))
        sources.extend([next_pair_blocks[number], next_single_blocks[number]])
    other_parts = (
        (early, (0,) * ranks, False),
        (
            tok_rows - early,
            (early,) + tuple(step * (tok_rows - early) for step in range(ranks - 1)),
            False,
        ),
    )
    late_sources = [part for number in own_blocks for part in (next_pair_blocks[number], next_single_blocks[number])]
    late_spots = list(spots)
    for at, number in enumerate(own_blocks):
        late_spots[number | top | first] = ((2 * at, 0), (2 * at, 1), (2 * at + 1, 0))
    own_query, own_squares, own_held = project(
        place,
        small[:2],
        modulation,
        own_parts,
        late,
        [hidden_all],
        tuple(late_spots),
        late_sources,
        partial,
        (k_gain, *tables[0]),
    )
    own_ahead = swap(own_held, first)
    other_query, other_squares, other_key, other_value = project(
        place,
        small_other[:2],
        modulation,
        other_parts,
        tuple(range(ring)),
        [other_rows] + early_shards + [other_rows] + [rest] * (ranks - 1),
        tuple(spots),
        sources,
        None,
        (k_gain, *tables[1]),
        joint=False,
    )
    value_ahead = swap(other_value, first)

    squares = jnp.stack([own_squares, other_squares])
    squares = squares + swap(squares, top)[::-1]
    bit = 1
    while bit < ranks:
        squares = squares + across(squares, bit)
        bit *= 2
    query = turn([own_query, other_query], squares[:, 1], q_gain, tables, width)
    key_squares = {0: squares[:, 0]}
    key_squares[first] = swap(key_squares[0], first)
    key_squares, query, own_ahead, value_ahead, other_key = lax.optimization_barrier(
        (key_squares, query, own_ahead, value_ahead, other_key)
    )
    key_ahead = swap(other_key, first)
    key_squares = spread(key_squares, rest_hops)
    blocks = jnp.stack([key_squares[n % top][n // top] for n in range(ring)])
    scale = lax.rsqrt(blocks / width + epsilon)
    scale = jnp.concatenate(
        [lax.dynamic_slice_in_dim(scale, me ^ owner, 1, 0) for owner in range(ring)]
    )
    factor = (scale * (HEAD_DIM ** (-0.5) * LOG2E)).reshape(-1, 1, KEY_TILE)
    scale = scale.reshape(-1, 1, PAGE)
    held = spread({0: own_held, first: own_ahead}, rest_hops)
    other_values = spread({0: other_value, first: value_ahead}, rest_hops)
    values = [(held[n], 1) for n in range(top)] + [(other_values[n], 0) for n in range(top)]
    values_picked = pick_pages(values, me, pages, None)
    key_ahead, values_picked, scale, factor = lax.optimization_barrier(
        (key_ahead, values_picked, scale, factor)
    )
    values_other = swap(values_picked[0], top)
    other_keys = spread({0: other_key, first: key_ahead}, rest_hops)
    keys = [(held[n], 0) for n in range(top)] + [(other_keys[n], 0) for n in range(top)]
    keys_picked = pick_pages(keys, me, pages, scale)
    query, keys_picked = lax.optimization_barrier((query, keys_picked))
    keys_other = swap(keys_picked[0], top)

    def attended(number):
        return attend(
            query[number], keys, values, me, bounds[number], query_segs[number], key_seg, factor
        )

    for_other = attended(1)
    query, for_other = lax.optimization_barrier((query, for_other))
    from_other = swap(for_other, top)
    for_me = attended(0)
    page_store = [
        in_order(keys_picked[1], keys_other, -1),
        in_order(values_picked[1], values_other, -1),
    ]
    return in_order(for_me, from_other, -1), jnp.stack(page_store)


def solution(mesh):
    ring, ranks = mesh.shape["row"], mesh.shape["col"]

    def body(
        hidden, modulation, w_query, w_key, w_value, q_gain, k_gain, positions, segment_ids, page_table
    ):
        rest = (
            hidden,
            modulation,
            (w_query, w_key, w_value),
            (q_gain, k_gain),
            positions,
            segment_ids,
            page_table,
        )
        heads = w_query.shape[1] // HEAD_DIM
        feats, shard = w_query.shape[0], hidden.shape[1]
        powers = ring & (ring - 1) == 0 and ranks & (ranks - 1) == 0
        if heads % 2 == 0 and ring >= 8 and powers and feats % 128 == 0 and shard % feats == 0:
            return split_heads(ring, ranks, *rest)
        return whole_heads(ring, *rest)

    in_specs = (
        P("row", "col"),
        P(),
        P("row", "col"),
        P("row", "col"),
        P("row", "col"),
        P("col"),
        P("col"),
        P(None, "row"),
        P(),
        P(),
    )
    out_specs = (P("row", "col"), P(None, "row", None, "col"))
    return jax.shard_map(body, mesh=mesh, in_specs=in_specs, out_specs=out_specs, check_vma=False)
```

```python
import functools
import jax
import jax.numpy as jnp
from jax import lax
from jax.experimental import pallas as pl
from jax.experimental.pallas import tpu as pltpu
from jax.sharding import PartitionSpec as P

HEAD_DIM = 128
PAGE = 128
KEY_TILE = 512
VMEM = 60 * 1024 * 1024
LOG2E = 1.4426950408889634

epsilon = 1e-06


def rotary_lanes(positions, head_dim):
    pair_count = head_dim // 2
    frame_pairs = pair_count - 2 * (pair_count // 3)
    side_pairs = pair_count // 3
    column = jnp.arange(head_dim) // 2
    frame_rate = 10000.0 ** (-column.astype(jnp.float32) / frame_pairs)
    height_rate = 10000.0 ** (-(column - frame_pairs).astype(jnp.float32) / side_pairs)
    width_rate = 10000.0 ** (-(column - frame_pairs - side_pairs).astype(jnp.float32) / side_pairs)
    coords = positions.astype(jnp.float32)
    angles = jnp.where(
        column < frame_pairs,
        coords[0][:, None] * frame_rate,
        jnp.where(
            column < frame_pairs + side_pairs,
            coords[1][:, None] * height_rate,
            coords[2][:, None] * width_rate,
        ),
    )
    sine = jnp.sin(angles)
    even = (jnp.arange(head_dim) % 2 == 0)[None, :]
    return jnp.cos(angles), jnp.where(even, -sine, 0.0), jnp.where(even, 0.0, sine)


def modulate(activations, modulation):
    average = jnp.mean(activations, axis=1, keepdims=True)
    centred = activations - average
    variance = jnp.mean(centred * centred, axis=1, keepdims=True)
    normed = centred * lax.rsqrt(variance + epsilon)
    return (normed * (1.0 + modulation[1]) + modulation[0]).astype(jnp.bfloat16)


def cut_kernel(half_ref, *refs):
    weights, outs, sems = refs[:3], refs[3:6], refs[6]
    cols = outs[0].shape[2]
    half = half_ref[0]
    copies = []
    for number, weight in enumerate(weights):
        send, at = (1, number) if number < 2 else (2, 0)
        for which, target in ((half, outs[0].at[number]), (1 - half, outs[send].at[at])):
            span = pl.ds(pl.multiple_of(which * cols, cols), cols)
            copies.append(
                pltpu.make_async_copy(
                    weight.at[:, span], target, sems.at[number, len(copies) % 2]
                )
            )
            copies[-1].start()
    for copy in copies:
        copy.wait()


def cut(weights, half):
    rows, width = weights[0].shape
    cols = width // 2
    whole = pl.BlockSpec(memory_space=pltpu.VMEM)
    return pl.pallas_call(
        cut_kernel,
        in_specs=[pl.BlockSpec(memory_space=pltpu.SMEM)] + [pl.BlockSpec(memory_space=pl.ANY)] * 3,
        out_specs=[whole] * 3,
        out_shape=[jax.ShapeDtypeStruct((size, rows, cols), jnp.bfloat16) for size in (3, 2, 1)],
        scratch_shapes=[pltpu.SemaphoreType.DMA((3, 2))],
        compiler_params=pltpu.CompilerParams(vmem_limit_bytes=VMEM),
        cost_estimate=pl.CostEstimate(
            flops=0, bytes_accessed=12 * rows * width, transcendentals=0
        ),
        name="cut",
    )(half.reshape(1), *weights)


def turned(values, gain, tables, at):
    dim = tables[0].shape[1]
    cols = slice(at * dim, (at + 1) * dim)
    own, upper, lower = tables
    part = values[:, cols] * gain[:, cols]
    return part * own + pltpu.roll(part, dim - 1, 1) * upper + pltpu.roll(part, 1, 1) * lower


def project_kernel(
    parts, blocks, spots, first, final, in_count, place_ref, stats_ref, modulation_ref, *refs
):
    shard_count = sum(len(part[1]) for part in parts)
    out_count = len(refs) - 6 - in_count
    shards, rest = refs[:shard_count], refs[shard_count:]
    total, raws, weights, ready, raw_sems, weight_sems = rest[-6:]
    outs, sources = rest[-6 - out_count : -6], rest[: -6 - out_count]
    if final:
        sources, (gain_ref, own_ref, upper_ref, lower_ref) = sources[:-4], sources[-4:]
    if not first:
        sources, partial_ref = sources[:-1], sources[-1]
    me, rank = place_ref[0], place_ref[1]
    feats, cols = weights.shape[2:]
    rows = raws.shape[1]
    per_rank = shards[0].shape[-1] // feats
    copies = {}
    for slot, block in enumerate(blocks):
        owner = me ^ block
        span = pl.ds(pl.multiple_of((owner % per_rank) * feats, feats), feats)
        holder = owner // per_rank
        mine, begin, at = [], 0, 0
        for number, (length, places, by_rank) in enumerate(parts):
            held = shards[at : at + len(places)]
            at += len(places)
            target = raws.at[slot, pl.ds(begin, length), :]
            begin += length
            sem = raw_sems.at[slot, number]
            if by_rank:
                copy = pltpu.make_async_copy(
                    held[0].at[holder, pl.ds(places[0], length), span], target, sem
                )
                copy.start()
            else:
                for step, (ref, skip) in enumerate(zip(held, places)):
                    source = ref.at[pl.ds(skip, length), span]

                    @pl.when((holder ^ rank) == step)
                    def _(source=source, target=target, sem=sem):
                        pltpu.make_async_copy(source, target, sem).start()

                copy = pltpu.make_async_copy(source, target, sem)
            mine.append(copy)
        matrices = [
            pltpu.make_async_copy(
                sources[source].at[place], weights.at[slot, number], weight_sems.at[slot, number]
            )
            for number, (source, place) in enumerate(spots[block])
        ]
        for copy in matrices:
            copy.start()
        copies[slot] = (mine, matrices)

    def column(at):
        return jnp.transpose(jnp.broadcast_to(stats_ref[at : at + 1, :], (128, rows)))

    mean, scale = column(0), column(1)

    def prepare(first_slot):
        for slot in (first_slot, first_slot + 1):
            for copy in copies[slot][0]:
                copy.wait()
            span = pl.ds(pl.multiple_of((me ^ blocks[slot]) * feats, feats), feats)
            shift = modulation_ref[0:1, span]
            gain = 1.0 + modulation_ref[1:2, span]
            left = (slot - first_slot) * feats
            for start in range(0, feats, 128):
                lanes = slice(start, start + 128)
                part = raws[slot, :, lanes].astype(jnp.float32)
                part = (part - mean) * scale * gain[:, lanes] + shift[:, lanes]
                ready[first_slot // 2 % 2, :, left + start : left + start + 128] = part.astype(
                    jnp.bfloat16
                )

    prepare(0)
    for slot in range(0, len(blocks), 2):
        for copy in copies[slot][1] + copies[slot + 1][1]:
            copy.wait()
        if slot + 2 < len(blocks):
            prepare(slot + 2)
        right = jnp.concatenate(
            [
                jnp.concatenate([weights[slot, m], weights[slot + 1, m]], axis=0)
                for m in range(3)
            ],
            axis=1,
        )
        part = jnp.dot(ready[slot // 2 % 2], right, preferred_element_type=jnp.float32)
        if slot:
            part = part + total[...]
        elif not first:
            part = part + partial_ref[...]
        if slot + 2 < len(blocks):
            total[...] = part
    if not final:
        outs[0][...] = part
        return
    query_ref, squares_ref = outs[:2]
    key_ref, value_ref = outs[2:] if len(outs) == 4 else (outs[2], outs[2])
    key, value, query = [part[:, m * cols : (m + 1) * cols] for m in range(3)]
    query_ref[...] = query
    value_ref[value_ref.shape[0] - 1] = value.astype(jnp.bfloat16)
    tables = (own_ref[...], upper_ref[...], lower_ref[...])
    for head in range(cols // HEAD_DIM):
        lanes = slice(head * HEAD_DIM, (head + 1) * HEAD_DIM)
        key_ref[0, :, lanes] = turned(key, gain_ref, tables, head).astype(jnp.bfloat16)
    for kind, raw in enumerate((key, query)):
        summed = jnp.sum(raw * raw, axis=1, keepdims=True)
        summed = jnp.transpose(jnp.broadcast_to(summed, (rows, 128)))
        squares_ref[kind : kind + 1, :] = summed[:1]


def project(
    place, stats, modulation, parts, blocks, shards, spots, sources, partial, finish, joint=True
):
    rows = sum(part[0] for part in parts)
    _, feats, cols = sources[0].shape
    count = len(blocks)
    anywhere = pl.BlockSpec(memory_space=pl.ANY)
    whole = pl.BlockSpec(memory_space=pltpu.VMEM)
    out_shape = [jax.ShapeDtypeStruct((rows, 3 * cols), jnp.float32)]
    extra = [] if partial is None else [partial]
    if finish is not None:
        extra.extend(finish)
        held = [2] if joint else [1, 1]
        out_shape = [
            jax.ShapeDtypeStruct((rows, cols), jnp.float32),
            jax.ShapeDtypeStruct((2, rows), jnp.float32),
        ] + [jax.ShapeDtypeStruct((size, rows, cols), jnp.bfloat16) for size in held]
    return pl.pallas_call(
        functools.partial(
            project_kernel,
            parts,
            blocks,
            spots,
            partial is None,
            finish is not None,
            len(shards) + len(sources) + len(extra),
        ),
        in_specs=[pl.BlockSpec(memory_space=pltpu.SMEM), whole, whole]
        + [anywhere] * (len(shards) + len(sources))
        + [whole] * len(extra),
        out_specs=[whole] * len(out_shape),
        out_shape=out_shape,
        scratch_shapes=[
            pltpu.VMEM((rows, 3 * cols), jnp.float32),
            pltpu.VMEM((count, rows, feats), jnp.bfloat16),
            pltpu.VMEM((count, 3, feats, cols), jnp.bfloat16),
            pltpu.VMEM((2, rows, 2 * feats), jnp.bfloat16),
            pltpu.SemaphoreType.DMA((count, len(parts))),
            pltpu.SemaphoreType.DMA((count, 3)),
        ],
        compiler_params=pltpu.CompilerParams(vmem_limit_bytes=VMEM),
        cost_estimate=pl.CostEstimate(
            flops=6 * rows * count * feats * cols,
            bytes_accessed=2 * count * feats * (rows + 3 * cols) + 12 * rows * cols,
            transcendentals=0,
        ),
        name="project",
    )(place, stats, modulation, *shards, *sources, *extra)


def turn_kernel(count, width, squares_ref, gain_ref, *refs):
    for number in range(count):
        raw_ref, out_ref = refs[number], refs[4 * count + number]
        tables = [ref[...] for ref in refs[count + 3 * number : count + 3 * number + 3]]
        rows, cols = raw_ref.shape
        scale = lax.rsqrt(squares_ref[number : number + 1, :] * (1.0 / width) + epsilon)
        raw = raw_ref[...] * jnp.transpose(jnp.broadcast_to(scale, (128, rows)))[:, :1]
        for head in range(cols // HEAD_DIM):
            out_ref[:, head * HEAD_DIM : (head + 1) * HEAD_DIM] = turned(
                raw, gain_ref, tables, head
            ).astype(jnp.bfloat16)


def turn(raws, squares, gain, tables, width):
    count = len(raws)
    rows, cols = raws[0].shape
    whole = pl.BlockSpec(memory_space=pltpu.VMEM)
    return pl.pallas_call(
        functools.partial(turn_kernel, count, width),
        in_specs=[whole] * (2 + 4 * count),
        out_specs=[whole] * count,
        out_shape=[jax.ShapeDtypeStruct((rows, cols), jnp.bfloat16)] * count,
        compiler_params=pltpu.CompilerParams(vmem_limit_bytes=VMEM),
        cost_estimate=pl.CostEstimate(flops=0, bytes_accessed=0, transcendentals=0),
        name="turn",
    )(squares, gain, *raws, *[part for table in tables for part in table])


def attend_kernel(places, me_ref, bounds_ref, q_ref, *refs):
    count = len(places)
    pieces, (query_seg_ref, key_seg_ref, factor_ref) = refs[:count], refs[count : count + 3]
    out_ref, keys, values, highest, mixed, sems = refs[count + 3 :]
    me = me_ref[0]
    rows = pieces[0].shape[1]
    low, high = bounds_ref[0], bounds_ref[1]
    first = low * KEY_TILE // rows
    end = (high * KEY_TILE + rows - 1) // rows
    for number, (piece, (kind, at)) in enumerate(zip(pieces, places)):
        owner = me ^ (number % (count // 2))
        held = (keys, values)[kind]
        target = held.at[pl.ds(pl.multiple_of(owner * rows, rows), rows), :]
        sem = sems.at[kind, owner]

        @pl.when((owner >= first) & (owner < end))
        def _(source=piece.at[at], target=target, sem=sem):
            pltpu.make_async_copy(source, target, sem).start()

    def arrive(owner, carry):
        for kind, held in enumerate((keys, values)):
            target = held.at[pl.ds(pl.multiple_of(owner * rows, rows), rows), :]
            pltpu.make_async_copy(pieces[0].at[0], target, sems.at[kind, owner]).wait()
        return carry

    dim = HEAD_DIM
    heads = q_ref.shape[1] // dim
    ones = jnp.ones((KEY_TILE, dim), jnp.bfloat16)
    highest[...] = jnp.full_like(highest, -1e29)
    mixed[...] = jnp.zeros_like(mixed)
    query_seg = jnp.transpose(jnp.broadcast_to(query_seg_ref[...], (128, rows)))[:, :1]

    def step(block, carry):
        begin = jnp.where(block == low, first, (block * KEY_TILE + rows - 1) // rows)
        lax.fori_loop(begin, ((block + 1) * KEY_TILE + rows - 1) // rows, arrive, 0)
        where = pl.ds(pl.multiple_of(block * KEY_TILE, KEY_TILE), KEY_TILE)
        same = query_seg == key_seg_ref[block]
        factor = factor_ref[block]
        for head in range(heads):
            cols = slice(head * dim, (head + 1) * dim)
            scores = lax.dot_general(
                q_ref[:, cols],
                keys[where, cols],
                (((1,), (1,)), ((), ())),
                preferred_element_type=jnp.float32,
            )
            scores = jnp.where(same, scores * factor, -1e30)
            former = highest[head]
            newest = jnp.maximum(former, jnp.max(scores, axis=1, keepdims=True))
            highest[head] = newest
            weights = jnp.exp2(scores - newest[:, :1]).astype(jnp.bfloat16)
            right = jnp.concatenate([values[where, cols], ones], axis=1)
            part = jnp.dot(weights, right, preferred_element_type=jnp.float32)
            shrink = jnp.exp2(former - newest)
            mixed[head, :, :dim] = mixed[head, :, :dim] * shrink + part[:, :dim]
            mixed[head, :, dim:] = mixed[head, :, dim:] * shrink + part[:, dim:]
        return carry

    lax.fori_loop(low, high, step, 0)
    for head in range(heads):
        out_ref[:, head * dim : (head + 1) * dim] = (
            mixed[head, :, :dim] / mixed[head, :, dim:]
        ).astype(out_ref.dtype)


def key_bounds(query_seg, segment_ids):
    low = jnp.sum(segment_ids < query_seg[0], dtype=jnp.int32)
    high = jnp.sum(segment_ids <= query_seg[-1], dtype=jnp.int32)
    return jnp.stack([low // KEY_TILE, (high + KEY_TILE - 1) // KEY_TILE])


def attend(query, keys, values, me, bounds, query_seg, key_seg, factor):
    rows, cols = query.shape
    pieces = [array for array, _ in keys + values]
    places = tuple((0, at) for _, at in keys) + tuple((1, at) for _, at in values)
    count = len(pieces)
    tokens = key_seg.shape[0] * KEY_TILE
    dim = HEAD_DIM
    heads = cols // dim
    smem = pl.BlockSpec(memory_space=pltpu.SMEM)
    whole = pl.BlockSpec(memory_space=pltpu.VMEM)
    return pl.pallas_call(
        functools.partial(attend_kernel, places),
        in_specs=[smem, smem, whole] + [pl.BlockSpec(memory_space=pl.ANY)] * count + [whole] * 3,
        out_specs=whole,
        scratch_shapes=[
            pltpu.VMEM((tokens, cols), jnp.bfloat16),
            pltpu.VMEM((tokens, cols), jnp.bfloat16),
            pltpu.VMEM((heads, rows, dim), jnp.float32),
            pltpu.VMEM((heads, rows, 2 * dim), jnp.float32),
            pltpu.SemaphoreType.DMA((2, count // 2)),
        ],
        out_shape=jax.ShapeDtypeStruct((rows, cols), jnp.bfloat16),
        compiler_params=pltpu.CompilerParams(vmem_limit_bytes=VMEM),
        cost_estimate=pl.CostEstimate(
            flops=2 * rows * tokens * cols,
            bytes_accessed=4 * tokens * cols + 4 * rows * cols,
            transcendentals=rows * tokens * heads // 2,
        ),
        name="attend",
    )(me.reshape(1), bounds, query, *pieces, query_seg, key_seg, factor)


def pages_kernel(places, me_ref, page_ref, *refs):
    count = len(places)
    pieces, rest = refs[:count], refs[count:]
    scale_ref, (out_refs, held, sems) = (rest[0] if len(rest) == 5 else None), (
        rest[-4:-2],
        rest[-2],
        rest[-1],
    )
    me = me_ref[0]
    wanted = held.shape[0]
    per_block = pieces[0].shape[1] // PAGE
    waits = []
    for number in range(wanted):
        page = page_ref[number]
        rows = pl.ds(pl.multiple_of((page % per_block) * PAGE, PAGE), PAGE)
        target, sem = held.at[number], sems.at[number]
        for owner, (piece, at) in enumerate(zip(pieces, places)):

            @pl.when((page // per_block) == (me ^ owner))
            def _(source=piece.at[at, rows, :], target=target, sem=sem):
                pltpu.make_async_copy(source, target, sem).start()

        waits.append(pltpu.make_async_copy(pieces[0].at[0, pl.ds(0, PAGE), :], target, sem))
    for number in range(wanted):
        waits[number].wait()
        page = held[number]
        if scale_ref is not None:
            scale = jnp.broadcast_to(scale_ref[page_ref[number]], (128, PAGE))
            page = page.astype(jnp.float32) * jnp.transpose(scale)[:, :1]
        each = wanted // 2
        out_refs[number // each][number % each] = page.astype(jnp.bfloat16)


def pick_pages(pieces, me, pages, scale):
    _, rows, cols = pieces[0][0].shape
    wanted = pages.shape[0]
    smem = pl.BlockSpec(memory_space=pltpu.SMEM)
    whole = pl.BlockSpec(memory_space=pltpu.VMEM)
    extra = [] if scale is None else [scale]
    return pl.pallas_call(
        functools.partial(pages_kernel, tuple(at for _, at in pieces)),
        in_specs=[smem, smem]
        + [pl.BlockSpec(memory_space=pl.ANY)] * len(pieces)
        + [whole] * len(extra),
        out_specs=[whole] * 2,
        out_shape=[jax.ShapeDtypeStruct((wanted // 2, PAGE, cols), jnp.bfloat16)] * 2,
        scratch_shapes=[
            pltpu.VMEM((wanted, PAGE, cols), jnp.bfloat16),
            pltpu.SemaphoreType.DMA((wanted,)),
        ],
        compiler_params=pltpu.CompilerParams(vmem_limit_bytes=VMEM),
        cost_estimate=pl.CostEstimate(flops=0, bytes_accessed=0, transcendentals=0),
        name="pick_pages",
    )(me.reshape(1), pages, *[array for array, _ in pieces], *extra)


def own_pages(page_table, start, count):
    page_total = page_table.shape[0]
    inverse = (
        jnp.zeros((page_total,), jnp.int32)
        .at[page_table]
        .set(jnp.arange(page_total, dtype=jnp.int32))
    )
    return lax.dynamic_slice_in_dim(inverse, start, count, 0)


def whole_heads(ring, hidden, modulation, weights, gains, positions, segment_ids, page_table):
    tok_rows = hidden.shape[0]
    me = lax.axis_index("row")
    full_rows = lax.all_gather(hidden, "col", axis=1, tiled=True)
    modulated = modulate(full_rows.astype(jnp.float32), modulation)
    width = full_rows.shape[1]
    raws = [
        jnp.dot(
            modulated,
            lax.all_gather(weight, "row", axis=0, tiled=True),
            preferred_element_type=jnp.float32,
        )
        for weight in weights
    ]
    squares = lax.psum(tuple(jnp.sum(raw * raw, axis=1) for raw in raws[:2]), "col")
    tables = rotary_lanes(positions, HEAD_DIM)
    query, key = [
        turn([raw], total[None], gain[None], [tables], width)[0]
        for raw, total, gain in zip(raws, squares, gains)
    ]
    held = lax.all_gather(jnp.stack([key, raws[2].astype(jnp.bfloat16)]), "row", axis=0)
    keys, values = [[(held[number], kind) for number in range(ring)] for kind in range(2)]
    none = jnp.zeros((), jnp.int32)
    query_seg = lax.dynamic_slice_in_dim(segment_ids, me * tok_rows, tok_rows, 0)
    key_seg = segment_ids.astype(jnp.float32).reshape(-1, 1, KEY_TILE)
    attended = attend(
        query,
        keys,
        values,
        none,
        key_bounds(query_seg, segment_ids),
        query_seg.astype(jnp.float32)[None, :],
        key_seg,
        jnp.full_like(key_seg, HEAD_DIM ** (-0.5) * LOG2E),
    )
    count = tok_rows // PAGE
    pages = own_pages(page_table, me * count, count)
    pages = jnp.concatenate([pages, pages])
    picked = [pick_pages(pieces, none, pages, None)[0] for pieces in (keys, values)]
    return attended, jnp.stack(picked)


def split_heads(ring, ranks, hidden, modulation, weights, gains, positions, segment_ids, page_table):
    tok_rows, shard = hidden.shape
    width = ranks * shard
    me = lax.axis_index("row")
    rank = lax.axis_index("col")
    top = ring // 2
    half = me // top
    cols = weights[0].shape[1] // 2
    hops = []
    bit = top // 2
    while bit:
        hops.append(bit)
        bit //= 2

    def swap(value, bit):
        return lax.ppermute(value, "row", [(i, i ^ bit) for i in range(ring)])

    def across(value, step):
        return lax.ppermute(value, "col", [(c, c ^ step) for c in range(ranks)])

    def spread(blocks, bits):
        for bit in bits:
            blocks.update({number | bit: swap(blocks[number], bit) for number in list(blocks)})
        return blocks

    def in_order(mine, other, axis):
        return jnp.where(
            half == 0,
            jnp.concatenate([mine, other], axis=axis),
            jnp.concatenate([other, mine], axis=axis),
        )

    hidden_all = lax.all_gather(hidden, "col", axis=0)
    w_query, w_key, w_value = weights
    own, send_pair, send_single = cut((w_key, w_value, w_query), half)
    first, rest_hops = hops[0], hops[1:]
    pair, single = swap(send_pair, top), swap(send_single, top)
    next_own = swap(own, first)
    own_blocks = spread({0: own}, rest_hops)

    rows = hidden.astype(jnp.float32)
    local_mean = jnp.mean(rows, axis=1)
    local_square = jnp.sum(jnp.square(rows - local_mean[:, None]), axis=1)
    stats = jnp.stack([local_mean, local_square])
    all_stats = [stats] + [across(stats, step) for step in range(1, ranks)]
    average = sum(part[0] for part in all_stats) / ranks
    variance = (
        sum(part[1] + shard * jnp.square(part[0] - average) for part in all_stats) / width
    )
    small = jnp.concatenate(
        [jnp.stack([average, lax.rsqrt(variance + epsilon)]), positions.astype(jnp.float32)]
    )
    small_other = swap(small, top)
    moved = (pair, single, next_own, own_blocks, small, small_other)
    moved, hidden_late = lax.optimization_barrier((moved, hidden))
    pair, single, next_own, own_blocks, small, small_other = moved

    next_single = swap(single, first)
    other_rows = swap(hidden_late, top)
    pair_blocks = spread({0: pair}, rest_hops)
    single_blocks = spread({0: single}, rest_hops)
    next_own_blocks = spread({0: next_own}, rest_hops)
    early = tok_rows * 11 // 24 // 16 * 16
    sent = jnp.concatenate(
        [
            lax.dynamic_slice(hidden_all, (rank ^ step, early, 0), (1, tok_rows - early, shard))
            for step in range(1, ranks)
        ]
    ).reshape(-1, shard)
    moved = (next_single, other_rows, pair_blocks, single_blocks, next_own_blocks, sent)
    plain = (small, small_other, segment_ids, page_table, gains)
    moved, hidden_all, plain = lax.optimization_barrier((moved, hidden_all, plain))
    next_single, other_rows, pair_blocks, single_blocks, next_own_blocks, sent = moved
    small, small_other, segment_ids, page_table, gains = plain

    rest = swap(sent, top)
    next_pair = swap(pair_blocks[0], first)
    early_shards = [across(other_rows[:early], step) for step in range(1, ranks)]
    sources, spots = [], [None] * ring
    for number in own_blocks:
        for offset, whole in ((0, own_blocks), (first, next_own_blocks)):
            spots[number | offset] = tuple((len(sources), m) for m in range(3))
            sources.append(whole[number])
        at = len(sources)
        spots[number | top] = ((at, 0), (at, 1), (at + 1, 0))
        sources.extend([pair_blocks[number], single_blocks[number]])
    here = tuple(number for number in range(ring) if spots[number] is not None)
    late = tuple(number for number in range(ring) if spots[number] is None)
    own_parts = ((tok_rows, (0,), True),)
    place = jnp.stack([me, rank]).astype(jnp.int32)
    (partial,) = project(
        place,
        small[:2],
        modulation,
        own_parts,
        here,
        [hidden_all],
        tuple(spots),
        list(sources),
        None,
        None,
    )
    tables = [rotary_lanes(part[2:], HEAD_DIM) for part in (small, small_other)]
    q_gain, k_gain = [
        lax.dynamic_slice_in_dim(gain, half * cols, cols, 0)[None, :] for gain in gains
    ]
    count = tok_rows // PAGE
    pages = jnp.concatenate(
        [own_pages(page_table, owner * count, count) for owner in (me ^ top, me)]
    )
    query_segs = [
        lax.dynamic_slice_in_dim(segment_ids, owner * tok_rows, tok_rows, 0)
        for owner in (me, me ^ top)
    ]
    bounds = [key_bounds(seg, segment_ids) for seg in query_segs]
    query_segs = [seg.astype(jnp.float32)[None, :] for seg in query_segs]
    key_seg = segment_ids.astype(jnp.float32).reshape(-1, 1, KEY_TILE)
    prepared = (tables, q_gain, k_gain, pages, query_segs, key_seg, bounds)
    moved = (next_pair, next_single, rest, early_shards)
    moved, prepared, partial = lax.optimization_barrier((moved, prepared, partial))
    next_pair, next_single, rest, early_shards = moved
    tables, q_gain, k_gain, pages, query_segs, key_seg, bounds = prepared

    next_pair_blocks = spread({0: next_pair}, rest_hops)
    next_single_blocks = spread({0: next_single}, rest_hops)
    for number in own_blocks:
        at = len(sources)
        spots[number | top | first] = ((at, 0), (at, 1), (at + 1, 0))
        sources.extend([next_pair_blocks[number], next_single_blocks[number]])
    other_parts = (
        (early, (0,) * ranks, False),
        (
            tok_rows - early,
            (early,) + tuple(step * (tok_rows - early) for step in range(ranks - 1)),
            False,
        ),
    )
    late_sources = [part for number in own_blocks for part in (next_pair_blocks[number], next_single_blocks[number])]
    late_spots = list(spots)
    for at, number in enumerate(own_blocks):
        late_spots[number | top | first] = ((2 * at, 0), (2 * at, 1), (2 * at + 1, 0))
    own_query, own_squares, own_held = project(
        place,
        small[:2],
        modulation,
        own_parts,
        late,
        [hidden_all],
        tuple(late_spots),
        late_sources,
        partial,
        (k_gain, *tables[0]),
    )
    own_ahead = swap(own_held, first)
    other_query, other_squares, other_key, other_value = project(
        place,
        small_other[:2],
        modulation,
        other_parts,
        tuple(range(ring)),
        [other_rows] + early_shards + [other_rows] + [rest] * (ranks - 1),
        tuple(spots),
        sources,
        None,
        (k_gain, *tables[1]),
        joint=False,
    )
    value_ahead = swap(other_value, first)

    squares = jnp.stack([own_squares, other_squares])
    squares = squares + swap(squares, top)[::-1]
    bit = 1
    while bit < ranks:
        squares = squares + across(squares, bit)
        bit *= 2
    query = turn([own_query, other_query], squares[:, 1], q_gain, tables, width)
    key_squares = {0: squares[:, 0]}
    key_squares[first] = swap(key_squares[0], first)
    key_ahead = swap(other_key, first)
    key_squares[0], query, own_ahead, value_ahead = lax.optimization_barrier(
        (key_squares[0], query, own_ahead, value_ahead)
    )
    key_squares = spread(key_squares, rest_hops)
    blocks = jnp.stack([key_squares[n % top][n // top] for n in range(ring)])
    scale = lax.rsqrt(blocks / width + epsilon)
    scale = jnp.concatenate(
        [lax.dynamic_slice_in_dim(scale, me ^ owner, 1, 0) for owner in range(ring)]
    )
    factor = (scale * (HEAD_DIM ** (-0.5) * LOG2E)).reshape(-1, 1, KEY_TILE)
    scale = scale.reshape(-1, 1, PAGE)
    held = spread({0: own_held, first: own_ahead}, rest_hops)
    other_values = spread({0: other_value, first: value_ahead}, rest_hops)
    values = [(held[n], 1) for n in range(top)] + [(other_values[n], 0) for n in range(top)]
    values_picked = pick_pages(values, me, pages, None)
    key_ahead, values_picked = lax.optimization_barrier((key_ahead, values_picked))
    values_other = swap(values_picked[0], top)
    other_keys = spread({0: other_key, first: key_ahead}, rest_hops)
    keys = [(held[n], 0) for n in range(top)] + [(other_keys[n], 0) for n in range(top)]
    keys_picked = pick_pages(keys, me, pages, scale)
    query, keys_picked = lax.optimization_barrier((query, keys_picked))
    keys_other = swap(keys_picked[0], top)

    def attended(number):
        return attend(
            query[number], keys, values, me, bounds[number], query_segs[number], key_seg, factor
        )

    for_other = attended(1)
    query, for_other = lax.optimization_barrier((query, for_other))
    from_other = swap(for_other, top)
    for_me = attended(0)
    page_store = [
        in_order(keys_picked[1], keys_other, -1),
        in_order(values_picked[1], values_other, -1),
    ]
    return in_order(for_me, from_other, -1), jnp.stack(page_store)


def solution(mesh):
    ring, ranks = mesh.shape["row"], mesh.shape["col"]

    def body(
        hidden, modulation, w_query, w_key, w_value, q_gain, k_gain, positions, segment_ids, page_table
    ):
        rest = (
            hidden,
            modulation,
            (w_query, w_key, w_value),
            (q_gain, k_gain),
            positions,
            segment_ids,
            page_table,
        )
        heads = w_query.shape[1] // HEAD_DIM
        feats, shard = w_query.shape[0], hidden.shape[1]
        powers = ring & (ring - 1) == 0 and ranks & (ranks - 1) == 0
        if heads % 2 == 0 and ring >= 8 and powers and feats % 128 == 0 and shard % feats == 0:
            return split_heads(ring, ranks, *rest)
        return whole_heads(ring, *rest)

    in_specs = (
        P("row", "col"),
        P(),
        P("row", "col"),
        P("row", "col"),
        P("row", "col"),
        P("col"),
        P("col"),
        P(None, "row"),
        P(),
        P(),
    )
    out_specs = (P("row", "col"), P(None, "row", None, "col"))
    return jax.shard_map(body, mesh=mesh, in_specs=in_specs, out_specs=out_specs, check_vma=False)
```

```python
import functools
import jax
import jax.numpy as jnp
from jax import lax
from jax.experimental import pallas as pl
from jax.experimental.pallas import tpu as pltpu
from jax.sharding import PartitionSpec as P

HEAD_DIM = 128
PAGE = 128
KEY_TILE = 512
VMEM = 60 * 1024 * 1024
LOG2E = 1.4426950408889634

epsilon = 1e-06


def rotary_lanes(positions, head_dim):
    pair_count = head_dim // 2
    frame_pairs = pair_count - 2 * (pair_count // 3)
    side_pairs = pair_count // 3
    column = jnp.arange(head_dim) // 2
    frame_rate = 10000.0 ** (-column.astype(jnp.float32) / frame_pairs)
    height_rate = 10000.0 ** (-(column - frame_pairs).astype(jnp.float32) / side_pairs)
    width_rate = 10000.0 ** (-(column - frame_pairs - side_pairs).astype(jnp.float32) / side_pairs)
    coords = positions.astype(jnp.float32)
    angles = jnp.where(
        column < frame_pairs,
        coords[0][:, None] * frame_rate,
        jnp.where(
            column < frame_pairs + side_pairs,
            coords[1][:, None] * height_rate,
            coords[2][:, None] * width_rate,
        ),
    )
    sine = jnp.sin(angles)
    even = (jnp.arange(head_dim) % 2 == 0)[None, :]
    return jnp.cos(angles), jnp.where(even, -sine, 0.0), jnp.where(even, 0.0, sine)


def modulate(activations, modulation):
    average = jnp.mean(activations, axis=1, keepdims=True)
    centred = activations - average
    variance = jnp.mean(centred * centred, axis=1, keepdims=True)
    normed = centred * lax.rsqrt(variance + epsilon)
    return (normed * (1.0 + modulation[1]) + modulation[0]).astype(jnp.bfloat16)


def cut_kernel(half_ref, *refs):
    weights, outs, sems = refs[:3], refs[3:6], refs[6]
    cols = outs[0].shape[2]
    half = half_ref[0]
    copies = []
    for number, weight in enumerate(weights):
        send, at = (1, number) if number < 2 else (2, 0)
        for which, target in ((half, outs[0].at[number]), (1 - half, outs[send].at[at])):
            span = pl.ds(pl.multiple_of(which * cols, cols), cols)
            copies.append(
                pltpu.make_async_copy(
                    weight.at[:, span], target, sems.at[number, len(copies) % 2]
                )
            )
            copies[-1].start()
    for copy in copies:
        copy.wait()


def cut(weights, half):
    rows, width = weights[0].shape
    cols = width // 2
    whole = pl.BlockSpec(memory_space=pltpu.VMEM)
    return pl.pallas_call(
        cut_kernel,
        in_specs=[pl.BlockSpec(memory_space=pltpu.SMEM)] + [pl.BlockSpec(memory_space=pl.ANY)] * 3,
        out_specs=[whole] * 3,
        out_shape=[jax.ShapeDtypeStruct((size, rows, cols), jnp.bfloat16) for size in (3, 2, 1)],
        scratch_shapes=[pltpu.SemaphoreType.DMA((3, 2))],
        compiler_params=pltpu.CompilerParams(vmem_limit_bytes=VMEM),
        cost_estimate=pl.CostEstimate(
            flops=0, bytes_accessed=12 * rows * width, transcendentals=0
        ),
        name="cut",
    )(half.reshape(1), *weights)


def turned(values, gain, tables, at):
    dim = tables[0].shape[1]
    cols = slice(at * dim, (at + 1) * dim)
    own, upper, lower = tables
    part = values[:, cols] * gain[:, cols]
    return part * own + pltpu.roll(part, dim - 1, 1) * upper + pltpu.roll(part, 1, 1) * lower


def project_kernel(
    parts, blocks, spots, first, final, in_count, place_ref, stats_ref, modulation_ref, *refs
):
    shard_count = sum(len(part[1]) for part in parts)
    out_count = len(refs) - 6 - in_count
    shards, rest = refs[:shard_count], refs[shard_count:]
    total, raws, weights, ready, raw_sems, weight_sems = rest[-6:]
    outs, sources = rest[-6 - out_count : -6], rest[: -6 - out_count]
    if final:
        sources, (gain_ref, own_ref, upper_ref, lower_ref) = sources[:-4], sources[-4:]
    if not first:
        sources, partial_ref = sources[:-1], sources[-1]
    me, rank = place_ref[0], place_ref[1]
    feats, cols = weights.shape[2:]
    rows = raws.shape[1]
    per_rank = shards[0].shape[-1] // feats
    copies = {}
    for slot, block in enumerate(blocks):
        owner = me ^ block
        span = pl.ds(pl.multiple_of((owner % per_rank) * feats, feats), feats)
        holder = owner // per_rank
        mine, begin, at = [], 0, 0
        for number, (length, places, by_rank) in enumerate(parts):
            held = shards[at : at + len(places)]
            at += len(places)
            target = raws.at[slot, pl.ds(begin, length), :]
            begin += length
            sem = raw_sems.at[slot, number]
            if by_rank:
                copy = pltpu.make_async_copy(
                    held[0].at[holder, pl.ds(places[0], length), span], target, sem
                )
                copy.start()
            else:
                for step, (ref, skip) in enumerate(zip(held, places)):
                    source = ref.at[pl.ds(skip, length), span]

                    @pl.when((holder ^ rank) == step)
                    def _(source=source, target=target, sem=sem):
                        pltpu.make_async_copy(source, target, sem).start()

                copy = pltpu.make_async_copy(source, target, sem)
            mine.append(copy)
        matrices = [
            pltpu.make_async_copy(
                sources[source].at[place], weights.at[slot, number], weight_sems.at[slot, number]
            )
            for number, (source, place) in enumerate(spots[block])
        ]
        for copy in matrices:
            copy.start()
        copies[slot] = (mine, matrices)

    def column(at):
        return jnp.transpose(jnp.broadcast_to(stats_ref[at : at + 1, :], (128, rows)))

    mean, scale = column(0), column(1)

    def prepare(first_slot):
        for slot in (first_slot, first_slot + 1):
            for copy in copies[slot][0]:
                copy.wait()
            span = pl.ds(pl.multiple_of((me ^ blocks[slot]) * feats, feats), feats)
            shift = modulation_ref[0:1, span]
            gain = 1.0 + modulation_ref[1:2, span]
            left = (slot - first_slot) * feats
            for start in range(0, feats, 128):
                lanes = slice(start, start + 128)
                part = raws[slot, :, lanes].astype(jnp.float32)
                part = (part - mean) * scale * gain[:, lanes] + shift[:, lanes]
                ready[first_slot // 2 % 2, :, left + start : left + start + 128] = part.astype(
                    jnp.bfloat16
                )

    prepare(0)
    for slot in range(0, len(blocks), 2):
        for copy in copies[slot][1] + copies[slot + 1][1]:
            copy.wait()
        if slot + 2 < len(blocks):
            prepare(slot + 2)
        right = jnp.concatenate(
            [
                jnp.concatenate([weights[slot, m], weights[slot + 1, m]], axis=0)
                for m in range(3)
            ],
            axis=1,
        )
        part = jnp.dot(ready[slot // 2 % 2], right, preferred_element_type=jnp.float32)
        if slot:
            part = part + total[...]
        elif not first:
            part = part + partial_ref[...]
        if slot + 2 < len(blocks):
            total[...] = part
    if not final:
        outs[0][...] = part
        return
    query_ref, squares_ref = outs[:2]
    key_ref, value_ref = outs[2:] if len(outs) == 4 else (outs[2], outs[2])
    key, value, query = [part[:, m * cols : (m + 1) * cols] for m in range(3)]
    query_ref[...] = query
    value_ref[value_ref.shape[0] - 1] = value.astype(jnp.bfloat16)
    tables = (own_ref[...], upper_ref[...], lower_ref[...])
    for head in range(cols // HEAD_DIM):
        lanes = slice(head * HEAD_DIM, (head + 1) * HEAD_DIM)
        key_ref[0, :, lanes] = turned(key, gain_ref, tables, head).astype(jnp.bfloat16)
    for kind, raw in enumerate((key, query)):
        summed = jnp.sum(raw * raw, axis=1, keepdims=True)
        summed = jnp.transpose(jnp.broadcast_to(summed, (rows, 128)))
        squares_ref[kind : kind + 1, :] = summed[:1]


def project(
    place, stats, modulation, parts, blocks, shards, spots, sources, partial, finish, joint=True
):
    rows = sum(part[0] for part in parts)
    _, feats, cols = sources[0].shape
    count = len(blocks)
    anywhere = pl.BlockSpec(memory_space=pl.ANY)
    whole = pl.BlockSpec(memory_space=pltpu.VMEM)
    out_shape = [jax.ShapeDtypeStruct((rows, 3 * cols), jnp.float32)]
    extra = [] if partial is None else [partial]
    if finish is not None:
        extra.extend(finish)
        held = [2] if joint else [1, 1]
        out_shape = [
            jax.ShapeDtypeStruct((rows, cols), jnp.float32),
            jax.ShapeDtypeStruct((2, rows), jnp.float32),
        ] + [jax.ShapeDtypeStruct((size, rows, cols), jnp.bfloat16) for size in held]
    return pl.pallas_call(
        functools.partial(
            project_kernel,
            parts,
            blocks,
            spots,
            partial is None,
            finish is not None,
            len(shards) + len(sources) + len(extra),
        ),
        in_specs=[pl.BlockSpec(memory_space=pltpu.SMEM), whole, whole]
        + [anywhere] * (len(shards) + len(sources))
        + [whole] * len(extra),
        out_specs=[whole] * len(out_shape),
        out_shape=out_shape,
        scratch_shapes=[
            pltpu.VMEM((rows, 3 * cols), jnp.float32),
            pltpu.VMEM((count, rows, feats), jnp.bfloat16),
            pltpu.VMEM((count, 3, feats, cols), jnp.bfloat16),
            pltpu.VMEM((2, rows, 2 * feats), jnp.bfloat16),
            pltpu.SemaphoreType.DMA((count, len(parts))),
            pltpu.SemaphoreType.DMA((count, 3)),
        ],
        compiler_params=pltpu.CompilerParams(vmem_limit_bytes=VMEM),
        cost_estimate=pl.CostEstimate(
            flops=6 * rows * count * feats * cols,
            bytes_accessed=2 * count * feats * (rows + 3 * cols) + 12 * rows * cols,
            transcendentals=0,
        ),
        name="project",
    )(place, stats, modulation, *shards, *sources, *extra)


def turn_kernel(count, width, squares_ref, gain_ref, *refs):
    for number in range(count):
        raw_ref, out_ref = refs[number], refs[4 * count + number]
        tables = [ref[...] for ref in refs[count + 3 * number : count + 3 * number + 3]]
        rows, cols = raw_ref.shape
        scale = lax.rsqrt(squares_ref[number : number + 1, :] * (1.0 / width) + epsilon)
        scale = jnp.transpose(jnp.broadcast_to(scale, (HEAD_DIM, rows)))
        for head in range(cols // HEAD_DIM):
            lanes = slice(head * HEAD_DIM, (head + 1) * HEAD_DIM)
            out_ref[:, lanes] = turned(
                raw_ref[:, lanes] * scale, gain_ref[:, lanes], tables, 0
            ).astype(jnp.bfloat16)


def turn(raws, squares, gain, tables, width):
    count = len(raws)
    rows, cols = raws[0].shape
    whole = pl.BlockSpec(memory_space=pltpu.VMEM)
    return pl.pallas_call(
        functools.partial(turn_kernel, count, width),
        in_specs=[whole] * (2 + 4 * count),
        out_specs=[whole] * count,
        out_shape=[jax.ShapeDtypeStruct((rows, cols), jnp.bfloat16)] * count,
        compiler_params=pltpu.CompilerParams(vmem_limit_bytes=VMEM),
        cost_estimate=pl.CostEstimate(flops=0, bytes_accessed=0, transcendentals=0),
        name="turn",
    )(squares, gain, *raws, *[part for table in tables for part in table])


def attend_kernel(places, me_ref, bounds_ref, q_ref, *refs):
    count = len(places)
    pieces, (query_seg_ref, key_seg_ref, factor_ref) = refs[:count], refs[count : count + 3]
    out_ref, keys, values, highest, mixed, sems = refs[count + 3 :]
    me = me_ref[0]
    rows = pieces[0].shape[1]
    low, high = bounds_ref[0], bounds_ref[1]
    first = low * KEY_TILE // rows
    end = (high * KEY_TILE + rows - 1) // rows
    for number, (piece, (kind, at)) in enumerate(zip(pieces, places)):
        owner = me ^ (number % (count // 2))
        held = (keys, values)[kind]
        target = held.at[pl.ds(pl.multiple_of(owner * rows, rows), rows), :]
        sem = sems.at[kind, owner]

        @pl.when((owner >= first) & (owner < end))
        def _(source=piece.at[at], target=target, sem=sem):
            pltpu.make_async_copy(source, target, sem).start()

    def arrive(owner, carry):
        for kind, held in enumerate((keys, values)):
            target = held.at[pl.ds(pl.multiple_of(owner * rows, rows), rows), :]
            pltpu.make_async_copy(pieces[0].at[0], target, sems.at[kind, owner]).wait()
        return carry

    dim = HEAD_DIM
    heads = q_ref.shape[1] // dim
    ones = jnp.ones((KEY_TILE, dim), jnp.bfloat16)
    highest[...] = jnp.full_like(highest, -1e29)
    mixed[...] = jnp.zeros_like(mixed)
    query_seg = jnp.transpose(jnp.broadcast_to(query_seg_ref[...], (dim, rows)))
    times = KEY_TILE // dim

    def step(block, carry):
        begin = jnp.where(block == low, first, (block * KEY_TILE + rows - 1) // rows)
        lax.fori_loop(begin, ((block + 1) * KEY_TILE + rows - 1) // rows, arrive, 0)
        where = pl.ds(pl.multiple_of(block * KEY_TILE, KEY_TILE), KEY_TILE)
        same = jnp.concatenate([query_seg] * times, axis=1) == key_seg_ref[block]
        factor = factor_ref[block]
        for head in range(heads):
            cols = slice(head * dim, (head + 1) * dim)
            scores = lax.dot_general(
                q_ref[:, cols],
                keys[where, cols],
                (((1,), (1,)), ((), ())),
                preferred_element_type=jnp.float32,
            )
            scores = jnp.where(same, scores * factor, -1e30)
            former = highest[head]
            newest = jnp.maximum(former, jnp.max(scores, axis=1, keepdims=True))
            highest[head] = newest
            weights = jnp.exp2(scores - jnp.concatenate([newest] * times, axis=1))
            weights = weights.astype(jnp.bfloat16)
            right = jnp.concatenate([values[where, cols], ones], axis=1)
            part = jnp.dot(weights, right, preferred_element_type=jnp.float32)
            shrink = jnp.exp2(former - newest)
            mixed[head, :, :dim] = mixed[head, :, :dim] * shrink + part[:, :dim]
            mixed[head, :, dim:] = mixed[head, :, dim:] * shrink + part[:, dim:]
        return carry

    lax.fori_loop(low, high, step, 0)
    for head in range(heads):
        out_ref[:, head * dim : (head + 1) * dim] = (
            mixed[head, :, :dim] / mixed[head, :, dim:]
        ).astype(out_ref.dtype)


def key_bounds(query_seg, segment_ids):
    low = jnp.sum(segment_ids < query_seg[0], dtype=jnp.int32)
    high = jnp.sum(segment_ids <= query_seg[-1], dtype=jnp.int32)
    return jnp.stack([low // KEY_TILE, (high + KEY_TILE - 1) // KEY_TILE])


def attend(query, keys, values, me, bounds, query_seg, key_seg, factor):
    rows, cols = query.shape
    pieces = [array for array, _ in keys + values]
    places = tuple((0, at) for _, at in keys) + tuple((1, at) for _, at in values)
    count = len(pieces)
    tokens = key_seg.shape[0] * KEY_TILE
    dim = HEAD_DIM
    heads = cols // dim
    smem = pl.BlockSpec(memory_space=pltpu.SMEM)
    whole = pl.BlockSpec(memory_space=pltpu.VMEM)
    return pl.pallas_call(
        functools.partial(attend_kernel, places),
        in_specs=[smem, smem, whole] + [pl.BlockSpec(memory_space=pl.ANY)] * count + [whole] * 3,
        out_specs=whole,
        scratch_shapes=[
            pltpu.VMEM((tokens, cols), jnp.bfloat16),
            pltpu.VMEM((tokens, cols), jnp.bfloat16),
            pltpu.VMEM((heads, rows, dim), jnp.float32),
            pltpu.VMEM((heads, rows, 2 * dim), jnp.float32),
            pltpu.SemaphoreType.DMA((2, count // 2)),
        ],
        out_shape=jax.ShapeDtypeStruct((rows, cols), jnp.bfloat16),
        compiler_params=pltpu.CompilerParams(vmem_limit_bytes=VMEM),
        cost_estimate=pl.CostEstimate(
            flops=2 * rows * tokens * cols,
            bytes_accessed=4 * tokens * cols + 4 * rows * cols,
            transcendentals=rows * tokens * heads // 2,
        ),
        name="attend",
    )(me.reshape(1), bounds, query, *pieces, query_seg, key_seg, factor)


def pages_kernel(places, me_ref, page_ref, scale_ref, *refs):
    count = len(places)
    pieces, (out_refs, held, sems) = refs[:count], (refs[count : count + 2], *refs[count + 2 :])
    me = me_ref[0]
    wanted = held.shape[0]
    each = wanted // 2
    per_block = pieces[0].shape[1] // PAGE
    waits = []
    for number in range(wanted):
        page = page_ref[number]
        rows = pl.ds(pl.multiple_of((page % per_block) * PAGE, PAGE), PAGE)
        targets = (held.at[number], out_refs[number // each].at[1, number % each])
        for at, (piece, (kind, place)) in enumerate(zip(pieces, places)):
            owner = me ^ (at % (count // 2))

            @pl.when((page // per_block) == owner)
            def _(
                source=piece.at[place, rows, :], target=targets[kind], sem=sems.at[kind, number]
            ):
                pltpu.make_async_copy(source, target, sem).start()

        for kind, target in enumerate(targets):
            waits.append(
                pltpu.make_async_copy(
                    pieces[0].at[0, pl.ds(0, PAGE), :], target, sems.at[kind, number]
                )
            )
    for number in range(wanted):
        waits[2 * number].wait()
        scale = jnp.transpose(jnp.broadcast_to(scale_ref[page_ref[number]], (HEAD_DIM, PAGE)))
        for start in range(0, held.shape[2], HEAD_DIM):
            lanes = slice(start, start + HEAD_DIM)
            page = held[number, :, lanes].astype(jnp.float32) * scale
            out_refs[number // each][0, number % each, :, lanes] = page.astype(jnp.bfloat16)
    for number in range(wanted):
        waits[2 * number + 1].wait()


def pick_pages(keys, values, me, pages, scale):
    pieces = [array for array, _ in keys + values]
    places = tuple((0, at) for _, at in keys) + tuple((1, at) for _, at in values)
    cols = pieces[0].shape[2]
    wanted = pages.shape[0]
    smem = pl.BlockSpec(memory_space=pltpu.SMEM)
    whole = pl.BlockSpec(memory_space=pltpu.VMEM)
    return pl.pallas_call(
        functools.partial(pages_kernel, places),
        in_specs=[smem, smem, whole] + [pl.BlockSpec(memory_space=pl.ANY)] * len(pieces),
        out_specs=[whole] * 2,
        out_shape=[jax.ShapeDtypeStruct((2, wanted // 2, PAGE, cols), jnp.bfloat16)] * 2,
        scratch_shapes=[
            pltpu.VMEM((wanted, PAGE, cols), jnp.bfloat16),
            pltpu.SemaphoreType.DMA((2, wanted)),
        ],
        compiler_params=pltpu.CompilerParams(vmem_limit_bytes=VMEM),
        cost_estimate=pl.CostEstimate(flops=0, bytes_accessed=0, transcendentals=0),
        name="pick_pages",
    )(me.reshape(1), pages, scale, *pieces)


def own_pages(page_table, start, count):
    page_total = page_table.shape[0]
    inverse = (
        jnp.zeros((page_total,), jnp.int32)
        .at[page_table]
        .set(jnp.arange(page_total, dtype=jnp.int32))
    )
    return lax.dynamic_slice_in_dim(inverse, start, count, 0)


def whole_heads(ring, hidden, modulation, weights, gains, positions, segment_ids, page_table):
    tok_rows = hidden.shape[0]
    me = lax.axis_index("row")
    full_rows = lax.all_gather(hidden, "col", axis=1, tiled=True)
    modulated = modulate(full_rows.astype(jnp.float32), modulation)
    width = full_rows.shape[1]
    raws = [
        jnp.dot(
            modulated,
            lax.all_gather(weight, "row", axis=0, tiled=True),
            preferred_element_type=jnp.float32,
        )
        for weight in weights
    ]
    squares = lax.psum(tuple(jnp.sum(raw * raw, axis=1) for raw in raws[:2]), "col")
    tables = rotary_lanes(positions, HEAD_DIM)
    query, key = [
        turn([raw], total[None], gain[None], [tables], width)[0]
        for raw, total, gain in zip(raws, squares, gains)
    ]
    held = lax.all_gather(jnp.stack([key, raws[2].astype(jnp.bfloat16)]), "row", axis=0)
    keys, values = [[(held[number], kind) for number in range(ring)] for kind in range(2)]
    none = jnp.zeros((), jnp.int32)
    query_seg = lax.dynamic_slice_in_dim(segment_ids, me * tok_rows, tok_rows, 0)
    key_seg = segment_ids.astype(jnp.float32).reshape(-1, 1, KEY_TILE)
    attended = attend(
        query,
        keys,
        values,
        none,
        key_bounds(query_seg, segment_ids),
        query_seg.astype(jnp.float32)[None, :],
        key_seg,
        jnp.full_like(key_seg, HEAD_DIM ** (-0.5) * LOG2E),
    )
    count = tok_rows // PAGE
    pages = own_pages(page_table, me * count, count)
    pages = jnp.concatenate([pages, pages])
    ones = jnp.ones((segment_ids.shape[0] // PAGE, 1, PAGE), jnp.float32)
    return attended, pick_pages(keys, values, none, pages, ones)[0]


def split_heads(ring, ranks, hidden, modulation, weights, gains, positions, segment_ids, page_table):
    tok_rows, shard = hidden.shape
    width = ranks * shard
    me = lax.axis_index("row")
    rank = lax.axis_index("col")
    top = ring // 2
    half = me // top
    cols = weights[0].shape[1] // 2
    hops = []
    bit = top // 2
    while bit:
        hops.append(bit)
        bit //= 2

    def swap(value, bit):
        return lax.ppermute(value, "row", [(i, i ^ bit) for i in range(ring)])

    def across(value, step):
        return lax.ppermute(value, "col", [(c, c ^ step) for c in range(ranks)])

    def spread(blocks, bits):
        for bit in bits:
            blocks.update({number | bit: swap(blocks[number], bit) for number in list(blocks)})
        return blocks

    def in_order(mine, other, axis):
        return jnp.where(
            half == 0,
            jnp.concatenate([mine, other], axis=axis),
            jnp.concatenate([other, mine], axis=axis),
        )

    hidden_all = lax.all_gather(hidden, "col", axis=0)
    w_query, w_key, w_value = weights
    own, send_pair, send_single = cut((w_key, w_value, w_query), half)
    first, rest_hops = hops[0], hops[1:]
    pair, single = swap(send_pair, top), swap(send_single, top)
    next_own = swap(own, first)
    own_blocks = spread({0: own}, rest_hops)

    rows = hidden.astype(jnp.float32)
    local_mean = jnp.mean(rows, axis=1)
    local_square = jnp.sum(jnp.square(rows - local_mean[:, None]), axis=1)
    stats = jnp.stack([local_mean, local_square])
    all_stats = [stats] + [across(stats, step) for step in range(1, ranks)]
    average = sum(part[0] for part in all_stats) / ranks
    variance = (
        sum(part[1] + shard * jnp.square(part[0] - average) for part in all_stats) / width
    )
    small = jnp.concatenate(
        [jnp.stack([average, lax.rsqrt(variance + epsilon)]), positions.astype(jnp.float32)]
    )
    small_other = swap(small, top)
    moved = (pair, single, next_own, own_blocks, small, small_other)
    moved, hidden_late = lax.optimization_barrier((moved, hidden))
    pair, single, next_own, own_blocks, small, small_other = moved

    next_single = swap(single, first)
    other_rows = swap(hidden_late, top)
    pair_blocks = spread({0: pair}, rest_hops)
    single_blocks = spread({0: single}, rest_hops)
    next_own_blocks = spread({0: next_own}, rest_hops)
    early = tok_rows * 11 // 24 // 16 * 16
    sent = jnp.concatenate(
        [
            lax.dynamic_slice(hidden_all, (rank ^ step, early, 0), (1, tok_rows - early, shard))
            for step in range(1, ranks)
        ]
    ).reshape(-1, shard)
    moved = (next_single, other_rows, pair_blocks, single_blocks, next_own_blocks, sent)
    plain = (small, small_other, segment_ids, page_table, gains)
    moved, hidden_all, plain = lax.optimization_barrier((moved, hidden_all, plain))
    next_single, other_rows, pair_blocks, single_blocks, next_own_blocks, sent = moved
    small, small_other, segment_ids, page_table, gains = plain

    rest = swap(sent, top)
    next_pair = swap(pair_blocks[0], first)
    early_shards = [across(other_rows[:early], step) for step in range(1, ranks)]
    sources, spots = [], [None] * ring
    for number in own_blocks:
        for offset, whole in ((0, own_blocks), (first, next_own_blocks)):
            spots[number | offset] = tuple((len(sources), m) for m in range(3))
            sources.append(whole[number])
        at = len(sources)
        spots[number | top] = ((at, 0), (at, 1), (at + 1, 0))
        sources.extend([pair_blocks[number], single_blocks[number]])
    here = tuple(number for number in range(ring) if spots[number] is not None)
    late = tuple(number for number in range(ring) if spots[number] is None)
    own_parts = ((tok_rows, (0,), True),)
    place = jnp.stack([me, rank]).astype(jnp.int32)
    (partial,) = project(
        place,
        small[:2],
        modulation,
        own_parts,
        here,
        [hidden_all],
        tuple(spots),
        list(sources),
        None,
        None,
    )
    tables = [rotary_lanes(part[2:], HEAD_DIM) for part in (small, small_other)]
    q_gain, k_gain = [
        lax.dynamic_slice_in_dim(gain, half * cols, cols, 0)[None, :] for gain in gains
    ]
    count = tok_rows // PAGE
    pages = jnp.concatenate(
        [own_pages(page_table, owner * count, count) for owner in (me ^ top, me)]
    )
    query_segs = [
        lax.dynamic_slice_in_dim(segment_ids, owner * tok_rows, tok_rows, 0)
        for owner in (me, me ^ top)
    ]
    bounds = [key_bounds(seg, segment_ids) for seg in query_segs]
    query_segs = [seg.astype(jnp.float32)[None, :] for seg in query_segs]
    key_seg = segment_ids.astype(jnp.float32).reshape(-1, 1, KEY_TILE)
    prepared = (tables, q_gain, k_gain, pages, query_segs, key_seg, bounds)
    moved = (next_pair, next_single, rest, early_shards)
    moved, prepared, partial = lax.optimization_barrier((moved, prepared, partial))
    next_pair, next_single, rest, early_shards = moved
    tables, q_gain, k_gain, pages, query_segs, key_seg, bounds = prepared

    next_pair_blocks = spread({0: next_pair}, rest_hops)
    next_single_blocks = spread({0: next_single}, rest_hops)
    for number in own_blocks:
        at = len(sources)
        spots[number | top | first] = ((at, 0), (at, 1), (at + 1, 0))
        sources.extend([next_pair_blocks[number], next_single_blocks[number]])
    other_parts = (
        (early, (0,) * ranks, False),
        (
            tok_rows - early,
            (early,) + tuple(step * (tok_rows - early) for step in range(ranks - 1)),
            False,
        ),
    )
    late_sources = [part for number in own_blocks for part in (next_pair_blocks[number], next_single_blocks[number])]
    late_spots = list(spots)
    for at, number in enumerate(own_blocks):
        late_spots[number | top | first] = ((2 * at, 0), (2 * at, 1), (2 * at + 1, 0))
    own_query, own_squares, own_held = project(
        place,
        small[:2],
        modulation,
        own_parts,
        late,
        [hidden_all],
        tuple(late_spots),
        late_sources,
        partial,
        (k_gain, *tables[0]),
    )
    own_ahead = swap(own_held, first)
    other_query, other_squares, other_key, other_value = project(
        place,
        small_other[:2],
        modulation,
        other_parts,
        tuple(range(ring)),
        [other_rows] + early_shards + [other_rows] + [rest] * (ranks - 1),
        tuple(spots),
        sources,
        None,
        (k_gain, *tables[1]),
        joint=False,
    )
    value_ahead = swap(other_value, first)

    squares = jnp.stack([own_squares, other_squares])
    squares = squares + swap(squares, top)[::-1]
    bit = 1
    while bit < ranks:
        squares = squares + across(squares, bit)
        bit *= 2
    query = turn([own_query, other_query], squares[:, 1], q_gain, tables, width)
    squares, query, own_ahead, value_ahead = lax.optimization_barrier(
        (squares, query, own_ahead, value_ahead)
    )
    key_ahead = swap(other_key, first)
    key_squares = spread({0: squares[:, 0]}, hops)
    key_squares, key_ahead, own_ahead, value_ahead = lax.optimization_barrier(
        (key_squares, key_ahead, own_ahead, value_ahead)
    )
    held = spread({0: own_held, first: own_ahead}, rest_hops)
    other_values = spread({0: other_value, first: value_ahead}, rest_hops)
    other_keys = spread({0: other_key, first: key_ahead}, rest_hops)
    values = [(held[n], 1) for n in range(top)] + [(other_values[n], 0) for n in range(top)]
    keys = [(held[n], 0) for n in range(top)] + [(other_keys[n], 0) for n in range(top)]
    blocks = jnp.stack([key_squares[n % top][n // top] for n in range(ring)])
    scale = lax.rsqrt(blocks / width + epsilon)
    scale = jnp.concatenate(
        [lax.dynamic_slice_in_dim(scale, me ^ owner, 1, 0) for owner in range(ring)]
    )
    factor = (scale * (HEAD_DIM ** (-0.5) * LOG2E)).reshape(-1, 1, KEY_TILE)
    picked = pick_pages(keys, values, me, pages, scale.reshape(-1, 1, PAGE))
    query, picked = lax.optimization_barrier((query, picked))
    pages_other = swap(picked[0], top)

    def attended(number):
        return attend(
            query[number], keys, values, me, bounds[number], query_segs[number], key_seg, factor
        )

    for_other = attended(1)
    query, for_other = lax.optimization_barrier((query, for_other))
    from_other = swap(for_other, top)
    for_me = attended(0)
    return in_order(for_me, from_other, -1), in_order(picked[1], pages_other, -1)


def solution(mesh):
    ring, ranks = mesh.shape["row"], mesh.shape["col"]

    def body(
        hidden, modulation, w_query, w_key, w_value, q_gain, k_gain, positions, segment_ids, page_table
    ):
        rest = (
            hidden,
            modulation,
            (w_query, w_key, w_value),
            (q_gain, k_gain),
            positions,
            segment_ids,
            page_table,
        )
        heads = w_query.shape[1] // HEAD_DIM
        feats, shard = w_query.shape[0], hidden.shape[1]
        powers = ring & (ring - 1) == 0 and ranks & (ranks - 1) == 0
        if heads % 2 == 0 and ring >= 8 and powers and feats % 128 == 0 and shard % feats == 0:
            return split_heads(ring, ranks, *rest)
        return whole_heads(ring, *rest)

    in_specs = (
        P("row", "col"),
        P(),
        P("row", "col"),
        P("row", "col"),
        P("row", "col"),
        P("col"),
        P("col"),
        P(None, "row"),
        P(),
        P(),
    )
    out_specs = (P("row", "col"), P(None, "row", None, "col"))
    return jax.shard_map(body, mesh=mesh, in_specs=in_specs, out_specs=out_specs, check_vma=False)
```

```python
import functools
import jax
import jax.numpy as jnp
from jax import lax
from jax.experimental import pallas as pl
from jax.experimental.pallas import tpu as pltpu
from jax.sharding import PartitionSpec as P

HEAD_DIM = 128
PAGE = 128
KEY_TILE = 512
VMEM = 60 * 1024 * 1024
LOG2E = 1.4426950408889634

epsilon = 1e-06


def rotary_lanes(positions, head_dim):
    pair_count = head_dim // 2
    frame_pairs = pair_count - 2 * (pair_count // 3)
    side_pairs = pair_count // 3
    column = jnp.arange(head_dim) // 2
    frame_rate = 10000.0 ** (-column.astype(jnp.float32) / frame_pairs)
    height_rate = 10000.0 ** (-(column - frame_pairs).astype(jnp.float32) / side_pairs)
    width_rate = 10000.0 ** (-(column - frame_pairs - side_pairs).astype(jnp.float32) / side_pairs)
    coords = positions.astype(jnp.float32)
    angles = jnp.where(
        column < frame_pairs,
        coords[0][:, None] * frame_rate,
        jnp.where(
            column < frame_pairs + side_pairs,
            coords[1][:, None] * height_rate,
            coords[2][:, None] * width_rate,
        ),
    )
    sine = jnp.sin(angles)
    even = (jnp.arange(head_dim) % 2 == 0)[None, :]
    return jnp.cos(angles), jnp.where(even, -sine, 0.0), jnp.where(even, 0.0, sine)


def modulate(activations, modulation):
    average = jnp.mean(activations, axis=1, keepdims=True)
    centred = activations - average
    variance = jnp.mean(centred * centred, axis=1, keepdims=True)
    normed = centred * lax.rsqrt(variance + epsilon)
    return (normed * (1.0 + modulation[1]) + modulation[0]).astype(jnp.bfloat16)


def cut_kernel(half_ref, *refs):
    weights, outs, sems = refs[:3], refs[3:6], refs[6]
    cols = outs[0].shape[2]
    half = half_ref[0]
    copies = []
    for number, weight in enumerate(weights):
        send, at = (1, number) if number < 2 else (2, 0)
        for which, target in ((half, outs[0].at[number]), (1 - half, outs[send].at[at])):
            span = pl.ds(pl.multiple_of(which * cols, cols), cols)
            copies.append(
                pltpu.make_async_copy(
                    weight.at[:, span], target, sems.at[number, len(copies) % 2]
                )
            )
            copies[-1].start()
    for copy in copies:
        copy.wait()


def cut(weights, half):
    rows, width = weights[0].shape
    cols = width // 2
    whole = pl.BlockSpec(memory_space=pltpu.VMEM)
    return pl.pallas_call(
        cut_kernel,
        in_specs=[pl.BlockSpec(memory_space=pltpu.SMEM)] + [pl.BlockSpec(memory_space=pl.ANY)] * 3,
        out_specs=[whole] * 3,
        out_shape=[jax.ShapeDtypeStruct((size, rows, cols), jnp.bfloat16) for size in (3, 2, 1)],
        scratch_shapes=[pltpu.SemaphoreType.DMA((3, 2))],
        compiler_params=pltpu.CompilerParams(vmem_limit_bytes=VMEM),
        cost_estimate=pl.CostEstimate(
            flops=0, bytes_accessed=12 * rows * width, transcendentals=0
        ),
        name="cut",
    )(half.reshape(1), *weights)


def turned(values, gain, tables, at):
    dim = tables[0].shape[1]
    cols = slice(at * dim, (at + 1) * dim)
    own, upper, lower = tables
    part = values[:, cols] * gain[:, cols]
    return part * own + pltpu.roll(part, dim - 1, 1) * upper + pltpu.roll(part, 1, 1) * lower


def project_kernel(
    parts, blocks, spots, first, final, in_count, place_ref, stats_ref, modulation_ref, *refs
):
    shard_count = sum(len(part[1]) for part in parts)
    out_count = len(refs) - 6 - in_count
    shards, rest = refs[:shard_count], refs[shard_count:]
    total, raws, weights, ready, raw_sems, weight_sems = rest[-6:]
    outs, sources = rest[-6 - out_count : -6], rest[: -6 - out_count]
    if final:
        sources, (gain_ref, own_ref, upper_ref, lower_ref) = sources[:-4], sources[-4:]
    if not first:
        sources, partial_ref = sources[:-1], sources[-1]
    me, rank = place_ref[0], place_ref[1]
    feats, cols = weights.shape[2:]
    rows = raws.shape[1]
    per_rank = shards[0].shape[-1] // feats
    copies = {}
    for slot, block in enumerate(blocks):
        owner = me ^ block
        span = pl.ds(pl.multiple_of((owner % per_rank) * feats, feats), feats)
        holder = owner // per_rank
        mine, begin, at = [], 0, 0
        for number, (length, places, by_rank) in enumerate(parts):
            held = shards[at : at + len(places)]
            at += len(places)
            target = raws.at[slot, pl.ds(begin, length), :]
            begin += length
            sem = raw_sems.at[slot, number]
            if by_rank:
                copy = pltpu.make_async_copy(
                    held[0].at[holder, pl.ds(places[0], length), span], target, sem
                )
                copy.start()
            else:
                for step, (ref, skip) in enumerate(zip(held, places)):
                    source = ref.at[pl.ds(skip, length), span]

                    @pl.when((holder ^ rank) == step)
                    def _(source=source, target=target, sem=sem):
                        pltpu.make_async_copy(source, target, sem).start()

                copy = pltpu.make_async_copy(source, target, sem)
            mine.append(copy)
        matrices = [
            pltpu.make_async_copy(
                sources[source].at[place], weights.at[slot, number], weight_sems.at[slot, number]
            )
            for number, (source, place) in enumerate(spots[block])
        ]
        for copy in matrices:
            copy.start()
        copies[slot] = (mine, matrices)

    def column(at):
        return jnp.transpose(jnp.broadcast_to(stats_ref[at : at + 1, :], (128, rows)))

    mean, scale = column(0), column(1)

    def prepare(first_slot):
        for slot in (first_slot, first_slot + 1):
            for copy in copies[slot][0]:
                copy.wait()
            span = pl.ds(pl.multiple_of((me ^ blocks[slot]) * feats, feats), feats)
            shift = modulation_ref[0:1, span]
            gain = 1.0 + modulation_ref[1:2, span]
            left = (slot - first_slot) * feats
            for start in range(0, feats, 128):
                lanes = slice(start, start + 128)
                part = raws[slot, :, lanes].astype(jnp.float32)
                part = (part - mean) * scale * gain[:, lanes] + shift[:, lanes]
                ready[first_slot // 2 % 2, :, left + start : left + start + 128] = part.astype(
                    jnp.bfloat16
                )

    prepare(0)
    for slot in range(0, len(blocks), 2):
        for copy in copies[slot][1] + copies[slot + 1][1]:
            copy.wait()
        if slot + 2 < len(blocks):
            prepare(slot + 2)
        right = jnp.concatenate(
            [
                jnp.concatenate([weights[slot, m], weights[slot + 1, m]], axis=0)
                for m in range(3)
            ],
            axis=1,
        )
        part = jnp.dot(ready[slot // 2 % 2], right, preferred_element_type=jnp.float32)
        if slot:
            part = part + total[...]
        elif not first:
            part = part + partial_ref[...]
        if slot + 2 < len(blocks):
            total[...] = part
    if not final:
        outs[0][...] = part
        return
    query_ref, squares_ref = outs[:2]
    key_ref, value_ref = outs[2:] if len(outs) == 4 else (outs[2], outs[2])
    key, value, query = [part[:, m * cols : (m + 1) * cols] for m in range(3)]
    query_ref[...] = query
    value_ref[value_ref.shape[0] - 1] = value.astype(jnp.bfloat16)
    tables = (own_ref[...], upper_ref[...], lower_ref[...])
    for head in range(cols // HEAD_DIM):
        lanes = slice(head * HEAD_DIM, (head + 1) * HEAD_DIM)
        key_ref[0, :, lanes] = turned(key, gain_ref, tables, head).astype(jnp.bfloat16)
    for kind, raw in enumerate((key, query)):
        summed = jnp.sum(raw * raw, axis=1, keepdims=True)
        summed = jnp.transpose(jnp.broadcast_to(summed, (rows, 128)))
        squares_ref[kind : kind + 1, :] = summed[:1]


def project(
    place, stats, modulation, parts, blocks, shards, spots, sources, partial, finish, joint=True
):
    rows = sum(part[0] for part in parts)
    _, feats, cols = sources[0].shape
    count = len(blocks)
    anywhere = pl.BlockSpec(memory_space=pl.ANY)
    whole = pl.BlockSpec(memory_space=pltpu.VMEM)
    out_shape = [jax.ShapeDtypeStruct((rows, 3 * cols), jnp.float32)]
    extra = [] if partial is None else [partial]
    if finish is not None:
        extra.extend(finish)
        held = [2] if joint else [1, 1]
        out_shape = [
            jax.ShapeDtypeStruct((rows, cols), jnp.float32),
            jax.ShapeDtypeStruct((2, rows), jnp.float32),
        ] + [jax.ShapeDtypeStruct((size, rows, cols), jnp.bfloat16) for size in held]
    return pl.pallas_call(
        functools.partial(
            project_kernel,
            parts,
            blocks,
            spots,
            partial is None,
            finish is not None,
            len(shards) + len(sources) + len(extra),
        ),
        in_specs=[pl.BlockSpec(memory_space=pltpu.SMEM), whole, whole]
        + [anywhere] * (len(shards) + len(sources))
        + [whole] * len(extra),
        out_specs=[whole] * len(out_shape),
        out_shape=out_shape,
        scratch_shapes=[
            pltpu.VMEM((rows, 3 * cols), jnp.float32),
            pltpu.VMEM((count, rows, feats), jnp.bfloat16),
            pltpu.VMEM((count, 3, feats, cols), jnp.bfloat16),
            pltpu.VMEM((2, rows, 2 * feats), jnp.bfloat16),
            pltpu.SemaphoreType.DMA((count, len(parts))),
            pltpu.SemaphoreType.DMA((count, 3)),
        ],
        compiler_params=pltpu.CompilerParams(vmem_limit_bytes=VMEM),
        cost_estimate=pl.CostEstimate(
            flops=6 * rows * count * feats * cols,
            bytes_accessed=2 * count * feats * (rows + 3 * cols) + 12 * rows * cols,
            transcendentals=0,
        ),
        name="project",
    )(place, stats, modulation, *shards, *sources, *extra)


def turn_kernel(count, width, squares_ref, gain_ref, *refs):
    for number in range(count):
        raw_ref, out_ref = refs[number], refs[4 * count + number]
        tables = [ref[...] for ref in refs[count + 3 * number : count + 3 * number + 3]]
        rows, cols = raw_ref.shape
        scale = lax.rsqrt(squares_ref[number : number + 1, :] * (1.0 / width) + epsilon)
        scale = jnp.transpose(jnp.broadcast_to(scale, (HEAD_DIM, rows)))
        for head in range(cols // HEAD_DIM):
            lanes = slice(head * HEAD_DIM, (head + 1) * HEAD_DIM)
            out_ref[:, lanes] = turned(
                raw_ref[:, lanes] * scale, gain_ref[:, lanes], tables, 0
            ).astype(jnp.bfloat16)


def turn(raws, squares, gain, tables, width):
    count = len(raws)
    rows, cols = raws[0].shape
    whole = pl.BlockSpec(memory_space=pltpu.VMEM)
    return pl.pallas_call(
        functools.partial(turn_kernel, count, width),
        in_specs=[whole] * (2 + 4 * count),
        out_specs=[whole] * count,
        out_shape=[jax.ShapeDtypeStruct((rows, cols), jnp.bfloat16)] * count,
        compiler_params=pltpu.CompilerParams(vmem_limit_bytes=VMEM),
        cost_estimate=pl.CostEstimate(flops=0, bytes_accessed=0, transcendentals=0),
        name="turn",
    )(squares, gain, *raws, *[part for table in tables for part in table])


def attend_kernel(places, me_ref, bounds_ref, q_ref, *refs):
    count = len(places)
    pieces, (query_seg_ref, key_seg_ref, factor_ref) = refs[:count], refs[count : count + 3]
    out_ref, keys, values, highest, mixed, sems = refs[count + 3 :]
    me = me_ref[0]
    rows = pieces[0].shape[1]
    low, high = bounds_ref[0], bounds_ref[1]
    first = low * KEY_TILE // rows
    end = (high * KEY_TILE + rows - 1) // rows
    for number, (piece, (kind, at)) in enumerate(zip(pieces, places)):
        owner = me ^ (number % (count // 2))
        held = (keys, values)[kind]
        target = held.at[pl.ds(pl.multiple_of(owner * rows, rows), rows), :]
        sem = sems.at[kind, owner]

        @pl.when((owner >= first) & (owner < end))
        def _(source=piece.at[at], target=target, sem=sem):
            pltpu.make_async_copy(source, target, sem).start()

    def arrive(owner, carry):
        for kind, held in enumerate((keys, values)):
            target = held.at[pl.ds(pl.multiple_of(owner * rows, rows), rows), :]
            pltpu.make_async_copy(pieces[0].at[0], target, sems.at[kind, owner]).wait()
        return carry

    dim = HEAD_DIM
    heads = q_ref.shape[1] // dim
    ones = jnp.ones((KEY_TILE, dim), jnp.bfloat16)
    highest[...] = jnp.full_like(highest, -1e29)
    mixed[...] = jnp.zeros_like(mixed)
    query_seg = jnp.transpose(jnp.broadcast_to(query_seg_ref[...], (dim, rows)))
    times = KEY_TILE // dim

    def step(block, carry):
        begin = jnp.where(block == low, first, (block * KEY_TILE + rows - 1) // rows)
        lax.fori_loop(begin, ((block + 1) * KEY_TILE + rows - 1) // rows, arrive, 0)
        where = pl.ds(pl.multiple_of(block * KEY_TILE, KEY_TILE), KEY_TILE)
        same = jnp.concatenate([query_seg] * times, axis=1) == key_seg_ref[block]
        factor = factor_ref[block]
        for head in range(heads):
            cols = slice(head * dim, (head + 1) * dim)
            scores = lax.dot_general(
                q_ref[:, cols],
                keys[where, cols],
                (((1,), (1,)), ((), ())),
                preferred_element_type=jnp.float32,
            )
            scores = jnp.where(same, scores * factor, -1e30)
            former = highest[head]
            newest = jnp.maximum(former, jnp.max(scores, axis=1, keepdims=True))
            highest[head] = newest
            weights = jnp.exp2(scores - jnp.concatenate([newest] * times, axis=1))
            weights = weights.astype(jnp.bfloat16)
            right = jnp.concatenate([values[where, cols], ones], axis=1)
            part = jnp.dot(weights, right, preferred_element_type=jnp.float32)
            shrink = jnp.exp2(former - newest)
            mixed[head, :, :dim] = mixed[head, :, :dim] * shrink + part[:, :dim]
            mixed[head, :, dim:] = mixed[head, :, dim:] * shrink + part[:, dim:]
        return carry

    lax.fori_loop(low, high, step, 0)
    for head in range(heads):
        out_ref[:, head * dim : (head + 1) * dim] = (
            mixed[head, :, :dim] / mixed[head, :, dim:]
        ).astype(out_ref.dtype)


def key_bounds(query_seg, segment_ids):
    low = jnp.sum(segment_ids < query_seg[0], dtype=jnp.int32)
    high = jnp.sum(segment_ids <= query_seg[-1], dtype=jnp.int32)
    return jnp.stack([low // KEY_TILE, (high + KEY_TILE - 1) // KEY_TILE])


def attend(query, keys, values, me, bounds, query_seg, key_seg, factor):
    rows, cols = query.shape
    pieces = [array for array, _ in keys + values]
    places = tuple((0, at) for _, at in keys) + tuple((1, at) for _, at in values)
    count = len(pieces)
    tokens = key_seg.shape[0] * KEY_TILE
    dim = HEAD_DIM
    heads = cols // dim
    smem = pl.BlockSpec(memory_space=pltpu.SMEM)
    whole = pl.BlockSpec(memory_space=pltpu.VMEM)
    return pl.pallas_call(
        functools.partial(attend_kernel, places),
        in_specs=[smem, smem, whole] + [pl.BlockSpec(memory_space=pl.ANY)] * count + [whole] * 3,
        out_specs=whole,
        scratch_shapes=[
            pltpu.VMEM((tokens, cols), jnp.bfloat16),
            pltpu.VMEM((tokens, cols), jnp.bfloat16),
            pltpu.VMEM((heads, rows, dim), jnp.float32),
            pltpu.VMEM((heads, rows, 2 * dim), jnp.float32),
            pltpu.SemaphoreType.DMA((2, count // 2)),
        ],
        out_shape=jax.ShapeDtypeStruct((rows, cols), jnp.bfloat16),
        compiler_params=pltpu.CompilerParams(vmem_limit_bytes=VMEM),
        cost_estimate=pl.CostEstimate(
            flops=2 * rows * tokens * cols,
            bytes_accessed=4 * tokens * cols + 4 * rows * cols,
            transcendentals=rows * tokens * heads // 2,
        ),
        name="attend",
    )(me.reshape(1), bounds, query, *pieces, query_seg, key_seg, factor)


def pages_kernel(places, me_ref, page_ref, *refs):
    count = len(places)
    pieces, rest = refs[:count], refs[count:]
    scale_ref, (out_refs, held, sems) = (rest[0] if len(rest) == 5 else None), (
        rest[-4:-2],
        rest[-2],
        rest[-1],
    )
    me = me_ref[0]
    wanted = held.shape[0]
    per_block = pieces[0].shape[1] // PAGE
    waits = []
    for number in range(wanted):
        page = page_ref[number]
        rows = pl.ds(pl.multiple_of((page % per_block) * PAGE, PAGE), PAGE)
        target, sem = held.at[number], sems.at[number]
        for owner, (piece, at) in enumerate(zip(pieces, places)):

            @pl.when((page // per_block) == (me ^ owner))
            def _(source=piece.at[at, rows, :], target=target, sem=sem):
                pltpu.make_async_copy(source, target, sem).start()

        waits.append(pltpu.make_async_copy(pieces[0].at[0, pl.ds(0, PAGE), :], target, sem))
    for number in range(wanted):
        waits[number].wait()
        each = wanted // 2
        out_ref = out_refs[number // each].at[number % each]
        if scale_ref is None:
            out_ref[...] = held[number]
            continue
        scale = jnp.transpose(jnp.broadcast_to(scale_ref[page_ref[number]], (HEAD_DIM, PAGE)))
        for start in range(0, held.shape[2], HEAD_DIM):
            lanes = slice(start, start + HEAD_DIM)
            page = held[number, :, lanes].astype(jnp.float32) * scale
            out_ref[:, lanes] = page.astype(jnp.bfloat16)


def pick_pages(pieces, me, pages, scale):
    _, rows, cols = pieces[0][0].shape
    wanted = pages.shape[0]
    smem = pl.BlockSpec(memory_space=pltpu.SMEM)
    whole = pl.BlockSpec(memory_space=pltpu.VMEM)
    extra = [] if scale is None else [scale]
    return pl.pallas_call(
        functools.partial(pages_kernel, tuple(at for _, at in pieces)),
        in_specs=[smem, smem]
        + [pl.BlockSpec(memory_space=pl.ANY)] * len(pieces)
        + [whole] * len(extra),
        out_specs=[whole] * 2,
        out_shape=[jax.ShapeDtypeStruct((wanted // 2, PAGE, cols), jnp.bfloat16)] * 2,
        scratch_shapes=[
            pltpu.VMEM((wanted, PAGE, cols), jnp.bfloat16),
            pltpu.SemaphoreType.DMA((wanted,)),
        ],
        compiler_params=pltpu.CompilerParams(vmem_limit_bytes=VMEM),
        cost_estimate=pl.CostEstimate(flops=0, bytes_accessed=0, transcendentals=0),
        name="pick_pages",
    )(me.reshape(1), pages, *[array for array, _ in pieces], *extra)


def own_pages(page_table, start, count):
    page_total = page_table.shape[0]
    inverse = (
        jnp.zeros((page_total,), jnp.int32)
        .at[page_table]
        .set(jnp.arange(page_total, dtype=jnp.int32))
    )
    return lax.dynamic_slice_in_dim(inverse, start, count, 0)


def whole_heads(ring, hidden, modulation, weights, gains, positions, segment_ids, page_table):
    tok_rows = hidden.shape[0]
    me = lax.axis_index("row")
    full_rows = lax.all_gather(hidden, "col", axis=1, tiled=True)
    modulated = modulate(full_rows.astype(jnp.float32), modulation)
    width = full_rows.shape[1]
    raws = [
        jnp.dot(
            modulated,
            lax.all_gather(weight, "row", axis=0, tiled=True),
            preferred_element_type=jnp.float32,
        )
        for weight in weights
    ]
    squares = lax.psum(tuple(jnp.sum(raw * raw, axis=1) for raw in raws[:2]), "col")
    tables = rotary_lanes(positions, HEAD_DIM)
    query, key = [
        turn([raw], total[None], gain[None], [tables], width)[0]
        for raw, total, gain in zip(raws, squares, gains)
    ]
    held = lax.all_gather(jnp.stack([key, raws[2].astype(jnp.bfloat16)]), "row", axis=0)
    keys, values = [[(held[number], kind) for number in range(ring)] for kind in range(2)]
    none = jnp.zeros((), jnp.int32)
    query_seg = lax.dynamic_slice_in_dim(segment_ids, me * tok_rows, tok_rows, 0)
    key_seg = segment_ids.astype(jnp.float32).reshape(-1, 1, KEY_TILE)
    attended = attend(
        query,
        keys,
        values,
        none,
        key_bounds(query_seg, segment_ids),
        query_seg.astype(jnp.float32)[None, :],
        key_seg,
        jnp.full_like(key_seg, HEAD_DIM ** (-0.5) * LOG2E),
    )
    count = tok_rows // PAGE
    pages = own_pages(page_table, me * count, count)
    pages = jnp.concatenate([pages, pages])
    picked = [pick_pages(pieces, none, pages, None)[0] for pieces in (keys, values)]
    return attended, jnp.stack(picked)


def split_heads(ring, ranks, hidden, modulation, weights, gains, positions, segment_ids, page_table):
    tok_rows, shard = hidden.shape
    width = ranks * shard
    me = lax.axis_index("row")
    rank = lax.axis_index("col")
    top = ring // 2
    half = me // top
    cols = weights[0].shape[1] // 2
    hops = []
    bit = top // 2
    while bit:
        hops.append(bit)
        bit //= 2

    def swap(value, bit):
        return lax.ppermute(value, "row", [(i, i ^ bit) for i in range(ring)])

    def across(value, step):
        return lax.ppermute(value, "col", [(c, c ^ step) for c in range(ranks)])

    def spread(blocks, bits):
        for bit in bits:
            blocks.update({number | bit: swap(blocks[number], bit) for number in list(blocks)})
        return blocks

    def in_order(mine, other, axis):
        return jnp.where(
            half == 0,
            jnp.concatenate([mine, other], axis=axis),
            jnp.concatenate([other, mine], axis=axis),
        )

    hidden_all = lax.all_gather(hidden, "col", axis=0)
    w_query, w_key, w_value = weights
    own, send_pair, send_single = cut((w_key, w_value, w_query), half)
    first, rest_hops = hops[0], hops[1:]
    pair, single = swap(send_pair, top), swap(send_single, top)
    next_own = swap(own, first)
    own_blocks = spread({0: own}, rest_hops)

    rows = hidden.astype(jnp.float32)
    local_mean = jnp.mean(rows, axis=1)
    local_square = jnp.sum(jnp.square(rows - local_mean[:, None]), axis=1)
    stats = jnp.stack([local_mean, local_square])
    all_stats = [stats] + [across(stats, step) for step in range(1, ranks)]
    average = sum(part[0] for part in all_stats) / ranks
    variance = (
        sum(part[1] + shard * jnp.square(part[0] - average) for part in all_stats) / width
    )
    small = jnp.concatenate(
        [jnp.stack([average, lax.rsqrt(variance + epsilon)]), positions.astype(jnp.float32)]
    )
    small_other = swap(small, top)
    moved = (pair, single, next_own, own_blocks, small, small_other)
    moved, hidden_late = lax.optimization_barrier((moved, hidden))
    pair, single, next_own, own_blocks, small, small_other = moved

    next_single = swap(single, first)
    other_rows = swap(hidden_late, top)
    pair_blocks = spread({0: pair}, rest_hops)
    single_blocks = spread({0: single}, rest_hops)
    next_own_blocks = spread({0: next_own}, rest_hops)
    early = tok_rows * 11 // 24 // 16 * 16
    sent = jnp.concatenate(
        [
            lax.dynamic_slice(hidden_all, (rank ^ step, early, 0), (1, tok_rows - early, shard))
            for step in range(1, ranks)
        ]
    ).reshape(-1, shard)
    moved = (next_single, other_rows, pair_blocks, single_blocks, next_own_blocks, sent)
    plain = (small, small_other, segment_ids, page_table, gains)
    moved, hidden_all, plain = lax.optimization_barrier((moved, hidden_all, plain))
    next_single, other_rows, pair_blocks, single_blocks, next_own_blocks, sent = moved
    small, small_other, segment_ids, page_table, gains = plain

    rest = swap(sent, top)
    next_pair = swap(pair_blocks[0], first)
    early_shards = [across(other_rows[:early], step) for step in range(1, ranks)]
    sources, spots = [], [None] * ring
    for number in own_blocks:
        for offset, whole in ((0, own_blocks), (first, next_own_blocks)):
            spots[number | offset] = tuple((len(sources), m) for m in range(3))
            sources.append(whole[number])
        at = len(sources)
        spots[number | top] = ((at, 0), (at, 1), (at + 1, 0))
        sources.extend([pair_blocks[number], single_blocks[number]])
    here = tuple(number for number in range(ring) if spots[number] is not None)
    late = tuple(number for number in range(ring) if spots[number] is None)
    own_parts = ((tok_rows, (0,), True),)
    place = jnp.stack([me, rank]).astype(jnp.int32)
    (partial,) = project(
        place,
        small[:2],
        modulation,
        own_parts,
        here,
        [hidden_all],
        tuple(spots),
        list(sources),
        None,
        None,
    )
    tables = [rotary_lanes(part[2:], HEAD_DIM) for part in (small, small_other)]
    q_gain, k_gain = [
        lax.dynamic_slice_in_dim(gain, half * cols, cols, 0)[None, :] for gain in gains
    ]
    count = tok_rows // PAGE
    pages = jnp.concatenate(
        [own_pages(page_table, owner * count, count) for owner in (me ^ top, me)]
    )
    query_segs = [
        lax.dynamic_slice_in_dim(segment_ids, owner * tok_rows, tok_rows, 0)
        for owner in (me, me ^ top)
    ]
    bounds = [key_bounds(seg, segment_ids) for seg in query_segs]
    query_segs = [seg.astype(jnp.float32)[None, :] for seg in query_segs]
    key_seg = segment_ids.astype(jnp.float32).reshape(-1, 1, KEY_TILE)
    prepared = (tables, q_gain, k_gain, pages, query_segs, key_seg, bounds)
    moved = (next_pair, next_single, rest, early_shards)
    moved, prepared, partial = lax.optimization_barrier((moved, prepared, partial))
    next_pair, next_single, rest, early_shards = moved
    tables, q_gain, k_gain, pages, query_segs, key_seg, bounds = prepared

    next_pair_blocks = spread({0: next_pair}, rest_hops)
    next_single_blocks = spread({0: next_single}, rest_hops)
    for number in own_blocks:
        at = len(sources)
        spots[number | top | first] = ((at, 0), (at, 1), (at + 1, 0))
        sources.extend([next_pair_blocks[number], next_single_blocks[number]])
    other_parts = (
        (early, (0,) * ranks, False),
        (
            tok_rows - early,
            (early,) + tuple(step * (tok_rows - early) for step in range(ranks - 1)),
            False,
        ),
    )
    late_sources = [part for number in own_blocks for part in (next_pair_blocks[number], next_single_blocks[number])]
    late_spots = list(spots)
    for at, number in enumerate(own_blocks):
        late_spots[number | top | first] = ((2 * at, 0), (2 * at, 1), (2 * at + 1, 0))
    own_query, own_squares, own_held = project(
        place,
        small[:2],
        modulation,
        own_parts,
        late,
        [hidden_all],
        tuple(late_spots),
        late_sources,
        partial,
        (k_gain, *tables[0]),
    )
    own_ahead = swap(own_held, first)
    other_query, other_squares, other_key, other_value = project(
        place,
        small_other[:2],
        modulation,
        other_parts,
        tuple(range(ring)),
        [other_rows] + early_shards + [other_rows] + [rest] * (ranks - 1),
        tuple(spots),
        sources,
        None,
        (k_gain, *tables[1]),
        joint=False,
    )
    value_ahead = swap(other_value, first)

    squares = jnp.stack([own_squares, other_squares])
    squares = squares + swap(squares, top)[::-1]
    bit = 1
    while bit < ranks:
        squares = squares + across(squares, bit)
        bit *= 2
    query = turn([own_query, other_query], squares[:, 1], q_gain, tables, width)
    key_squares = {0: squares[:, 0]}
    key_squares[first] = swap(key_squares[0], first)
    key_ahead = swap(other_key, first)
    key_squares[0], query, own_ahead, value_ahead = lax.optimization_barrier(
        (key_squares[0], query, own_ahead, value_ahead)
    )
    key_squares = spread(key_squares, rest_hops)
    blocks = jnp.stack([key_squares[n % top][n // top] for n in range(ring)])
    scale = lax.rsqrt(blocks / width + epsilon)
    scale = jnp.concatenate(
        [lax.dynamic_slice_in_dim(scale, me ^ owner, 1, 0) for owner in range(ring)]
    )
    factor = (scale * (HEAD_DIM ** (-0.5) * LOG2E)).reshape(-1, 1, KEY_TILE)
    scale = scale.reshape(-1, 1, PAGE)
    held = spread({0: own_held, first: own_ahead}, rest_hops)
    other_values = spread({0: other_value, first: value_ahead}, rest_hops)
    values = [(held[n], 1) for n in range(top)] + [(other_values[n], 0) for n in range(top)]
    values_picked = pick_pages(values, me, pages, None)
    key_ahead, values_picked = lax.optimization_barrier((key_ahead, values_picked))
    values_other = swap(values_picked[0], top)
    other_keys = spread({0: other_key, first: key_ahead}, rest_hops)
    keys = [(held[n], 0) for n in range(top)] + [(other_keys[n], 0) for n in range(top)]
    keys_picked = pick_pages(keys, me, pages, scale)
    query, keys_picked = lax.optimization_barrier((query, keys_picked))
    keys_other = swap(keys_picked[0], top)

    def attended(number):
        return attend(
            query[number], keys, values, me, bounds[number], query_segs[number], key_seg, factor
        )

    for_other = attended(1)
    query, for_other = lax.optimization_barrier((query, for_other))
    from_other = swap(for_other, top)
    for_me = attended(0)
    page_store = [
        in_order(keys_picked[1], keys_other, -1),
        in_order(values_picked[1], values_other, -1),
    ]
    return in_order(for_me, from_other, -1), jnp.stack(page_store)


def solution(mesh):
    ring, ranks = mesh.shape["row"], mesh.shape["col"]

    def body(
        hidden, modulation, w_query, w_key, w_value, q_gain, k_gain, positions, segment_ids, page_table
    ):
        rest = (
            hidden,
            modulation,
            (w_query, w_key, w_value),
            (q_gain, k_gain),
            positions,
            segment_ids,
            page_table,
        )
        heads = w_query.shape[1] // HEAD_DIM
        feats, shard = w_query.shape[0], hidden.shape[1]
        powers = ring & (ring - 1) == 0 and ranks & (ranks - 1) == 0
        if heads % 2 == 0 and ring >= 8 and powers and feats % 128 == 0 and shard % feats == 0:
            return split_heads(ring, ranks, *rest)
        return whole_heads(ring, *rest)

    in_specs = (
        P("row", "col"),
        P(),
        P("row", "col"),
        P("row", "col"),
        P("row", "col"),
        P("col"),
        P("col"),
        P(None, "row"),
        P(),
        P(),
    )
    out_specs = (P("row", "col"), P(None, "row", None, "col"))
    return jax.shard_map(body, mesh=mesh, in_specs=in_specs, out_specs=out_specs, check_vma=False)
```

```python
import functools
import jax
import jax.numpy as jnp
from jax import lax
from jax.experimental import pallas as pl
from jax.experimental.pallas import tpu as pltpu
from jax.sharding import PartitionSpec as P

HEAD_DIM = 128
PAGE = 128
KEY_TILE = 512
VMEM = 60 * 1024 * 1024
LOG2E = 1.4426950408889634

epsilon = 1e-06


def rotary_lanes(positions, head_dim):
    pair_count = head_dim // 2
    frame_pairs = pair_count - 2 * (pair_count // 3)
    side_pairs = pair_count // 3
    column = jnp.arange(head_dim) // 2
    frame_rate = 10000.0 ** (-column.astype(jnp.float32) / frame_pairs)
    height_rate = 10000.0 ** (-(column - frame_pairs).astype(jnp.float32) / side_pairs)
    width_rate = 10000.0 ** (-(column - frame_pairs - side_pairs).astype(jnp.float32) / side_pairs)
    coords = positions.astype(jnp.float32)
    angles = jnp.where(
        column < frame_pairs,
        coords[0][:, None] * frame_rate,
        jnp.where(
            column < frame_pairs + side_pairs,
            coords[1][:, None] * height_rate,
            coords[2][:, None] * width_rate,
        ),
    )
    sine = jnp.sin(angles)
    even = (jnp.arange(head_dim) % 2 == 0)[None, :]
    return jnp.cos(angles), jnp.where(even, -sine, 0.0), jnp.where(even, 0.0, sine)


def modulate(activations, modulation):
    average = jnp.mean(activations, axis=1, keepdims=True)
    centred = activations - average
    variance = jnp.mean(centred * centred, axis=1, keepdims=True)
    normed = centred * lax.rsqrt(variance + epsilon)
    return (normed * (1.0 + modulation[1]) + modulation[0]).astype(jnp.bfloat16)


def cut_kernel(half_ref, *refs):
    weights, outs, sems = refs[:3], refs[3:6], refs[6]
    cols = outs[0].shape[2]
    half = half_ref[0]
    copies = []
    for number, weight in enumerate(weights):
        send, at = (1, number) if number < 2 else (2, 0)
        for which, target in ((half, outs[0].at[number]), (1 - half, outs[send].at[at])):
            span = pl.ds(pl.multiple_of(which * cols, cols), cols)
            copies.append(
                pltpu.make_async_copy(
                    weight.at[:, span], target, sems.at[number, len(copies) % 2]
                )
            )
            copies[-1].start()
    for copy in copies:
        copy.wait()


def cut(weights, half):
    rows, width = weights[0].shape
    cols = width // 2
    whole = pl.BlockSpec(memory_space=pltpu.VMEM)
    return pl.pallas_call(
        cut_kernel,
        in_specs=[pl.BlockSpec(memory_space=pltpu.SMEM)] + [pl.BlockSpec(memory_space=pl.ANY)] * 3,
        out_specs=[whole] * 3,
        out_shape=[jax.ShapeDtypeStruct((size, rows, cols), jnp.bfloat16) for size in (3, 2, 1)],
        scratch_shapes=[pltpu.SemaphoreType.DMA((3, 2))],
        compiler_params=pltpu.CompilerParams(vmem_limit_bytes=VMEM),
        cost_estimate=pl.CostEstimate(
            flops=0, bytes_accessed=12 * rows * width, transcendentals=0
        ),
        name="cut",
    )(half.reshape(1), *weights)


def turned(values, gain, tables, at):
    dim = tables[0].shape[1]
    cols = slice(at * dim, (at + 1) * dim)
    own, upper, lower = tables
    part = values[:, cols] * gain[:, cols]
    return part * own + pltpu.roll(part, dim - 1, 1) * upper + pltpu.roll(part, 1, 1) * lower


def project_kernel(
    parts, blocks, spots, first, final, in_count, place_ref, stats_ref, modulation_ref, *refs
):
    shard_count = sum(len(part[1]) for part in parts)
    out_count = len(refs) - 6 - in_count
    shards, rest = refs[:shard_count], refs[shard_count:]
    total, raws, weights, ready, raw_sems, weight_sems = rest[-6:]
    outs, sources = rest[-6 - out_count : -6], rest[: -6 - out_count]
    if final:
        sources, (gain_ref, own_ref, upper_ref, lower_ref) = sources[:-4], sources[-4:]
    if not first:
        sources, partial_ref = sources[:-1], sources[-1]
    me, rank = place_ref[0], place_ref[1]
    feats, cols = weights.shape[2:]
    rows = raws.shape[1]
    per_rank = shards[0].shape[-1] // feats
    copies = {}
    for slot, block in enumerate(blocks):
        owner = me ^ block
        span = pl.ds(pl.multiple_of((owner % per_rank) * feats, feats), feats)
        holder = owner // per_rank
        mine, begin, at = [], 0, 0
        for number, (length, places, by_rank) in enumerate(parts):
            held = shards[at : at + len(places)]
            at += len(places)
            target = raws.at[slot, pl.ds(begin, length), :]
            begin += length
            sem = raw_sems.at[slot, number]
            if by_rank:
                copy = pltpu.make_async_copy(
                    held[0].at[holder, pl.ds(places[0], length), span], target, sem
                )
                copy.start()
            else:
                for step, (ref, skip) in enumerate(zip(held, places)):
                    source = ref.at[pl.ds(skip, length), span]

                    @pl.when((holder ^ rank) == step)
                    def _(source=source, target=target, sem=sem):
                        pltpu.make_async_copy(source, target, sem).start()

                copy = pltpu.make_async_copy(source, target, sem)
            mine.append(copy)
        matrices = [
            pltpu.make_async_copy(
                sources[source].at[place], weights.at[slot, number], weight_sems.at[slot, number]
            )
            for number, (source, place) in enumerate(spots[block])
        ]
        for copy in matrices:
            copy.start()
        copies[slot] = (mine, matrices)

    def column(at):
        return jnp.transpose(jnp.broadcast_to(stats_ref[at : at + 1, :], (128, rows)))

    mean, scale = column(0), column(1)

    def prepare(first_slot):
        for slot in (first_slot, first_slot + 1):
            for copy in copies[slot][0]:
                copy.wait()
            span = pl.ds(pl.multiple_of((me ^ blocks[slot]) * feats, feats), feats)
            shift = modulation_ref[0:1, span]
            gain = 1.0 + modulation_ref[1:2, span]
            left = (slot - first_slot) * feats
            for start in range(0, feats, 128):
                lanes = slice(start, start + 128)
                part = raws[slot, :, lanes].astype(jnp.float32)
                part = (part - mean) * scale * gain[:, lanes] + shift[:, lanes]
                ready[first_slot // 2 % 2, :, left + start : left + start + 128] = part.astype(
                    jnp.bfloat16
                )

    prepare(0)
    for slot in range(0, len(blocks), 2):
        for copy in copies[slot][1] + copies[slot + 1][1]:
            copy.wait()
        if slot + 2 < len(blocks):
            prepare(slot + 2)
        right = jnp.concatenate(
            [
                jnp.concatenate([weights[slot, m], weights[slot + 1, m]], axis=0)
                for m in range(3)
            ],
            axis=1,
        )
        part = jnp.dot(ready[slot // 2 % 2], right, preferred_element_type=jnp.float32)
        if slot:
            part = part + total[...]
        elif not first:
            part = part + partial_ref[...]
        if slot + 2 < len(blocks):
            total[...] = part
    if not final:
        outs[0][...] = part
        return
    query_ref, squares_ref = outs[:2]
    key_ref, value_ref = outs[2:] if len(outs) == 4 else (outs[2], outs[2])
    key, value, query = [part[:, m * cols : (m + 1) * cols] for m in range(3)]
    query_ref[...] = query
    value_ref[value_ref.shape[0] - 1] = value.astype(jnp.bfloat16)
    tables = (own_ref[...], upper_ref[...], lower_ref[...])
    for head in range(cols // HEAD_DIM):
        lanes = slice(head * HEAD_DIM, (head + 1) * HEAD_DIM)
        key_ref[0, :, lanes] = turned(key, gain_ref, tables, head).astype(jnp.bfloat16)
    for kind, raw in enumerate((key, query)):
        summed = jnp.sum(raw * raw, axis=1, keepdims=True)
        summed = jnp.transpose(jnp.broadcast_to(summed, (rows, 128)))
        squares_ref[kind : kind + 1, :] = summed[:1]


def project(
    place, stats, modulation, parts, blocks, shards, spots, sources, partial, finish, joint=True
):
    rows = sum(part[0] for part in parts)
    _, feats, cols = sources[0].shape
    count = len(blocks)
    anywhere = pl.BlockSpec(memory_space=pl.ANY)
    whole = pl.BlockSpec(memory_space=pltpu.VMEM)
    out_shape = [jax.ShapeDtypeStruct((rows, 3 * cols), jnp.float32)]
    extra = [] if partial is None else [partial]
    if finish is not None:
        extra.extend(finish)
        held = [2] if joint else [1, 1]
        out_shape = [
            jax.ShapeDtypeStruct((rows, cols), jnp.float32),
            jax.ShapeDtypeStruct((2, rows), jnp.float32),
        ] + [jax.ShapeDtypeStruct((size, rows, cols), jnp.bfloat16) for size in held]
    return pl.pallas_call(
        functools.partial(
            project_kernel,
            parts,
            blocks,
            spots,
            partial is None,
            finish is not None,
            len(shards) + len(sources) + len(extra),
        ),
        in_specs=[pl.BlockSpec(memory_space=pltpu.SMEM), whole, whole]
        + [anywhere] * (len(shards) + len(sources))
        + [whole] * len(extra),
        out_specs=[whole] * len(out_shape),
        out_shape=out_shape,
        scratch_shapes=[
            pltpu.VMEM((rows, 3 * cols), jnp.float32),
            pltpu.VMEM((count, rows, feats), jnp.bfloat16),
            pltpu.VMEM((count, 3, feats, cols), jnp.bfloat16),
            pltpu.VMEM((2, rows, 2 * feats), jnp.bfloat16),
            pltpu.SemaphoreType.DMA((count, len(parts))),
            pltpu.SemaphoreType.DMA((count, 3)),
        ],
        compiler_params=pltpu.CompilerParams(vmem_limit_bytes=VMEM),
        cost_estimate=pl.CostEstimate(
            flops=6 * rows * count * feats * cols,
            bytes_accessed=2 * count * feats * (rows + 3 * cols) + 12 * rows * cols,
            transcendentals=0,
        ),
        name="project",
    )(place, stats, modulation, *shards, *sources, *extra)


def turn_kernel(count, width, squares_ref, gain_ref, *refs):
    for number in range(count):
        raw_ref, out_ref = refs[number], refs[4 * count + number]
        tables = [ref[...] for ref in refs[count + 3 * number : count + 3 * number + 3]]
        rows, cols = raw_ref.shape
        scale = lax.rsqrt(squares_ref[number : number + 1, :] * (1.0 / width) + epsilon)
        scale = jnp.transpose(jnp.broadcast_to(scale, (HEAD_DIM, rows)))
        for head in range(cols // HEAD_DIM):
            lanes = slice(head * HEAD_DIM, (head + 1) * HEAD_DIM)
            out_ref[:, lanes] = turned(
                raw_ref[:, lanes] * scale, gain_ref[:, lanes], tables, 0
            ).astype(jnp.bfloat16)


def turn(raws, squares, gain, tables, width):
    count = len(raws)
    rows, cols = raws[0].shape
    whole = pl.BlockSpec(memory_space=pltpu.VMEM)
    return pl.pallas_call(
        functools.partial(turn_kernel, count, width),
        in_specs=[whole] * (2 + 4 * count),
        out_specs=[whole] * count,
        out_shape=[jax.ShapeDtypeStruct((rows, cols), jnp.bfloat16)] * count,
        compiler_params=pltpu.CompilerParams(vmem_limit_bytes=VMEM),
        cost_estimate=pl.CostEstimate(flops=0, bytes_accessed=0, transcendentals=0),
        name="turn",
    )(squares, gain, *raws, *[part for table in tables for part in table])


def attend_kernel(places, me_ref, bounds_ref, q_ref, *refs):
    count = len(places)
    pieces, (query_seg_ref, key_seg_ref, factor_ref) = refs[:count], refs[count : count + 3]
    out_ref, keys, values, highest, mixed, sems = refs[count + 3 :]
    me = me_ref[0]
    rows = pieces[0].shape[1]
    low, high = bounds_ref[0], bounds_ref[1]
    first = low * KEY_TILE // rows
    end = (high * KEY_TILE + rows - 1) // rows
    for number, (piece, (kind, at)) in enumerate(zip(pieces, places)):
        owner = me ^ (number % (count // 2))
        held = (keys, values)[kind]
        target = held.at[pl.ds(pl.multiple_of(owner * rows, rows), rows), :]
        sem = sems.at[kind, owner]

        @pl.when((owner >= first) & (owner < end))
        def _(source=piece.at[at], target=target, sem=sem):
            pltpu.make_async_copy(source, target, sem).start()

    def arrive(owner, carry):
        for kind, held in enumerate((keys, values)):
            target = held.at[pl.ds(pl.multiple_of(owner * rows, rows), rows), :]
            pltpu.make_async_copy(pieces[0].at[0], target, sems.at[kind, owner]).wait()
        return carry

    dim = HEAD_DIM
    heads = q_ref.shape[1] // dim
    ones = jnp.ones((KEY_TILE, dim), jnp.bfloat16)
    highest[...] = jnp.full_like(highest, -1e29)
    mixed[...] = jnp.zeros_like(mixed)
    query_seg = jnp.transpose(jnp.broadcast_to(query_seg_ref[...], (dim, rows)))
    times = KEY_TILE // dim

    def step(block, carry):
        begin = jnp.where(block == low, first, (block * KEY_TILE + rows - 1) // rows)
        lax.fori_loop(begin, ((block + 1) * KEY_TILE + rows - 1) // rows, arrive, 0)
        where = pl.ds(pl.multiple_of(block * KEY_TILE, KEY_TILE), KEY_TILE)
        same = jnp.concatenate([query_seg] * times, axis=1) == key_seg_ref[block]
        factor = factor_ref[block]
        for head in range(heads):
            cols = slice(head * dim, (head + 1) * dim)
            scores = lax.dot_general(
                q_ref[:, cols],
                keys[where, cols],
                (((1,), (1,)), ((), ())),
                preferred_element_type=jnp.float32,
            )
            scores = jnp.where(same, scores * factor, -1e30)
            former = highest[head]
            newest = jnp.maximum(former, jnp.max(scores, axis=1, keepdims=True))
            highest[head] = newest
            weights = jnp.exp2(scores - jnp.concatenate([newest] * times, axis=1))
            weights = weights.astype(jnp.bfloat16)
            right = jnp.concatenate([values[where, cols], ones], axis=1)
            part = jnp.dot(weights, right, preferred_element_type=jnp.float32)
            shrink = jnp.exp2(former - newest)
            mixed[head, :, :dim] = mixed[head, :, :dim] * shrink + part[:, :dim]
            mixed[head, :, dim:] = mixed[head, :, dim:] * shrink + part[:, dim:]
        return carry

    lax.fori_loop(low, high, step, 0)
    for head in range(heads):
        out_ref[:, head * dim : (head + 1) * dim] = (
            mixed[head, :, :dim] / mixed[head, :, dim:]
        ).astype(out_ref.dtype)


def key_bounds(query_seg, segment_ids):
    low = jnp.sum(segment_ids < query_seg[0], dtype=jnp.int32)
    high = jnp.sum(segment_ids <= query_seg[-1], dtype=jnp.int32)
    return jnp.stack([low // KEY_TILE, (high + KEY_TILE - 1) // KEY_TILE])


def attend(query, keys, values, me, bounds, query_seg, key_seg, factor):
    rows, cols = query.shape
    pieces = [array for array, _ in keys + values]
    places = tuple((0, at) for _, at in keys) + tuple((1, at) for _, at in values)
    count = len(pieces)
    tokens = key_seg.shape[0] * KEY_TILE
    dim = HEAD_DIM
    heads = cols // dim
    smem = pl.BlockSpec(memory_space=pltpu.SMEM)
    whole = pl.BlockSpec(memory_space=pltpu.VMEM)
    return pl.pallas_call(
        functools.partial(attend_kernel, places),
        in_specs=[smem, smem, whole] + [pl.BlockSpec(memory_space=pl.ANY)] * count + [whole] * 3,
        out_specs=whole,
        scratch_shapes=[
            pltpu.VMEM((tokens, cols), jnp.bfloat16),
            pltpu.VMEM((tokens, cols), jnp.bfloat16),
            pltpu.VMEM((heads, rows, dim), jnp.float32),
            pltpu.VMEM((heads, rows, 2 * dim), jnp.float32),
            pltpu.SemaphoreType.DMA((2, count // 2)),
        ],
        out_shape=jax.ShapeDtypeStruct((rows, cols), jnp.bfloat16),
        compiler_params=pltpu.CompilerParams(vmem_limit_bytes=VMEM),
        cost_estimate=pl.CostEstimate(
            flops=2 * rows * tokens * cols,
            bytes_accessed=4 * tokens * cols + 4 * rows * cols,
            transcendentals=rows * tokens * heads // 2,
        ),
        name="attend",
    )(me.reshape(1), bounds, query, *pieces, query_seg, key_seg, factor)


def pages_kernel(places, me_ref, page_ref, *refs):
    count = len(places)
    pieces, rest = refs[:count], refs[count:]
    scale_ref, (out_refs, held, sems) = (rest[0] if len(rest) == 5 else None), (
        rest[-4:-2],
        rest[-2],
        rest[-1],
    )
    me = me_ref[0]
    wanted = held.shape[0]
    per_block = pieces[0].shape[1] // PAGE
    waits = []
    for number in range(wanted):
        page = page_ref[number]
        rows = pl.ds(pl.multiple_of((page % per_block) * PAGE, PAGE), PAGE)
        target, sem = held.at[number], sems.at[number]
        for owner, (piece, at) in enumerate(zip(pieces, places)):

            @pl.when((page // per_block) == (me ^ owner))
            def _(source=piece.at[at, rows, :], target=target, sem=sem):
                pltpu.make_async_copy(source, target, sem).start()

        waits.append(pltpu.make_async_copy(pieces[0].at[0, pl.ds(0, PAGE), :], target, sem))
    for number in range(wanted):
        waits[number].wait()
        each = wanted // 2
        out_ref = out_refs[number // each].at[number % each]
        if scale_ref is None:
            out_ref[...] = held[number]
            continue
        scale = jnp.transpose(jnp.broadcast_to(scale_ref[page_ref[number]], (HEAD_DIM, PAGE)))
        for start in range(0, held.shape[2], HEAD_DIM):
            lanes = slice(start, start + HEAD_DIM)
            page = held[number, :, lanes].astype(jnp.float32) * scale
            out_ref[:, lanes] = page.astype(jnp.bfloat16)


def pick_pages(pieces, me, pages, scale):
    _, rows, cols = pieces[0][0].shape
    wanted = pages.shape[0]
    smem = pl.BlockSpec(memory_space=pltpu.SMEM)
    whole = pl.BlockSpec(memory_space=pltpu.VMEM)
    extra = [] if scale is None else [scale]
    return pl.pallas_call(
        functools.partial(pages_kernel, tuple(at for _, at in pieces)),
        in_specs=[smem, smem]
        + [pl.BlockSpec(memory_space=pl.ANY)] * len(pieces)
        + [whole] * len(extra),
        out_specs=[whole] * 2,
        out_shape=[jax.ShapeDtypeStruct((wanted // 2, PAGE, cols), jnp.bfloat16)] * 2,
        scratch_shapes=[
            pltpu.VMEM((wanted, PAGE, cols), jnp.bfloat16),
            pltpu.SemaphoreType.DMA((wanted,)),
        ],
        compiler_params=pltpu.CompilerParams(vmem_limit_bytes=VMEM),
        cost_estimate=pl.CostEstimate(flops=0, bytes_accessed=0, transcendentals=0),
        name="pick_pages",
    )(me.reshape(1), pages, *[array for array, _ in pieces], *extra)


def own_pages(page_table, start, count):
    page_total = page_table.shape[0]
    inverse = (
        jnp.zeros((page_total,), jnp.int32)
        .at[page_table]
        .set(jnp.arange(page_total, dtype=jnp.int32))
    )
    return lax.dynamic_slice_in_dim(inverse, start, count, 0)


def whole_heads(ring, hidden, modulation, weights, gains, positions, segment_ids, page_table):
    tok_rows = hidden.shape[0]
    me = lax.axis_index("row")
    full_rows = lax.all_gather(hidden, "col", axis=1, tiled=True)
    modulated = modulate(full_rows.astype(jnp.float32), modulation)
    width = full_rows.shape[1]
    raws = [
        jnp.dot(
            modulated,
            lax.all_gather(weight, "row", axis=0, tiled=True),
            preferred_element_type=jnp.float32,
        )
        for weight in weights
    ]
    squares = lax.psum(tuple(jnp.sum(raw * raw, axis=1) for raw in raws[:2]), "col")
    tables = rotary_lanes(positions, HEAD_DIM)
    query, key = [
        turn([raw], total[None], gain[None], [tables], width)[0]
        for raw, total, gain in zip(raws, squares, gains)
    ]
    held = lax.all_gather(jnp.stack([key, raws[2].astype(jnp.bfloat16)]), "row", axis=0)
    keys, values = [[(held[number], kind) for number in range(ring)] for kind in range(2)]
    none = jnp.zeros((), jnp.int32)
    query_seg = lax.dynamic_slice_in_dim(segment_ids, me * tok_rows, tok_rows, 0)
    key_seg = segment_ids.astype(jnp.float32).reshape(-1, 1, KEY_TILE)
    attended = attend(
        query,
        keys,
        values,
        none,
        key_bounds(query_seg, segment_ids),
        query_seg.astype(jnp.float32)[None, :],
        key_seg,
        jnp.full_like(key_seg, HEAD_DIM ** (-0.5) * LOG2E),
    )
    count = tok_rows // PAGE
    pages = own_pages(page_table, me * count, count)
    pages = jnp.concatenate([pages, pages])
    picked = [pick_pages(pieces, none, pages, None)[0] for pieces in (keys, values)]
    return attended, jnp.stack(picked)


def split_heads(ring, ranks, hidden, modulation, weights, gains, positions, segment_ids, page_table):
    tok_rows, shard = hidden.shape
    width = ranks * shard
    me = lax.axis_index("row")
    rank = lax.axis_index("col")
    top = ring // 2
    half = me // top
    cols = weights[0].shape[1] // 2
    hops = []
    bit = top // 2
    while bit:
        hops.append(bit)
        bit //= 2

    def swap(value, bit):
        return lax.ppermute(value, "row", [(i, i ^ bit) for i in range(ring)])

    def across(value, step):
        return lax.ppermute(value, "col", [(c, c ^ step) for c in range(ranks)])

    def spread(blocks, bits):
        for bit in bits:
            blocks.update({number | bit: swap(blocks[number], bit) for number in list(blocks)})
        return blocks

    def in_order(mine, other, axis):
        return jnp.where(
            half == 0,
            jnp.concatenate([mine, other], axis=axis),
            jnp.concatenate([other, mine], axis=axis),
        )

    hidden_all = lax.all_gather(hidden, "col", axis=0)
    w_query, w_key, w_value = weights
    own, send_pair, send_single = cut((w_key, w_value, w_query), half)
    first, rest_hops = hops[0], hops[1:]
    pair, single = swap(send_pair, top), swap(send_single, top)
    next_own = swap(own, first)
    own_blocks = spread({0: own}, rest_hops)

    rows = hidden.astype(jnp.float32)
    local_mean = jnp.mean(rows, axis=1)
    local_square = jnp.sum(jnp.square(rows - local_mean[:, None]), axis=1)
    stats = jnp.stack([local_mean, local_square])
    all_stats = [stats] + [across(stats, step) for step in range(1, ranks)]
    average = sum(part[0] for part in all_stats) / ranks
    variance = (
        sum(part[1] + shard * jnp.square(part[0] - average) for part in all_stats) / width
    )
    small = jnp.concatenate(
        [jnp.stack([average, lax.rsqrt(variance + epsilon)]), positions.astype(jnp.float32)]
    )
    small_other = swap(small, top)
    moved = (pair, single, next_own, own_blocks, small, small_other)
    moved, hidden_late = lax.optimization_barrier((moved, hidden))
    pair, single, next_own, own_blocks, small, small_other = moved

    next_single = swap(single, first)
    other_rows = swap(hidden_late, top)
    pair_blocks = spread({0: pair}, rest_hops)
    single_blocks = spread({0: single}, rest_hops)
    next_own_blocks = spread({0: next_own}, rest_hops)
    early = tok_rows * 11 // 24 // 16 * 16
    sent = jnp.concatenate(
        [
            lax.dynamic_slice(hidden_all, (rank ^ step, early, 0), (1, tok_rows - early, shard))
            for step in range(1, ranks)
        ]
    ).reshape(-1, shard)
    moved = (next_single, other_rows, pair_blocks, single_blocks, next_own_blocks, sent)
    plain = (small, small_other, segment_ids, page_table, gains)
    moved, hidden_all, plain = lax.optimization_barrier((moved, hidden_all, plain))
    next_single, other_rows, pair_blocks, single_blocks, next_own_blocks, sent = moved
    small, small_other, segment_ids, page_table, gains = plain

    rest = swap(sent, top)
    next_pair = swap(pair_blocks[0], first)
    early_shards = [across(other_rows[:early], step) for step in range(1, ranks)]
    sources, spots = [], [None] * ring
    for number in own_blocks:
        for offset, whole in ((0, own_blocks), (first, next_own_blocks)):
            spots[number | offset] = tuple((len(sources), m) for m in range(3))
            sources.append(whole[number])
        at = len(sources)
        spots[number | top] = ((at, 0), (at, 1), (at + 1, 0))
        sources.extend([pair_blocks[number], single_blocks[number]])
    here = tuple(number for number in range(ring) if spots[number] is not None)
    late = tuple(number for number in range(ring) if spots[number] is None)
    own_parts = ((tok_rows, (0,), True),)
    place = jnp.stack([me, rank]).astype(jnp.int32)
    (partial,) = project(
        place,
        small[:2],
        modulation,
        own_parts,
        here,
        [hidden_all],
        tuple(spots),
        list(sources),
        None,
        None,
    )
    tables = [rotary_lanes(part[2:], HEAD_DIM) for part in (small, small_other)]
    q_gain, k_gain = [
        lax.dynamic_slice_in_dim(gain, half * cols, cols, 0)[None, :] for gain in gains
    ]
    count = tok_rows // PAGE
    pages = jnp.concatenate(
        [own_pages(page_table, owner * count, count) for owner in (me ^ top, me)]
    )
    query_segs = [
        lax.dynamic_slice_in_dim(segment_ids, owner * tok_rows, tok_rows, 0)
        for owner in (me, me ^ top)
    ]
    bounds = [key_bounds(seg, segment_ids) for seg in query_segs]
    query_segs = [seg.astype(jnp.float32)[None, :] for seg in query_segs]
    key_seg = segment_ids.astype(jnp.float32).reshape(-1, 1, KEY_TILE)
    prepared = (tables, q_gain, k_gain, pages, query_segs, key_seg, bounds)
    moved = (next_pair, next_single, rest, early_shards)
    moved, prepared, partial = lax.optimization_barrier((moved, prepared, partial))
    next_pair, next_single, rest, early_shards = moved
    tables, q_gain, k_gain, pages, query_segs, key_seg, bounds = prepared

    next_pair_blocks = spread({0: next_pair}, rest_hops)
    next_single_blocks = spread({0: next_single}, rest_hops)
    for number in own_blocks:
        at = len(sources)
        spots[number | top | first] = ((at, 0), (at, 1), (at + 1, 0))
        sources.extend([next_pair_blocks[number], next_single_blocks[number]])
    other_parts = (
        (early, (0,) * ranks, False),
        (
            tok_rows - early,
            (early,) + tuple(step * (tok_rows - early) for step in range(ranks - 1)),
            False,
        ),
    )
    late_sources = [part for number in own_blocks for part in (next_pair_blocks[number], next_single_blocks[number])]
    late_spots = list(spots)
    for at, number in enumerate(own_blocks):
        late_spots[number | top | first] = ((2 * at, 0), (2 * at, 1), (2 * at + 1, 0))
    own_query, own_squares, own_held = project(
        place,
        small[:2],
        modulation,
        own_parts,
        late,
        [hidden_all],
        tuple(late_spots),
        late_sources,
        partial,
        (k_gain, *tables[0]),
    )
    own_ahead = swap(own_held, first)
    other_query, other_squares, other_key, other_value = project(
        place,
        small_other[:2],
        modulation,
        other_parts,
        tuple(range(ring)),
        [other_rows] + early_shards + [other_rows] + [rest] * (ranks - 1),
        tuple(spots),
        sources,
        None,
        (k_gain, *tables[1]),
        joint=False,
    )
    value_ahead = swap(other_value, first)

    squares = jnp.stack([own_squares, other_squares])
    squares = squares + swap(squares, top)[::-1]
    bit = 1
    while bit < ranks:
        squares = squares + across(squares, bit)
        bit *= 2
    query = turn([own_query, other_query], squares[:, 1], q_gain, tables, width)
    key_squares = {0: squares[:, 0]}
    key_squares[first] = swap(key_squares[0], first)
    key_ahead = swap(other_key, first)
    key_squares[0], query, own_ahead, value_ahead = lax.optimization_barrier(
        (key_squares[0], query, own_ahead, value_ahead)
    )
    key_squares = spread(key_squares, rest_hops)
    blocks = jnp.stack([key_squares[n % top][n // top] for n in range(ring)])
    scale = lax.rsqrt(blocks / width + epsilon)
    scale = jnp.concatenate(
        [lax.dynamic_slice_in_dim(scale, me ^ owner, 1, 0) for owner in range(ring)]
    )
    factor = (scale * (HEAD_DIM ** (-0.5) * LOG2E)).reshape(-1, 1, KEY_TILE)
    scale = scale.reshape(-1, 1, PAGE)
    held = spread({0: own_held, first: own_ahead}, rest_hops)
    other_values = spread({0: other_value, first: value_ahead}, rest_hops)
    values = [(held[n], 1) for n in range(top)] + [(other_values[n], 0) for n in range(top)]
    values_picked = pick_pages(values, me, pages, None)
    values_other = swap(values_picked[0], top)
    key_ahead, values_other = lax.optimization_barrier((key_ahead, values_other))
    other_keys = spread({0: other_key, first: key_ahead}, rest_hops)
    keys = [(held[n], 0) for n in range(top)] + [(other_keys[n], 0) for n in range(top)]
    keys_picked = pick_pages(keys, me, pages, scale)
    query, keys_picked = lax.optimization_barrier((query, keys_picked))
    keys_other = swap(keys_picked[0], top)

    def attended(number):
        return attend(
            query[number], keys, values, me, bounds[number], query_segs[number], key_seg, factor
        )

    for_other = attended(1)
    query, for_other = lax.optimization_barrier((query, for_other))
    from_other = swap(for_other, top)
    for_me = attended(0)
    page_store = [
        in_order(keys_picked[1], keys_other, -1),
        in_order(values_picked[1], values_other, -1),
    ]
    return in_order(for_me, from_other, -1), jnp.stack(page_store)


def solution(mesh):
    ring, ranks = mesh.shape["row"], mesh.shape["col"]

    def body(
        hidden, modulation, w_query, w_key, w_value, q_gain, k_gain, positions, segment_ids, page_table
    ):
        rest = (
            hidden,
            modulation,
            (w_query, w_key, w_value),
            (q_gain, k_gain),
            positions,
            segment_ids,
            page_table,
        )
        heads = w_query.shape[1] // HEAD_DIM
        feats, shard = w_query.shape[0], hidden.shape[1]
        powers = ring & (ring - 1) == 0 and ranks & (ranks - 1) == 0
        if heads % 2 == 0 and ring >= 8 and powers and feats % 128 == 0 and shard % feats == 0:
            return split_heads(ring, ranks, *rest)
        return whole_heads(ring, *rest)

    in_specs = (
        P("row", "col"),
        P(),
        P("row", "col"),
        P("row", "col"),
        P("row", "col"),
        P("col"),
        P("col"),
        P(None, "row"),
        P(),
        P(),
    )
    out_specs = (P("row", "col"), P(None, "row", None, "col"))
    return jax.shard_map(body, mesh=mesh, in_specs=in_specs, out_specs=out_specs, check_vma=False)
```

```python
import functools
import jax
import jax.numpy as jnp
from jax import lax
from jax.experimental import pallas as pl
from jax.experimental.pallas import tpu as pltpu
from jax.sharding import PartitionSpec as P

HEAD_DIM = 128
PAGE = 128
KEY_TILE = 512
VMEM = 60 * 1024 * 1024
LOG2E = 1.4426950408889634

epsilon = 1e-06


def rotary_lanes(positions, head_dim):
    pair_count = head_dim // 2
    frame_pairs = pair_count - 2 * (pair_count // 3)
    side_pairs = pair_count // 3
    column = jnp.arange(head_dim) // 2
    frame_rate = 10000.0 ** (-column.astype(jnp.float32) / frame_pairs)
    height_rate = 10000.0 ** (-(column - frame_pairs).astype(jnp.float32) / side_pairs)
    width_rate = 10000.0 ** (-(column - frame_pairs - side_pairs).astype(jnp.float32) / side_pairs)
    coords = positions.astype(jnp.float32)
    angles = jnp.where(
        column < frame_pairs,
        coords[0][:, None] * frame_rate,
        jnp.where(
            column < frame_pairs + side_pairs,
            coords[1][:, None] * height_rate,
            coords[2][:, None] * width_rate,
        ),
    )
    sine = jnp.sin(angles)
    even = (jnp.arange(head_dim) % 2 == 0)[None, :]
    return jnp.cos(angles), jnp.where(even, -sine, 0.0), jnp.where(even, 0.0, sine)


def modulate(activations, modulation):
    average = jnp.mean(activations, axis=1, keepdims=True)
    centred = activations - average
    variance = jnp.mean(centred * centred, axis=1, keepdims=True)
    normed = centred * lax.rsqrt(variance + epsilon)
    return (normed * (1.0 + modulation[1]) + modulation[0]).astype(jnp.bfloat16)


def cut_kernel(picks, half_ref, *refs):
    weights, outs, sems = refs[:3], refs[3:-1], refs[-1]
    cols = outs[0].shape[2]
    copies = []
    for out, chosen in zip(outs, picks):
        for at, (number, other) in enumerate(chosen):
            which = 1 - half_ref[0] if other else half_ref[0]
            span = pl.ds(pl.multiple_of(which * cols, cols), cols)
            copies.append(
                pltpu.make_async_copy(
                    weights[number].at[:, span], out.at[at], sems.at[number, int(other)]
                )
            )
            copies[-1].start()
    for copy in copies:
        copy.wait()


def cut(weights, half, picks):
    rows, width = weights[0].shape
    cols = width // 2
    whole = pl.BlockSpec(memory_space=pltpu.VMEM)
    return pl.pallas_call(
        functools.partial(cut_kernel, picks),
        in_specs=[pl.BlockSpec(memory_space=pltpu.SMEM)] + [pl.BlockSpec(memory_space=pl.ANY)] * 3,
        out_specs=[whole] * len(picks),
        out_shape=[
            jax.ShapeDtypeStruct((len(chosen), rows, cols), jnp.bfloat16) for chosen in picks
        ],
        scratch_shapes=[pltpu.SemaphoreType.DMA((3, 2))],
        compiler_params=pltpu.CompilerParams(vmem_limit_bytes=VMEM),
        cost_estimate=pl.CostEstimate(
            flops=0, bytes_accessed=4 * sum(map(len, picks)) * rows * cols, transcendentals=0
        ),
        name="cut",
    )(half.reshape(1), *weights)


def turned(values, gain, tables, at):
    dim = tables[0].shape[1]
    cols = slice(at * dim, (at + 1) * dim)
    own, upper, lower = tables
    part = values[:, cols] * gain[:, cols]
    return part * own + pltpu.roll(part, dim - 1, 1) * upper + pltpu.roll(part, 1, 1) * lower


def project_kernel(
    parts, blocks, spots, first, final, in_count, place_ref, stats_ref, modulation_ref, *refs
):
    shard_count = sum(len(part[1]) for part in parts)
    out_count = len(refs) - 6 - in_count
    shards, rest = refs[:shard_count], refs[shard_count:]
    total, raws, weights, ready, raw_sems, weight_sems = rest[-6:]
    outs, sources = rest[-6 - out_count : -6], rest[: -6 - out_count]
    if final:
        sources, (gain_ref, own_ref, upper_ref, lower_ref) = sources[:-4], sources[-4:]
    if not first:
        sources, partial_ref = sources[:-1], sources[-1]
    me, rank = place_ref[0], place_ref[1]
    feats, cols = weights.shape[2:]
    rows = raws.shape[1]
    per_rank = shards[0].shape[-1] // feats
    copies = {}
    for slot, block in enumerate(blocks):
        owner = me ^ block
        span = pl.ds(pl.multiple_of((owner % per_rank) * feats, feats), feats)
        holder = owner // per_rank
        mine, begin, at = [], 0, 0
        for number, (length, places, by_rank) in enumerate(parts):
            held = shards[at : at + len(places)]
            at += len(places)
            target = raws.at[slot, pl.ds(begin, length), :]
            begin += length
            sem = raw_sems.at[slot, number]
            if by_rank:
                copy = pltpu.make_async_copy(
                    held[0].at[holder, pl.ds(places[0], length), span], target, sem
                )
                copy.start()
            else:
                for step, (ref, skip) in enumerate(zip(held, places)):
                    source = ref.at[pl.ds(skip, length), span]

                    @pl.when((holder ^ rank) == step)
                    def _(source=source, target=target, sem=sem):
                        pltpu.make_async_copy(source, target, sem).start()

                copy = pltpu.make_async_copy(source, target, sem)
            mine.append(copy)
        matrices = [
            pltpu.make_async_copy(
                sources[source].at[place], weights.at[slot, number], weight_sems.at[slot, number]
            )
            for number, (source, place) in enumerate(spots[block])
        ]
        for copy in matrices:
            copy.start()
        copies[slot] = (mine, matrices)

    def column(at):
        return jnp.transpose(jnp.broadcast_to(stats_ref[at : at + 1, :], (128, rows)))

    mean, scale = column(0), column(1)

    def prepare(first_slot):
        for slot in (first_slot, first_slot + 1):
            for copy in copies[slot][0]:
                copy.wait()
            span = pl.ds(pl.multiple_of((me ^ blocks[slot]) * feats, feats), feats)
            shift = modulation_ref[0:1, span]
            gain = 1.0 + modulation_ref[1:2, span]
            left = (slot - first_slot) * feats
            for start in range(0, feats, 128):
                lanes = slice(start, start + 128)
                part = raws[slot, :, lanes].astype(jnp.float32)
                part = (part - mean) * scale * gain[:, lanes] + shift[:, lanes]
                ready[first_slot // 2 % 2, :, left + start : left + start + 128] = part.astype(
                    jnp.bfloat16
                )

    prepare(0)
    for slot in range(0, len(blocks), 2):
        for copy in copies[slot][1] + copies[slot + 1][1]:
            copy.wait()
        if slot + 2 < len(blocks):
            prepare(slot + 2)
        right = jnp.concatenate(
            [
                jnp.concatenate([weights[slot, m], weights[slot + 1, m]], axis=0)
                for m in range(3)
            ],
            axis=1,
        )
        part = jnp.dot(ready[slot // 2 % 2], right, preferred_element_type=jnp.float32)
        if slot:
            part = part + total[...]
        elif not first:
            part = part + partial_ref[...]
        if slot + 2 < len(blocks):
            total[...] = part
    if not final:
        outs[0][...] = part
        return
    query_ref, squares_ref = outs[:2]
    key_ref, value_ref = outs[2:] if len(outs) == 4 else (outs[2], outs[2])
    key, value, query = [part[:, m * cols : (m + 1) * cols] for m in range(3)]
    query_ref[...] = query
    value_ref[value_ref.shape[0] - 1] = value.astype(jnp.bfloat16)
    tables = (own_ref[...], upper_ref[...], lower_ref[...])
    for head in range(cols // HEAD_DIM):
        lanes = slice(head * HEAD_DIM, (head + 1) * HEAD_DIM)
        key_ref[0, :, lanes] = turned(key, gain_ref, tables, head).astype(jnp.bfloat16)
    for kind, raw in enumerate((key, query)):
        summed = jnp.sum(raw * raw, axis=1, keepdims=True)
        summed = jnp.transpose(jnp.broadcast_to(summed, (rows, 128)))
        squares_ref[kind : kind + 1, :] = summed[:1]


def project(
    place, stats, modulation, parts, blocks, shards, spots, sources, partial, finish, joint=True
):
    rows = sum(part[0] for part in parts)
    _, feats, cols = sources[0].shape
    count = len(blocks)
    anywhere = pl.BlockSpec(memory_space=pl.ANY)
    whole = pl.BlockSpec(memory_space=pltpu.VMEM)
    out_shape = [jax.ShapeDtypeStruct((rows, 3 * cols), jnp.float32)]
    extra = [] if partial is None else [partial]
    if finish is not None:
        extra.extend(finish)
        held = [2] if joint else [1, 1]
        out_shape = [
            jax.ShapeDtypeStruct((rows, cols), jnp.float32),
            jax.ShapeDtypeStruct((2, rows), jnp.float32),
        ] + [jax.ShapeDtypeStruct((size, rows, cols), jnp.bfloat16) for size in held]
    return pl.pallas_call(
        functools.partial(
            project_kernel,
            parts,
            blocks,
            spots,
            partial is None,
            finish is not None,
            len(shards) + len(sources) + len(extra),
        ),
        in_specs=[pl.BlockSpec(memory_space=pltpu.SMEM), whole, whole]
        + [anywhere] * (len(shards) + len(sources))
        + [whole] * len(extra),
        out_specs=[whole] * len(out_shape),
        out_shape=out_shape,
        scratch_shapes=[
            pltpu.VMEM((rows, 3 * cols), jnp.float32),
            pltpu.VMEM((count, rows, feats), jnp.bfloat16),
            pltpu.VMEM((count, 3, feats, cols), jnp.bfloat16),
            pltpu.VMEM((2, rows, 2 * feats), jnp.bfloat16),
            pltpu.SemaphoreType.DMA((count, len(parts))),
            pltpu.SemaphoreType.DMA((count, 3)),
        ],
        compiler_params=pltpu.CompilerParams(vmem_limit_bytes=VMEM),
        cost_estimate=pl.CostEstimate(
            flops=6 * rows * count * feats * cols,
            bytes_accessed=2 * count * feats * (rows + 3 * cols) + 12 * rows * cols,
            transcendentals=0,
        ),
        name="project",
    )(place, stats, modulation, *shards, *sources, *extra)


def turn_kernel(count, width, squares_ref, gain_ref, *refs):
    for number in range(count):
        raw_ref, out_ref = refs[number], refs[4 * count + number]
        tables = [ref[...] for ref in refs[count + 3 * number : count + 3 * number + 3]]
        rows, cols = raw_ref.shape
        scale = lax.rsqrt(squares_ref[number : number + 1, :] * (1.0 / width) + epsilon)
        scale = jnp.transpose(jnp.broadcast_to(scale, (HEAD_DIM, rows)))
        for head in range(cols // HEAD_DIM):
            lanes = slice(head * HEAD_DIM, (head + 1) * HEAD_DIM)
            out_ref[:, lanes] = turned(
                raw_ref[:, lanes] * scale, gain_ref[:, lanes], tables, 0
            ).astype(jnp.bfloat16)


def turn(raws, squares, gain, tables, width):
    count = len(raws)
    rows, cols = raws[0].shape
    whole = pl.BlockSpec(memory_space=pltpu.VMEM)
    return pl.pallas_call(
        functools.partial(turn_kernel, count, width),
        in_specs=[whole] * (2 + 4 * count),
        out_specs=[whole] * count,
        out_shape=[jax.ShapeDtypeStruct((rows, cols), jnp.bfloat16)] * count,
        compiler_params=pltpu.CompilerParams(vmem_limit_bytes=VMEM),
        cost_estimate=pl.CostEstimate(flops=0, bytes_accessed=0, transcendentals=0),
        name="turn",
    )(squares, gain, *raws, *[part for table in tables for part in table])


def attend_kernel(places, me_ref, bounds_ref, q_ref, *refs):
    count = len(places)
    pieces, (query_seg_ref, key_seg_ref, factor_ref) = refs[:count], refs[count : count + 3]
    out_ref, keys, values, highest, mixed, sems = refs[count + 3 :]
    me = me_ref[0]
    rows = pieces[0].shape[1]
    low, high = bounds_ref[0], bounds_ref[1]
    first = low * KEY_TILE // rows
    end = (high * KEY_TILE + rows - 1) // rows
    for number, (piece, (kind, at)) in enumerate(zip(pieces, places)):
        owner = me ^ (number % (count // 2))
        held = (keys, values)[kind]
        target = held.at[pl.ds(pl.multiple_of(owner * rows, rows), rows), :]
        sem = sems.at[kind, owner]

        @pl.when((owner >= first) & (owner < end))
        def _(source=piece.at[at], target=target, sem=sem):
            pltpu.make_async_copy(source, target, sem).start()

    def arrive(owner, carry):
        for kind, held in enumerate((keys, values)):
            target = held.at[pl.ds(pl.multiple_of(owner * rows, rows), rows), :]
            pltpu.make_async_copy(pieces[0].at[0], target, sems.at[kind, owner]).wait()
        return carry

    dim = HEAD_DIM
    heads = q_ref.shape[1] // dim
    ones = jnp.ones((KEY_TILE, dim), jnp.bfloat16)
    highest[...] = jnp.full_like(highest, -1e29)
    mixed[...] = jnp.zeros_like(mixed)
    query_seg = jnp.transpose(jnp.broadcast_to(query_seg_ref[...], (dim, rows)))
    times = KEY_TILE // dim

    def step(block, carry):
        begin = jnp.where(block == low, first, (block * KEY_TILE + rows - 1) // rows)
        lax.fori_loop(begin, ((block + 1) * KEY_TILE + rows - 1) // rows, arrive, 0)
        where = pl.ds(pl.multiple_of(block * KEY_TILE, KEY_TILE), KEY_TILE)
        same = jnp.concatenate([query_seg] * times, axis=1) == key_seg_ref[block]
        factor = factor_ref[block]
        for head in range(heads):
            cols = slice(head * dim, (head + 1) * dim)
            scores = lax.dot_general(
                q_ref[:, cols],
                keys[where, cols],
                (((1,), (1,)), ((), ())),
                preferred_element_type=jnp.float32,
            )
            scores = jnp.where(same, scores * factor, -1e30)
            former = highest[head]
            newest = jnp.maximum(former, jnp.max(scores, axis=1, keepdims=True))
            highest[head] = newest
            weights = jnp.exp2(scores - jnp.concatenate([newest] * times, axis=1))
            weights = weights.astype(jnp.bfloat16)
            right = jnp.concatenate([values[where, cols], ones], axis=1)
            part = jnp.dot(weights, right, preferred_element_type=jnp.float32)
            shrink = jnp.exp2(former - newest)
            mixed[head, :, :dim] = mixed[head, :, :dim] * shrink + part[:, :dim]
            mixed[head, :, dim:] = mixed[head, :, dim:] * shrink + part[:, dim:]
        return carry

    lax.fori_loop(low, high, step, 0)
    for head in range(heads):
        out_ref[:, head * dim : (head + 1) * dim] = (
            mixed[head, :, :dim] / mixed[head, :, dim:]
        ).astype(out_ref.dtype)


def key_bounds(query_seg, segment_ids):
    low = jnp.sum(segment_ids < query_seg[0], dtype=jnp.int32)
    high = jnp.sum(segment_ids <= query_seg[-1], dtype=jnp.int32)
    return jnp.stack([low // KEY_TILE, (high + KEY_TILE - 1) // KEY_TILE])


def attend(query, keys, values, me, bounds, query_seg, key_seg, factor):
    rows, cols = query.shape
    pieces = [array for array, _ in keys + values]
    places = tuple((0, at) for _, at in keys) + tuple((1, at) for _, at in values)
    count = len(pieces)
    tokens = key_seg.shape[0] * KEY_TILE
    dim = HEAD_DIM
    heads = cols // dim
    smem = pl.BlockSpec(memory_space=pltpu.SMEM)
    whole = pl.BlockSpec(memory_space=pltpu.VMEM)
    return pl.pallas_call(
        functools.partial(attend_kernel, places),
        in_specs=[smem, smem, whole] + [pl.BlockSpec(memory_space=pl.ANY)] * count + [whole] * 3,
        out_specs=whole,
        scratch_shapes=[
            pltpu.VMEM((tokens, cols), jnp.bfloat16),
            pltpu.VMEM((tokens, cols), jnp.bfloat16),
            pltpu.VMEM((heads, rows, dim), jnp.float32),
            pltpu.VMEM((heads, rows, 2 * dim), jnp.float32),
            pltpu.SemaphoreType.DMA((2, count // 2)),
        ],
        out_shape=jax.ShapeDtypeStruct((rows, cols), jnp.bfloat16),
        compiler_params=pltpu.CompilerParams(vmem_limit_bytes=VMEM),
        cost_estimate=pl.CostEstimate(
            flops=2 * rows * tokens * cols,
            bytes_accessed=4 * tokens * cols + 4 * rows * cols,
            transcendentals=rows * tokens * heads // 2,
        ),
        name="attend",
    )(me.reshape(1), bounds, query, *pieces, query_seg, key_seg, factor)


def pages_kernel(places, me_ref, page_ref, *refs):
    count = len(places)
    pieces, rest = refs[:count], refs[count:]
    scale_ref, (out_refs, held, sems) = (rest[0] if len(rest) == 5 else None), (
        rest[-4:-2],
        rest[-2],
        rest[-1],
    )
    me = me_ref[0]
    wanted = held.shape[0]
    per_block = pieces[0].shape[1] // PAGE
    waits = []
    for number in range(wanted):
        page = page_ref[number]
        rows = pl.ds(pl.multiple_of((page % per_block) * PAGE, PAGE), PAGE)
        target, sem = held.at[number], sems.at[number]
        for owner, (piece, at) in enumerate(zip(pieces, places)):

            @pl.when((page // per_block) == (me ^ owner))
            def _(source=piece.at[at, rows, :], target=target, sem=sem):
                pltpu.make_async_copy(source, target, sem).start()

        waits.append(pltpu.make_async_copy(pieces[0].at[0, pl.ds(0, PAGE), :], target, sem))
    for number in range(wanted):
        waits[number].wait()
        each = wanted // 2
        out_ref = out_refs[number // each].at[number % each]
        if scale_ref is None:
            out_ref[...] = held[number]
            continue
        scale = jnp.transpose(jnp.broadcast_to(scale_ref[page_ref[number]], (HEAD_DIM, PAGE)))
        for start in range(0, held.shape[2], HEAD_DIM):
            lanes = slice(start, start + HEAD_DIM)
            page = held[number, :, lanes].astype(jnp.float32) * scale
            out_ref[:, lanes] = page.astype(jnp.bfloat16)


def pick_pages(pieces, me, pages, scale):
    _, rows, cols = pieces[0][0].shape
    wanted = pages.shape[0]
    smem = pl.BlockSpec(memory_space=pltpu.SMEM)
    whole = pl.BlockSpec(memory_space=pltpu.VMEM)
    extra = [] if scale is None else [scale]
    return pl.pallas_call(
        functools.partial(pages_kernel, tuple(at for _, at in pieces)),
        in_specs=[smem, smem]
        + [pl.BlockSpec(memory_space=pl.ANY)] * len(pieces)
        + [whole] * len(extra),
        out_specs=[whole] * 2,
        out_shape=[jax.ShapeDtypeStruct((wanted // 2, PAGE, cols), jnp.bfloat16)] * 2,
        scratch_shapes=[
            pltpu.VMEM((wanted, PAGE, cols), jnp.bfloat16),
            pltpu.SemaphoreType.DMA((wanted,)),
        ],
        compiler_params=pltpu.CompilerParams(vmem_limit_bytes=VMEM),
        cost_estimate=pl.CostEstimate(flops=0, bytes_accessed=0, transcendentals=0),
        name="pick_pages",
    )(me.reshape(1), pages, *[array for array, _ in pieces], *extra)


def own_pages(page_table, start, count):
    page_total = page_table.shape[0]
    inverse = (
        jnp.zeros((page_total,), jnp.int32)
        .at[page_table]
        .set(jnp.arange(page_total, dtype=jnp.int32))
    )
    return lax.dynamic_slice_in_dim(inverse, start, count, 0)


def whole_heads(ring, hidden, modulation, weights, gains, positions, segment_ids, page_table):
    tok_rows = hidden.shape[0]
    me = lax.axis_index("row")
    full_rows = lax.all_gather(hidden, "col", axis=1, tiled=True)
    modulated = modulate(full_rows.astype(jnp.float32), modulation)
    width = full_rows.shape[1]
    raws = [
        jnp.dot(
            modulated,
            lax.all_gather(weight, "row", axis=0, tiled=True),
            preferred_element_type=jnp.float32,
        )
        for weight in weights
    ]
    squares = lax.psum(tuple(jnp.sum(raw * raw, axis=1) for raw in raws[:2]), "col")
    tables = rotary_lanes(positions, HEAD_DIM)
    query, key = [
        turn([raw], total[None], gain[None], [tables], width)[0]
        for raw, total, gain in zip(raws, squares, gains)
    ]
    held = lax.all_gather(jnp.stack([key, raws[2].astype(jnp.bfloat16)]), "row", axis=0)
    keys, values = [[(held[number], kind) for number in range(ring)] for kind in range(2)]
    none = jnp.zeros((), jnp.int32)
    query_seg = lax.dynamic_slice_in_dim(segment_ids, me * tok_rows, tok_rows, 0)
    key_seg = segment_ids.astype(jnp.float32).reshape(-1, 1, KEY_TILE)
    attended = attend(
        query,
        keys,
        values,
        none,
        key_bounds(query_seg, segment_ids),
        query_seg.astype(jnp.float32)[None, :],
        key_seg,
        jnp.full_like(key_seg, HEAD_DIM ** (-0.5) * LOG2E),
    )
    count = tok_rows // PAGE
    pages = own_pages(page_table, me * count, count)
    pages = jnp.concatenate([pages, pages])
    picked = [pick_pages(pieces, none, pages, None)[0] for pieces in (keys, values)]
    return attended, jnp.stack(picked)


def split_heads(ring, ranks, hidden, modulation, weights, gains, positions, segment_ids, page_table):
    tok_rows, shard = hidden.shape
    width = ranks * shard
    me = lax.axis_index("row")
    rank = lax.axis_index("col")
    top = ring // 2
    half = me // top
    cols = weights[0].shape[1] // 2
    hops = []
    bit = top // 2
    while bit:
        hops.append(bit)
        bit //= 2

    def swap(value, bit):
        return lax.ppermute(value, "row", [(i, i ^ bit) for i in range(ring)])

    def across(value, step):
        return lax.ppermute(value, "col", [(c, c ^ step) for c in range(ranks)])

    def spread(blocks, bits):
        for bit in bits:
            blocks.update({number | bit: swap(blocks[number], bit) for number in list(blocks)})
        return blocks

    def in_order(mine, other, axis):
        return jnp.where(
            half == 0,
            jnp.concatenate([mine, other], axis=axis),
            jnp.concatenate([other, mine], axis=axis),
        )

    hidden_all = lax.all_gather(hidden, "col", axis=0)
    w_query, w_key, w_value = weights
    ordered = (w_key, w_value, w_query)
    (send_pair,) = cut(ordered, half, (((0, True), (1, True)),))
    own, send_single = cut(ordered, half, (((0, False), (1, False), (2, False)), ((2, True),)))
    first, rest_hops = hops[0], hops[1:]
    pair, single = swap(send_pair, top), swap(send_single, top)
    next_own = swap(own, first)
    own_blocks = spread({0: own}, rest_hops)

    rows = hidden.astype(jnp.float32)
    local_mean = jnp.mean(rows, axis=1)
    local_square = jnp.sum(jnp.square(rows - local_mean[:, None]), axis=1)
    stats = jnp.stack([local_mean, local_square])
    all_stats = [stats] + [across(stats, step) for step in range(1, ranks)]
    average = sum(part[0] for part in all_stats) / ranks
    variance = (
        sum(part[1] + shard * jnp.square(part[0] - average) for part in all_stats) / width
    )
    small = jnp.concatenate(
        [jnp.stack([average, lax.rsqrt(variance + epsilon)]), positions.astype(jnp.float32)]
    )
    small_other = swap(small, top)
    moved = (pair, single, next_own, own_blocks, small, small_other)
    moved, hidden_late = lax.optimization_barrier((moved, hidden))
    pair, single, next_own, own_blocks, small, small_other = moved

    next_single = swap(single, first)
    other_rows = swap(hidden_late, top)
    pair_blocks = spread({0: pair}, rest_hops)
    single_blocks = spread({0: single}, rest_hops)
    next_own_blocks = spread({0: next_own}, rest_hops)
    early = tok_rows * 11 // 24 // 16 * 16
    sent = jnp.concatenate(
        [
            lax.dynamic_slice(hidden_all, (rank ^ step, early, 0), (1, tok_rows - early, shard))
            for step in range(1, ranks)
        ]
    ).reshape(-1, shard)
    moved = (next_single, other_rows, pair_blocks, single_blocks, next_own_blocks, sent)
    plain = (small, small_other, segment_ids, page_table, gains)
    moved, hidden_all, plain = lax.optimization_barrier((moved, hidden_all, plain))
    next_single, other_rows, pair_blocks, single_blocks, next_own_blocks, sent = moved
    small, small_other, segment_ids, page_table, gains = plain

    rest = swap(sent, top)
    next_pair = swap(pair_blocks[0], first)
    early_shards = [across(other_rows[:early], step) for step in range(1, ranks)]
    sources, spots = [], [None] * ring
    for number in own_blocks:
        for offset, whole in ((0, own_blocks), (first, next_own_blocks)):
            spots[number | offset] = tuple((len(sources), m) for m in range(3))
            sources.append(whole[number])
        at = len(sources)
        spots[number | top] = ((at, 0), (at, 1), (at + 1, 0))
        sources.extend([pair_blocks[number], single_blocks[number]])
    here = tuple(number for number in range(ring) if spots[number] is not None)
    late = tuple(number for number in range(ring) if spots[number] is None)
    own_parts = ((tok_rows, (0,), True),)
    place = jnp.stack([me, rank]).astype(jnp.int32)
    (partial,) = project(
        place,
        small[:2],
        modulation,
        own_parts,
        here,
        [hidden_all],
        tuple(spots),
        list(sources),
        None,
        None,
    )
    tables = [rotary_lanes(part[2:], HEAD_DIM) for part in (small, small_other)]
    q_gain, k_gain = [
        lax.dynamic_slice_in_dim(gain, half * cols, cols, 0)[None, :] for gain in gains
    ]
    count = tok_rows // PAGE
    pages = jnp.concatenate(
        [own_pages(page_table, owner * count, count) for owner in (me ^ top, me)]
    )
    query_segs = [
        lax.dynamic_slice_in_dim(segment_ids, owner * tok_rows, tok_rows, 0)
        for owner in (me, me ^ top)
    ]
    bounds = [key_bounds(seg, segment_ids) for seg in query_segs]
    query_segs = [seg.astype(jnp.float32)[None, :] for seg in query_segs]
    key_seg = segment_ids.astype(jnp.float32).reshape(-1, 1, KEY_TILE)
    prepared = (tables, q_gain, k_gain, pages, query_segs, key_seg, bounds)
    moved = (next_pair, next_single, rest, early_shards)
    moved, prepared, partial = lax.optimization_barrier((moved, prepared, partial))
    next_pair, next_single, rest, early_shards = moved
    tables, q_gain, k_gain, pages, query_segs, key_seg, bounds = prepared

    next_pair_blocks = spread({0: next_pair}, rest_hops)
    next_single_blocks = spread({0: next_single}, rest_hops)
    for number in own_blocks:
        at = len(sources)
        spots[number | top | first] = ((at, 0), (at, 1), (at + 1, 0))
        sources.extend([next_pair_blocks[number], next_single_blocks[number]])
    other_parts = (
        (early, (0,) * ranks, False),
        (
            tok_rows - early,
            (early,) + tuple(step * (tok_rows - early) for step in range(ranks - 1)),
            False,
        ),
    )
    late_sources = [part for number in own_blocks for part in (next_pair_blocks[number], next_single_blocks[number])]
    late_spots = list(spots)
    for at, number in enumerate(own_blocks):
        late_spots[number | top | first] = ((2 * at, 0), (2 * at, 1), (2 * at + 1, 0))
    own_query, own_squares, own_held = project(
        place,
        small[:2],
        modulation,
        own_parts,
        late,
        [hidden_all],
        tuple(late_spots),
        late_sources,
        partial,
        (k_gain, *tables[0]),
    )
    own_ahead = swap(own_held, first)
    other_query, other_squares, other_key, other_value = project(
        place,
        small_other[:2],
        modulation,
        other_parts,
        tuple(range(ring)),
        [other_rows] + early_shards + [other_rows] + [rest] * (ranks - 1),
        tuple(spots),
        sources,
        None,
        (k_gain, *tables[1]),
        joint=False,
    )
    value_ahead = swap(other_value, first)

    squares = jnp.stack([own_squares, other_squares])
    squares = squares + swap(squares, top)[::-1]
    bit = 1
    while bit < ranks:
        squares = squares + across(squares, bit)
        bit *= 2
    query = turn([own_query, other_query], squares[:, 1], q_gain, tables, width)
    key_squares = {0: squares[:, 0]}
    key_squares[first] = swap(key_squares[0], first)
    key_ahead = swap(other_key, first)
    key_squares[0], query, own_ahead, value_ahead = lax.optimization_barrier(
        (key_squares[0], query, own_ahead, value_ahead)
    )
    key_squares = spread(key_squares, rest_hops)
    blocks = jnp.stack([key_squares[n % top][n // top] for n in range(ring)])
    scale = lax.rsqrt(blocks / width + epsilon)
    scale = jnp.concatenate(
        [lax.dynamic_slice_in_dim(scale, me ^ owner, 1, 0) for owner in range(ring)]
    )
    factor = (scale * (HEAD_DIM ** (-0.5) * LOG2E)).reshape(-1, 1, KEY_TILE)
    scale = scale.reshape(-1, 1, PAGE)
    held = spread({0: own_held, first: own_ahead}, rest_hops)
    other_values = spread({0: other_value, first: value_ahead}, rest_hops)
    values = [(held[n], 1) for n in range(top)] + [(other_values[n], 0) for n in range(top)]
    values_picked = pick_pages(values, me, pages, None)
    values_other = swap(values_picked[0], top)
    key_ahead, values_other = lax.optimization_barrier((key_ahead, values_other))
    other_keys = spread({0: other_key, first: key_ahead}, rest_hops)
    keys = [(held[n], 0) for n in range(top)] + [(other_keys[n], 0) for n in range(top)]
    keys_picked = pick_pages(keys, me, pages, scale)
    query, keys_picked = lax.optimization_barrier((query, keys_picked))
    keys_other = swap(keys_picked[0], top)

    def attended(number):
        return attend(
            query[number], keys, values, me, bounds[number], query_segs[number], key_seg, factor
        )

    for_other = attended(1)
    query, for_other = lax.optimization_barrier((query, for_other))
    from_other = swap(for_other, top)
    for_me = attended(0)
    page_store = [
        in_order(keys_picked[1], keys_other, -1),
        in_order(values_picked[1], values_other, -1),
    ]
    return in_order(for_me, from_other, -1), jnp.stack(page_store)


def solution(mesh):
    ring, ranks = mesh.shape["row"], mesh.shape["col"]

    def body(
        hidden, modulation, w_query, w_key, w_value, q_gain, k_gain, positions, segment_ids, page_table
    ):
        rest = (
            hidden,
            modulation,
            (w_query, w_key, w_value),
            (q_gain, k_gain),
            positions,
            segment_ids,
            page_table,
        )
        heads = w_query.shape[1] // HEAD_DIM
        feats, shard = w_query.shape[0], hidden.shape[1]
        powers = ring & (ring - 1) == 0 and ranks & (ranks - 1) == 0
        if heads % 2 == 0 and ring >= 8 and powers and feats % 128 == 0 and shard % feats == 0:
            return split_heads(ring, ranks, *rest)
        return whole_heads(ring, *rest)

    in_specs = (
        P("row", "col"),
        P(),
        P("row", "col"),
        P("row", "col"),
        P("row", "col"),
        P("col"),
        P("col"),
        P(None, "row"),
        P(),
        P(),
    )
    out_specs = (P("row", "col"), P(None, "row", None, "col"))
    return jax.shard_map(body, mesh=mesh, in_specs=in_specs, out_specs=out_specs, check_vma=False)
```
